32 devices in a mesh: rep: 2 (over x), seq: 4 (over y, core), fsdp: 4 (over z).
Axes of the slice: x: 2, y: 2, z: 4, core: 2. Of those that a mesh axis runs over, the one named last changes fastest.
Arguments:
- inputs: bfloat16 [8, 1024, 768], P(('rep', 'fsdp'), 'seq'), may hold values from -6 to 6
- expert_choice: int32 [2, 8, 1024, 2], P(None, ('rep', 'fsdp'), 'seq'), may hold values from 0 to 3, all different within a row
- pair_order: int32 [2, 8, 4, 512], P(None, ('rep', 'fsdp'), 'seq'), may hold values from 0 to 511, each once within a row
- norm_gains: bfloat16 [2, 2, 768], P(None, None, ('seq', 'fsdp')), may hold values from 0.099609375 to 1.8984375
- attn_qkv: bfloat16 [2, 768, 2304], P(None, ('seq', 'fsdp')), may hold values from -0.21875 to 0.21875
- attn_out: bfloat16 [2, 768, 768], P(None, ('seq', 'fsdp')), may hold values from -1.25 to 1.25
- router: bfloat16 [2, 768, 4], P(None, ('seq', 'fsdp')), may hold values from -0.109375 to 0.109375
- shared_in: bfloat16 [2, 768, 4096], P(None, ('seq', 'fsdp')), may hold values from -0.21875 to 0.21875
- shared_out: bfloat16 [2, 2048, 768], P(None, ('seq', 'fsdp')), may hold values from -0.125 to 0.125
- expert_in: bfloat16 [2, 4, 768, 4096], P(None, None, ('seq', 'fsdp')), may hold values from -0.21875 to 0.21875
- expert_out: bfloat16 [2, 4, 2048, 768], P(None, None, ('seq', 'fsdp')), may hold values from -0.125 to 0.125
- cotangent: bfloat16 [8, 1024, 768], P(('rep', 'fsdp'), 'seq'), may hold values from -6 to 6
Outputs:
- output: bfloat16 [8, 1024, 768], P(('rep', 'fsdp'), 'seq')
- input_grad: float32 [8, 1024, 768], P(('rep', 'fsdp'), 'seq')
- grad_norm_gains: float32 [2, 2, 768], P(None, None, ('seq', 'fsdp'))
- grad_attn_qkv: float32 [2, 768, 2304], P(None, ('seq', 'fsdp'))
- grad_attn_out: float32 [2, 768, 768], P(None, ('seq', 'fsdp'))
- grad_router: float32 [2, 768, 4], P(None, ('seq', 'fsdp'))
- grad_shared_in: float32 [2, 768, 4096], P(None, ('seq', 'fsdp'))
- grad_shared_out: float32 [2, 2048, 768], P(None, ('seq', 'fsdp'))
- grad_expert_in: float32 [2, 4, 768, 4096], P(None, None, ('seq', 'fsdp'))
- grad_expert_out: float32 [2, 4, 2048, 768], P(None, None, ('seq', 'fsdp'))
The draws below stay inside these ranges and needn't reach their ends.
Inputs may be any that keep to these rules, and one draw needn't show every extreme that they name: `expert_choice`: each token's two choices in a layer are different experts. `pair_order`: each row lists each of the 512 pairs of one block once.
All inputs are finite; a program needn't handle non-finite values.
Results may differ from the reference program's by a relative error of at most 0.03.
Values may be sent and summed in bfloat16 or wider, within the bound.
A program may use at most 320 MiB of HBM per device.

```python
import jax
import jax.numpy as jnp
from jax import lax

D = 768
HEADS = 12
HEAD_DIM = 64
FF = 2048
EXPERTS = 4
LAYERS = 2
TOK_DEV = 256
PAIRS = 512
CAP = 144
SEQ_BLOCKS = 4
LENGTH = 1024
SEQUENCES = 8


def block_levels(stream_key, shape, pieces, low, top_value):
    level = 1.0
    for dim, shards_of in pieces:
        heights = jax.random.uniform(jax.random.fold_in(jax.random.fold_in(stream_key, 6), dim), (shards_of,), jnp.float32, low / len(pieces), top_value / len(pieces))
        level = level * jnp.repeat(jnp.exp(heights), shape[dim] // shards_of).reshape((-1,) + (1,) * (len(shape) - 1 - dim))
    return level


def picks_of(key, rows, amount, top, lift):
    sequence = jax.random.permutation(jax.random.fold_in(key, 1), amount)
    boost = sequence
    for power in range(3):
        boost = boost * boost // amount
    boost = boost * lift // amount
    tickets = jax.random.randint(jax.random.fold_in(key, 2), (rows, amount), 0, 4096) + boost
    holders = jax.random.permutation(jax.random.fold_in(key, 3), rows)[jnp.arange(amount) % rows]
    tickets = jnp.where(jnp.arange(rows)[:, None] == holders[None, :], 1 << 14, tickets)
    merit = tickets * amount + jnp.arange(amount)
    return lax.top_k(merit.astype(jnp.int32), top)[1].astype(jnp.int32)


def centred(own_key, shape, spread, most, shards=(), kind=jnp.bfloat16):
    factor_of = block_levels(own_key, shape, shards, -0.22, 0.18) if shards else 1.0
    values = jax.random.normal(own_key, shape, jnp.float32) * spread * factor_of
    return jnp.minimum(jnp.maximum(values, -most), most).astype(kind)


def setup_inputs(seed: int = 0) -> dict:
    key_list = jax.random.split(jax.random.key(seed), 13)
    return {
        "inputs": centred(key_list[0], (SEQUENCES, LENGTH, D), 1.0, 6.0, ((0, 8), (1, 4))),
        "expert_choice": picks_of(key_list[1], LAYERS * SEQUENCES * LENGTH, EXPERTS, 2, 8192).reshape((LAYERS, SEQUENCES, LENGTH, 2)),
        "pair_order": jax.vmap(lambda own: jax.random.permutation(own, PAIRS))(jax.random.split(key_list[2], LAYERS * SEQUENCES * SEQ_BLOCKS)).reshape((LAYERS, SEQUENCES, SEQ_BLOCKS, PAIRS)).astype(jnp.int32),
        "norm_gains": jnp.clip(1.0 + 0.18 * jax.random.normal(key_list[3], (LAYERS, 2, D), jnp.float32), 0.099609375, 1.8984375).astype(jnp.bfloat16),
        "attn_qkv": centred(key_list[4], (LAYERS, D, 3 * D), D ** -0.5, 0.21875, ((1, 16),)),
        "attn_out": centred(key_list[5], (LAYERS, D, D), (D // 32) ** -0.5, 1.25, ((1, 16),)),
        "router": centred(key_list[6], (LAYERS, D, EXPERTS), (4 * D) ** -0.5, 0.109375, ((1, 16),)),
        "shared_in": centred(key_list[7], (LAYERS, D, 2 * FF), D ** -0.5, 0.21875, ((1, 16),)),
        "shared_out": centred(key_list[8], (LAYERS, FF, D), FF ** -0.5, 0.125, ((1, 16),)),
        "expert_in": centred(key_list[9], (LAYERS, EXPERTS, D, 2 * FF), D ** -0.5, 0.21875, ((2, 16),)),
        "expert_out": centred(key_list[10], (LAYERS, EXPERTS, FF, D), FF ** -0.5, 0.125, ((2, 16),)),
        "cotangent": centred(key_list[11], (SEQUENCES, LENGTH, D), 1.0, 6.0, ((0, 8), (1, 4))),
    }


epsilon = 1e-06
masked_value = -1e+30
highest = lax.Precision.HIGHEST

@jax.custom_vjp
def low(v):
    return lax.optimization_barrier(v.astype(jnp.bfloat16)).astype(jnp.float32)

@jax.custom_vjp
def low_back(v):
    return v

def low_keep(v):
    return (low(v), None)

def low_pass(kept, grad):
    return (grad,)

def back_keep(v):
    return (v, None)

def back_low(kept, grad):
    return (low(grad),)
low.defvjp(low_keep, low_pass)
low_back.defvjp(back_keep, back_low)

def rms_norm(hidden_state, gain_row):
    return hidden_state * lax.rsqrt(lax.optimization_barrier(jnp.mean(hidden_state * hidden_state, -1, keepdims=True)) + epsilon) * gain_row

def rotary(length_here):
    half_dim = HEAD_DIM // 2
    inverse = jnp.exp(-jnp.log(10000.0) * jnp.arange(half_dim, dtype=jnp.float32) * 2.0 / HEAD_DIM)
    position = jnp.arange(length_here, dtype=jnp.int32).astype(jnp.float32)
    angle = position[:, None] * inverse[None, :]
    return (jnp.cos(angle)[:, None, :], jnp.sin(angle)[:, None, :])

def rotate(heads_in, cosine, sine_table):
    half_dim = heads_in.shape[-1] // 2
    first_half = heads_in[..., :half_dim]
    second_half = heads_in[..., half_dim:]
    return jnp.concatenate([first_half * cosine - second_half * sine_table, second_half * cosine + first_half * sine_table], -1)

def routing(choices_here, order_here):
    tokens_here = choices_here.shape[0]
    pair_expert = choices_here.reshape(-1).astype(jnp.int32)
    placed = pair_expert[order_here]
    onehot = (placed[:, None] == jnp.arange(EXPERTS, dtype=jnp.int32)[None, :]).astype(jnp.int32)
    before = (jnp.cumsum(onehot, 0) - onehot).astype(jnp.int32)
    slot_placed = lax.optimization_barrier(jnp.sum(before * onehot, 1)).astype(jnp.int32)
    slot_pair = jnp.zeros((2 * tokens_here,), jnp.int32).at[order_here].set(slot_placed)
    kept = slot_pair < CAP
    destination = jnp.where(kept, pair_expert * CAP + slot_pair, EXPERTS * CAP).astype(jnp.int32)
    row_pair = jnp.full((EXPERTS * CAP,), 2 * tokens_here, jnp.int32).at[destination].set(jnp.arange(2 * tokens_here, dtype=jnp.int32), mode='drop')
    return (kept.reshape(tokens_here, 2), destination, row_pair)

def expert_block(normed, logits, choices_here, order_here, weight_first, weight_second):
    tokens_here = normed.shape[0]
    kept, destination, row_pair = routing(choices_here, order_here)
    gates = jax.nn.softmax(jnp.take_along_axis(logits, choices_here, 1), -1)
    padded = jnp.concatenate([normed, jnp.zeros((1, D), normed.dtype)], 0)
    buffer_rows = padded[row_pair // 2].reshape(EXPERTS, CAP, D)
    joint = low_back(jnp.einsum('ecd,edf->ecf', buffer_rows, weight_first, precision=highest))
    hidden_rows = low(jax.nn.silu(joint[..., :FF]) * joint[..., FF:])
    yields = low_back(jnp.einsum('ecf,efd->ecd', hidden_rows, weight_second, precision=highest))
    flat = jnp.concatenate([yields.reshape(EXPERTS * CAP, D), jnp.zeros((1, D), yields.dtype)], 0)
    gathered = flat[destination].reshape(tokens_here, 2, D)
    scaled = gates * kept.astype(gates.dtype)
    return lax.optimization_barrier(jnp.sum(gathered * scaled[..., None], 1))

def layer_apply(hidden_state, choices_here, orders_here, layer_weights, cosine, sine_table, visible):
    gain_pair, qkv_weight, out_weight, router_weight, shared_first, shared_second, expert_first, expert_second = layer_weights
    length_here = hidden_state.shape[0]
    head_shape = (length_here, HEADS, HEAD_DIM)
    normed_first = low(rms_norm(hidden_state, gain_pair[0]))
    joint_qkv = low_back(jnp.dot(normed_first, qkv_weight, precision=highest))
    queries = low(rotate(joint_qkv[:, :D].reshape(head_shape), cosine, sine_table))
    keys_all = low(rotate(joint_qkv[:, D:2 * D].reshape(head_shape), cosine, sine_table))
    values_all = low(joint_qkv[:, 2 * D:].reshape(head_shape))
    scores = low_back(jnp.einsum('qhd,khd->hqk', queries, keys_all, precision=highest) * HEAD_DIM ** (-0.5))
    scores = jnp.where(visible[None], scores, masked_value)
    attention = low(jax.nn.softmax(scores, -1))
    attended = jnp.einsum('hqk,khd->qhd', attention, values_all, precision=highest).reshape(length_here, D)
    attended = low(low_back(attended))
    middle = hidden_state + low_back(jnp.dot(attended, out_weight, precision=highest))
    normed_second = low(rms_norm(middle, gain_pair[1]))
    logits = low_back(jnp.dot(normed_second, router_weight, precision=highest))
    joint_shared = low_back(jnp.dot(normed_second, shared_first, precision=highest))
    hidden_shared = low(jax.nn.silu(joint_shared[:, :FF]) * joint_shared[:, FF:])
    branch_shared = low_back(jnp.dot(hidden_shared, shared_second, precision=highest))
    mixture = jax.vmap(expert_block, in_axes=(0, 0, 0, 0, None, None))(normed_second.reshape(SEQ_BLOCKS, TOK_DEV, D), logits.reshape(SEQ_BLOCKS, TOK_DEV, EXPERTS), choices_here.reshape(SEQ_BLOCKS, TOK_DEV, 2), orders_here, expert_first, expert_second).reshape(length_here, D)
    return middle + branch_shared + mixture

def reference(inputs, expert_choice, pair_order, norm_gains, attn_qkv, attn_out, router, shared_in, shared_out, expert_in, expert_out, cotangent):
    weights = (norm_gains.astype(jnp.float32), attn_qkv.astype(jnp.float32), attn_out.astype(jnp.float32), router.astype(jnp.float32), shared_in.astype(jnp.float32), shared_out.astype(jnp.float32), expert_in.astype(jnp.float32), expert_out.astype(jnp.float32))
    cosine, sine_table = rotary(LENGTH)
    position = jnp.arange(LENGTH, dtype=jnp.int32)
    visible = position[:, None] >= position[None, :]

    def forward(sequence_in, weight_set, choices_here, orders_here):
        hidden_state = sequence_in
        for layer_index in range(LAYERS):
            layer_weights = tuple((member[layer_index] for member in weight_set))
            hidden_state = layer_apply(hidden_state, choices_here[layer_index], orders_here[layer_index], layer_weights, cosine, sine_table, visible)
        return hidden_state

    def per_sequence(totals, items):
        sequence_in, choices_here, orders_here, cotangent_here = items
        result, pullback = jax.vjp(lambda state_in, weight_set: forward(state_in, weight_set, choices_here, orders_here), sequence_in.astype(jnp.float32), weights)
        state_grad, weight_grads = pullback(cotangent_here.astype(jnp.float32))
        totals = tuple((total + added_grad for total, added_grad in zip(totals, weight_grads)))
        return (totals, (result.astype(jnp.bfloat16), state_grad))
    zeros_init = tuple((jnp.zeros(member.shape, jnp.float32) for member in weights))
    totals, (outputs, state_grads) = lax.scan(per_sequence, zeros_init, (inputs, jnp.moveaxis(expert_choice, 1, 0), jnp.moveaxis(pair_order, 1, 0), cotangent))
    return (outputs, state_grads, totals[0], totals[1], totals[2], totals[3], totals[4], totals[5], totals[6], totals[7])
```

```python
import functools

import jax
import jax.numpy as jnp
from jax import lax
from jax.experimental import pallas as pl
from jax.experimental.pallas import tpu as pltpu
from jax.sharding import PartitionSpec as P

D = 768
HEADS = 12
HEAD_DIM = 64
FF = 2048
EXPERTS = 4
LAYERS = 2
CAP = 144
EPS = 1e-06
MASKED = -1e30
SEQ = 4
FSDP = 4
HEADS_DEV = HEADS // SEQ
COLS = HEADS_DEV * HEAD_DIM
FF_DEV = FF // SEQ
FF_CORE = FF // 2
SLOTS = EXPERTS * CAP
bf16 = jnp.bfloat16
f32 = jnp.float32
MESH = pl.DeviceIdType.MESH

SIB = [(i, i ^ 1) for i in range(SEQ)]
FAR = [(i, i ^ 2) for i in range(SEQ)]


def dot(a, b):
    return jnp.dot(a, b, preferred_element_type=f32)


def dot_nt(a, b):
    return lax.dot_general(a, b, (((1,), (1,)), ((), ())), preferred_element_type=f32)


def dot_tn(a, b):
    return lax.dot_general(a, b, (((0,), (0,)), ((), ())), preferred_element_type=f32)


def exchange_kernel(x, o, send, recv, local_sem):
    z = lax.axis_index("fsdp")
    barrier = pltpu.get_barrier_semaphore()
    for k in (1, 2, 3):
        pl.semaphore_signal(
            barrier, inc=1, device_id={"fsdp": lax.rem(z + k, FSDP)}, device_id_type=MESH
        )
    pl.semaphore_wait(barrier, 3)
    copies = []
    for k in (2, 1, 3):
        peer = lax.rem(z + k, FSDP)
        copy = pltpu.make_async_remote_copy(
            src_ref=x.at[peer],
            dst_ref=o.at[z],
            send_sem=send.at[k],
            recv_sem=recv.at[k],
            device_id={"fsdp": peer},
            device_id_type=MESH,
        )
        copy.start()
        copies.append(copy)
    own = pltpu.make_async_copy(x.at[z], o.at[z], local_sem)
    own.start()
    own.wait()
    for copy in copies:
        copy.wait()


def exchange(x, cid):
    return pl.pallas_call(
        exchange_kernel,
        out_shape=jax.ShapeDtypeStruct(x.shape, x.dtype),
        in_specs=[pl.BlockSpec(memory_space=pltpu.VMEM)],
        out_specs=pl.BlockSpec(memory_space=pltpu.VMEM),
        scratch_shapes=[
            pltpu.SemaphoreType.DMA((4,)),
            pltpu.SemaphoreType.DMA((4,)),
            pltpu.SemaphoreType.DMA,
        ],
        compiler_params=pltpu.CompilerParams(
            collective_id=cid, has_side_effects=True, vmem_limit_bytes=32 << 20
        ),
    )(x)


def gather_seq(x):
    far = lax.ppermute(x, "seq", FAR)
    both = lax.ppermute(jnp.stack([x, far]), "seq", SIB)
    return jnp.concatenate([x, both[0], far, both[1]], 0)


def scatter_seq(partial):
    blocks = partial.astype(bf16).reshape(4, -1, partial.shape[-1])
    kept = partial.reshape(4, -1, partial.shape[-1])
    near = lax.ppermute(jnp.stack([blocks[1], blocks[3]]), "seq", SIB).astype(f32)
    away = (kept[2] + near[1]).astype(bf16)
    return kept[0] + near[0] + lax.ppermute(away, "seq", FAR).astype(f32)


def rep_pairs(reps):
    return [(i, i ^ 1) for i in range(reps)]


def rep_rest(x, reps):
    bit = 2
    while bit < reps:
        x = x + lax.ppermute(x, "rep", [(i, i ^ bit) for i in range(reps)])
        bit *= 2
    return x


def scatter_rep(x, reps, r):
    half = lax.rem(r, 2)
    mine = lax.dynamic_index_in_dim(x, half, 0, False)
    other = lax.dynamic_index_in_dim(x, 1 - half, 0, False)
    got = lax.ppermute(other, "rep", rep_pairs(reps))
    return rep_rest((mine.astype(f32) + got.astype(f32)).astype(bf16), reps)


def gather_rep(x, reps, r, axis):
    half = lax.rem(r, 2)
    got = lax.ppermute(x, "rep", rep_pairs(reps))
    return jnp.stack([jnp.where(half == 0, x, got), jnp.where(half == 0, got, x)], axis)


def absolute(blocks, s):
    return jnp.stack([lax.dynamic_index_in_dim(blocks, s ^ i, 0, False) for i in range(4)])


def fetch_dense(qkv, out, first, second):
    columns = jnp.concatenate(
        [
            qkv.reshape(48, 3, 4, COLS).transpose(2, 0, 1, 3).reshape(4, 48, 3 * COLS),
            first.reshape(48, 2, 4, FF_DEV).transpose(2, 0, 1, 3).reshape(4, 48, 2 * FF_DEV),
        ],
        2,
    )
    columns = lax.all_to_all(columns, "seq", split_axis=0, concat_axis=0, tiled=True)
    columns = lax.all_gather(columns, "fsdp", axis=1).reshape(D, -1)
    rows = lax.all_gather(jnp.concatenate([out, second], 0), "fsdp", axis=0)
    return (
        columns[:, : 3 * COLS],
        columns[:, 3 * COLS :],
        rows[:, :48].reshape(COLS, D),
        rows[:, 48:].reshape(FF_DEV, D),
    )


def fetch_expert(first, second, s):
    core = lax.rem(s, 2)
    far = s // 2
    first = lax.all_to_all(first, "fsdp", split_axis=0, concat_axis=0, tiled=True)
    first = first.reshape(4, 48, 2, 2, 2, FF_DEV)
    own = lax.dynamic_index_in_dim(first, core, 4, False).reshape(4, 48, 2 * FF_CORE)
    sent = lax.dynamic_index_in_dim(first, 1 - core, 4, False).reshape(4, 48, 2 * FF_CORE)
    pair = jnp.stack([own, lax.ppermute(sent, "seq", SIB)])
    pair = jnp.concatenate([pair, lax.ppermute(pair, "seq", FAR)], 0)
    first = absolute(pair, s).reshape(D, 2 * FF_CORE)
    second = lax.all_to_all(second, "fsdp", split_axis=0, concat_axis=0, tiled=True)
    other = lax.ppermute(second, "seq", FAR)
    second = jnp.stack([jnp.where(far == 0, second, other), jnp.where(far == 0, other, second)])
    return first, second.reshape(FF_CORE, D)


def return_dense(d_columns, d_rows, s, z, r, reps):
    width = d_columns.shape[1]
    d_columns = d_columns.astype(bf16).reshape(4, 4, 2, 24, width).transpose(2, 1, 0, 3, 4)
    d_columns = scatter_rep(d_columns, reps, r)
    d_columns = lax.psum_scatter(d_columns, "fsdp", scatter_dimension=0)
    d_columns = lax.all_to_all(d_columns, "seq", split_axis=0, concat_axis=0, tiled=True)
    d_columns = gather_rep(d_columns, reps, r, 1).reshape(4, 48, width)
    d_qkv = d_columns[..., : 3 * COLS].reshape(4, 48, 3, COLS).transpose(1, 2, 0, 3)
    d_first = d_columns[..., 3 * COLS :].reshape(4, 48, 2, FF_DEV).transpose(1, 2, 0, 3)
    d_rows = d_rows.astype(bf16).reshape(4, 2, 88, D).transpose(1, 0, 2, 3)
    d_rows = scatter_rep(d_rows, reps, r)
    d_rows = lax.psum_scatter(d_rows, "fsdp", scatter_dimension=0)
    d_rows = gather_rep(d_rows, reps, r, 0).reshape(176, D)
    return (
        d_qkv.reshape(48, 3 * D).astype(f32),
        d_rows[:48].astype(f32),
        d_first.reshape(48, 2 * FF).astype(f32),
        d_rows[48:].astype(f32),
    )


def return_expert(d_first, d_second, s, r, reps):
    core = lax.rem(s, 2)
    far = s // 2
    d_first = d_first.astype(bf16).reshape(2, 2, 4, 48, 2, 2, FF_DEV)
    d_first = scatter_rep(d_first.transpose(5, 0, 1, 2, 3, 4, 6), reps, r)
    mine = lax.dynamic_index_in_dim(d_first, far, 0, False)
    other = lax.dynamic_index_in_dim(d_first, 1 - far, 0, False)
    d_first = mine + lax.ppermute(other, "seq", FAR)
    own = lax.dynamic_index_in_dim(d_first, core, 0, False)
    sent = lax.dynamic_index_in_dim(d_first, 1 - core, 0, False)
    got = lax.ppermute(sent, "seq", SIB)
    d_first = jnp.stack([jnp.where(core == 0, own, got), jnp.where(core == 0, got, own)], 3)
    d_first = lax.all_to_all(d_first, "fsdp", split_axis=0, concat_axis=0, tiled=True)
    d_first = gather_rep(d_first, reps, r, 3).reshape(4, 48, 2 * FF)
    d_second = d_second.astype(bf16).reshape(2, 4, 2, 64, D).transpose(2, 0, 1, 3, 4)
    d_second = scatter_rep(d_second, reps, r)
    mine = lax.dynamic_index_in_dim(d_second, far, 0, False)
    other = lax.dynamic_index_in_dim(d_second, 1 - far, 0, False)
    d_second = mine + lax.ppermute(other, "seq", FAR)
    d_second = lax.all_to_all(d_second, "fsdp", split_axis=0, concat_axis=0, tiled=True)
    d_second = gather_rep(d_second, reps, r, 1).reshape(4, 128, D)
    return d_first.astype(f32), d_second.astype(f32)


def rms_forward(hidden_state, gain_row):
    factor = lax.rsqrt(jnp.mean(hidden_state * hidden_state, -1, keepdims=True) + EPS)
    return hidden_state * factor * gain_row, factor


def rms_backward(hidden_state, factor, gain_row, gradient):
    weighted = gradient * gain_row
    inner = jnp.mean(weighted * hidden_state, -1, keepdims=True)
    d_state = factor * weighted - hidden_state * (factor * factor * factor) * inner
    d_gain = jnp.sum(gradient * hidden_state * factor, 0)
    return d_state, d_gain


def swiglu(joint):
    half = joint.shape[-1] // 2
    return (jax.nn.silu(joint[..., :half]) * joint[..., half:]).astype(bf16)


def swiglu_back(joint, gradient):
    half = joint.shape[-1] // 2
    gate, up = joint[..., :half], joint[..., half:]
    sig = jax.nn.sigmoid(gate)
    d_gate = gradient * up * sig * (1.0 + gate * (1.0 - sig))
    d_up = gradient * gate * sig
    return jnp.concatenate([d_gate, d_up], -1).astype(bf16)


def routing(choices, order):
    tokens = choices.shape[0]
    pairs = 2 * tokens
    flat = choices.reshape(-1)
    ids = jnp.arange(pairs, dtype=jnp.int32)
    place = (order[:, None] == ids[None, :]).astype(bf16)
    experts = (flat[:, None] == jnp.arange(EXPERTS, dtype=jnp.int32)[None, :]).astype(bf16)
    placed = dot(place, experts).astype(bf16)
    lower = (ids[:, None] > ids[None, :]).astype(bf16)
    slot_placed = jnp.minimum(jnp.sum(dot(lower, placed) * placed.astype(f32), 1), float(CAP))
    slot = dot_tn(place, slot_placed[:, None].astype(bf16))[:, 0].astype(jnp.int32)
    kept = slot < CAP
    target = jnp.where(kept, flat * CAP + slot, SLOTS).reshape(tokens, 2)
    target = target.T.reshape(-1)
    chosen = (target[None, :] == jnp.arange(SLOTS, dtype=jnp.int32)[:, None]).astype(bf16)
    return kept.reshape(tokens, 2).astype(f32), chosen


def rotate(x, cosine, sine):
    half = HEAD_DIM // 2
    a, b = x[..., :half], x[..., half:]
    return jnp.concatenate([a * cosine - b * sine, b * cosine + a * sine], -1)


def attention(queries, keys, values, visible):
    scores = jnp.einsum("qhd,khd->hqk", queries, keys, preferred_element_type=f32)
    scores = jnp.where(visible[None], scores * HEAD_DIM**-0.5, MASKED)
    top = jnp.max(scores, -1, keepdims=True)
    total = top + jnp.log(jnp.sum(jnp.exp(scores - top), -1, keepdims=True))
    weights = jnp.exp(scores - total).astype(bf16)
    return jnp.einsum("hqk,khd->qhd", weights, values, preferred_element_type=f32), total


def attention_back(queries, keys, values, visible, total, attended, d_attended):
    scale = HEAD_DIM**-0.5
    scores = jnp.einsum("qhd,khd->hqk", queries, keys, preferred_element_type=f32)
    scores = jnp.where(visible[None], scores * scale, MASKED)
    weights = jnp.exp(scores - total)
    delta = jnp.sum(d_attended.astype(f32) * attended, -1).T[..., None]
    d_weights = jnp.einsum("qhd,khd->hqk", d_attended, values, preferred_element_type=f32)
    d_scores = (weights * (d_weights - delta)).astype(bf16)
    d_q = jnp.einsum("hqk,khd->qhd", d_scores, keys, preferred_element_type=f32) * scale
    d_k = jnp.einsum("hqk,qhd->khd", d_scores, queries, preferred_element_type=f32) * scale
    d_v = jnp.einsum("hqk,qhd->khd", weights.astype(bf16), d_attended, preferred_element_type=f32)
    return d_q, d_k, d_v


def layer_forward(layer, h, dense, expert, gains, router, choices, routes, cosine, sine, visible):
    w_qkv, w_first, w_out, w_second = dense
    e_first, e_second = expert
    kept, chosen = routes
    tokens = h.shape[0]
    normed, factor_one = rms_forward(h, gains[0])
    normed_all = gather_seq(normed.astype(bf16))
    joint = dot(normed_all, w_qkv).reshape(-1, 3, HEADS_DEV, HEAD_DIM)
    queries = rotate(joint[:, 0], cosine, sine).astype(bf16)
    keys = rotate(joint[:, 1], cosine, sine).astype(bf16)
    values = joint[:, 2].astype(bf16)
    attended, total = attention(queries, keys, values, visible)
    attended_low = attended.reshape(-1, COLS).astype(bf16)
    middle = h + scatter_seq(dot(attended_low, w_out))
    normed, factor_two = rms_forward(middle, gains[1])
    second = normed.astype(bf16)
    logits = dot(second, router)
    onehot = (choices[..., None] == jnp.arange(EXPERTS, dtype=jnp.int32)).astype(f32)
    gates = jax.nn.softmax(jnp.sum(onehot * logits[:, None, :], -1), -1)
    second_all = gather_seq(second)
    joint_shared = dot(second_all, w_first)
    hidden_shared = swiglu(joint_shared)
    shared_part = dot(hidden_shared, w_second)
    picked = chosen[:, :tokens] + chosen[:, tokens:]
    rows = dot(picked, second).astype(bf16).reshape(EXPERTS, CAP, D)
    rows = exchange(rows, 1 + 4 * layer).reshape(SLOTS, D)
    rows_all = jnp.concatenate([rows, lax.ppermute(rows, "seq", SIB)], 0)
    joint_expert = dot(rows_all, e_first)
    hidden_expert = swiglu(joint_expert)
    produced = dot(hidden_expert, e_second)
    got = lax.ppermute(produced[SLOTS:].astype(bf16), "seq", SIB)
    produced = (produced[:SLOTS] + got.astype(f32)).astype(bf16)
    yields = exchange(produced.reshape(EXPERTS, CAP, D), 2 + 4 * layer).reshape(SLOTS, D)
    gathered = dot_tn(chosen, yields)
    mixture = gates[:, :1] * gathered[:tokens] + gates[:, 1:] * gathered[tokens:]
    result = middle + scatter_seq(shared_part) + mixture
    stored = (
        h, factor_one, normed_all, queries, keys, values, total, attended, attended_low, middle,
        factor_two, second, gates, onehot, second_all, joint_shared, hidden_shared, rows_all,
        joint_expert, hidden_expert, gathered,
    )
    return result, stored


def layer_backward(layer, grad, dense, expert, gains, router, routes, stored, cosine, sine, visible):
    w_qkv, w_first, w_out, w_second = dense
    e_first, e_second = expert
    kept, chosen = routes
    (
        h, factor_one, normed_all, queries, keys, values, total, attended, attended_low, middle,
        factor_two, second, gates, onehot, second_all, joint_shared, hidden_shared, rows_all,
        joint_expert, hidden_expert, gathered,
    ) = stored
    tokens = grad.shape[0]
    scaled = gates * kept
    d_yields = jnp.concatenate([grad * scaled[:, :1], grad * scaled[:, 1:]], 0).astype(bf16)
    d_yields = dot(chosen, d_yields).astype(bf16).reshape(EXPERTS, CAP, D)
    d_rows = exchange(d_yields, 3 + 4 * layer).reshape(SLOTS, D)
    d_rows = jnp.concatenate([d_rows, lax.ppermute(d_rows, "seq", SIB)], 0)
    de_second = dot_tn(hidden_expert, d_rows)
    d_joint = swiglu_back(joint_expert, dot_nt(d_rows, e_second))
    de_first = dot_tn(rows_all, d_joint)
    back = dot_nt(d_joint, e_first)
    got = lax.ppermute(back[SLOTS:].astype(bf16), "seq", SIB)
    back = (back[:SLOTS] + got.astype(f32)).astype(bf16)
    back = exchange(back.reshape(EXPERTS, CAP, D), 4 + 4 * layer).reshape(SLOTS, D)
    picked = chosen[:, :tokens] + chosen[:, tokens:]

    grad_all = gather_seq(grad.astype(bf16))
    d_second_w = dot_tn(hidden_shared, grad_all)
    d_joint_shared = swiglu_back(joint_shared, dot_nt(grad_all, w_second))
    d_first_w = dot_tn(second_all, d_joint_shared)
    d_normed = scatter_seq(dot_nt(d_joint_shared, w_first))

    d_gates = kept * jnp.stack(
        [jnp.sum(grad * gathered[:tokens], -1), jnp.sum(grad * gathered[tokens:], -1)], -1
    )
    d_chosen = gates * (d_gates - jnp.sum(gates * d_gates, -1, keepdims=True))
    d_logits = jnp.sum(d_chosen[..., None] * onehot, 1).astype(bf16)
    d_router = dot_tn(second, d_logits)
    d_normed = d_normed + dot_nt(d_logits, router) + dot_tn(picked, back)
    d_middle, d_gain_two = rms_backward(middle, factor_two, gains[1], d_normed)
    d_middle = grad + d_middle
    middle_all = gather_seq(d_middle.astype(bf16))
    d_out_w = dot_tn(attended_low, middle_all)
    d_attended = dot_nt(middle_all, w_out).astype(bf16).reshape(-1, HEADS_DEV, HEAD_DIM)
    d_q, d_k, d_v = attention_back(queries, keys, values, visible, total, attended, d_attended)
    d_qkv = jnp.stack([rotate(d_q, cosine, -sine), rotate(d_k, cosine, -sine), d_v], 1)
    d_qkv = d_qkv.reshape(-1, 3 * COLS).astype(bf16)
    d_qkv_w = dot_tn(normed_all, d_qkv)
    d_first = scatter_seq(dot_nt(d_qkv, w_qkv))
    d_state, d_gain_one = rms_backward(h, factor_one, gains[0], d_first)
    d_columns = jnp.concatenate([d_qkv_w, d_first_w], 1)
    d_rows_w = jnp.concatenate([d_out_w.reshape(4, 48, D), d_second_w.reshape(4, 128, D)], 1)
    small = jnp.concatenate([jnp.stack([d_gain_one, d_gain_two]), d_router.T], 0)
    return d_middle + d_state, (d_columns, d_rows_w), (de_first, de_second), small


def local(
    reps, inputs, expert_choice, pair_order, norm_gains, attn_qkv, attn_out, router, shared_in,
    shared_out, expert_in, expert_out, cotangent,
):
    r, s, z = lax.axis_index("rep"), lax.axis_index("seq"), lax.axis_index("fsdp")
    tokens = inputs.shape[1]
    position = jnp.concatenate([(s ^ j) * tokens + jnp.arange(tokens, dtype=jnp.int32) for j in range(4)])
    half = HEAD_DIM // 2
    inverse = jnp.exp(-jnp.log(10000.0) * jnp.arange(half, dtype=f32) * 2.0 / HEAD_DIM)
    angle = position.astype(f32)[:, None] * inverse[None, :]
    cosine, sine = jnp.cos(angle)[:, None, :], jnp.sin(angle)[:, None, :]
    visible = position[:, None] >= position[None, :]
    small = jnp.concatenate([norm_gains, router.transpose(0, 2, 1)], 1)
    small = lax.all_gather(small, ("seq", "fsdp"), axis=2, tiled=True)
    gains = small[:, :2].astype(f32)
    routers = small[:, 2:].transpose(0, 2, 1)
    h = inputs[0].astype(f32)
    kept_layers = []
    for layer in range(LAYERS):
        dense = fetch_dense(attn_qkv[layer], attn_out[layer], shared_in[layer], shared_out[layer])
        expert = fetch_expert(expert_in[layer], expert_out[layer], s)
        routes = routing(expert_choice[layer, 0], pair_order[layer, 0, 0])
        h, stored = layer_forward(
            layer, h, dense, expert, gains[layer], routers[layer], expert_choice[layer, 0], routes,
            cosine, sine, visible,
        )
        kept_layers.append((dense, expert, routes, stored))
    output = h.astype(bf16)[None]
    grad = cotangent[0].astype(f32)
    grads = [None] * LAYERS
    smalls = [None] * LAYERS
    for layer in reversed(range(LAYERS)):
        dense, expert, routes, stored = kept_layers[layer]
        grad, d_dense, d_expert, smalls[layer] = layer_backward(
            layer, grad, dense, expert, gains[layer], routers[layer], routes, stored, cosine, sine,
            visible,
        )
        grads[layer] = return_dense(*d_dense, s, z, r, reps) + return_expert(*d_expert, s, r, reps)
    total = lax.psum(jnp.stack(smalls), ("rep", "seq", "fsdp"))
    total = lax.dynamic_slice_in_dim(total, (s * FSDP + z) * 48, 48, 2)
    d_qkv, d_out, d_in, d_so, d_ein, d_eout = (
        jnp.stack([grads[layer][k] for layer in range(LAYERS)]) for k in range(6)
    )
    return (
        output, grad[None], total[:, :2], d_qkv, d_out, total[:, 2:].transpose(0, 2, 1), d_in, d_so,
        d_ein, d_eout,
    )


def solution(mesh):
    tokens = P(("rep", "fsdp"), "seq", None)
    routes = P(None, ("rep", "fsdp"), "seq", None)
    gains = P(None, None, ("seq", "fsdp"))
    dense = P(None, ("seq", "fsdp"), None)
    expert = P(None, None, ("seq", "fsdp"), None)
    in_specs = (
        tokens, routes, routes, gains, dense, dense, dense, dense, dense, expert, expert, tokens,
    )
    out_specs = (tokens, tokens, gains, dense, dense, dense, dense, dense, expert, expert)
    return jax.shard_map(
        functools.partial(local, mesh.shape["rep"]),
        mesh=mesh, in_specs=in_specs, out_specs=out_specs, check_vma=False,
    )
```

```python
import functools

import jax
import jax.numpy as jnp
from jax import lax
from jax.experimental import pallas as pl
from jax.experimental.pallas import tpu as pltpu
from jax.sharding import PartitionSpec as P

D = 768
HEADS = 12
HEAD_DIM = 64
FF = 2048
EXPERTS = 4
LAYERS = 2
CAP = 144
EPS = 1e-06
MASKED = -1e30
SEQ = 4
FSDP = 4
HEADS_DEV = HEADS // SEQ
COLS = HEADS_DEV * HEAD_DIM
FF_DEV = FF // SEQ
FF_CORE = FF // 2
SLOTS = EXPERTS * CAP
bf16 = jnp.bfloat16
f32 = jnp.float32
MESH = pl.DeviceIdType.MESH

SIB = [(i, i ^ 1) for i in range(SEQ)]
FAR = [(i, i ^ 2) for i in range(SEQ)]


def dot(a, b):
    return jnp.dot(a, b, preferred_element_type=f32)


def dot_nt(a, b):
    return lax.dot_general(a, b, (((1,), (1,)), ((), ())), preferred_element_type=f32)


def dot_tn(a, b):
    return lax.dot_general(a, b, (((0,), (0,)), ((), ())), preferred_element_type=f32)


def exchange_kernel(x, o, send, recv, local_sem):
    z = lax.axis_index("fsdp")
    barrier = pltpu.get_barrier_semaphore()
    for k in (1, 2, 3):
        pl.semaphore_signal(
            barrier, inc=1, device_id={"fsdp": lax.rem(z + k, FSDP)}, device_id_type=MESH
        )
    pl.semaphore_wait(barrier, 3)
    copies = []
    for k in (2, 1, 3):
        peer = lax.rem(z + k, FSDP)
        copy = pltpu.make_async_remote_copy(
            src_ref=x.at[peer],
            dst_ref=o.at[z],
            send_sem=send.at[k],
            recv_sem=recv.at[k],
            device_id={"fsdp": peer},
            device_id_type=MESH,
        )
        copy.start()
        copies.append(copy)
    own = pltpu.make_async_copy(x.at[z], o.at[z], local_sem)
    own.start()
    own.wait()
    for copy in copies:
        copy.wait()


def exchange(x, cid):
    return pl.pallas_call(
        exchange_kernel,
        out_shape=jax.ShapeDtypeStruct(x.shape, x.dtype),
        in_specs=[pl.BlockSpec(memory_space=pltpu.VMEM)],
        out_specs=pl.BlockSpec(memory_space=pltpu.VMEM),
        scratch_shapes=[
            pltpu.SemaphoreType.DMA((4,)),
            pltpu.SemaphoreType.DMA((4,)),
            pltpu.SemaphoreType.DMA,
        ],
        compiler_params=pltpu.CompilerParams(
            collective_id=cid, has_side_effects=True, vmem_limit_bytes=32 << 20
        ),
    )(x)


def gather_seq(x, s):
    far = lax.ppermute(x, "seq", FAR)
    both = lax.ppermute(jnp.stack([x, far]), "seq", SIB)
    return absolute(jnp.stack([x, both[0], far, both[1]]), s).reshape(-1, x.shape[-1])


def scatter_seq(partial, s):
    kept = absolute(partial.reshape(4, -1, partial.shape[-1]), s)
    blocks = kept.astype(bf16)
    near = lax.ppermute(jnp.stack([blocks[1], blocks[3]]), "seq", SIB).astype(f32)
    away = (kept[2] + near[1]).astype(bf16)
    return kept[0] + near[0] + lax.ppermute(away, "seq", FAR).astype(f32)


def rep_pairs(reps):
    return [(i, i ^ 1) for i in range(reps)]


def rep_rest(x, reps):
    bit = 2
    while bit < reps:
        x = x + lax.ppermute(x, "rep", [(i, i ^ bit) for i in range(reps)])
        bit *= 2
    return x


def scatter_rep(x, reps, r):
    half = lax.rem(r, 2)
    mine = lax.dynamic_index_in_dim(x, half, 0, False)
    other = lax.dynamic_index_in_dim(x, 1 - half, 0, False)
    got = lax.ppermute(other, "rep", rep_pairs(reps))
    return rep_rest((mine.astype(f32) + got.astype(f32)).astype(bf16), reps)


def gather_rep(x, reps, r, axis):
    half = lax.rem(r, 2)
    got = lax.ppermute(x, "rep", rep_pairs(reps))
    return jnp.stack([jnp.where(half == 0, x, got), jnp.where(half == 0, got, x)], axis)


def absolute(blocks, s):
    return jnp.stack([lax.dynamic_index_in_dim(blocks, s ^ i, 0, False) for i in range(4)])


def return_dense(d_columns, d_rows, s, z, r, reps):
    width = d_columns.shape[1]
    d_columns = d_columns.astype(bf16).reshape(4, 4, 2, 24, width).transpose(2, 1, 0, 3, 4)
    d_columns = scatter_rep(d_columns, reps, r)
    d_columns = lax.psum_scatter(d_columns, "fsdp", scatter_dimension=0)
    d_columns = lax.all_to_all(d_columns, "seq", split_axis=0, concat_axis=0, tiled=True)
    d_columns = gather_rep(d_columns, reps, r, 1).reshape(4, 48, width)
    d_qkv = d_columns[..., : 3 * COLS].reshape(4, 48, 3, COLS).transpose(1, 2, 0, 3)
    d_first = d_columns[..., 3 * COLS :].reshape(4, 48, 2, FF_DEV).transpose(1, 2, 0, 3)
    d_rows = d_rows.astype(bf16).reshape(4, 2, 88, D).transpose(1, 0, 2, 3)
    d_rows = scatter_rep(d_rows, reps, r)
    d_rows = lax.psum_scatter(d_rows, "fsdp", scatter_dimension=0)
    d_rows = gather_rep(d_rows, reps, r, 0).reshape(176, D)
    return (
        d_qkv.reshape(48, 3 * D).astype(f32),
        d_rows[:48].astype(f32),
        d_first.reshape(48, 2 * FF).astype(f32),
        d_rows[48:].astype(f32),
    )


def return_expert(d_first, d_second, s, r, reps):
    core = lax.rem(s, 2)
    far = s // 2
    d_first = d_first.astype(bf16).reshape(2, 2, 4, 48, 2, 2, FF_DEV)
    d_first = scatter_rep(d_first.transpose(5, 0, 1, 2, 3, 4, 6), reps, r)
    mine = lax.dynamic_index_in_dim(d_first, far, 0, False)
    other = lax.dynamic_index_in_dim(d_first, 1 - far, 0, False)
    d_first = mine + lax.ppermute(other, "seq", FAR)
    own = lax.dynamic_index_in_dim(d_first, core, 0, False)
    sent = lax.dynamic_index_in_dim(d_first, 1 - core, 0, False)
    got = lax.ppermute(sent, "seq", SIB)
    d_first = jnp.stack([jnp.where(core == 0, own, got), jnp.where(core == 0, got, own)], 3)
    d_first = lax.all_to_all(d_first, "fsdp", split_axis=0, concat_axis=0, tiled=True)
    d_first = gather_rep(d_first, reps, r, 3).reshape(4, 48, 2 * FF)
    d_second = d_second.astype(bf16).reshape(2, 4, 2, 64, D).transpose(2, 0, 1, 3, 4)
    d_second = scatter_rep(d_second, reps, r)
    mine = lax.dynamic_index_in_dim(d_second, far, 0, False)
    other = lax.dynamic_index_in_dim(d_second, 1 - far, 0, False)
    d_second = mine + lax.ppermute(other, "seq", FAR)
    d_second = lax.all_to_all(d_second, "fsdp", split_axis=0, concat_axis=0, tiled=True)
    d_second = gather_rep(d_second, reps, r, 1).reshape(4, 128, D)
    return d_first.astype(f32), d_second.astype(f32)


def rms_forward(hidden_state, gain_row):
    factor = lax.rsqrt(jnp.mean(hidden_state * hidden_state, -1, keepdims=True) + EPS)
    return hidden_state * factor * gain_row, factor


def rms_backward(hidden_state, factor, gain_row, gradient):
    weighted = gradient * gain_row
    inner = jnp.mean(weighted * hidden_state, -1, keepdims=True)
    d_state = factor * weighted - hidden_state * (factor * factor * factor) * inner
    d_gain = jnp.sum(gradient * hidden_state * factor, 0)
    return d_state, d_gain


def swiglu(joint):
    half = joint.shape[-1] // 2
    return (jax.nn.silu(joint[..., :half]) * joint[..., half:]).astype(bf16)


def swiglu_back(joint, gradient):
    half = joint.shape[-1] // 2
    gate, up = joint[..., :half], joint[..., half:]
    sig = jax.nn.sigmoid(gate)
    d_gate = gradient * up * sig * (1.0 + gate * (1.0 - sig))
    d_up = gradient * gate * sig
    return jnp.concatenate([d_gate, d_up], -1).astype(bf16)


def routing(choices, order):
    tokens = choices.shape[0]
    pairs = 2 * tokens
    flat = choices.reshape(-1)
    ids = jnp.arange(pairs, dtype=jnp.int32)
    place = (order[:, None] == ids[None, :]).astype(bf16)
    experts = (flat[:, None] == jnp.arange(EXPERTS, dtype=jnp.int32)[None, :]).astype(bf16)
    placed = dot(place, experts).astype(bf16)
    lower = (ids[:, None] > ids[None, :]).astype(bf16)
    slot_placed = jnp.minimum(jnp.sum(dot(lower, placed) * placed.astype(f32), 1), float(CAP))
    slot = dot_tn(place, slot_placed[:, None].astype(bf16))[:, 0].astype(jnp.int32)
    kept = slot < CAP
    target = jnp.where(kept, flat * CAP + slot, SLOTS).reshape(tokens, 2)
    target = target.T.reshape(-1)
    chosen = (target[None, :] == jnp.arange(SLOTS, dtype=jnp.int32)[:, None]).astype(bf16)
    return kept.reshape(tokens, 2).astype(f32), chosen


def rotate(x, cosine, sine):
    half = HEAD_DIM // 2
    a, b = x[..., :half], x[..., half:]
    return jnp.concatenate([a * cosine - b * sine, b * cosine + a * sine], -1)


def attention_back(queries, keys, values, visible, total, attended, d_attended):
    scale = HEAD_DIM**-0.5
    scores = jnp.einsum("qhd,khd->hqk", queries, keys, preferred_element_type=f32)
    scores = jnp.where(visible[None], scores * scale, MASKED)
    weights = jnp.exp(scores - total)
    delta = jnp.sum(d_attended.astype(f32) * attended, -1).T[..., None]
    d_weights = jnp.einsum("qhd,khd->hqk", d_attended, values, preferred_element_type=f32)
    d_scores = (weights * (d_weights - delta)).astype(bf16)
    d_q = jnp.einsum("hqk,khd->qhd", d_scores, keys, preferred_element_type=f32) * scale
    d_k = jnp.einsum("hqk,qhd->khd", d_scores, queries, preferred_element_type=f32) * scale
    d_v = jnp.einsum("hqk,qhd->khd", weights.astype(bf16), d_attended, preferred_element_type=f32)
    return d_q, d_k, d_v


class Net:
    def __init__(self, send, recv, local_sems):
        self.send, self.recv, self.local_sems = send, recv, local_sems
        self.count = 0
        self.local_count = 0
        self.r, self.s, self.z = (lax.axis_index(a) for a in ("rep", "seq", "fsdp"))
        self.half = lax.rem(self.r, 2)
        self.core = lax.rem(self.s, 2)
        self.far = self.s // 2
        self.partner = self.r + 1 - 2 * self.half

    def seq(self, d):
        core = self.core if d % 2 == 0 else 1 - self.core
        far = self.far if d < 2 else 1 - self.far
        return far * 2 + core

    def plane(self, k):
        return lax.rem(self.z + k, FSDP)

    def copy(self, src, dst, **device):
        k = self.count
        self.count += 1
        out = pltpu.make_async_remote_copy(
            src_ref=src, dst_ref=dst, send_sem=self.send.at[k], recv_sem=self.recv.at[k],
            device_id=device, device_id_type=MESH,
        )
        out.start()
        return out

    def move(self, src, dst):
        k = self.local_count
        self.local_count += 1
        out = pltpu.make_async_copy(src, dst, self.local_sems.at[k])
        out.start()
        return out

    def greet(self, devices):
        self.barrier = pltpu.get_barrier_semaphore()
        for device in devices:
            pl.semaphore_signal(self.barrier, inc=1, device_id=device, device_id_type=MESH)
        self.greeted = len(devices)

    def met(self):
        pl.semaphore_wait(self.barrier, self.greeted)

    def everyone(self):
        seqs = [{"seq": self.seq(d)} for d in (1, 2, 3)]
        planes = [{"fsdp": self.plane(k)} for k in (1, 2, 3)]
        both = [{"seq": self.seq(1), "fsdp": self.plane(k)} for k in (1, 2, 3)]
        return seqs + planes + both + [{"rep": self.partner}]


def columns(start, size):
    return pl.ds(pl.multiple_of(start, 128), size)


class ExpertJob:
    inputs = ("expert_in", "expert_out")
    shapes = ((2, 2, 4, 4, 48, FF_DEV), (2, 4, 128, D))

    def __init__(self, net, layer, ins, outs):
        self.net, self.layer = net, layer
        self.first, self.second = ins
        self.w1, self.w2 = outs

    def stages(self):
        return [self.begin, self.second_hop, self.third_hop, self.finish]

    def begin(self):
        n = self.net
        self.first_copies, self.second_copies = [], []
        for k in (2, 1, 3, 0):
            e = n.plane(k)
            for d in (0, 1):
                core = n.core if d == 0 else 1 - n.core
                for gu in (0, 1):
                    src = self.first.at[
                        self.layer, e, :, columns(gu * FF + n.half * FF_CORE + core * FF_DEV, FF_DEV)
                    ]
                    dst = self.w1.at[n.half, gu, n.s, n.z]
                    if k == 0 and d == 0:
                        self.first_copies.append(n.move(src, dst))
                    else:
                        self.first_copies.append(n.copy(src, dst, seq=n.seq(d), fsdp=e))
            src = self.second.at[self.layer, e, :, columns(n.half * 384, 384)]
            dst = self.w2.at[n.far, n.z, :, columns(n.half * 384, 384)]
            if k == 0:
                self.second_copies.append(n.move(src, dst))
            else:
                self.second_copies.append(n.copy(src, dst, fsdp=e))

    def second_hop(self):
        n = self.net
        for copy in self.first_copies:
            copy.wait()
        part = self.w1.at[n.half, :, pl.ds(2 * n.far, 2)]
        self.first_copies = [n.copy(part, part, seq=n.seq(2))]
        for copy in self.second_copies:
            copy.wait()
        part = self.w2.at[n.far, :, :, columns(n.half * 384, 384)]
        self.second_copies = [n.copy(part, part, rep=n.partner)]

    def third_hop(self):
        n = self.net
        for copy in self.first_copies + self.second_copies:
            copy.wait()
        self.first_copies = [n.copy(self.w1.at[n.half], self.w1.at[n.half], rep=n.partner)]
        self.second_copies = [n.copy(self.w2.at[n.far], self.w2.at[n.far], seq=n.seq(2))]

    def finish(self):
        for copy in self.first_copies + self.second_copies:
            copy.wait()


class SharedJob:
    inputs = ("shared_in", "shared_out")
    shapes = ((2, 4, 4, 48, FF_DEV), (4, 128, D))

    def __init__(self, net, layer, ins, outs):
        self.net, self.layer = net, layer
        self.first, self.second = ins
        self.w_in, self.w_out = outs

    def stages(self):
        return [self.begin, self.second_hop, self.third_hop, self.finish]

    def begin(self):
        n = self.net
        self.first_copies, self.second_copies = [], []
        for d in (3, 2, 1, 0):
            src = self.first.at[
                self.layer, :, columns(n.half * FF + n.seq(d) * FF_DEV, FF_DEV)
            ]
            dst = self.w_in.at[n.half, n.s, n.z]
            if d == 0:
                self.first_copies.append(n.move(src, dst))
            else:
                self.first_copies.append(n.copy(src, dst, seq=n.seq(d)))
        for k in (2, 1, 3, 0):
            src = self.second.at[self.layer, :, columns(n.half * 384, 384)]
            dst = self.w_out.at[n.z, :, columns(n.half * 384, 384)]
            if k == 0:
                self.second_copies.append(n.move(src, dst))
            else:
                self.second_copies.append(n.copy(src, dst, fsdp=n.plane(k)))

    def second_hop(self):
        n = self.net
        for copy in self.first_copies:
            copy.wait()
        part = self.w_in.at[n.half, :, n.z]
        self.first_copies = [n.copy(part, part, fsdp=n.plane(k)) for k in (2, 1, 3)]
        for copy in self.second_copies:
            copy.wait()
        part = self.w_out.at[:, :, columns(n.half * 384, 384)]
        self.second_copies = [n.copy(part, part, rep=n.partner)]

    def third_hop(self):
        n = self.net
        for copy in self.first_copies:
            copy.wait()
        self.first_copies = [n.copy(self.w_in.at[n.half], self.w_in.at[n.half], rep=n.partner)]

    def finish(self):
        for copy in self.first_copies + self.second_copies:
            copy.wait()


class AttnJob:
    inputs = ("attn_qkv", "attn_out")
    shapes = ((4, 4, 48, 3 * COLS), (4, 48, D))

    def __init__(self, net, layer, ins, outs):
        self.net, self.layer = net, layer
        self.qkv, self.out = ins
        self.w_qkv, self.w_out = outs

    def stages(self):
        return [self.begin, self.second_hop, self.finish]

    def begin(self):
        n = self.net
        self.copies, self.rest = [], []
        for d in (3, 2, 1):
            self.copies.append(
                n.copy(self.qkv.at[self.layer, n.seq(d)], self.w_qkv.at[n.s, n.z], seq=n.seq(d))
            )
        self.copies.append(n.move(self.qkv.at[self.layer, n.s], self.w_qkv.at[n.s, n.z]))
        for k in (2, 1, 3):
            self.rest.append(n.copy(self.out.at[self.layer], self.w_out.at[n.z], fsdp=n.plane(k)))
        self.rest.append(n.move(self.out.at[self.layer], self.w_out.at[n.z]))

    def second_hop(self):
        n = self.net
        for copy in self.copies:
            copy.wait()
        part = self.w_qkv.at[:, n.z]
        self.copies = [n.copy(part, part, fsdp=n.plane(k)) for k in (2, 1, 3)]

    def finish(self):
        for copy in self.copies + self.rest:
            copy.wait()


class SmallJob:
    inputs = ("small",)
    shapes = ((4, 4, 16, 128),)

    def __init__(self, net, layer, ins, outs):
        self.net = net
        (self.src,) = ins
        (self.dst,) = outs

    def stages(self):
        return [self.begin, self.second_hop, self.finish]

    def begin(self):
        n = self.net
        self.copies = [
            n.copy(self.src, self.dst.at[n.s, n.z], seq=n.seq(d)) for d in (3, 2, 1)
        ] + [n.move(self.src, self.dst.at[n.s, n.z])]

    def second_hop(self):
        n = self.net
        for copy in self.copies:
            copy.wait()
        part = self.dst.at[:, n.z]
        self.copies = [n.copy(part, part, fsdp=n.plane(k)) for k in (2, 1, 3)]

    def finish(self):
        for copy in self.copies:
            copy.wait()


class Background:
    def __init__(self, net, jobs, refs):
        ins = sum(len(j.inputs) for j, _ in jobs)
        given, results = refs[:ins], refs[ins:]
        self.queues = []
        for job, layer in jobs:
            a, b = len(job.inputs), len(job.shapes)
            made = job(net, layer, given[:a], results[:b])
            self.queues.append(made.stages())
            given, results = given[a:], results[b:]

    def step(self):
        for queue in self.queues:
            if queue:
                queue.pop(0)()

    def drain(self):
        while any(self.queues):
            self.step()


def job_inputs(jobs, shards):
    return [shards[name] for job, _ in jobs for name in job.inputs]


def job_outputs(jobs):
    return [jax.ShapeDtypeStruct(shape, bf16) for job, _ in jobs for shape in job.shapes]


COPIES = 80


def call(kernel, inputs, outputs, scratch, jobs, shards, cid, flops=0):
    given = job_inputs(jobs, shards)
    results = job_outputs(jobs)
    vmem, anywhere = pl.BlockSpec(memory_space=pltpu.VMEM), pl.BlockSpec(memory_space=pl.ANY)

    def body(*refs):
        a = len(inputs)
        b = a + len(given)
        c = b + len(outputs)
        d = c + len(results)
        e = d + len(scratch)
        net = Net(*refs[e:])
        ground = Background(net, jobs, refs[a:b] + refs[c:d])
        kernel(net, ground, *refs[:a], *refs[b:c], *refs[d:e])

    made = pl.pallas_call(
        body,
        out_shape=[jax.ShapeDtypeStruct(shape, kind) for shape, kind in outputs] + results,
        in_specs=[vmem] * len(inputs) + [anywhere] * len(given),
        out_specs=[vmem] * len(outputs) + [anywhere] * len(results),
        scratch_shapes=[pltpu.VMEM(shape, kind) for shape, kind in scratch]
        + [
            pltpu.SemaphoreType.DMA((COPIES,)),
            pltpu.SemaphoreType.DMA((COPIES,)),
            pltpu.SemaphoreType.DMA((16,)),
        ],
        compiler_params=pltpu.CompilerParams(
            collective_id=cid, has_side_effects=True, vmem_limit_bytes=56 << 20
        ),
        cost_estimate=pl.CostEstimate(flops=flops, bytes_accessed=1 << 20, transcendentals=0),
    )(*inputs, *given)
    return made[: len(outputs)], made[len(outputs) :]


def prologue_kernel(net, ground):
    net.greet(net.everyone())
    net.met()
    ground.drain()


def rms_rows(x):
    return lax.rsqrt(jnp.mean(x * x, -1, keepdims=True) + EPS)


def turn(x, cosine, sine):
    half = HEAD_DIM // 2
    return x * cosine + jnp.concatenate([x[:, half:], x[:, :half]], 1) * sine


def attn_forward_kernel(
    net, ground, h, gains, w_qkv, w_out, cosine, sine,
    middle, second, every, queries, keys, values, attended, totals,
    near_out, near_in, away_out, away_in,
):
    net.greet(net.everyone())
    x = h[...]
    every[net.s] = (x * rms_rows(x) * gains[0:1, :]).astype(bf16)
    net.met()
    far = net.copy(every.at[net.s], every.at[net.s], seq=net.seq(2))
    near = net.copy(every.at[net.s], every.at[net.s], seq=net.seq(1))
    ground.step()

    def project(b):
        joint = dot(every[b], w_qkv[...])
        c, sn = cosine[b], sine[b]
        for i in range(HEADS_DEV):
            at = i * HEAD_DIM
            queries[i, b] = turn(joint[:, at : at + HEAD_DIM], c, sn).astype(bf16)
            at += COLS
            keys[i, b] = turn(joint[:, at : at + HEAD_DIM], c, sn).astype(bf16)
            at += COLS
            values[i, b] = joint[:, at : at + HEAD_DIM].astype(bf16)

    project(net.s)
    near.wait_recv()
    project(net.seq(1))
    far.wait_recv()
    passed = net.copy(every.at[net.seq(2)], every.at[net.seq(2)], seq=net.seq(1))
    project(net.seq(2))
    passed.wait_recv()
    project(net.seq(3))
    ground.step()
    tokens = h.shape[0]

    def head(i, carry):
        for b in range(SEQ):
            size = (b + 1) * tokens
            scores = dot_nt(queries[i, b], keys[i, : b + 1].reshape(size, HEAD_DIM))
            row = lax.broadcasted_iota(jnp.int32, (tokens, size), 0) + b * tokens
            col = lax.broadcasted_iota(jnp.int32, (tokens, size), 1)
            scores = jnp.where(row >= col, scores * HEAD_DIM**-0.5, MASKED)
            top = jnp.max(scores, -1, keepdims=True)
            weights = jnp.exp(scores - top)
            total = jnp.sum(weights, -1, keepdims=True)
            weights = (weights * (1.0 / total)).astype(bf16)
            attended[i, b] = dot(weights, values[i, : b + 1].reshape(size, HEAD_DIM))
            totals[i, b] = jnp.broadcast_to(top + jnp.log(total), (tokens, 128))
        return carry

    lax.fori_loop(0, HEADS_DEV, head, 0)
    ground.step()

    def part(b):
        low = jnp.concatenate([attended[i, b].astype(bf16) for i in range(HEADS_DEV)], 1)
        return dot(low, w_out[...])

    near_out[0] = part(net.seq(1)).astype(bf16)
    near_out[1] = part(net.seq(3)).astype(bf16)
    near_sum = net.copy(near_out, near_in, seq=net.seq(1))
    away = part(net.seq(2))
    own = part(net.s)
    near_sum.wait_recv()
    away_out[...] = (away + near_in[1].astype(f32)).astype(bf16)
    away_sum = net.copy(away_out, away_in, seq=net.seq(2))
    own = h[...] + own + near_in[0].astype(f32)
    ground.step()
    away_sum.wait_recv()
    own = own + away_in[...].astype(f32)
    middle[...] = own
    second[...] = (own * rms_rows(own) * gains[1:2, :]).astype(bf16)
    for copy in (far, near, passed, near_sum, away_sum):
        copy.wait_send()
    ground.drain()


def attn_forward(h, gains, w_qkv, w_out, cosine, sine, jobs, shards, cid):
    t = h.shape[0]
    head = (HEADS_DEV, SEQ, t, HEAD_DIM)
    return call(
        attn_forward_kernel,
        [h, gains, w_qkv, w_out, cosine, sine],
        [
            ((t, D), f32), ((t, D), bf16), ((SEQ, t, D), bf16), (head, bf16), (head, bf16),
            (head, bf16), (head, f32), ((HEADS_DEV, SEQ, t, 128), f32),
        ],
        [((2, t, D), bf16), ((2, t, D), bf16), ((t, D), bf16), ((t, D), bf16)],
        jobs, shards, cid,
    )


def silu_gate(g, u):
    return g / (1.0 + jnp.exp(-g)) * u


def ffn_forward_kernel(
    net, ground, second, middle, router, onehot, chosen, w_in, w_so, w1, w2,
    result, gates, gathered, every, joint, hidden, rows, joint_e, hidden_e,
    rows_out, prod_out, prod_in, prod_own, back_out, yields, near_out, near_in, away_out, away_in,
):
    t = second.shape[0]
    net.greet(net.everyone())
    picked = chosen[:, :t] + chosen[:, t:]
    rows_out[...] = dot(picked, second[...]).astype(bf16).reshape(EXPERTS, CAP, D)
    every[net.s] = second[...]
    net.met()
    sent = {}
    for k in (2, 1, 3):
        e = net.plane(k)
        sent[k] = net.copy(rows_out.at[e], rows.at[net.core, net.z], fsdp=e)
    far = net.copy(every.at[net.s], every.at[net.s], seq=net.seq(2))
    near = net.copy(every.at[net.s], every.at[net.s], seq=net.seq(1))
    rows[net.core, net.z] = rows_out[net.z]
    passed = []

    def pass_rows(k):
        if k:
            sent[k].wait_recv()
        part = rows.at[net.core, net.plane(FSDP - k)]
        passed.append(net.copy(part, part, seq=net.seq(1)))

    pass_rows(0)
    ground.step()
    logits = dot(second[...], router[...])
    l0 = jnp.sum(onehot[0] * logits, -1, keepdims=True)
    l1 = jnp.sum(onehot[1] * logits, -1, keepdims=True)
    top = jnp.maximum(l0, l1)
    e0, e1 = jnp.exp(l0 - top), jnp.exp(l1 - top)
    g0, g1 = e0 / (e0 + e1), e1 / (e0 + e1)
    lane = lax.broadcasted_iota(jnp.int32, (t, 128), 1)
    gates[...] = jnp.where(lane == 0, g0, jnp.where(lane == 1, g1, 0.0))

    def shared(b):
        g, u = dot(every[b], w_in[0]), dot(every[b], w_in[1])
        joint[0, b] = g.astype(bf16)
        joint[1, b] = u.astype(bf16)
        low = silu_gate(g, u).astype(bf16)
        hidden[b] = low
        return dot(low, w_so[...])

    own_part = shared(net.s)
    near.wait_recv()
    near_out[0] = shared(net.seq(1)).astype(bf16)
    pass_rows(1)
    pass_rows(3)
    far.wait_recv()
    passed_far = net.copy(every.at[net.seq(2)], every.at[net.seq(2)], seq=net.seq(1))
    far_part = shared(net.seq(2))
    pass_rows(2)
    passed_far.wait_recv()
    near_out[1] = shared(net.seq(3)).astype(bf16)
    near_sum = net.copy(near_out, near_in, seq=net.seq(1))
    ground.step()

    def expert(core):
        x = rows[core].reshape(SLOTS, D)
        total = None
        for half in (0, 1):
            g, u = dot(x, w1[half, 0]), dot(x, w1[half, 1])
            joint_e[core, half, 0] = g.astype(bf16)
            joint_e[core, half, 1] = u.astype(bf16)
            low = silu_gate(g, u).astype(bf16)
            hidden_e[core, half] = low
            new = dot(low, w2[half * FF_DEV : (half + 1) * FF_DEV, :])
            total = new if total is None else total + new
        return total

    for copy in passed:
        copy.wait_recv()
    prod_out[...] = expert(1 - net.core).astype(bf16)
    prod_sum = net.copy(prod_out, prod_in, seq=net.seq(1))
    near_sum.wait_recv()
    away_out[...] = (far_part + near_in[1].astype(f32)).astype(bf16)
    away_sum = net.copy(away_out, away_in, seq=net.seq(2))
    prod_own[...] = expert(net.core)
    prod_sum.wait_recv()
    back_out[...] = (prod_own[...] + prod_in[...].astype(f32)).astype(bf16).reshape(EXPERTS, CAP, D)
    returned = []
    for k in (2, 1, 3):
        e = net.plane(k)
        returned.append(net.copy(back_out.at[e], yields.at[net.z], fsdp=e))
    yields[net.z] = back_out[net.z]
    ground.step()
    away_sum.wait_recv()
    base = middle[...] + own_part + near_in[0].astype(f32) + away_in[...].astype(f32)
    for copy in returned:
        copy.wait_recv()
    got = dot_tn(chosen[...], yields[...].reshape(SLOTS, D))
    gathered[...] = got.astype(bf16)
    result[...] = base + g0 * got[:t] + g1 * got[t:]
    for copy in [far, near, passed_far, near_sum, prod_sum, away_sum, *passed, *sent.values(), *returned]:
        copy.wait_send()
    ground.drain()


def ffn_forward(second, middle, router, onehot, chosen, w_in, w_so, w1, w2, jobs, shards, cid):
    t = second.shape[0]
    return call(
        ffn_forward_kernel,
        [second, middle, router, onehot, chosen, w_in, w_so, w1, w2],
        [
            ((t, D), f32), ((t, 128), f32), ((2 * t, D), bf16), ((SEQ, t, D), bf16),
            ((2, SEQ, t, FF_DEV), bf16), ((SEQ, t, FF_DEV), bf16), ((2, EXPERTS, CAP, D), bf16),
            ((2, 2, 2, SLOTS, FF_DEV), bf16), ((2, 2, SLOTS, FF_DEV), bf16),
        ],
        [
            ((EXPERTS, CAP, D), bf16), ((SLOTS, D), bf16), ((SLOTS, D), bf16), ((SLOTS, D), f32),
            ((EXPERTS, CAP, D), bf16), ((EXPERTS, CAP, D), bf16), ((2, t, D), bf16),
            ((2, t, D), bf16), ((t, D), bf16), ((t, D), bf16),
        ],
        jobs, shards, cid,
    )


def layer_backward(layer, s, grad, dense, expert, gains, router, routes, stored, cosine, sine, visible):
    w_qkv, w_first, w_out, w_second = dense
    e_first, e_second = expert
    kept, chosen = routes
    (
        h, factor_one, normed_all, queries, keys, values, total, attended, attended_low, middle,
        factor_two, second, gates, onehot, second_all, joint_shared, hidden_shared, rows_all,
        joint_expert, hidden_expert, gathered,
    ) = stored
    tokens = grad.shape[0]
    scaled = gates * kept
    d_yields = jnp.concatenate([grad * scaled[:, :1], grad * scaled[:, 1:]], 0).astype(bf16)
    d_yields = dot(chosen, d_yields).astype(bf16).reshape(EXPERTS, CAP, D)
    d_rows = exchange(d_yields, 3 + 4 * layer).reshape(SLOTS, D)
    other = lax.ppermute(d_rows, "seq", SIB)
    core = lax.rem(s, 2)
    d_rows = jnp.concatenate([jnp.where(core == 0, d_rows, other), jnp.where(core == 0, other, d_rows)], 0)
    de_second = dot_tn(hidden_expert, d_rows)
    d_joint = swiglu_back(joint_expert, dot_nt(d_rows, e_second))
    de_first = dot_tn(rows_all, d_joint)
    back = dot_nt(d_joint, e_first)
    back = back.reshape(2, SLOTS, D)
    own = lax.dynamic_index_in_dim(back, core, 0, False)
    got = lax.ppermute(
        lax.dynamic_index_in_dim(back, 1 - core, 0, False).astype(bf16), "seq", SIB
    )
    back = (own + got.astype(f32)).astype(bf16)
    back = exchange(back.reshape(EXPERTS, CAP, D), 4 + 4 * layer).reshape(SLOTS, D)
    picked = chosen[:, :tokens] + chosen[:, tokens:]

    grad_all = gather_seq(grad.astype(bf16), s)
    d_second_w = dot_tn(hidden_shared, grad_all)
    d_joint_shared = swiglu_back(joint_shared, dot_nt(grad_all, w_second))
    d_first_w = dot_tn(second_all, d_joint_shared)
    d_normed = scatter_seq(dot_nt(d_joint_shared, w_first), s)

    d_gates = kept * jnp.stack(
        [jnp.sum(grad * gathered[:tokens], -1), jnp.sum(grad * gathered[tokens:], -1)], -1
    )
    d_chosen = gates * (d_gates - jnp.sum(gates * d_gates, -1, keepdims=True))
    d_logits = jnp.sum(d_chosen[..., None] * onehot, 1).astype(bf16)
    d_router = dot_tn(second, d_logits)
    d_normed = d_normed + dot_nt(d_logits, router) + dot_tn(picked, back)
    d_middle, d_gain_two = rms_backward(middle, factor_two, gains[1], d_normed)
    d_middle = grad + d_middle
    middle_all = gather_seq(d_middle.astype(bf16), s)
    d_out_w = dot_tn(attended_low, middle_all)
    d_attended = dot_nt(middle_all, w_out).astype(bf16).reshape(-1, HEADS_DEV, HEAD_DIM)
    d_q, d_k, d_v = attention_back(queries, keys, values, visible, total, attended, d_attended)
    d_qkv = jnp.stack([rotate(d_q, cosine, -sine), rotate(d_k, cosine, -sine), d_v], 1)
    d_qkv = d_qkv.reshape(-1, 3 * COLS).astype(bf16)
    d_qkv_w = dot_tn(normed_all, d_qkv)
    d_first = scatter_seq(dot_nt(d_qkv, w_qkv), s)
    d_state, d_gain_one = rms_backward(h, factor_one, gains[0], d_first)
    d_columns = jnp.concatenate([d_qkv_w, d_first_w], 1)
    d_rows_w = jnp.concatenate([d_out_w.reshape(4, 48, D), d_second_w.reshape(4, 128, D)], 1)
    small = jnp.concatenate([jnp.stack([d_gain_one, d_gain_two]), d_router.T], 0)
    return d_middle + d_state, (d_columns, d_rows_w), (de_first, de_second), small


def local(
    reps, inputs, expert_choice, pair_order, norm_gains, attn_qkv, attn_out, router, shared_in,
    shared_out, expert_in, expert_out, cotangent,
):
    r, s, z = lax.axis_index("rep"), lax.axis_index("seq"), lax.axis_index("fsdp")
    tokens = inputs.shape[1]
    position = jnp.arange(SEQ * tokens, dtype=jnp.int32)
    half = HEAD_DIM // 2
    inverse = jnp.exp(-jnp.log(10000.0) * jnp.arange(half, dtype=f32) * 2.0 / HEAD_DIM)
    angle = position.astype(f32)[:, None] * inverse[None, :]
    cosine, sine = jnp.cos(angle)[:, None, :], jnp.sin(angle)[:, None, :]
    table_cos = jnp.concatenate([cosine, cosine], -1).reshape(SEQ, tokens, HEAD_DIM)
    table_sin = jnp.concatenate([-sine, sine], -1).reshape(SEQ, tokens, HEAD_DIM)
    visible = position[:, None] >= position[None, :]
    small = jnp.concatenate([norm_gains, router.transpose(0, 2, 1)], 1).reshape(12, 48)
    shards = {
        "small": jnp.pad(small, ((0, 4), (0, 80))),
        "attn_qkv": attn_qkv.reshape(LAYERS, 48, 3, SEQ, COLS)
        .transpose(0, 3, 1, 2, 4)
        .reshape(LAYERS, SEQ, 48, 3 * COLS),
        "attn_out": attn_out,
        "shared_in": shared_in,
        "shared_out": shared_out,
        "expert_in": expert_in,
        "expert_out": expert_out,
    }
    h = inputs[0].astype(f32)
    kept_layers = []
    _, (small, *attn) = call(
        prologue_kernel, [], [], [], [(SmallJob, 0), (AttnJob, 0)], shards, 11
    )
    small = small.reshape(16, 16, 128)[:, :12, :48].transpose(1, 0, 2).reshape(LAYERS, 6, D)
    gains = small[:, :2].astype(f32)
    routers = small[:, 2:].transpose(0, 2, 1)
    branch = None
    for layer in range(LAYERS):
        first = layer == 0
        routes = routing(expert_choice[layer, 0], pair_order[layer, 0, 0])
        onehot = expert_choice[layer, 0].T[..., None] == jnp.arange(128, dtype=jnp.int32)
        onehot = onehot.astype(f32)
        w_qkv, w_out = attn[0].reshape(D, 3 * COLS), attn[1].reshape(COLS, D)
        jobs = [(ExpertJob, layer)] + ([(SharedJob, layer)] if first else [])
        (middle, second, every_one, queries, keys, values, attended, totals), fetched = attn_forward(
            h, gains[layer], w_qkv, w_out, table_cos, table_sin, jobs, shards, 12 + layer
        )
        w1, w2 = fetched[0].reshape(2, 2, D, FF_DEV), fetched[1].reshape(FF_CORE, D)
        if first:
            branch = fetched[2:]
        w_in, w_so = branch[0].reshape(2, D, FF_DEV), branch[1].reshape(FF_DEV, D)
        router_pad = jnp.pad(routers[layer], ((0, 0), (0, 124)))
        jobs = [(AttnJob, 1), (SharedJob, 1)] if first else []
        outs, fetched = ffn_forward(
            second, middle, router_pad, onehot, routes[1], w_in, w_so, w1, w2, jobs, shards,
            14 + layer,
        )
        if first:
            attn, branch = fetched[:2], fetched[2:]
        result, gates, gathered, every_two, joint, hidden, rows, joint_e, hidden_e = outs
        dense = (
            w_qkv, jnp.concatenate([w_in[0], w_in[1]], 1), w_out, w_so,
        )
        expert = (
            jnp.concatenate([w1[0, 0], w1[1, 0], w1[0, 1], w1[1, 1]], 1), w2,
        )
        heads = lambda x: x.reshape(HEADS_DEV, -1, HEAD_DIM).transpose(1, 0, 2)
        stored = (
            h, rms_rows(h), every_one.reshape(-1, D), heads(queries), heads(keys), heads(values),
            totals[..., :1].reshape(HEADS_DEV, -1, 1), heads(attended),
            heads(attended).reshape(-1, COLS).astype(bf16), middle, rms_rows(middle), second,
            gates[:, :2], onehot.transpose(1, 0, 2)[..., :EXPERTS], every_two.reshape(-1, D),
            joint.transpose(1, 2, 0, 3).reshape(-1, 2 * FF_DEV).astype(f32),
            hidden.reshape(-1, FF_DEV), rows.reshape(-1, D),
            joint_e.transpose(0, 3, 2, 1, 4).reshape(2 * SLOTS, -1).astype(f32),
            hidden_e.transpose(0, 2, 1, 3).reshape(2 * SLOTS, -1), gathered.astype(f32),
        )
        h = result
        kept_layers.append((dense, expert, routes, stored))
    output = h.astype(bf16)[None]
    grad = cotangent[0].astype(f32)
    grads = [None] * LAYERS
    smalls = [None] * LAYERS
    for layer in reversed(range(LAYERS)):
        dense, expert, routes, stored = kept_layers[layer]
        grad, d_dense, d_expert, smalls[layer] = layer_backward(
            layer, s, grad, dense, expert, gains[layer], routers[layer], routes, stored, cosine, sine,
            visible,
        )
        grads[layer] = return_dense(*d_dense, s, z, r, reps) + return_expert(*d_expert, s, r, reps)
    total = lax.psum(jnp.stack(smalls), ("rep", "seq", "fsdp"))
    total = lax.dynamic_slice_in_dim(total, (s * FSDP + z) * 48, 48, 2)
    d_qkv, d_out, d_in, d_so, d_ein, d_eout = (
        jnp.stack([grads[layer][k] for layer in range(LAYERS)]) for k in range(6)
    )
    return (
        output, grad[None], total[:, :2], d_qkv, d_out, total[:, 2:].transpose(0, 2, 1), d_in, d_so,
        d_ein, d_eout,
    )


def solution(mesh):
    tokens = P(("rep", "fsdp"), "seq", None)
    routes = P(None, ("rep", "fsdp"), "seq", None)
    gains = P(None, None, ("seq", "fsdp"))
    dense = P(None, ("seq", "fsdp"), None)
    expert = P(None, None, ("seq", "fsdp"), None)
    in_specs = (
        tokens, routes, routes, gains, dense, dense, dense, dense, dense, expert, expert, tokens,
    )
    out_specs = (tokens, tokens, gains, dense, dense, dense, dense, dense, expert, expert)
    return jax.shard_map(
        functools.partial(local, mesh.shape["rep"]),
        mesh=mesh, in_specs=in_specs, out_specs=out_specs, check_vma=False,
    )
```

```python
import functools

import jax
import jax.numpy as jnp
from jax import lax
from jax.experimental import pallas as pl
from jax.experimental.pallas import tpu as pltpu
from jax.sharding import PartitionSpec as P

D = 768
HEADS = 12
HEAD_DIM = 64
FF = 2048
EXPERTS = 4
LAYERS = 2
CAP = 144
EPS = 1e-06
MASKED = -1e30
SEQ = 4
FSDP = 4
HEADS_DEV = HEADS // SEQ
COLS = HEADS_DEV * HEAD_DIM
FF_DEV = FF // SEQ
FF_CORE = FF // 2
SLOTS = EXPERTS * CAP
bf16 = jnp.bfloat16
f32 = jnp.float32
MESH = pl.DeviceIdType.MESH


def dot(a, b):
    return jnp.dot(a, b, preferred_element_type=f32)


def dot_nt(a, b):
    return lax.dot_general(a, b, (((1,), (1,)), ((), ())), preferred_element_type=f32)


def dot_tn(a, b):
    return lax.dot_general(a, b, (((0,), (0,)), ((), ())), preferred_element_type=f32)


def rep_rest(x, reps):
    bit = 2
    while bit < reps:
        x = x + lax.ppermute(x, "rep", [(i, i ^ bit) for i in range(reps)])
        bit *= 2
    return x


def routing(choices, order):
    tokens = choices.shape[0]
    pairs = 2 * tokens
    flat = choices.reshape(-1)
    ids = jnp.arange(pairs, dtype=jnp.int32)
    place = (order[:, None] == ids[None, :]).astype(bf16)
    experts = (flat[:, None] == jnp.arange(EXPERTS, dtype=jnp.int32)[None, :]).astype(bf16)
    placed = dot(place, experts).astype(bf16)
    lower = (ids[:, None] > ids[None, :]).astype(bf16)
    slot_placed = jnp.minimum(jnp.sum(dot(lower, placed) * placed.astype(f32), 1), float(CAP))
    slot = dot_tn(place, slot_placed[:, None].astype(bf16))[:, 0].astype(jnp.int32)
    kept = slot < CAP
    target = jnp.where(kept, flat * CAP + slot, SLOTS).reshape(tokens, 2)
    target = target.T.reshape(-1)
    chosen = (target[None, :] == jnp.arange(SLOTS, dtype=jnp.int32)[:, None]).astype(bf16)
    return kept.reshape(tokens, 2).astype(f32), chosen


class Net:
    def __init__(self, send, recv, local_sems):
        self.send, self.recv, self.local_sems = send, recv, local_sems
        self.count = 0
        self.local_count = 0
        self.r, self.s, self.z = (lax.axis_index(a) for a in ("rep", "seq", "fsdp"))
        self.half = lax.rem(self.r, 2)
        self.core = lax.rem(self.s, 2)
        self.far = self.s // 2
        self.partner = self.r + 1 - 2 * self.half

    def seq(self, d):
        core = self.core if d % 2 == 0 else 1 - self.core
        far = self.far if d < 2 else 1 - self.far
        return far * 2 + core

    def plane(self, k):
        return lax.rem(self.z + k, FSDP)

    def copy(self, src, dst, **device):
        k = self.count
        self.count += 1
        out = pltpu.make_async_remote_copy(
            src_ref=src, dst_ref=dst, send_sem=self.send.at[k], recv_sem=self.recv.at[k],
            device_id=device, device_id_type=MESH,
        )
        out.start()
        return out

    def move(self, src, dst):
        k = self.local_count
        self.local_count += 1
        out = pltpu.make_async_copy(src, dst, self.local_sems.at[k])
        out.start()
        return out

    def greet(self, devices):
        self.barrier = pltpu.get_barrier_semaphore()
        for device in devices:
            pl.semaphore_signal(self.barrier, inc=1, device_id=device, device_id_type=MESH)
        self.greeted = len(devices)

    def met(self):
        pl.semaphore_wait(self.barrier, self.greeted)

    def everyone(self):
        seqs = [{"seq": self.seq(d)} for d in (1, 2, 3)]
        planes = [{"fsdp": self.plane(k)} for k in (1, 2, 3)]
        both = [{"seq": self.seq(1), "fsdp": self.plane(k)} for k in (1, 2, 3)]
        return seqs + planes + both + [{"rep": self.partner}]


def columns(start, size):
    return pl.ds(pl.multiple_of(start, 128), size)


def wait_all(copies):
    for copy in copies:
        copy.wait()


class Job:
    space = pl.ANY
    out_space = pl.ANY
    scratch = ()
    kind = bf16

    def __init__(self, net, layer, ins, outs, scratch):
        self.net, self.layer = net, layer
        self.bind(ins, outs, scratch)


class ExpertPlane(Job):
    inputs = ("expert_in", "expert_out")
    shapes = ((2, 2, 4, 48, FF_DEV), (4, 128, 384))

    def bind(self, ins, outs, scratch):
        self.first, self.second = ins
        self.p1, self.p2 = outs

    def stages(self):
        return [self.plane_begin, self.plane_finish]

    def plane_begin(self):
        n = self.net
        self.copies = []
        for k in (2, 1, 3, 0):
            e = n.plane(k)
            for d in (0, 1):
                core = n.core if d == 0 else 1 - n.core
                for gu in (0, 1):
                    src = self.first.at[
                        self.layer, e, :, columns(gu * FF + n.half * FF_CORE + core * FF_DEV, FF_DEV)
                    ]
                    dst = self.p1.at[gu, n.core, n.z]
                    if k == 0 and d == 0:
                        self.copies.append(n.move(src, dst))
                    else:
                        self.copies.append(n.copy(src, dst, seq=n.seq(d), fsdp=e))
            src = self.second.at[self.layer, e, :, columns(n.half * 384, 384)]
            dst = self.p2.at[n.z]
            self.copies.append(n.move(src, dst) if k == 0 else n.copy(src, dst, fsdp=e))

    def plane_finish(self):
        wait_all(self.copies)


class ExpertSides(Job):
    inputs = ("p1", "p2")
    shapes = ((2, 2, 4, 4, 48, FF_DEV), (2, 4, 128, D))

    def bind(self, ins, outs, scratch):
        self.p1, self.p2 = ins
        self.w1, self.w2 = outs

    def stages(self):
        return [self.sides_begin, self.sides_second, self.sides_finish]

    def quarter(self, half, far):
        return self.w1.at[half, :, pl.ds(2 * far, 2)]

    def corner(self, half, far, zs):
        return self.w2.at[far, zs, :, columns(half * 384, 384)]

    def sides_begin(self):
        n = self.net
        own, corner = self.quarter(n.half, n.far), self.corner(n.half, n.far, pl.ds(0, 4))
        self.across = [n.copy(self.p1, own, rep=n.partner), n.copy(self.p2, corner, rep=n.partner)]
        self.along = [n.copy(self.p1, own, seq=n.seq(2)), n.copy(self.p2, corner, seq=n.seq(2))]
        self.kept = [n.move(self.p1, own), n.move(self.p2, corner)]

    def sides_second(self):
        n = self.net
        wait_all(self.along)
        part = self.w1.at[n.half, 0, pl.ds(2 * (1 - n.far), 2)]
        corner = self.corner(n.half, 1 - n.far, pl.ds(0, 2))
        self.along = [n.copy(part, part, rep=n.partner), n.copy(corner, corner, rep=n.partner)]
        wait_all(self.across)
        part = self.w1.at[1 - n.half, 1, pl.ds(2 * n.far, 2)]
        corner = self.corner(1 - n.half, n.far, pl.ds(2, 2))
        self.across = [n.copy(part, part, seq=n.seq(2)), n.copy(corner, corner, seq=n.seq(2))]

    def sides_finish(self):
        wait_all(self.across + self.along + self.kept)


class ExpertFetch(ExpertPlane, ExpertSides):
    inputs = ExpertPlane.inputs
    shapes = ExpertSides.shapes
    scratch = ExpertPlane.shapes

    def bind(self, ins, outs, scratch):
        ExpertPlane.bind(self, ins, scratch, ())
        ExpertSides.bind(self, scratch, outs, ())

    def stages(self):
        def turn_over():
            self.plane_finish()
            self.sides_begin()

        return [self.plane_begin, turn_over, self.sides_second, self.sides_finish]


class SharedFetch(Job):
    inputs = ("shared_in", "shared_out")
    shapes = ((2, 4, 4, 48, FF_DEV), (4, 128, D))

    def bind(self, ins, outs, scratch):
        self.first, self.second = ins
        self.w_in, self.w_out = outs

    def stages(self):
        return [self.begin, self.second_hop, self.third_hop, self.finish]

    def begin(self):
        n = self.net
        self.firsts, self.seconds = [], []
        for d in (3, 2, 1, 0):
            src = self.first.at[self.layer, :, columns(n.half * FF + n.seq(d) * FF_DEV, FF_DEV)]
            dst = self.w_in.at[n.half, n.s, n.z]
            self.firsts.append(n.move(src, dst) if d == 0 else n.copy(src, dst, seq=n.seq(d)))
        for k in (2, 1, 3, 0):
            src = self.second.at[self.layer, :, columns(n.half * 384, 384)]
            dst = self.w_out.at[n.z, :, columns(n.half * 384, 384)]
            self.seconds.append(n.move(src, dst) if k == 0 else n.copy(src, dst, fsdp=n.plane(k)))

    def second_hop(self):
        n = self.net
        wait_all(self.firsts)
        part = self.w_in.at[n.half, :, n.z]
        self.firsts = [n.copy(part, part, fsdp=n.plane(k)) for k in (2, 1, 3)]
        self.across = [n.copy(part, part, rep=n.partner)]
        wait_all(self.seconds)
        part = self.w_out.at[:, :, columns(n.half * 384, 384)]
        self.across.append(n.copy(part, part, rep=n.partner))

    def third_hop(self):
        n = self.net
        for copy, k in zip(self.firsts[1:] + self.firsts[:1], (1, 3, 2)):
            copy.wait()
            part = self.w_in.at[n.half, :, n.plane(FSDP - k)]
            self.across.append(n.copy(part, part, rep=n.partner))

    def finish(self):
        wait_all(self.across)


class AttnFetch(Job):
    inputs = ("attn_qkv", "attn_out")
    shapes = ((4, 4, 48, 3 * COLS), (4, 48, D))

    def bind(self, ins, outs, scratch):
        self.qkv, self.out = ins
        self.w_qkv, self.w_out = outs

    def stages(self):
        return [self.begin, self.second_hop, self.third_hop, self.finish]

    def begin(self):
        n = self.net
        self.firsts, self.seconds = [], []
        for d in (3, 2, 1, 0):
            src, dst = self.qkv.at[self.layer, n.seq(d)], self.w_qkv.at[n.s, n.z]
            self.firsts.append(n.move(src, dst) if d == 0 else n.copy(src, dst, seq=n.seq(d)))
        for k in (2, 1, 3, 0):
            src = self.out.at[self.layer, :, columns(n.half * 384, 384)]
            dst = self.w_out.at[n.z, :, columns(n.half * 384, 384)]
            self.seconds.append(n.move(src, dst) if k == 0 else n.copy(src, dst, fsdp=n.plane(k)))

    def second_hop(self):
        n = self.net
        wait_all(self.firsts)
        part = self.w_qkv.at[pl.ds(2 * n.half, 2), n.z]
        self.firsts = [n.copy(part, part, fsdp=n.plane(k)) for k in (2, 1, 3)]
        wait_all(self.seconds)
        part = self.w_out.at[:, :, columns(n.half * 384, 384)]
        self.across = [n.copy(part, part, rep=n.partner)]

    def third_hop(self):
        n = self.net
        for copy, k in zip(self.firsts[1:] + self.firsts[:1], (1, 3, 2)):
            copy.wait()
            part = self.w_qkv.at[pl.ds(2 * n.half, 2), n.plane(FSDP - k)]
            self.across.append(n.copy(part, part, rep=n.partner))

    def finish(self):
        wait_all(self.across)


class AttnFetchHere(AttnFetch):
    out_space = pltpu.VMEM


class SmallFetch(Job):
    inputs = ("small",)
    shapes = ((4, 4, 16, 128),)

    def bind(self, ins, outs, scratch):
        (self.src,), (self.dst,) = ins, outs

    def stages(self):
        return [self.begin, self.second_hop, self.finish]

    def begin(self):
        n = self.net
        dst = self.dst.at[n.s, n.z]
        self.copies = [n.copy(self.src, dst, seq=n.seq(d)) for d in (3, 2, 1)]
        self.copies.append(n.move(self.src, dst))

    def second_hop(self):
        n = self.net
        wait_all(self.copies)
        part = self.dst.at[:, n.z]
        self.copies = [n.copy(part, part, fsdp=n.plane(k)) for k in (2, 1, 3)]

    def finish(self):
        wait_all(self.copies)


def total(*parts):
    out = parts[0].astype(f32)
    for part in parts[1:]:
        out = out + part.astype(f32)
    return out.astype(bf16)


class ExpertSidesReturn(Job):
    space = pltpu.VMEM
    out_space = pltpu.VMEM
    inputs = ("d_w1", "d_w2")
    shapes = ((2, 2, 4, 48, FF_DEV), (4, 128, 384))
    scratch = (
        (4, 4, 48, FF_DEV), (2, 2, 4, 48, FF_DEV), (2, 2, 128, 384), (2, 128, D),
    )

    def bind(self, ins, outs, scratch):
        self.d1, self.d2 = ins
        self.q1, self.q2 = outs
        self.ra, self.rb, self.rc, self.rd = scratch[:4]

    def stages(self):
        return [self.sides_begin, self.sides_second, self.sides_finish]

    def sides_begin(self):
        n = self.net
        other, half_cols = 1 - n.far, columns((1 - n.half) * 384, 384)
        self.across = [
            n.copy(self.d1.at[1 - n.half, 0], self.ra, rep=n.partner),
            n.copy(self.d2.at[:, pl.ds(0, 2), :, half_cols], self.rc, rep=n.partner),
        ]
        self.along = [
            n.copy(self.d1.at[:, 1, pl.ds(2 * other, 2)], self.rb, seq=n.seq(2)),
            n.copy(self.d2.at[other, pl.ds(2, 2)], self.rd, seq=n.seq(2)),
        ]

    def sides_second(self):
        n = self.net
        other, far = 1 - n.far, n.far
        wait_all(self.along)
        rows = pl.ds(2 * far, 2)
        self.rb[1 - n.half] = total(self.rb[1 - n.half], self.d1[1 - n.half, 1, rows])
        mine, rest = columns(n.half * 384, 384), columns((1 - n.half) * 384, 384)
        self.rd[...] = total(self.rd[...], self.d2[far, pl.ds(2, 2)])
        self.along = [
            n.copy(self.rb.at[1 - n.half], self.q1.at[1], rep=n.partner),
            n.copy(self.rd.at[:, :, rest], self.q2.at[pl.ds(2, 2)], rep=n.partner),
        ]
        wait_all(self.across)
        rows = pl.ds(2 * other, 2)
        self.ra[rows] = total(self.ra[rows], self.d1[n.half, 0, rows])
        self.rc[other] = total(self.rc[other], self.d2[other, pl.ds(0, 2), :, mine])
        self.across = [
            n.copy(self.ra.at[rows], self.q1.at[0], seq=n.seq(2)),
            n.copy(self.rc.at[other], self.q2.at[pl.ds(0, 2)], seq=n.seq(2)),
        ]
        rows = pl.ds(2 * far, 2)
        self.rb[n.half] = total(self.rb[n.half], self.d1[n.half, 1, rows])
        self.ra[rows] = total(self.ra[rows], self.d1[n.half, 0, rows])
        self.rc[far] = total(self.rc[far], self.d2[far, pl.ds(0, 2), :, mine])

    def sides_finish(self):
        n = self.net
        wait_all(self.across + self.along)
        self.q1[0] = total(self.q1[0], self.ra[pl.ds(2 * n.far, 2)])
        self.q1[1] = total(self.q1[1], self.rb[n.half])
        self.q2[0:2] = total(self.q2[0:2], self.rc[n.far])
        self.q2[2:4] = total(self.q2[2:4], self.rd[:, :, columns(n.half * 384, 384)])


class ExpertPlaneReturn(Job):
    space = pltpu.VMEM
    inputs = ("q1", "q2")
    shapes = ((EXPERTS, 48, 2 * FF), (EXPERTS, 128, D))

    def bind(self, ins, outs, scratch):
        self.q1, self.q2 = ins
        self.o1, self.o2 = outs

    def stages(self):
        return [self.plane_begin, self.plane_second, self.plane_finish]

    def plane_begin(self):
        n = self.net
        self.firsts, self.seconds = [], []
        for k in (2, 1, 3, 0):
            for d in (1, 0):
                core = n.core if d == 0 else 1 - n.core
                for gu in (0, 1):
                    src = self.q1.at[gu, core, n.plane(k)]
                    dst = self.o1.at[
                        n.z, :, columns(gu * FF + n.half * FF_CORE + n.core * FF_DEV, FF_DEV)
                    ]
                    if k == 0 and d == 0:
                        self.firsts.append(n.move(src, dst))
                    else:
                        self.firsts.append(n.copy(src, dst, seq=n.seq(d), fsdp=n.plane(k)))
            src = self.q2.at[n.plane(k)]
            dst = self.o2.at[n.z, :, columns(n.half * 384, 384)]
            self.seconds.append(n.move(src, dst) if k == 0 else n.copy(src, dst, fsdp=n.plane(k)))

    def plane_second(self):
        n = self.net
        wait_all(self.seconds)
        part = self.o2.at[:, :, columns(n.half * 384, 384)]
        self.seconds = [n.copy(part, part, rep=n.partner)]
        wait_all(self.firsts)
        self.firsts = []
        for gu in (0, 1):
            part = self.o1.at[:, :, columns(gu * FF + n.half * FF_CORE, FF_CORE)]
            self.firsts.append(n.copy(part, part, rep=n.partner))

    def plane_finish(self):
        wait_all(self.firsts + self.seconds)


class ExpertReturn(ExpertSidesReturn, ExpertPlaneReturn):
    out_space = pl.ANY
    inputs = ExpertSidesReturn.inputs
    shapes = ExpertPlaneReturn.shapes
    scratch = ExpertSidesReturn.scratch + ExpertSidesReturn.shapes

    def bind(self, ins, outs, scratch):
        ExpertSidesReturn.bind(self, ins, scratch[4:], scratch[:4])
        ExpertPlaneReturn.bind(self, scratch[4:], outs, ())

    def stages(self):
        def turn_over():
            self.sides_finish()
            self.plane_begin()

        return [
            self.sides_begin, self.sides_second, turn_over, self.plane_second, self.plane_finish,
        ]


class SharedReturn(Job):
    space = pltpu.VMEM
    inputs = ("d_w_in", "d_w_so")
    shapes = ((48, 2 * FF), (128, D))
    scratch = (
        (4, 4, 48, FF_DEV), (3, 4, 48, FF_DEV), (4, 48, FF_DEV), (4, 128, 384), (3, 128, 384),
        (128, 384),
    )

    def bind(self, ins, outs, scratch):
        self.d1, self.d2 = ins
        self.o1, self.o2 = outs
        self.r1, self.r1z, self.s1, self.r2, self.r2z, self.s2 = scratch

    def stages(self):
        return [self.begin, self.second_hop, self.third_hop, self.fourth_hop, self.finish]

    def begin(self):
        n = self.net
        self.firsts = [n.copy(self.d1.at[1 - n.half], self.r1, rep=n.partner)]
        part = self.d2.at[:, :, columns((1 - n.half) * 384, 384)]
        self.seconds = [n.copy(part, self.r2, rep=n.partner)]

    def second_hop(self):
        n = self.net
        wait_all(self.firsts)
        self.r1[...] = total(self.r1[...], self.d1[n.half])
        self.firsts = [
            n.copy(self.r1.at[:, n.plane(k)], self.r1z.at[k - 1], fsdp=n.plane(k))
            for k in (2, 1, 3)
        ]
        wait_all(self.seconds)
        self.r2[...] = total(self.r2[...], self.d2[:, :, columns(n.half * 384, 384)])
        self.seconds = [
            n.copy(self.r2.at[n.plane(k)], self.r2z.at[k - 1], fsdp=n.plane(k)) for k in (2, 1, 3)
        ]

    def third_hop(self):
        n = self.net
        wait_all(self.firsts + self.seconds)
        self.s1[...] = total(self.r1[:, n.z], self.r1z[0], self.r1z[1], self.r1z[2])
        self.firsts = []
        for d in (3, 2, 1, 0):
            src = self.s1.at[n.seq(d)]
            dst = self.o1.at[:, columns(n.half * FF + n.s * FF_DEV, FF_DEV)]
            self.firsts.append(n.move(src, dst) if d == 0 else n.copy(src, dst, seq=n.seq(d)))
        self.s2[...] = total(self.r2[n.z], self.r2z[0], self.r2z[1], self.r2z[2])
        dst = self.o2.at[:, columns(n.half * 384, 384)]
        self.seconds = [n.copy(self.s2, dst, rep=n.partner), n.move(self.s2, dst)]

    def fourth_hop(self):
        n = self.net
        wait_all(self.firsts)
        part = self.o1.at[:, columns(n.half * FF, FF)]
        self.firsts = [n.copy(part, part, rep=n.partner)]

    def finish(self):
        wait_all(self.firsts + self.seconds)


class AttnReturn(Job):
    space = pltpu.VMEM
    inputs = ("d_w_qkv", "d_w_out")
    shapes = ((4, 48, 3 * COLS), (48, D))
    scratch = (
        (2, 4, 48, 3 * COLS), (3, 2, 48, 3 * COLS), (4, 48, 3 * COLS), (4, 48, 384), (3, 48, 384),
        (48, 384),
    )

    def bind(self, ins, outs, scratch):
        self.d1, self.d2 = ins
        self.o1, self.o2 = outs
        self.r1, self.r1z, self.s1, self.r2, self.r2z, self.s2 = scratch

    def stages(self):
        return [self.begin, self.second_hop, self.third_hop, self.fourth_hop, self.finish]

    def begin(self):
        n = self.net
        self.firsts = [n.copy(self.d1.at[pl.ds(2 * (1 - n.half), 2)], self.r1, rep=n.partner)]
        part = self.d2.at[:, :, columns((1 - n.half) * 384, 384)]
        self.seconds = [n.copy(part, self.r2, rep=n.partner)]

    def second_hop(self):
        n = self.net
        wait_all(self.firsts)
        self.r1[...] = total(self.r1[...], self.d1[pl.ds(2 * n.half, 2)])
        self.firsts = [
            n.copy(self.r1.at[:, n.plane(k)], self.r1z.at[k - 1], fsdp=n.plane(k))
            for k in (2, 1, 3)
        ]
        wait_all(self.seconds)
        self.r2[...] = total(self.r2[...], self.d2[:, :, columns(n.half * 384, 384)])
        self.seconds = [
            n.copy(self.r2.at[n.plane(k)], self.r2z.at[k - 1], fsdp=n.plane(k)) for k in (2, 1, 3)
        ]

    def third_hop(self):
        n = self.net
        wait_all(self.firsts + self.seconds)
        pair = pl.ds(2 * n.half, 2)
        self.s1[pair] = total(self.r1[:, n.z], self.r1z[0], self.r1z[1], self.r1z[2])
        self.firsts = [n.copy(self.s1.at[pair], self.s1.at[pair], rep=n.partner)]
        self.s2[...] = total(self.r2[n.z], self.r2z[0], self.r2z[1], self.r2z[2])
        dst = self.o2.at[:, columns(n.half * 384, 384)]
        self.seconds = [n.copy(self.s2, dst, rep=n.partner), n.move(self.s2, dst)]

    def fourth_hop(self):
        n = self.net
        wait_all(self.firsts)
        self.firsts = []
        for d in (3, 2, 1, 0):
            src, dst = self.s1.at[n.seq(d)], self.o1.at[n.s]
            self.firsts.append(n.move(src, dst) if d == 0 else n.copy(src, dst, seq=n.seq(d)))

    def finish(self):
        wait_all(self.firsts + self.seconds)


class AttnReturnHere(AttnReturn):
    inputs = ()
    own = (2, 3)


class SmallReturnHere(Job):
    inputs = ("small_rows",)
    space = pltpu.VMEM
    out_space = pltpu.VMEM
    kind = f32
    own = (1,)
    shapes = ((16, D),)
    scratch = ((16, D), (16, D), (3, 16, D), (3, 16, D))

    def bind(self, ins, outs, scratch):
        self.rows, self.gain = ins
        (self.out,) = outs
        self.acc, self.rx, self.rz, self.rs = scratch

    def stages(self):
        return [self.begin, self.second_hop, self.third_hop, self.finish]

    def begin(self):
        n = self.net
        self.acc[...] = self.rows[...]
        self.acc[0:8] += self.gain[...]
        self.copies = [n.copy(self.acc, self.rx, rep=n.partner)]

    def second_hop(self):
        n = self.net
        wait_all(self.copies)
        self.rx[...] = self.acc[...] + self.rx[...]
        self.copies = [n.copy(self.rx, self.rz.at[k - 1], fsdp=n.plane(k)) for k in (2, 1, 3)]

    def third_hop(self):
        n = self.net
        wait_all(self.copies)
        self.acc[...] = self.rx[...] + self.rz[0] + self.rz[1] + self.rz[2]
        self.copies = [n.copy(self.acc, self.rs.at[d - 1], seq=n.seq(d)) for d in (3, 2, 1)]

    def finish(self):
        wait_all(self.copies)
        self.out[...] = self.acc[...] + self.rs[0] + self.rs[1] + self.rs[2]


class Background:
    def __init__(self, net, jobs, ins, own_outs, outs, scratch):
        self.queues, self.made = [], []
        for job, layer, points in jobs:
            a, b, c = len(job.inputs), len(job.shapes), len(job.scratch)
            given = list(ins[:a]) + [own_outs[i] for i in getattr(job, "own", ())]
            made = job(net, layer, given, outs[:b], scratch[:c])
            self.made.append((made, outs[:b]))
            stages = made.stages()
            last = points[-1]
            points = tuple(points) + (last,) * (len(stages) - len(points))
            self.queues.append(list(zip(points, stages)))
            ins, outs, scratch = ins[a:], outs[b:], scratch[c:]

    def at(self, point):
        for queue in self.queues:
            while queue and queue[0][0] <= point:
                queue.pop(0)[1]()

    def drain(self):
        while any(self.queues):
            for queue in self.queues:
                if queue:
                    queue.pop(0)[1]()


COPIES = 112


def call(kernel, inputs, outputs, scratch, jobs, shards, cid):
    given = [shards[name] for job, *_ in jobs for name in job.inputs]
    results = [
        (jax.ShapeDtypeStruct(shape, job.kind), job.out_space)
        for job, *_ in jobs
        for shape in job.shapes
    ]
    vmem = pl.BlockSpec(memory_space=pltpu.VMEM)
    job_scratch = [pltpu.VMEM(shape, job.kind) for job, *_ in jobs for shape in job.scratch]

    def body(*refs):
        a = len(inputs)
        b = a + len(given)
        c = b + len(outputs)
        d = c + len(results)
        e = d + len(scratch)
        f = e + len(job_scratch)
        net = Net(*refs[f:])
        ground = Background(net, jobs, refs[a:b], refs[b:c], refs[c:d], refs[e:f])
        kernel(net, ground, *refs[:a], *refs[b:c], *refs[d:e])

    made = pl.pallas_call(
        body,
        out_shape=[jax.ShapeDtypeStruct(shape, kind) for shape, kind in outputs]
        + [shape for shape, _ in results],
        in_specs=[vmem] * len(inputs)
        + [pl.BlockSpec(memory_space=job.space) for job, *_ in jobs for _ in job.inputs],
        out_specs=[vmem] * len(outputs) + [pl.BlockSpec(memory_space=where) for _, where in results],
        scratch_shapes=[pltpu.VMEM(shape, kind) for shape, kind in scratch]
        + job_scratch
        + [
            pltpu.SemaphoreType.DMA((COPIES,)),
            pltpu.SemaphoreType.DMA((COPIES,)),
            pltpu.SemaphoreType.DMA((32,)),
        ],
        compiler_params=pltpu.CompilerParams(
            collective_id=cid, has_side_effects=True, vmem_limit_bytes=60 << 20
        ),
        cost_estimate=pl.CostEstimate(flops=0, bytes_accessed=1 << 20, transcendentals=0),
    )(*inputs, *given)
    return made[: len(outputs)], made[len(outputs) :]


def prologue_kernel(net, ground):
    net.greet(net.everyone())
    net.met()
    ground.drain()


def rms_rows(x):
    return lax.rsqrt(jnp.mean(x * x, -1, keepdims=True) + EPS)


def turn(x, cosine, sine):
    half = HEAD_DIM // 2
    return x * cosine + jnp.concatenate([x[:, half:], x[:, :half]], 1) * sine


def attn_forward_kernel(
    here, net, ground, h, gains, cosine, sine, *refs
):
    if here:
        w_qkv, w_out = ground.made[0][1]
    else:
        w_qkv, w_out, *refs = refs
    (
        middle, second, every, queries, keys, values, attended, totals,
        near_out, near_in, away_out, away_in,
    ) = refs
    net.greet(net.everyone())
    x = h[...]
    every[net.s] = (x * rms_rows(x) * gains[0:1, :]).astype(bf16)
    net.met()
    ground.at(0)
    far = net.copy(every.at[net.s], every.at[net.s], seq=net.seq(2))
    near = net.copy(every.at[net.s], every.at[net.s], seq=net.seq(1))
    ground.at(1)

    def project(b):
        joint = dot(every[b], w_qkv[...].reshape(D, 3 * COLS))
        c, sn = cosine[b], sine[b]
        for i in range(HEADS_DEV):
            at = i * HEAD_DIM
            queries[i, b] = turn(joint[:, at : at + HEAD_DIM], c, sn).astype(bf16)
            at += COLS
            keys[i, b] = turn(joint[:, at : at + HEAD_DIM], c, sn).astype(bf16)
            at += COLS
            values[i, b] = joint[:, at : at + HEAD_DIM].astype(bf16)

    if not here:
        project(net.s)
    near.wait_recv()
    ground.at(2)
    if not here:
        project(net.seq(1))
    far.wait_recv()
    passed = net.copy(every.at[net.seq(2)], every.at[net.seq(2)], seq=net.seq(1))
    ground.at(3)
    if here:
        project(net.s)
        project(net.seq(1))
    project(net.seq(2))
    passed.wait_recv()
    project(net.seq(3))
    ground.at(4)
    tokens = h.shape[0]

    def head(i):
        for b in range(SEQ):
            size = (b + 1) * tokens
            scores = dot_nt(queries[i, b], keys[i, : b + 1].reshape(size, HEAD_DIM))
            row = lax.broadcasted_iota(jnp.int32, (tokens, size), 0) + b * tokens
            col = lax.broadcasted_iota(jnp.int32, (tokens, size), 1)
            scores = jnp.where(row >= col, scores * HEAD_DIM**-0.5, MASKED)
            top = jnp.max(scores, -1, keepdims=True)
            weights = jnp.exp(scores - top)
            total = jnp.sum(weights, -1, keepdims=True)
            weights = (weights * (1.0 / total)).astype(bf16)
            attended[i, b] = dot(weights, values[i, : b + 1].reshape(size, HEAD_DIM))
            totals[i, b] = jnp.broadcast_to(top + jnp.log(total), (tokens, 128))

    for i in range(HEADS_DEV):
        head(i)
        ground.at(5 + i)

    def part(b):
        low = jnp.concatenate([attended[i, b].astype(bf16) for i in range(HEADS_DEV)], 1)
        return dot(low, w_out[...].reshape(COLS, D))

    near_out[0] = part(net.seq(1)).astype(bf16)
    near_out[1] = part(net.seq(3)).astype(bf16)
    near_sum = net.copy(near_out, near_in, seq=net.seq(1))
    away = part(net.seq(2))
    own = part(net.s)
    near_sum.wait_recv()
    away_out[...] = (away + near_in[1].astype(f32)).astype(bf16)
    away_sum = net.copy(away_out, away_in, seq=net.seq(2))
    own = h[...] + own + near_in[0].astype(f32)
    ground.at(8)
    away_sum.wait_recv()
    own = own + away_in[...].astype(f32)
    middle[...] = own
    second[...] = (own * rms_rows(own) * gains[1:2, :]).astype(bf16)
    for copy in (far, near, passed, near_sum, away_sum):
        copy.wait_send()
    ground.drain()


def attn_forward(h, gains, weights, tables, jobs, shards, cid):
    t = h.shape[0]
    head = (HEADS_DEV, SEQ, t, HEAD_DIM)
    return call(
        functools.partial(attn_forward_kernel, not weights),
        [h, gains, *tables, *weights],
        [
            ((t, D), f32), ((t, D), bf16), ((SEQ, t, D), bf16), (head, bf16), (head, bf16),
            (head, bf16), (head, f32), ((HEADS_DEV, SEQ, t, 128), f32),
        ],
        [((2, t, D), bf16), ((2, t, D), bf16), ((t, D), bf16), ((t, D), bf16)],
        jobs, shards, cid,
    )


def silu_gate(g, u):
    return g / (1.0 + jnp.exp(-g)) * u


def ffn_forward_kernel(
    net, ground, second, middle, router, onehot, chosen, w_in, w_so, w1, w2,
    result, gates, gathered, every, joint, hidden, rows, joint_e, hidden_e,
    rows_out, prod_out, prod_in, prod_own, back_out, yields, near_out, near_in, away_out, away_in,
):
    t = second.shape[0]
    net.greet(net.everyone())
    picked = chosen[:, :t] + chosen[:, t:]
    rows_out[...] = dot(picked, second[...]).astype(bf16).reshape(EXPERTS, CAP, D)
    every[net.s] = second[...]
    net.met()
    sent = {}
    for k in (2, 1, 3):
        e = net.plane(k)
        sent[k] = net.copy(rows_out.at[e], rows.at[net.core, net.z], fsdp=e)
    far = net.copy(every.at[net.s], every.at[net.s], seq=net.seq(2))
    near = net.copy(every.at[net.s], every.at[net.s], seq=net.seq(1))
    rows[net.core, net.z] = rows_out[net.z]
    passed = []

    def pass_rows(k):
        if k:
            sent[k].wait_recv()
        part = rows.at[net.core, net.plane(FSDP - k)]
        passed.append(net.copy(part, part, seq=net.seq(1)))

    pass_rows(0)
    ground.at(0)
    logits = dot(second[...], router[...])
    l0 = jnp.sum(onehot[0] * logits, -1, keepdims=True)
    l1 = jnp.sum(onehot[1] * logits, -1, keepdims=True)
    top = jnp.maximum(l0, l1)
    e0, e1 = jnp.exp(l0 - top), jnp.exp(l1 - top)
    g0, g1 = e0 / (e0 + e1), e1 / (e0 + e1)
    lane = lax.broadcasted_iota(jnp.int32, (t, 128), 1)
    gates[...] = jnp.where(lane == 0, g0, jnp.where(lane == 1, g1, 0.0))

    def shared(b):
        g, u = dot(every[b], w_in[0]), dot(every[b], w_in[1])
        joint[0, b] = g.astype(bf16)
        joint[1, b] = u.astype(bf16)
        low = silu_gate(g, u).astype(bf16)
        hidden[b] = low
        return dot(low, w_so[...])

    own_part = shared(net.s)
    ground.at(1)
    near.wait_recv()
    near_out[0] = shared(net.seq(1)).astype(bf16)
    pass_rows(1)
    pass_rows(3)
    far.wait_recv()
    passed_far = net.copy(every.at[net.seq(2)], every.at[net.seq(2)], seq=net.seq(1))
    far_part = shared(net.seq(2))
    pass_rows(2)
    ground.at(2)
    passed_far.wait_recv()
    near_out[1] = shared(net.seq(3)).astype(bf16)
    near_sum = net.copy(near_out, near_in, seq=net.seq(1))
    ground.at(3)

    def expert(core):
        x = rows[core].reshape(SLOTS, D)
        total = None
        for half in (0, 1):
            g, u = dot(x, w1[half, 0]), dot(x, w1[half, 1])
            joint_e[core, half, 0] = g.astype(bf16)
            joint_e[core, half, 1] = u.astype(bf16)
            low = silu_gate(g, u).astype(bf16)
            hidden_e[core, half] = low
            new = dot(low, w2[half * FF_DEV : (half + 1) * FF_DEV, :])
            total = new if total is None else total + new
        return total

    for copy in passed:
        copy.wait_recv()
    prod_out[...] = expert(1 - net.core).astype(bf16)
    prod_sum = net.copy(prod_out, prod_in, seq=net.seq(1))
    near_sum.wait_recv()
    away_out[...] = (far_part + near_in[1].astype(f32)).astype(bf16)
    away_sum = net.copy(away_out, away_in, seq=net.seq(2))
    ground.at(4)
    prod_own[...] = expert(net.core)
    ground.at(5)
    prod_sum.wait_recv()
    back_out[...] = (prod_own[...] + prod_in[...].astype(f32)).astype(bf16).reshape(EXPERTS, CAP, D)
    returned = []
    for k in (2, 1, 3):
        e = net.plane(k)
        returned.append(net.copy(back_out.at[e], yields.at[net.z], fsdp=e))
    yields[net.z] = back_out[net.z]
    ground.at(6)
    away_sum.wait_recv()
    base = middle[...] + own_part + near_in[0].astype(f32) + away_in[...].astype(f32)
    for copy in returned:
        copy.wait_recv()
    got = dot_tn(chosen[...], yields[...].reshape(SLOTS, D))
    gathered[...] = got.astype(bf16)
    result[...] = base + g0 * got[:t] + g1 * got[t:]
    for copy in [far, near, passed_far, near_sum, prod_sum, away_sum, *passed, *sent.values(), *returned]:
        copy.wait_send()
    ground.drain()


def ffn_forward(second, middle, router, onehot, chosen, w_in, w_so, w1, w2, jobs, shards, cid):
    t = second.shape[0]
    return call(
        ffn_forward_kernel,
        [second, middle, router, onehot, chosen, w_in, w_so, w1, w2],
        [
            ((t, D), f32), ((t, 128), f32), ((2 * t, D), bf16), ((SEQ, t, D), bf16),
            ((2, SEQ, t, FF_DEV), bf16), ((SEQ, t, FF_DEV), bf16), ((2, EXPERTS, CAP, D), bf16),
            ((2, 2, 2, SLOTS, FF_DEV), bf16), ((2, 2, SLOTS, FF_DEV), bf16),
        ],
        [
            ((EXPERTS, CAP, D), bf16), ((SLOTS, D), bf16), ((SLOTS, D), bf16), ((SLOTS, D), f32),
            ((EXPERTS, CAP, D), bf16), ((EXPERTS, CAP, D), bf16), ((2, t, D), bf16),
            ((2, t, D), bf16), ((t, D), bf16), ((t, D), bf16),
        ],
        jobs, shards, cid,
    )


def norm_back(x, gain, gradient):
    factor = rms_rows(x)
    weighted = gradient * gain
    inner = jnp.mean(weighted * x, -1, keepdims=True)
    d_x = factor * weighted - x * (factor * factor * factor) * inner
    return d_x, jnp.sum(gradient * x * factor, 0, keepdims=True)


def gate_back(g, u, gradient):
    sig = 1.0 / (1.0 + jnp.exp(-g))
    d_g = gradient * u * sig * (1.0 + g * (1.0 - sig))
    return d_g.astype(bf16), (gradient * g * sig).astype(bf16)


def ffn_backward_kernel(
    net, ground, grad, gates, onehot, chosen, gathered, middle, second, gains, router, every,
    joint, hidden, rows, joint_e, hidden_e, w_in, w_so, w1, w2,
    d_middle, small, d_w1, d_w2, d_w_in, d_w_so,
    every_g, d_joint, rows_out, d_rows, d_joint_e, prod_out, prod_in, prod_own, back_out, back_in,
    near_out, near_in, away_out, away_in,
):
    t = grad.shape[0]
    net.greet(net.everyone())
    g0, g1 = gates[:, 0:1], gates[:, 1:2]
    up = grad[...]
    pairs = jnp.concatenate([(up * g0).astype(bf16), (up * g1).astype(bf16)], 0)
    rows_out[...] = dot(chosen[...], pairs).astype(bf16).reshape(EXPERTS, CAP, D)
    every_g[net.s] = up.astype(bf16)
    net.met()
    sent = {}
    for k in (2, 1, 3):
        e = net.plane(k)
        sent[k] = net.copy(rows_out.at[e], d_rows.at[net.core, net.z], fsdp=e)
    far = net.copy(every_g.at[net.s], every_g.at[net.s], seq=net.seq(2))
    near = net.copy(every_g.at[net.s], every_g.at[net.s], seq=net.seq(1))
    d_rows[net.core, net.z] = rows_out[net.z]
    passed = []

    def pass_rows(k):
        if k:
            sent[k].wait_recv()
        part = d_rows.at[net.core, net.plane(FSDP - k)]
        passed.append(net.copy(part, part, seq=net.seq(1)))

    pass_rows(0)
    ground.at(0)
    d0 = jnp.sum(up * gathered[:t].astype(f32), -1, keepdims=True)
    d1 = jnp.sum(up * gathered[t:].astype(f32), -1, keepdims=True)
    mean = g0 * d0 + g1 * d1
    d_logits = (g0 * (d0 - mean) * onehot[0] + g1 * (d1 - mean) * onehot[1]).astype(bf16)
    small[8:16, :] = dot_tn(d_logits, second[...])[:8]
    local = dot_nt(d_logits, router[...])

    def shared(b):
        d_hidden = dot_nt(every_g[b], w_so[...])
        d_g, d_u = gate_back(joint[0, b].astype(f32), joint[1, b].astype(f32), d_hidden)
        d_joint[0, b] = d_g
        d_joint[1, b] = d_u
        return dot_nt(d_g, w_in[0]) + dot_nt(d_u, w_in[1])

    local = local + shared(net.s)
    ground.at(1)
    near.wait_recv()
    near_out[0] = shared(net.seq(1)).astype(bf16)
    pass_rows(1)
    pass_rows(3)
    far.wait_recv()
    passed_far = net.copy(every_g.at[net.seq(2)], every_g.at[net.seq(2)], seq=net.seq(1))
    far_part = shared(net.seq(2))
    pass_rows(2)
    ground.at(2)
    passed_far.wait_recv()
    near_out[1] = shared(net.seq(3)).astype(bf16)
    near_sum = net.copy(near_out, near_in, seq=net.seq(1))
    ground.at(3)

    def expert(core):
        x = d_rows[core].reshape(SLOTS, D)
        out = None
        for half in (0, 1):
            d_hidden = dot_nt(x, w2[half * FF_DEV : (half + 1) * FF_DEV, :])
            d_g, d_u = gate_back(
                joint_e[core, half, 0].astype(f32), joint_e[core, half, 1].astype(f32), d_hidden
            )
            d_joint_e[half, 0, core] = d_g
            d_joint_e[half, 1, core] = d_u
            new = dot_nt(d_g, w1[half, 0]) + dot_nt(d_u, w1[half, 1])
            out = new if out is None else out + new
        return out

    for copy in passed:
        copy.wait_recv()
    prod_out[...] = expert(1 - net.core).astype(bf16)
    prod_sum = net.copy(prod_out, prod_in, seq=net.seq(1))
    near_sum.wait_recv()
    away_out[...] = (far_part + near_in[1].astype(f32)).astype(bf16)
    away_sum = net.copy(away_out, away_in, seq=net.seq(2))
    ground.at(4)
    prod_own[...] = expert(net.core)
    ground.at(5)
    prod_sum.wait_recv()
    back_out[...] = (prod_own[...] + prod_in[...].astype(f32)).astype(bf16).reshape(EXPERTS, CAP, D)
    returned = []
    for k in (2, 1, 3):
        e = net.plane(k)
        returned.append(net.copy(back_out.at[e], back_in.at[net.z], fsdp=e))
    back_in[net.z] = back_out[net.z]
    ground.at(6)
    rows_all = rows[...].reshape(2 * SLOTS, D)
    d_rows_all = d_rows[...].reshape(2 * SLOTS, D)
    for half in (0, 1):
        for gu in (0, 1):
            d_w1[half, gu] = dot_tn(rows_all, d_joint_e[half, gu].reshape(2 * SLOTS, FF_DEV)).astype(
                bf16
            )
        low = jnp.concatenate([hidden_e[0, half], hidden_e[1, half]], 0)
        d_w2[half] = dot_tn(low, d_rows_all).astype(bf16)
        ground.at(6 + half)
    ground.at(8)
    tokens = every[...].reshape(SEQ * t, D)
    for gu in (0, 1):
        d_w_in[gu] = dot_tn(tokens, d_joint[gu].reshape(SEQ * t, FF_DEV)).astype(bf16)
    ground.at(9)
    d_w_so[...] = dot_tn(hidden[...].reshape(SEQ * t, FF_DEV), every_g[...].reshape(SEQ * t, D)).astype(
        bf16
    )
    away_sum.wait_recv()
    for copy in returned:
        copy.wait_recv()
    picked = chosen[:, :t] + chosen[:, t:]
    d_normed = local + near_in[0].astype(f32) + away_in[...].astype(f32)
    d_normed = d_normed + dot_tn(picked, back_in[...].reshape(SLOTS, D))
    d_x, d_gain = norm_back(middle[...], gains[1:2, :], d_normed)
    d_middle[...] = up + d_x
    small[0:8, :] = jnp.broadcast_to(d_gain, (8, D))
    for copy in [far, near, passed_far, near_sum, prod_sum, away_sum, *passed, *sent.values(), *returned]:
        copy.wait_send()
    ground.drain()


def ffn_backward(grad, saved, gains, router, weights, jobs, shards, cid):
    t = grad.shape[0]
    gates, onehot, chosen, gathered, middle, second, every, joint, hidden, rows, joint_e, hidden_e = saved
    slots = (EXPERTS, CAP, D)
    return call(
        ffn_backward_kernel,
        [
            grad, gates, onehot, chosen, gathered, middle, second, gains, router, every, joint,
            hidden, rows, joint_e, hidden_e, *weights,
        ],
        [
            ((t, D), f32), ((16, D), f32), ((2, 2, D, FF_DEV), bf16), ((2, FF_DEV, D), bf16),
            ((2, D, FF_DEV), bf16), ((FF_DEV, D), bf16),
        ],
        [
            ((SEQ, t, D), bf16), ((2, SEQ, t, FF_DEV), bf16), (slots, bf16), ((2, *slots), bf16),
            ((2, 2, 2, SLOTS, FF_DEV), bf16), ((SLOTS, D), bf16), ((SLOTS, D), bf16),
            ((SLOTS, D), f32), (slots, bf16), (slots, bf16), ((2, t, D), bf16), ((2, t, D), bf16),
            ((t, D), bf16), ((t, D), bf16),
        ],
        jobs, shards, cid,
    )


def attn_backward_kernel(
    net, ground, d_middle, h, gains, every, queries, keys, values, attended, totals, w_qkv, w_out,
    cosine, sine,
    grad, d_gain, d_w_qkv, d_w_out,
    every_m, d_att, d_q, d_k, d_v, d_joint, near_out, near_in, away_out, away_in,
):
    t = h.shape[0]
    net.greet(net.everyone())
    up = d_middle[...]
    every_m[net.s] = up.astype(bf16)
    net.met()
    far = net.copy(every_m.at[net.s], every_m.at[net.s], seq=net.seq(2))
    near = net.copy(every_m.at[net.s], every_m.at[net.s], seq=net.seq(1))
    ground.at(0)

    def project(b):
        d = dot_nt(every_m[b], w_out[...].reshape(COLS, D)).astype(bf16)
        for i in range(HEADS_DEV):
            d_att[i, b] = d[:, i * HEAD_DIM : (i + 1) * HEAD_DIM]

    project(net.s)
    near.wait_recv()
    project(net.seq(1))
    far.wait_recv()
    passed = net.copy(every_m.at[net.seq(2)], every_m.at[net.seq(2)], seq=net.seq(1))
    project(net.seq(2))
    passed.wait_recv()
    project(net.seq(3))
    ground.at(1)
    tokens = every_m[...].reshape(SEQ * t, D)
    low = jnp.concatenate(
        [attended[i].reshape(SEQ * t, HEAD_DIM).astype(bf16) for i in range(HEADS_DEV)], 1
    )
    d_w_out[...] = dot_tn(low, tokens).astype(bf16).reshape(SEQ, 48, D)
    scale = HEAD_DIM**-0.5

    def head(i):
        d_k[i] = jnp.zeros_like(d_k[i])
        d_v[i] = jnp.zeros_like(d_v[i])
        for b in range(SEQ):
            size = (b + 1) * t
            q, d = queries[i, b], d_att[i, b]
            k = keys[i, : b + 1].reshape(size, HEAD_DIM)
            v = values[i, : b + 1].reshape(size, HEAD_DIM)
            delta = jnp.sum(d.astype(f32) * attended[i, b], -1, keepdims=True)
            row = lax.broadcasted_iota(jnp.int32, (t, size), 0) + b * t
            col = lax.broadcasted_iota(jnp.int32, (t, size), 1)
            scores = jnp.where(row >= col, dot_nt(q, k) * scale, MASKED)
            weights = jnp.exp(scores - totals[i, b][:, 0:1])
            d_scores = (weights * (dot_nt(d, v) - delta)).astype(bf16)
            d_q[i, b] = dot(d_scores, k) * scale
            shape = (b + 1, t, HEAD_DIM)
            d_k[i, : b + 1] += (dot_tn(d_scores, q) * scale).reshape(shape)
            d_v[i, : b + 1] += dot_tn(weights.astype(bf16), d).reshape(shape)

    for i in range(HEADS_DEV):
        head(i)
        ground.at(2 + i)

    def part(b):
        c, sn = cosine[b], -sine[b]
        pieces = [turn(d_q[i, b], c, sn) for i in range(HEADS_DEV)]
        pieces += [turn(d_k[i, b], c, sn) for i in range(HEADS_DEV)]
        pieces += [d_v[i, b] for i in range(HEADS_DEV)]
        d = jnp.concatenate(pieces, 1).astype(bf16)
        d_joint[b] = d
        return dot_nt(d, w_qkv[...].reshape(D, 3 * COLS))

    near_out[0] = part(net.seq(1)).astype(bf16)
    near_out[1] = part(net.seq(3)).astype(bf16)
    near_sum = net.copy(near_out, near_in, seq=net.seq(1))
    away = part(net.seq(2))
    own = part(net.s)
    near_sum.wait_recv()
    away_out[...] = (away + near_in[1].astype(f32)).astype(bf16)
    away_sum = net.copy(away_out, away_in, seq=net.seq(2))
    own = own + near_in[0].astype(f32)
    ground.at(5)
    d_w = dot_tn(every[...].reshape(SEQ * t, D), d_joint[...].reshape(SEQ * t, 3 * COLS))
    d_w_qkv[...] = d_w.astype(bf16).reshape(4, 4, 48, 3 * COLS)
    ground.at(6)
    away_sum.wait_recv()
    d_x, gain = norm_back(h[...], gains[0:1, :], own + away_in[...].astype(f32))
    grad[...] = up + d_x
    row = lax.broadcasted_iota(jnp.int32, (8, D), 0)
    d_gain[...] = jnp.where(row == 0, gain, 0.0)
    ground.at(7)
    for copy in (far, near, passed, near_sum, away_sum):
        copy.wait_send()
    ground.drain()


def attn_backward(d_middle, saved, gains, weights, tables, jobs, shards, cid):
    t = d_middle.shape[0]
    h, every, queries, keys, values, attended, totals = saved
    head = (HEADS_DEV, SEQ, t, HEAD_DIM)
    return call(
        attn_backward_kernel,
        [d_middle, h, gains, every, queries, keys, values, attended, totals, *weights, *tables],
        [((t, D), f32), ((8, D), f32), ((4, 4, 48, 3 * COLS), bf16), ((4, 48, D), bf16)],
        [
            ((SEQ, t, D), bf16), (head, bf16), (head, f32), (head, f32), (head, f32),
            ((SEQ, t, 3 * COLS), bf16), ((2, t, D), bf16), ((2, t, D), bf16), ((t, D), bf16),
            ((t, D), bf16),
        ],
        jobs, shards, cid,
    )


FORWARD_ATTN_FIRST = (
    (AttnFetchHere, 0, (0, 1, 3, 3)),
    (ExpertFetch, 0, (1, 4, 6, 9)),
    (SharedFetch, 0, (2, 4, 7, 9)),
    (AttnFetch, 1, (4, 7, 8, 9)),
)
FORWARD_FFN_FIRST = ((ExpertPlane, 1, (3, 9)),)
FORWARD_ATTN = ((ExpertSides, 1, (1, 5, 9)), (SharedFetch, 1, (1, 2, 5, 9)))
BACKWARD_FFN = ((ExpertPlaneReturn, 1, (3, 6, 9)), (AttnReturn, 1, (0, 3, 6, 8, 9)))
BACKWARD_ATTN = ((ExpertSidesReturn, 1, (0, 4, 9)), (SharedReturn, 1, (0, 3, 5, 9)))
BACKWARD_ATTN_LAST = (
    (ExpertReturn, 0, (0, 3, 5, 9)),
    (SharedReturn, 0, (0, 3, 5, 9)),
    (AttnReturnHere, 0, (6, 9)),
    (SmallReturnHere, 0, (7, 9)),
)


def local(
    reps, inputs, expert_choice, pair_order, norm_gains, attn_qkv, attn_out, router, shared_in,
    shared_out, expert_in, expert_out, cotangent,
):
    r, s, z = lax.axis_index("rep"), lax.axis_index("seq"), lax.axis_index("fsdp")
    tokens = inputs.shape[1]
    position = jnp.arange(SEQ * tokens, dtype=jnp.int32)
    half = HEAD_DIM // 2
    inverse = jnp.exp(-jnp.log(10000.0) * jnp.arange(half, dtype=f32) * 2.0 / HEAD_DIM)
    angle = position.astype(f32)[:, None] * inverse[None, :]
    cosine, sine = jnp.cos(angle)[:, None, :], jnp.sin(angle)[:, None, :]
    table_cos = jnp.concatenate([cosine, cosine], -1).reshape(SEQ, tokens, HEAD_DIM)
    table_sin = jnp.concatenate([-sine, sine], -1).reshape(SEQ, tokens, HEAD_DIM)
    small = jnp.concatenate([norm_gains, router.transpose(0, 2, 1)], 1).reshape(12, 48)
    shards = {
        "small": jnp.pad(small, ((0, 4), (0, 80))),
        "attn_qkv": attn_qkv.reshape(LAYERS, 48, 3, SEQ, COLS)
        .transpose(0, 3, 1, 2, 4)
        .reshape(LAYERS, SEQ, 48, 3 * COLS),
        "attn_out": attn_out,
        "shared_in": shared_in,
        "shared_out": shared_out,
        "expert_in": expert_in,
        "expert_out": expert_out,
    }
    h = inputs[0].astype(f32)
    kept_layers = []
    _, (small,) = call(prologue_kernel, [], [], [], [(SmallFetch, 0, (0,))], shards, 11)
    small = small.reshape(16, 16, 128)[:, :12, :48].transpose(1, 0, 2).reshape(LAYERS, 6, D)
    gains = small[:, :2].astype(f32)
    routers = small[:, 2:].transpose(0, 2, 1)
    tables = (table_cos, table_sin)
    attn = ()
    for layer in range(LAYERS):
        first = layer == 0
        routes = routing(expert_choice[layer, 0], pair_order[layer, 0, 0])
        onehot = expert_choice[layer, 0].T[..., None] == jnp.arange(128, dtype=jnp.int32)
        onehot = onehot.astype(f32)
        if first:
            jobs = FORWARD_ATTN_FIRST
        else:
            jobs = FORWARD_ATTN
        (middle, second, every_one, queries, keys, values, attended, totals), fetched = attn_forward(
            h, gains[layer], attn, tables, jobs, shards, 12 + layer
        )
        if first:
            attn, fetched, next_attn = fetched[:2], fetched[2:6], fetched[6:]
        w_qkv, w_out = attn
        w1, w2 = fetched[0].reshape(2, 2, D, FF_DEV), fetched[1].reshape(FF_CORE, D)
        w_in, w_so = fetched[2].reshape(2, D, FF_DEV), fetched[3].reshape(FF_DEV, D)
        router_pad = jnp.pad(routers[layer], ((0, 0), (0, 124)))
        outs, fetched = ffn_forward(
            second, middle, router_pad, onehot, routes[1], w_in, w_so, w1, w2,
            FORWARD_FFN_FIRST if first else (), shards, 14 + layer,
        )
        attn_weights, ffn_weights = attn, (w_in, w_so, w1, w2)
        if first:
            attn = next_attn
            shards["p1"], shards["p2"] = fetched
        result, gates, gathered, every_two, joint, hidden, rows, joint_e, hidden_e = outs
        attn_saved = (h, every_one, queries, keys, values, attended, totals)
        ffn_saved = (
            gates, onehot, routes[1], gathered, middle, second, every_two, joint, hidden, rows,
            joint_e, hidden_e,
        )
        h = result
        kept_layers.append((attn_weights, ffn_weights, attn_saved, ffn_saved, router_pad))
    output = h.astype(bf16)[None]
    grad = cotangent[0].astype(f32)
    smalls = [None] * LAYERS
    returned = {}
    grads = {}
    for layer in reversed(range(LAYERS)):
        last = layer == 0
        attn_weights, ffn_weights, attn_saved, ffn_saved, router_pad = kept_layers[layer]
        (d_middle, small, d_w1, d_w2, d_w_in, d_w_so), done = ffn_backward(
            grad, ffn_saved, gains[layer], router_pad, ffn_weights, BACKWARD_FFN if last else (),
            grads, 18 + layer,
        )
        if last:
            returned["d_expert", 1], returned["d_attn", 1] = done[:2], done[2:]
        grads["d_w1"] = d_w1.reshape(2, 2, 4, 4, 48, FF_DEV)
        grads["d_w2"] = d_w2.reshape(2, 4, 128, D)
        grads["d_w_in"] = d_w_in.reshape(2, 4, 4, 48, FF_DEV)
        grads["d_w_so"] = d_w_so.reshape(4, 128, D)
        smalls[layer] = jnp.concatenate([small[:1], small[8:12]], 0)
        if last:
            rows = jnp.concatenate([jnp.zeros((1, D), f32), smalls[0], d_gain[:1], smalls[1]], 0)
            grads["small_rows"] = jnp.pad(rows, ((0, 4), (0, 0)))
        (grad, d_gain, d_w_qkv, d_w_out), done = attn_backward(
            d_middle, attn_saved, gains[layer], attn_weights, tables,
            BACKWARD_ATTN_LAST if last else BACKWARD_ATTN, grads, 16 + layer,
        )
        if last:
            returned["d_expert", 0], returned["d_shared", 0] = done[:2], done[2:4]
            returned["d_attn", 0], total_small = done[4:6], done[6]
        else:
            grads["q1"], grads["q2"] = done[:2]
            returned["d_shared", 1] = done[2:]
            grads["d_w_qkv"], grads["d_w_out"] = d_w_qkv, d_w_out
    total_small = rep_rest(total_small, reps)[:12].reshape(LAYERS, 6, D)
    total_small = lax.dynamic_slice_in_dim(total_small, (s * FSDP + z) * 48, 48, 2)

    def stack(name, k):
        return jnp.stack([rep_rest(returned[name, i][k], reps) for i in range(LAYERS)]).astype(f32)

    d_qkv = stack("d_attn", 0).reshape(LAYERS, SEQ, 48, 3, COLS).transpose(0, 2, 3, 1, 4)
    return (
        output, grad[None], total_small[:, :2], d_qkv.reshape(LAYERS, 48, 3 * D),
        stack("d_attn", 1), total_small[:, 2:].transpose(0, 2, 1), stack("d_shared", 0),
        stack("d_shared", 1), stack("d_expert", 0), stack("d_expert", 1),
    )


def solution(mesh):
    tokens = P(("rep", "fsdp"), "seq", None)
    routes = P(None, ("rep", "fsdp"), "seq", None)
    gains = P(None, None, ("seq", "fsdp"))
    dense = P(None, ("seq", "fsdp"), None)
    expert = P(None, None, ("seq", "fsdp"), None)
    in_specs = (
        tokens, routes, routes, gains, dense, dense, dense, dense, dense, expert, expert, tokens,
    )
    out_specs = (tokens, tokens, gains, dense, dense, dense, dense, dense, expert, expert)
    return jax.shard_map(
        functools.partial(local, mesh.shape["rep"]),
        mesh=mesh, in_specs=in_specs, out_specs=out_specs, check_vma=False,
    )
```

```python
import functools

import jax
import jax.numpy as jnp
from jax import lax
from jax.experimental import pallas as pl
from jax.experimental.pallas import tpu as pltpu
from jax.sharding import PartitionSpec as P

D = 768
HEADS = 12
HEAD_DIM = 64
FF = 2048
EXPERTS = 4
LAYERS = 2
CAP = 144
EPS = 1e-06
MASKED = -1e30
SEQ = 4
FSDP = 4
HEADS_DEV = HEADS // SEQ
COLS = HEADS_DEV * HEAD_DIM
FF_DEV = FF // SEQ
FF_CORE = FF // 2
SLOTS = EXPERTS * CAP
bf16 = jnp.bfloat16
f32 = jnp.float32
MESH = pl.DeviceIdType.MESH


def dot(a, b):
    return jnp.dot(a, b, preferred_element_type=f32)


def dot_nt(a, b):
    return lax.dot_general(a, b, (((1,), (1,)), ((), ())), preferred_element_type=f32)


def dot_tn(a, b):
    return lax.dot_general(a, b, (((0,), (0,)), ((), ())), preferred_element_type=f32)


def rep_rest(x, reps):
    bit = 2
    while bit < reps:
        x = x + lax.ppermute(x, "rep", [(i, i ^ bit) for i in range(reps)])
        bit *= 2
    return x


def routing(choices, order):
    tokens = choices.shape[0]
    pairs = 2 * tokens
    flat = choices.reshape(-1)
    ids = jnp.arange(pairs, dtype=jnp.int32)
    place = (order[:, None] == ids[None, :]).astype(bf16)
    experts = (flat[:, None] == jnp.arange(EXPERTS, dtype=jnp.int32)[None, :]).astype(bf16)
    placed = dot(place, experts).astype(bf16)
    lower = (ids[:, None] > ids[None, :]).astype(bf16)
    slot_placed = jnp.minimum(jnp.sum(dot(lower, placed) * placed.astype(f32), 1), float(CAP))
    slot = dot_tn(place, slot_placed[:, None].astype(bf16))[:, 0].astype(jnp.int32)
    kept = slot < CAP
    target = jnp.where(kept, flat * CAP + slot, SLOTS).reshape(tokens, 2)
    target = target.T.reshape(-1)
    chosen = (target[None, :] == jnp.arange(SLOTS, dtype=jnp.int32)[:, None]).astype(bf16)
    return kept.reshape(tokens, 2).astype(f32), chosen


class Net:
    def __init__(self, send, recv, local_sems):
        self.send, self.recv, self.local_sems = send, recv, local_sems
        self.count = 0
        self.local_count = 0
        self.r, self.s, self.z = (lax.axis_index(a) for a in ("rep", "seq", "fsdp"))
        self.half = lax.rem(self.r, 2)
        self.core = lax.rem(self.s, 2)
        self.far = self.s // 2
        self.partner = self.r + 1 - 2 * self.half

    def seq(self, d):
        core = self.core if d % 2 == 0 else 1 - self.core
        far = self.far if d < 2 else 1 - self.far
        return far * 2 + core

    def plane(self, k):
        return lax.rem(self.z + k, FSDP)

    def copy(self, src, dst, **device):
        k = self.count
        self.count += 1
        out = pltpu.make_async_remote_copy(
            src_ref=src, dst_ref=dst, send_sem=self.send.at[k], recv_sem=self.recv.at[k],
            device_id=device, device_id_type=MESH,
        )
        out.start()
        return out

    def move(self, src, dst):
        k = self.local_count
        self.local_count += 1
        out = pltpu.make_async_copy(src, dst, self.local_sems.at[k])
        out.start()
        return out

    def need(self, *refs):
        for ref in refs:
            self.coming.pop(id(ref)).wait()

    def done(self, *refs):
        for ref in refs:
            self.going.append(self.move(ref, self.there.pop(id(ref))))

    def greet(self, devices):
        self.barrier = pltpu.get_barrier_semaphore()
        for device in devices:
            pl.semaphore_signal(self.barrier, inc=1, device_id=device, device_id_type=MESH)
        self.greeted = len(devices)

    def met(self):
        pl.semaphore_wait(self.barrier, self.greeted)

    def everyone(self):
        seqs = [{"seq": self.seq(d)} for d in (1, 2, 3)]
        planes = [{"fsdp": self.plane(k)} for k in (1, 2, 3)]
        both = [{"seq": self.seq(1), "fsdp": self.plane(k)} for k in (1, 2, 3)]
        return seqs + planes + both + [{"rep": self.partner}]


def columns(start, size):
    return pl.ds(pl.multiple_of(start, 128), size)


def wait_all(copies):
    for copy in copies:
        copy.wait()


class Job:
    space = pl.ANY
    out_space = pl.ANY
    scratch = ()
    kind = bf16

    def __init__(self, net, layer, ins, outs, scratch):
        self.net, self.layer = net, layer
        self.bind(ins, outs, scratch)


class ExpertPlane(Job):
    inputs = ("expert_in", "expert_out")
    shapes = ((2, 2, 4, 48, FF_DEV), (4, 128, 384))

    def bind(self, ins, outs, scratch):
        self.first, self.second = ins
        self.p1, self.p2 = outs

    def stages(self):
        return [self.plane_begin, self.plane_finish]

    def plane_begin(self):
        n = self.net
        self.copies = []
        for k in (2, 1, 3, 0):
            e = n.plane(k)
            for d in (0, 1):
                core = n.core if d == 0 else 1 - n.core
                for gu in (0, 1):
                    src = self.first.at[
                        self.layer, e, :, columns(gu * FF + n.half * FF_CORE + core * FF_DEV, FF_DEV)
                    ]
                    dst = self.p1.at[gu, n.core, n.z]
                    if k == 0 and d == 0:
                        self.copies.append(n.move(src, dst))
                    else:
                        self.copies.append(n.copy(src, dst, seq=n.seq(d), fsdp=e))
            src = self.second.at[self.layer, e, :, columns(n.half * 384, 384)]
            dst = self.p2.at[n.z]
            self.copies.append(n.move(src, dst) if k == 0 else n.copy(src, dst, fsdp=e))

    def plane_finish(self):
        wait_all(self.copies)


class ExpertFetch(ExpertPlane):
    shapes = ExpertPlane.shapes + ((2, 2, 4, 48, FF_DEV), (2, 2, 4, 48, FF_DEV)) + (
        (4, 128, 384), (4, 128, 384),
    )

    def bind(self, ins, outs, scratch):
        ExpertPlane.bind(self, ins, outs[:2], ())
        self.ax, self.ay, self.bx, self.by = outs[2:]

    def stages(self):
        def turn_over():
            self.plane_finish()
            self.near_begin()

        return [self.plane_begin, turn_over, self.near_finish]

    def near_begin(self):
        n = self.net
        self.sides = [
            n.copy(self.p1, self.ax, rep=n.partner), n.copy(self.p1, self.ay, seq=n.seq(2)),
            n.copy(self.p2, self.bx, rep=n.partner), n.copy(self.p2, self.by, seq=n.seq(2)),
        ]

    def near_finish(self):
        wait_all(self.sides)


class ExpertNear(ExpertFetch):
    inputs = ("p1", "p2")
    shapes = ExpertFetch.shapes[2:]

    def bind(self, ins, outs, scratch):
        self.p1, self.p2 = ins
        self.ax, self.ay, self.bx, self.by = outs

    def stages(self):
        return [self.near_begin, self.near_finish]


class ExpertJoin(Job):
    inputs = ("p1", "p2", "ax", "ay", "bx", "by")
    shapes = ((2, 2, 4, 4, 48, FF_DEV), (2, 4, 128, D))
    scratch = shapes

    def bind(self, ins, outs, scratch):
        self.p1, self.p2, self.ax, self.ay, self.bx, self.by = ins
        self.outs = outs
        self.w1, self.w2 = scratch

    def stages(self):
        return [self.begin, self.finish, self.written]

    def begin(self):
        n = self.net
        here, there = pl.ds(2 * n.far, 2), pl.ds(2 * (1 - n.far), 2)
        mine, rest = columns(n.half * 384, 384), columns((1 - n.half) * 384, 384)
        low, high = pl.ds(0, 2), pl.ds(2, 2)
        w1, w2 = self.w1, self.w2
        self.copies = [
            n.copy(self.ay.at[0], w1.at[n.half, 0, there], rep=n.partner),
            n.copy(self.ax.at[1], w1.at[1 - n.half, 1, here], seq=n.seq(2)),
            n.copy(self.by.at[low], w2.at[1 - n.far, low, :, mine], rep=n.partner),
            n.copy(self.bx.at[high], w2.at[n.far, high, :, rest], seq=n.seq(2)),
            n.move(self.p1, w1.at[n.half, :, here]),
            n.move(self.ax, w1.at[1 - n.half, :, here]),
            n.move(self.ay, w1.at[n.half, :, there]),
            n.move(self.p2, w2.at[n.far, :, :, mine]),
            n.move(self.bx, w2.at[n.far, :, :, rest]),
            n.move(self.by, w2.at[1 - n.far, :, :, mine]),
        ]

    def finish(self):
        wait_all(self.copies)
        self.copies = [
            self.net.move(self.w1, self.outs[0]), self.net.move(self.w2, self.outs[1])
        ]

    def written(self):
        wait_all(self.copies)


class SharedFetch(Job):
    inputs = ("shared_in", "shared_out")
    shapes = ((2, 4, 4, 48, FF_DEV), (4, 128, D))

    def bind(self, ins, outs, scratch):
        self.first, self.second = ins
        self.w_in, self.w_out = outs

    def stages(self):
        return [self.begin, self.second_hop, self.third_hop, self.finish]

    def begin(self):
        n = self.net
        self.firsts, self.seconds = [], []
        for d in (3, 2, 1, 0):
            src = self.first.at[self.layer, :, columns(n.half * FF + n.seq(d) * FF_DEV, FF_DEV)]
            dst = self.w_in.at[n.half, n.s, n.z]
            self.firsts.append(n.move(src, dst) if d == 0 else n.copy(src, dst, seq=n.seq(d)))
        for k in (2, 1, 3, 0):
            src = self.second.at[self.layer, :, columns(n.half * 384, 384)]
            dst = self.w_out.at[n.z, :, columns(n.half * 384, 384)]
            self.seconds.append(n.move(src, dst) if k == 0 else n.copy(src, dst, fsdp=n.plane(k)))

    def second_hop(self):
        n = self.net
        wait_all(self.firsts)
        part = self.w_in.at[n.half, :, n.z]
        self.firsts = [n.copy(part, part, fsdp=n.plane(k)) for k in (2, 1, 3)]
        self.across = [n.copy(part, part, rep=n.partner)]
        wait_all(self.seconds)
        part = self.w_out.at[:, :, columns(n.half * 384, 384)]
        self.across.append(n.copy(part, part, rep=n.partner))

    def third_hop(self):
        n = self.net
        for copy, k in zip(self.firsts[1:] + self.firsts[:1], (1, 3, 2)):
            copy.wait()
            part = self.w_in.at[n.half, :, n.plane(FSDP - k)]
            self.across.append(n.copy(part, part, rep=n.partner))

    def finish(self):
        wait_all(self.across)


class AttnFetch(Job):
    inputs = ("attn_qkv", "attn_out")
    shapes = ((4, 4, 48, 3 * COLS), (4, 48, D))

    def bind(self, ins, outs, scratch):
        self.qkv, self.out = ins
        self.w_qkv, self.w_out = outs

    def stages(self):
        return [self.begin, self.second_hop, self.third_hop, self.finish]

    def begin(self):
        n = self.net
        self.firsts, self.seconds = [], []
        for d in (3, 2, 1, 0):
            src, dst = self.qkv.at[self.layer, n.seq(d)], self.w_qkv.at[n.s, n.z]
            self.firsts.append(n.move(src, dst) if d == 0 else n.copy(src, dst, seq=n.seq(d)))
        for k in (2, 1, 3, 0):
            src = self.out.at[self.layer, :, columns(n.half * 384, 384)]
            dst = self.w_out.at[n.z, :, columns(n.half * 384, 384)]
            self.seconds.append(n.move(src, dst) if k == 0 else n.copy(src, dst, fsdp=n.plane(k)))

    def second_hop(self):
        n = self.net
        wait_all(self.firsts)
        part = self.w_qkv.at[pl.ds(2 * n.half, 2), n.z]
        self.firsts = [n.copy(part, part, fsdp=n.plane(k)) for k in (2, 1, 3)]
        wait_all(self.seconds)
        part = self.w_out.at[:, :, columns(n.half * 384, 384)]
        self.across = [n.copy(part, part, rep=n.partner)]

    def third_hop(self):
        n = self.net
        for copy, k in zip(self.firsts[1:] + self.firsts[:1], (1, 3, 2)):
            copy.wait()
            part = self.w_qkv.at[pl.ds(2 * n.half, 2), n.plane(FSDP - k)]
            self.across.append(n.copy(part, part, rep=n.partner))

    def finish(self):
        wait_all(self.across)


class AttnFetchHere(AttnFetch):
    out_space = pltpu.VMEM


class SmallFetch(Job):
    inputs = ("small",)
    shapes = ((4, 4, 16, 128),)

    def bind(self, ins, outs, scratch):
        (self.src,), (self.dst,) = ins, outs

    def stages(self):
        return [self.begin, self.second_hop, self.finish]

    def begin(self):
        n = self.net
        dst = self.dst.at[n.s, n.z]
        self.copies = [n.copy(self.src, dst, seq=n.seq(d)) for d in (3, 2, 1)]
        self.copies.append(n.move(self.src, dst))

    def second_hop(self):
        n = self.net
        wait_all(self.copies)
        part = self.dst.at[:, n.z]
        self.copies = [n.copy(part, part, fsdp=n.plane(k)) for k in (2, 1, 3)]

    def finish(self):
        wait_all(self.copies)


def total(*parts):
    out = parts[0].astype(f32)
    for part in parts[1:]:
        out = out + part.astype(f32)
    return out.astype(bf16)


class FirstSides(Job):
    inputs = ("d_w1",)
    out_space = pltpu.VMEM
    shapes = ((2, 4, 48, FF_DEV),)
    scratch = ((2, 2, 4, 48, FF_DEV), (2, 2, 4, 48, FF_DEV))

    def bind(self, ins, outs, scratch):
        (self.d,), (self.q,) = ins, outs
        self.own, self.got = scratch

    def stages(self):
        return [self.sides_begin, self.sides_second, self.sides_finish]

    def sides_begin(self):
        n = self.net
        if self.gu == 0:
            src = [self.d.at[1 - n.half, 0, pl.ds(2 * f, 2)] for f in (0, 1)]
            kept = [self.d.at[n.half, 0, pl.ds(2 * f, 2)] for f in (0, 1)]
            device = {"rep": n.partner}
        else:
            src = [self.d.at[h, 1, pl.ds(2 * (1 - n.far), 2)] for h in (0, 1)]
            kept = [self.d.at[h, 1, pl.ds(2 * n.far, 2)] for h in (0, 1)]
            device = {"seq": n.seq(2)}
        self.sent = [n.copy(src[i], self.got.at[i], **device) for i in (0, 1)]
        self.sent += [n.move(kept[i], self.own.at[i]) for i in (0, 1)]

    def sides_second(self):
        n = self.net
        wait_all(self.sent)
        stays = n.far if self.gu == 0 else n.half
        device = {"seq": n.seq(2)} if self.gu == 0 else {"rep": n.partner}
        goes = 1 - stays
        self.got[goes] = total(self.got[goes], self.own[goes])
        self.sent = [n.copy(self.got.at[goes], self.q, **device)]
        self.got[stays] = total(self.got[stays], self.own[stays])

    def sides_finish(self):
        n = self.net
        wait_all(self.sent)
        self.q[...] = total(self.q[...], self.got[n.far if self.gu == 0 else n.half])


class FirstPlane(Job):
    space = pltpu.VMEM
    shapes = ((EXPERTS, 48, FF),)

    def bind(self, ins, outs, scratch):
        (self.q,), (self.o,) = ins, outs

    def stages(self):
        return [self.plane_begin, self.plane_second, self.plane_finish]

    def plane_begin(self):
        n = self.net
        self.sent = []
        dst = self.o.at[n.z, :, columns(n.half * FF_CORE + n.core * FF_DEV, FF_DEV)]
        for k in (2, 1, 3, 0):
            for d in (1, 0):
                core = n.core if d == 0 else 1 - n.core
                src = self.q.at[core, n.plane(k)]
                if k == 0 and d == 0:
                    self.sent.append(n.move(src, dst))
                else:
                    self.sent.append(n.copy(src, dst, seq=n.seq(d), fsdp=n.plane(k)))

    def plane_second(self):
        n = self.net
        wait_all(self.sent)
        part = self.o.at[:, :, columns(n.half * FF_CORE, FF_CORE)]
        self.sent = [n.copy(part, part, rep=n.partner)]

    def plane_finish(self):
        wait_all(self.sent)


class FirstReturn(FirstSides, FirstPlane):
    space = pl.ANY
    out_space = pl.ANY
    shapes = FirstPlane.shapes
    scratch = FirstSides.scratch + FirstSides.shapes

    def bind(self, ins, outs, scratch):
        FirstSides.bind(self, ins, scratch[2:], scratch[:2])
        FirstPlane.bind(self, scratch[2:], outs, ())

    def stages(self):
        def turn_over():
            self.sides_finish()
            self.plane_begin()

        return [
            self.sides_begin, self.sides_second, turn_over, self.plane_second, self.plane_finish,
        ]


class GateSides(FirstSides):
    gu = 0


class UpSides(FirstSides):
    gu = 1


class GatePlane(FirstPlane):
    inputs = ("q_gate",)


class UpPlane(FirstPlane):
    inputs = ("q_up",)


class GateReturn(FirstReturn):
    gu = 0


class UpReturn(FirstReturn):
    gu = 1


class SecondSides(Job):
    inputs = ("d_w2",)
    out_space = pltpu.VMEM
    shapes = ((4, 128, 384),)
    scratch = ((2, 4, 128, 384), (2, 4, 128, 384))

    def bind(self, ins, outs, scratch):
        (self.d,), (self.q,) = ins, outs
        self.own, self.got = scratch

    def stages(self):
        return [self.sides_begin, self.sides_second, self.sides_finish]

    def sides_begin(self):
        n = self.net
        src = self.d.at[:, :, :, columns((1 - n.half) * 384, 384)]
        kept = self.d.at[:, :, :, columns(n.half * 384, 384)]
        self.sent = [n.copy(src, self.got, rep=n.partner), n.move(kept, self.own)]

    def sides_second(self):
        n = self.net
        wait_all(self.sent)
        goes = 1 - n.far
        self.got[goes] = total(self.got[goes], self.own[goes])
        self.sent = [n.copy(self.got.at[goes], self.q, seq=n.seq(2))]
        self.got[n.far] = total(self.got[n.far], self.own[n.far])

    def sides_finish(self):
        n = self.net
        wait_all(self.sent)
        self.q[...] = total(self.q[...], self.got[n.far])


class SecondPlane(Job):
    space = pltpu.VMEM
    inputs = ("q_second",)
    shapes = ((EXPERTS, 128, D),)

    def bind(self, ins, outs, scratch):
        (self.q,), (self.o,) = ins, outs

    def stages(self):
        return [self.plane_begin, self.plane_second, self.plane_finish]

    def plane_begin(self):
        n = self.net
        self.sent = []
        dst = self.o.at[n.z, :, columns(n.half * 384, 384)]
        for k in (2, 1, 3, 0):
            src = self.q.at[n.plane(k)]
            self.sent.append(n.move(src, dst) if k == 0 else n.copy(src, dst, fsdp=n.plane(k)))

    def plane_second(self):
        n = self.net
        wait_all(self.sent)
        part = self.o.at[:, :, columns(n.half * 384, 384)]
        self.sent = [n.copy(part, part, rep=n.partner)]

    def plane_finish(self):
        wait_all(self.sent)


class SecondReturn(SecondSides, SecondPlane):
    space = pl.ANY
    out_space = pl.ANY
    inputs = SecondSides.inputs
    shapes = SecondPlane.shapes
    scratch = SecondSides.scratch + SecondSides.shapes

    def bind(self, ins, outs, scratch):
        SecondSides.bind(self, ins, scratch[2:], scratch[:2])
        SecondPlane.bind(self, scratch[2:], outs, ())

    stages = FirstReturn.stages


class SharedAcross(Job):
    inputs = ()
    own = (-2, -1)
    out_space = pltpu.VMEM
    shapes = ((4, 4, 48, FF_DEV), (4, 128, 384))

    def bind(self, ins, outs, scratch):
        self.d1, self.d2 = ins
        self.r1, self.r2 = outs

    def stages(self):
        return [self.begin, self.finish]

    def begin(self):
        n = self.net
        part = self.d2.at[:, :, columns((1 - n.half) * 384, 384)]
        self.sent = [
            n.copy(self.d1.at[1 - n.half], self.r1, rep=n.partner),
            n.copy(part, self.r2, rep=n.partner),
        ]

    def finish(self):
        n = self.net
        wait_all(self.sent)
        self.r1[...] = total(self.r1[...], self.d1[n.half])
        self.r2[...] = total(self.r2[...], self.d2[:, :, columns(n.half * 384, 384)])


class SharedReturn(Job):
    space = pltpu.VMEM
    inputs = ("r1", "r2")
    shapes = ((48, 2 * FF), (128, D))
    scratch = ((3, 4, 48, FF_DEV), (4, 48, FF_DEV), (3, 128, 384), (128, 384))

    def bind(self, ins, outs, scratch):
        self.r1, self.r2 = ins
        self.o1, self.o2 = outs
        self.r1z, self.s1, self.r2z, self.s2 = scratch

    def stages(self):
        return [self.second_hop, self.third_hop, self.fourth_hop, self.finish]

    def second_hop(self):
        n = self.net
        self.firsts = [
            n.copy(self.r1.at[:, n.plane(k)], self.r1z.at[k - 1], fsdp=n.plane(k))
            for k in (2, 1, 3)
        ]
        self.seconds = [
            n.copy(self.r2.at[n.plane(k)], self.r2z.at[k - 1], fsdp=n.plane(k)) for k in (2, 1, 3)
        ]

    def third_hop(self):
        n = self.net
        wait_all(self.firsts + self.seconds)
        self.s1[...] = total(self.r1[:, n.z], self.r1z[0], self.r1z[1], self.r1z[2])
        self.firsts = []
        for d in (3, 2, 1, 0):
            src = self.s1.at[n.seq(d)]
            dst = self.o1.at[:, columns(n.half * FF + n.s * FF_DEV, FF_DEV)]
            self.firsts.append(n.move(src, dst) if d == 0 else n.copy(src, dst, seq=n.seq(d)))
        self.s2[...] = total(self.r2[n.z], self.r2z[0], self.r2z[1], self.r2z[2])
        dst = self.o2.at[:, columns(n.half * 384, 384)]
        self.seconds = [n.copy(self.s2, dst, rep=n.partner), n.move(self.s2, dst)]

    def fourth_hop(self):
        n = self.net
        wait_all(self.firsts)
        part = self.o1.at[:, columns(n.half * FF, FF)]
        self.firsts = [n.copy(part, part, rep=n.partner)]

    def finish(self):
        wait_all(self.firsts + self.seconds)


class AttnReturn(Job):
    space = pltpu.VMEM
    inputs = ("d_w_qkv", "d_w_out")
    shapes = ((4, 48, 3 * COLS), (48, D))
    scratch = (
        (2, 4, 48, 3 * COLS), (3, 2, 48, 3 * COLS), (4, 48, 3 * COLS), (4, 48, 384), (3, 48, 384),
        (48, 384),
    )

    def bind(self, ins, outs, scratch):
        self.d1, self.d2 = ins
        self.o1, self.o2 = outs
        self.r1, self.r1z, self.s1, self.r2, self.r2z, self.s2 = scratch

    def stages(self):
        return [self.begin, self.second_hop, self.third_hop, self.fourth_hop, self.finish]

    def begin(self):
        n = self.net
        self.firsts = [n.copy(self.d1.at[pl.ds(2 * (1 - n.half), 2)], self.r1, rep=n.partner)]
        part = self.d2.at[:, :, columns((1 - n.half) * 384, 384)]
        self.seconds = [n.copy(part, self.r2, rep=n.partner)]

    def second_hop(self):
        n = self.net
        wait_all(self.firsts)
        self.r1[...] = total(self.r1[...], self.d1[pl.ds(2 * n.half, 2)])
        self.firsts = [
            n.copy(self.r1.at[:, n.plane(k)], self.r1z.at[k - 1], fsdp=n.plane(k))
            for k in (2, 1, 3)
        ]
        wait_all(self.seconds)
        self.r2[...] = total(self.r2[...], self.d2[:, :, columns(n.half * 384, 384)])
        self.seconds = [
            n.copy(self.r2.at[n.plane(k)], self.r2z.at[k - 1], fsdp=n.plane(k)) for k in (2, 1, 3)
        ]

    def third_hop(self):
        n = self.net
        wait_all(self.firsts + self.seconds)
        pair = pl.ds(2 * n.half, 2)
        self.s1[pair] = total(self.r1[:, n.z], self.r1z[0], self.r1z[1], self.r1z[2])
        self.firsts = [n.copy(self.s1.at[pair], self.s1.at[pair], rep=n.partner)]
        self.s2[...] = total(self.r2[n.z], self.r2z[0], self.r2z[1], self.r2z[2])
        dst = self.o2.at[:, columns(n.half * 384, 384)]
        self.seconds = [n.copy(self.s2, dst, rep=n.partner), n.move(self.s2, dst)]

    def fourth_hop(self):
        n = self.net
        wait_all(self.firsts)
        self.firsts = []
        for d in (3, 2, 1, 0):
            src, dst = self.s1.at[n.seq(d)], self.o1.at[n.s]
            self.firsts.append(n.move(src, dst) if d == 0 else n.copy(src, dst, seq=n.seq(d)))

    def finish(self):
        wait_all(self.firsts + self.seconds)


class AttnReturnHere(AttnReturn):
    inputs = ()
    own = (2, 3)


class SmallReturnHere(Job):
    inputs = ("small_rows",)
    space = pltpu.VMEM
    out_space = pltpu.VMEM
    kind = f32
    own = (1,)
    shapes = ((16, D),)
    scratch = ((16, D), (16, D), (3, 16, D), (3, 16, D))

    def bind(self, ins, outs, scratch):
        self.rows, self.gain = ins
        (self.out,) = outs
        self.acc, self.rx, self.rz, self.rs = scratch

    def stages(self):
        return [self.begin, self.second_hop, self.third_hop, self.finish]

    def begin(self):
        n = self.net
        self.acc[...] = self.rows[...]
        self.acc[0:8] += self.gain[...]
        self.copies = [n.copy(self.acc, self.rx, rep=n.partner)]

    def second_hop(self):
        n = self.net
        wait_all(self.copies)
        self.rx[...] = self.acc[...] + self.rx[...]
        self.copies = [n.copy(self.rx, self.rz.at[k - 1], fsdp=n.plane(k)) for k in (2, 1, 3)]

    def third_hop(self):
        n = self.net
        wait_all(self.copies)
        self.acc[...] = self.rx[...] + self.rz[0] + self.rz[1] + self.rz[2]
        self.copies = [n.copy(self.acc, self.rs.at[d - 1], seq=n.seq(d)) for d in (3, 2, 1)]

    def finish(self):
        wait_all(self.copies)
        self.out[...] = self.acc[...] + self.rs[0] + self.rs[1] + self.rs[2]


class Background:
    def __init__(self, net, jobs, ins, own_outs, outs, scratch):
        self.queues, self.made = [], []
        for job, layer, points in jobs:
            a, b, c = len(job.inputs), len(job.shapes), len(job.scratch)
            given = list(ins[:a]) + [own_outs[i] for i in getattr(job, "own", ())]
            made = job(net, layer, given, outs[:b], scratch[:c])
            self.made.append((made, outs[:b]))
            stages = made.stages()
            last = points[-1]
            points = tuple(points) + (last,) * (len(stages) - len(points))
            self.queues.append(list(zip(points, stages)))
            ins, outs, scratch = ins[a:], outs[b:], scratch[c:]

    def at(self, point):
        for queue in self.queues:
            while queue and queue[0][0] <= point:
                queue.pop(0)[1]()

    def drain(self):
        while any(self.queues):
            for queue in self.queues:
                if queue:
                    queue.pop(0)[1]()


COPIES = 112


class Late:
    def __init__(self, array):
        self.array = array


def call(kernel, inputs, outputs, scratch, jobs, shards, cid):
    given = [shards[name] for job, *_ in jobs for name in job.inputs]
    results = [
        (jax.ShapeDtypeStruct(shape, job.kind), job.out_space)
        for job, *_ in jobs
        for shape in job.shapes
    ]
    vmem, anywhere = pl.BlockSpec(memory_space=pltpu.VMEM), pl.BlockSpec(memory_space=pl.ANY)
    job_scratch = [pltpu.VMEM(shape, job.kind) for job, *_ in jobs for shape in job.scratch]
    late_in = [i for i, x in enumerate(inputs) if isinstance(x, Late)]
    arrays = [x.array if isinstance(x, Late) else x for x in inputs]
    late_out = [i for i, x in enumerate(outputs) if len(x) == 3]
    late = [pltpu.VMEM(arrays[i].shape, arrays[i].dtype) for i in late_in]
    late += [pltpu.VMEM(outputs[i][0], outputs[i][1]) for i in late_out]

    def body(*refs):
        a = len(inputs)
        b = a + len(given)
        c = b + len(outputs)
        d = c + len(results)
        e = d + len(scratch)
        f = e + len(job_scratch)
        g = f + len(late)
        net = Net(*refs[g:])
        ins, outs = list(refs[:a]), list(refs[b:c])
        net.coming, net.going = {}, []
        for i, ref in zip(late_in, refs[f:]):
            net.coming[id(ref)] = net.move(ins[i], ref)
            ins[i] = ref
        there = {}
        for i, ref in zip(late_out, refs[f + len(late_in) : g]):
            there[id(ref)] = outs[i]
            outs[i] = ref
        net.there = there
        ground = Background(net, jobs, refs[a:b], outs + list(refs[d:e]), refs[c:d], refs[e:f])
        kernel(net, ground, *ins, *outs, *refs[d:e])
        assert not net.coming and not there
        wait_all(net.going)

    made = pl.pallas_call(
        body,
        out_shape=[jax.ShapeDtypeStruct(x[0], x[1]) for x in outputs] + [shape for shape, _ in results],
        in_specs=[anywhere if i in late_in else vmem for i in range(len(inputs))]
        + [pl.BlockSpec(memory_space=job.space) for job, *_ in jobs for _ in job.inputs],
        out_specs=[anywhere if i in late_out else vmem for i in range(len(outputs))]
        + [pl.BlockSpec(memory_space=where) for _, where in results],
        scratch_shapes=[pltpu.VMEM(shape, kind) for shape, kind in scratch]
        + job_scratch
        + late
        + [
            pltpu.SemaphoreType.DMA((COPIES,)),
            pltpu.SemaphoreType.DMA((COPIES,)),
            pltpu.SemaphoreType.DMA((56,)),
        ],
        compiler_params=pltpu.CompilerParams(
            collective_id=cid, has_side_effects=True, vmem_limit_bytes=60 << 20
        ),
        cost_estimate=pl.CostEstimate(flops=0, bytes_accessed=1 << 20, transcendentals=0),
    )(*arrays, *given)
    return made[: len(outputs)], made[len(outputs) :]


def prologue_kernel(net, ground):
    net.greet(net.everyone())
    net.met()
    ground.drain()


def rms_rows(x):
    return lax.rsqrt(jnp.mean(x * x, -1, keepdims=True) + EPS)


def turn(x, cosine, sine):
    half = HEAD_DIM // 2
    return x * cosine + jnp.concatenate([x[:, half:], x[:, :half]], 1) * sine


def attn_forward_kernel(
    here, net, ground, h, gains, cosine, sine, *refs
):
    if here:
        w_qkv, w_out = ground.made[0][1]
    else:
        w_qkv, w_out, *refs = refs
    (
        middle, second, every, queries, keys, values, attended, totals,
        near_out, near_in, away_out, away_in,
    ) = refs
    net.greet(net.everyone())
    x = h[...]
    every[net.s] = (x * rms_rows(x) * gains[0:1, :]).astype(bf16)
    net.met()
    ground.at(0)
    far = net.copy(every.at[net.s], every.at[net.s], seq=net.seq(2))
    near = net.copy(every.at[net.s], every.at[net.s], seq=net.seq(1))
    ground.at(1)

    def project(b):
        joint = dot(every[b], w_qkv[...].reshape(D, 3 * COLS))
        c, sn = cosine[b], sine[b]
        for i in range(HEADS_DEV):
            at = i * HEAD_DIM
            queries[i, b] = turn(joint[:, at : at + HEAD_DIM], c, sn).astype(bf16)
            at += COLS
            keys[i, b] = turn(joint[:, at : at + HEAD_DIM], c, sn).astype(bf16)
            at += COLS
            values[i, b] = joint[:, at : at + HEAD_DIM].astype(bf16)

    if not here:
        project(net.s)
    near.wait_recv()
    ground.at(2)
    if not here:
        project(net.seq(1))
    far.wait_recv()
    passed = net.copy(every.at[net.seq(2)], every.at[net.seq(2)], seq=net.seq(1))
    ground.at(3)
    if here:
        project(net.s)
        project(net.seq(1))
    project(net.seq(2))
    passed.wait_recv()
    project(net.seq(3))
    net.done(every, queries, keys, values)
    ground.at(4)
    tokens = h.shape[0]

    def head(i):
        for b in range(SEQ):
            size = (b + 1) * tokens
            scores = dot_nt(queries[i, b], keys[i, : b + 1].reshape(size, HEAD_DIM))
            row = lax.broadcasted_iota(jnp.int32, (tokens, size), 0) + b * tokens
            col = lax.broadcasted_iota(jnp.int32, (tokens, size), 1)
            scores = jnp.where(row >= col, scores * HEAD_DIM**-0.5, MASKED)
            top = jnp.max(scores, -1, keepdims=True)
            weights = jnp.exp(scores - top)
            total = jnp.sum(weights, -1, keepdims=True)
            weights = (weights * (1.0 / total)).astype(bf16)
            attended[i, b] = dot(weights, values[i, : b + 1].reshape(size, HEAD_DIM))
            totals[i, b] = jnp.broadcast_to(top + jnp.log(total), (tokens, 128))

    for i in range(HEADS_DEV):
        head(i)
        ground.at(5 + i)
    net.done(attended, totals)

    def part(b):
        low = jnp.concatenate([attended[i, b].astype(bf16) for i in range(HEADS_DEV)], 1)
        return dot(low, w_out[...].reshape(COLS, D))

    near_out[0] = part(net.seq(1)).astype(bf16)
    near_out[1] = part(net.seq(3)).astype(bf16)
    near_sum = net.copy(near_out, near_in, seq=net.seq(1))
    away = part(net.seq(2))
    own = part(net.s)
    near_sum.wait_recv()
    away_out[...] = (away + near_in[1].astype(f32)).astype(bf16)
    away_sum = net.copy(away_out, away_in, seq=net.seq(2))
    own = h[...] + own + near_in[0].astype(f32)
    ground.at(8)
    away_sum.wait_recv()
    own = own + away_in[...].astype(f32)
    middle[...] = own
    second[...] = (own * rms_rows(own) * gains[1:2, :]).astype(bf16)
    for copy in (far, near, passed, near_sum, away_sum):
        copy.wait_send()
    ground.drain()


def attn_forward(h, gains, weights, tables, jobs, shards, cid):
    t = h.shape[0]
    head = (HEADS_DEV, SEQ, t, HEAD_DIM)
    return call(
        functools.partial(attn_forward_kernel, not weights),
        [h, gains, *tables, *weights],
        [
            ((t, D), f32), ((t, D), bf16), ((SEQ, t, D), bf16, 1), (head, bf16, 1), (head, bf16, 1),
            (head, bf16, 1), (head, f32, 1), ((HEADS_DEV, SEQ, t, 128), f32, 1),
        ],
        [((2, t, D), bf16), ((2, t, D), bf16), ((t, D), bf16), ((t, D), bf16)],
        jobs, shards, cid,
    )


def silu_gate(g, u):
    return g / (1.0 + jnp.exp(-g)) * u


CHUNKS = ((0, 80), (80, 64))


class SlotTrip:
    def __init__(self, net, out, into):
        self.net, self.into = net, into
        self.sent, self.passed = {}, {}
        for c, (at, size) in enumerate(CHUNKS):
            for k in (2, 1, 3):
                e = net.plane(k)
                self.sent[c, k] = net.copy(
                    out.at[e, pl.ds(at, size)], into.at[net.core, net.z, pl.ds(at, size)], fsdp=e
                )
        into[net.core, net.z] = out[net.z]

    def hand_on(self, c):
        net, (at, size) = self.net, CHUNKS[c]
        self.passed[c] = []
        for k in (0, 1, 3, 2):
            if k:
                self.sent[c, k].wait_recv()
            part = self.into.at[net.core, net.plane(FSDP - k), pl.ds(at, size)]
            self.passed[c].append(net.copy(part, part, seq=net.seq(1)))

    def here(self, c):
        for copy in self.passed[c]:
            copy.wait_recv()

    def close(self):
        for copy in [*self.sent.values(), *self.passed[0], *self.passed[1]]:
            copy.wait_send()


class SlotReturn:
    def __init__(self, net, out, into, own, back, home):
        self.net, self.out, self.into, self.own = net, out, into, own
        self.back, self.home = back, home
        self.near, self.sent = {}, []

    def other(self, c, rows):
        at, size = CHUNKS[c]
        self.out[:, at : at + size] = rows.astype(bf16).reshape(EXPERTS, size, D)
        part = pl.ds(at, size)
        self.near[c] = self.net.copy(self.out.at[:, part], self.into.at[:, part], seq=self.net.seq(1))

    def mine(self, c, rows):
        net, (at, size) = self.net, CHUNKS[c]
        self.own[0 : EXPERTS * size] = rows
        self.near[c].wait_recv()
        got = self.into[:, at : at + size].astype(f32).reshape(EXPERTS * size, D)
        both = (self.own[0 : EXPERTS * size] + got).astype(bf16)
        self.back[:, at : at + size] = both.reshape(EXPERTS, size, D)
        for k in (2, 1, 3):
            e = net.plane(k)
            part = pl.ds(at, size)
            self.sent.append(net.copy(self.back.at[e, part], self.home.at[net.z, part], fsdp=e))
        self.home[net.z, at : at + size] = self.back[net.z, at : at + size]

    def wait(self):
        for copy in self.sent:
            copy.wait_recv()

    def close(self):
        for copy in [*self.sent, *self.near.values()]:
            copy.wait_send()


def ffn_forward_kernel(
    net, ground, second, middle, router, onehot, chosen, w_in, w_so,
    result, gates, gathered, every, joint, hidden, rows, joint_e, hidden_e,
    rows_out, prod_out, prod_in, prod_own, back_out, yields, near_out, near_in, away_out, away_in,
):
    t = second.shape[0]
    w1, w2 = ground.made[0][0].w1, ground.made[0][0].w2
    net.greet(net.everyone())
    picked = chosen[:, :t] + chosen[:, t:]
    rows_out[...] = dot(picked, second[...]).astype(bf16).reshape(EXPERTS, CAP, D)
    every[net.s] = second[...]
    net.met()
    trip = SlotTrip(net, rows_out, rows)
    far = net.copy(every.at[net.s], every.at[net.s], seq=net.seq(2))
    near = net.copy(every.at[net.s], every.at[net.s], seq=net.seq(1))
    ground.at(0)
    logits = dot(second[...], router[...])
    l0 = jnp.sum(onehot[0] * logits, -1, keepdims=True)
    l1 = jnp.sum(onehot[1] * logits, -1, keepdims=True)
    top = jnp.maximum(l0, l1)
    e0, e1 = jnp.exp(l0 - top), jnp.exp(l1 - top)
    g0, g1 = e0 / (e0 + e1), e1 / (e0 + e1)
    lane = lax.broadcasted_iota(jnp.int32, (t, 128), 1)
    gates[...] = jnp.where(lane == 0, g0, jnp.where(lane == 1, g1, 0.0))
    net.need(w_in, w_so)

    def shared(b):
        g, u = dot(every[b], w_in[0]), dot(every[b], w_in[1])
        joint[0, b] = g.astype(bf16)
        joint[1, b] = u.astype(bf16)
        low = silu_gate(g, u).astype(bf16)
        hidden[b] = low
        return dot(low, w_so[...])

    own_part = shared(net.s)
    ground.at(1)
    near.wait_recv()
    near_out[0] = shared(net.seq(1)).astype(bf16)
    far.wait_recv()
    passed_far = net.copy(every.at[net.seq(2)], every.at[net.seq(2)], seq=net.seq(1))
    away_out[...] = shared(net.seq(2)).astype(bf16)
    trip.hand_on(0)
    ground.at(2)
    passed_far.wait_recv()
    near_out[1] = shared(net.seq(3)).astype(bf16)
    near_sum = net.copy(near_out, near_in, seq=net.seq(1))
    net.done(every, joint, hidden)

    def expert(core, c):
        at, size = CHUNKS[c]
        part = slice(at, at + size)
        x = rows[core, :, part].reshape(EXPERTS * size, D)
        total = None
        for half in (0, 1):
            g = dot(x, w1[half, 0].reshape(D, FF_DEV))
            u = dot(x, w1[half, 1].reshape(D, FF_DEV))
            shape = (EXPERTS, size, FF_DEV)
            joint_e[core, half, 0, :, part] = g.astype(bf16).reshape(shape)
            joint_e[core, half, 1, :, part] = u.astype(bf16).reshape(shape)
            low = silu_gate(g, u).astype(bf16)
            hidden_e[core, half, :, part] = low.reshape(shape)
            new = dot(low, w2[half].reshape(FF_DEV, D))
            total = new if total is None else total + new
        return total

    trip.here(0)
    ground.at(3)
    back = SlotReturn(net, prod_out, prod_in, prod_own, back_out, yields)
    back.other(0, expert(1 - net.core, 0))
    trip.hand_on(1)
    near_sum.wait_recv()
    away_out[...] = (away_out[...].astype(f32) + near_in[1].astype(f32)).astype(bf16)
    away_sum = net.copy(away_out, away_in, seq=net.seq(2))
    ground.at(4)
    back.mine(0, expert(net.core, 0))
    ground.at(5)
    trip.here(1)
    back.other(1, expert(1 - net.core, 1))
    back.mine(1, expert(net.core, 1))
    net.done(rows, joint_e, hidden_e)
    ground.at(6)
    net.need(middle)
    away_sum.wait_recv()
    base = middle[...] + own_part + near_in[0].astype(f32) + away_in[...].astype(f32)
    back.wait()
    got = dot_tn(chosen[...], yields[...].reshape(SLOTS, D))
    gathered[...] = got.astype(bf16)
    result[...] = base + g0 * got[:t] + g1 * got[t:]
    for copy in [far, near, passed_far, near_sum, away_sum]:
        copy.wait_send()
    trip.close()
    back.close()
    ground.drain()


def ffn_forward(second, middle, router, onehot, chosen, w_in, w_so, jobs, shards, cid):
    t = second.shape[0]
    slots = (EXPERTS, CAP, FF_DEV)
    return call(
        ffn_forward_kernel,
        [second, Late(middle), router, onehot, chosen, Late(w_in), Late(w_so)],
        [
            ((t, D), f32), ((t, 128), f32), ((2 * t, D), bf16), ((SEQ, t, D), bf16, 1),
            ((2, SEQ, t, FF_DEV), bf16, 1), ((SEQ, t, FF_DEV), bf16, 1),
            ((2, EXPERTS, CAP, D), bf16, 1), ((2, 2, 2, *slots), bf16, 1), ((2, 2, *slots), bf16, 1),
        ],
        [
            ((EXPERTS, CAP, D), bf16), ((EXPERTS, CAP, D), bf16), ((EXPERTS, CAP, D), bf16),
            ((EXPERTS * CHUNKS[0][1], D), f32), ((EXPERTS, CAP, D), bf16),
            ((EXPERTS, CAP, D), bf16), ((2, t, D), bf16), ((2, t, D), bf16), ((t, D), bf16),
            ((t, D), bf16),
        ],
        jobs, shards, cid,
    )


def norm_back(x, gain, gradient):
    factor = rms_rows(x)
    weighted = gradient * gain
    inner = jnp.mean(weighted * x, -1, keepdims=True)
    d_x = factor * weighted - x * (factor * factor * factor) * inner
    return d_x, jnp.sum(gradient * x * factor, 0, keepdims=True)


def gate_back(g, u, gradient):
    sig = 1.0 / (1.0 + jnp.exp(-g))
    d_g = gradient * u * sig * (1.0 + g * (1.0 - sig))
    return d_g.astype(bf16), (gradient * g * sig).astype(bf16)


def ffn_backward_kernel(
    net, ground, grad, gates, onehot, chosen, gathered, middle, second, gains, router, every,
    joint, hidden, rows, joint_e, hidden_e, w_in, w_so, w1, w2,
    d_middle, small, d_w1, d_w2,
    every_g, d_joint, rows_out, d_rows, d_joint_e, prod_out, prod_in, prod_own, back_out, back_in,
    near_out, near_in, away_out, away_in, d_w_in, d_w_so,
):
    t = grad.shape[0]
    net.greet(net.everyone())
    g0, g1 = gates[:, 0:1], gates[:, 1:2]
    up = grad[...]
    pairs = jnp.concatenate([(up * g0).astype(bf16), (up * g1).astype(bf16)], 0)
    rows_out[...] = dot(chosen[...], pairs).astype(bf16).reshape(EXPERTS, CAP, D)
    every_g[net.s] = up.astype(bf16)
    net.met()
    trip = SlotTrip(net, rows_out, d_rows)
    far = net.copy(every_g.at[net.s], every_g.at[net.s], seq=net.seq(2))
    near = net.copy(every_g.at[net.s], every_g.at[net.s], seq=net.seq(1))
    ground.at(0)
    net.need(w_so, joint, w_in)

    def shared(b):
        d_hidden = dot_nt(every_g[b], w_so[...])
        d_g, d_u = gate_back(joint[0, b].astype(f32), joint[1, b].astype(f32), d_hidden)
        d_joint[0, b] = d_g
        d_joint[1, b] = d_u
        return dot_nt(d_g, w_in[0]) + dot_nt(d_u, w_in[1])

    local = shared(net.s)
    ground.at(1)
    near.wait_recv()
    near_out[0] = shared(net.seq(1)).astype(bf16)
    far.wait_recv()
    passed_far = net.copy(every_g.at[net.seq(2)], every_g.at[net.seq(2)], seq=net.seq(1))
    away_out[...] = shared(net.seq(2)).astype(bf16)
    trip.hand_on(0)
    ground.at(2)
    passed_far.wait_recv()
    near_out[1] = shared(net.seq(3)).astype(bf16)
    near_sum = net.copy(near_out, near_in, seq=net.seq(1))
    net.need(every, hidden)
    tokens = every[...].reshape(SEQ * t, D)
    for gu in (0, 1):
        d_w = dot_tn(tokens, d_joint[gu].reshape(SEQ * t, FF_DEV))
        d_w_in[gu] = d_w.astype(bf16).reshape(4, 4, 48, FF_DEV)
    d_w = dot_tn(hidden[...].reshape(SEQ * t, FF_DEV), every_g[...].reshape(SEQ * t, D))
    d_w_so[...] = d_w.astype(bf16).reshape(4, 128, D)
    net.need(w2, w1, joint_e)

    def expert(core, c):
        at, size = CHUNKS[c]
        part = slice(at, at + size)
        x = d_rows[core, :, part].reshape(EXPERTS * size, D)
        out = None
        for half in (0, 1):
            d_hidden = dot_nt(x, w2[half].reshape(FF_DEV, D))
            flat, shape = (EXPERTS * size, FF_DEV), (EXPERTS, size, FF_DEV)
            g = joint_e[core, half, 0, :, part].astype(f32).reshape(flat)
            u = joint_e[core, half, 1, :, part].astype(f32).reshape(flat)
            d_g, d_u = gate_back(g, u, d_hidden)
            d_joint_e[half, 0, core, :, part] = d_g.reshape(shape)
            d_joint_e[half, 1, core, :, part] = d_u.reshape(shape)
            new = dot_nt(d_g, w1[half, 0].reshape(D, FF_DEV))
            new = new + dot_nt(d_u, w1[half, 1].reshape(D, FF_DEV))
            out = new if out is None else out + new
        return out

    trip.here(0)
    ground.at(3)
    back = SlotReturn(net, prod_out, prod_in, prod_own, back_out, back_in)
    back.other(0, expert(1 - net.core, 0))
    trip.hand_on(1)
    near_sum.wait_recv()
    away_out[...] = (away_out[...].astype(f32) + near_in[1].astype(f32)).astype(bf16)
    away_sum = net.copy(away_out, away_in, seq=net.seq(2))
    ground.at(4)
    back.mine(0, expert(net.core, 0))
    ground.at(5)
    trip.here(1)
    back.other(1, expert(1 - net.core, 1))
    back.mine(1, expert(net.core, 1))
    ground.at(6)
    net.need(rows, hidden_e)
    for half in (0, 1):
        d_rows_all = d_rows[...].reshape(2 * SLOTS, D)
        for gu in (0, 1):
            d_w = dot_tn(
                rows[...].reshape(2 * SLOTS, D), d_joint_e[half, gu].reshape(2 * SLOTS, FF_DEV)
            )
            d_w1[half, gu] = d_w.astype(bf16).reshape(4, 4, 48, FF_DEV)
        low = jnp.concatenate(
            [hidden_e[core, half].reshape(SLOTS, FF_DEV) for core in (0, 1)], 0
        )
        d_w2[half] = dot_tn(low, d_rows_all).astype(bf16).reshape(4, 128, D)
        ground.at(7 + half)
    net.done(d_w1, d_w2)
    net.need(gathered, onehot, second, router, middle)
    d0 = jnp.sum(up * gathered[:t].astype(f32), -1, keepdims=True)
    d1 = jnp.sum(up * gathered[t:].astype(f32), -1, keepdims=True)
    mean = g0 * d0 + g1 * d1
    d_logits = (g0 * (d0 - mean) * onehot[0] + g1 * (d1 - mean) * onehot[1]).astype(bf16)
    small[8:16, :] = dot_tn(d_logits, second[...])[:8]
    local = local + dot_nt(d_logits, router[...])
    away_sum.wait_recv()
    local = local + near_in[0].astype(f32) + away_in[...].astype(f32)
    back.wait()
    picked = chosen[:, :t] + chosen[:, t:]
    d_normed = local + dot_tn(picked, back_in[...].reshape(SLOTS, D))
    d_x, d_gain = norm_back(middle[...], gains[1:2, :], d_normed)
    d_middle[...] = up + d_x
    small[0:8, :] = jnp.broadcast_to(d_gain, (8, D))
    for copy in [far, near, passed_far, near_sum, away_sum]:
        copy.wait_send()
    trip.close()
    back.close()
    ground.drain()


def ffn_backward(grad, saved, gains, router, weights, jobs, shards, cid):
    t = grad.shape[0]
    gates, onehot, chosen, gathered, middle, second, every, joint, hidden, rows, joint_e, hidden_e = saved
    w_in, w_so, w1, w2 = weights
    slots = (EXPERTS, CAP, D)
    late = {}
    for name, x in (
        ("w_so", w_so), ("joint", joint), ("w_in", w_in), ("every", every), ("hidden", hidden),
        ("w2", w2), ("joint_e", joint_e), ("w1", w1), ("rows", rows), ("hidden_e", hidden_e),
        ("gathered", gathered), ("onehot", onehot), ("second", second), ("router", router),
        ("middle", middle),
    ):
        late[name] = Late(x)
    return call(
        ffn_backward_kernel,
        [
            grad, gates, late["onehot"], chosen, late["gathered"], late["middle"], late["second"],
            gains, late["router"], late["every"], late["joint"], late["hidden"], late["rows"],
            late["joint_e"], late["hidden_e"], late["w_in"], late["w_so"], late["w1"], late["w2"],
        ],
        [
            ((t, D), f32), ((16, D), f32), ((2, 2, 4, 4, 48, FF_DEV), bf16, 1),
            ((2, 4, 128, D), bf16, 1),
        ],
        [
            ((SEQ, t, D), bf16), ((2, SEQ, t, FF_DEV), bf16), (slots, bf16), ((2, *slots), bf16),
            ((2, 2, 2, EXPERTS, CAP, FF_DEV), bf16), (slots, bf16), (slots, bf16),
            ((EXPERTS * CHUNKS[0][1], D), f32), (slots, bf16), (slots, bf16), ((2, t, D), bf16),
            ((2, t, D), bf16), ((t, D), bf16), ((t, D), bf16), ((2, 4, 4, 48, FF_DEV), bf16),
            ((4, 128, D), bf16),
        ],
        jobs, shards, cid,
    )


def attn_backward_kernel(
    net, ground, d_middle, h, gains, every, queries, keys, values, attended, totals, w_qkv, w_out,
    cosine, sine,
    grad, d_gain, d_w_qkv, d_w_out,
    every_m, d_att, d_q, d_k, d_v, d_joint, near_out, near_in, away_out, away_in,
):
    t = h.shape[0]
    net.greet(net.everyone())
    up = d_middle[...]
    every_m[net.s] = up.astype(bf16)
    net.met()
    far = net.copy(every_m.at[net.s], every_m.at[net.s], seq=net.seq(2))
    near = net.copy(every_m.at[net.s], every_m.at[net.s], seq=net.seq(1))
    ground.at(0)

    net.need(w_out)

    def project(b):
        d = dot_nt(every_m[b], w_out[...].reshape(COLS, D)).astype(bf16)
        for i in range(HEADS_DEV):
            d_att[i, b] = d[:, i * HEAD_DIM : (i + 1) * HEAD_DIM]

    project(net.s)
    near.wait_recv()
    project(net.seq(1))
    far.wait_recv()
    passed = net.copy(every_m.at[net.seq(2)], every_m.at[net.seq(2)], seq=net.seq(1))
    project(net.seq(2))
    passed.wait_recv()
    project(net.seq(3))
    ground.at(1)
    net.need(attended)
    tokens = every_m[...].reshape(SEQ * t, D)
    low = jnp.concatenate(
        [attended[i].reshape(SEQ * t, HEAD_DIM).astype(bf16) for i in range(HEADS_DEV)], 1
    )
    d_w_out[...] = dot_tn(low, tokens).astype(bf16).reshape(SEQ, 48, D)
    scale = HEAD_DIM**-0.5
    net.need(queries, keys, values, totals)

    def head(i):
        d_k[i] = jnp.zeros_like(d_k[i])
        d_v[i] = jnp.zeros_like(d_v[i])
        for b in range(SEQ):
            size = (b + 1) * t
            q, d = queries[i, b], d_att[i, b]
            k = keys[i, : b + 1].reshape(size, HEAD_DIM)
            v = values[i, : b + 1].reshape(size, HEAD_DIM)
            delta = jnp.sum(d.astype(f32) * attended[i, b], -1, keepdims=True)
            row = lax.broadcasted_iota(jnp.int32, (t, size), 0) + b * t
            col = lax.broadcasted_iota(jnp.int32, (t, size), 1)
            scores = jnp.where(row >= col, dot_nt(q, k) * scale, MASKED)
            weights = jnp.exp(scores - totals[i, b][:, 0:1])
            d_scores = (weights * (dot_nt(d, v) - delta)).astype(bf16)
            d_q[i, b] = dot(d_scores, k) * scale
            shape = (b + 1, t, HEAD_DIM)
            d_k[i, : b + 1] += (dot_tn(d_scores, q) * scale).reshape(shape)
            d_v[i, : b + 1] += dot_tn(weights.astype(bf16), d).reshape(shape)

    for i in range(HEADS_DEV):
        head(i)
        ground.at(2 + i)

    net.need(cosine, sine, w_qkv)

    def part(b):
        c, sn = cosine[b], -sine[b]
        pieces = [turn(d_q[i, b], c, sn) for i in range(HEADS_DEV)]
        pieces += [turn(d_k[i, b], c, sn) for i in range(HEADS_DEV)]
        pieces += [d_v[i, b] for i in range(HEADS_DEV)]
        d = jnp.concatenate(pieces, 1).astype(bf16)
        d_joint[b] = d
        return dot_nt(d, w_qkv[...].reshape(D, 3 * COLS))

    near_out[0] = part(net.seq(1)).astype(bf16)
    near_out[1] = part(net.seq(3)).astype(bf16)
    near_sum = net.copy(near_out, near_in, seq=net.seq(1))
    away = part(net.seq(2))
    own = part(net.s)
    near_sum.wait_recv()
    away_out[...] = (away + near_in[1].astype(f32)).astype(bf16)
    away_sum = net.copy(away_out, away_in, seq=net.seq(2))
    own = own + near_in[0].astype(f32)
    ground.at(5)
    net.need(every)
    d_w = dot_tn(every[...].reshape(SEQ * t, D), d_joint[...].reshape(SEQ * t, 3 * COLS))
    d_w_qkv[...] = d_w.astype(bf16).reshape(4, 4, 48, 3 * COLS)
    ground.at(6)
    away_sum.wait_recv()
    net.need(h)
    d_x, gain = norm_back(h[...], gains[0:1, :], own + away_in[...].astype(f32))
    grad[...] = up + d_x
    row = lax.broadcasted_iota(jnp.int32, (8, D), 0)
    d_gain[...] = jnp.where(row == 0, gain, 0.0)
    ground.at(7)
    for copy in (far, near, passed, near_sum, away_sum):
        copy.wait_send()
    ground.drain()


def attn_backward(d_middle, saved, gains, weights, tables, jobs, shards, cid):
    t = d_middle.shape[0]
    h, every, queries, keys, values, attended, totals = saved
    head = (HEADS_DEV, SEQ, t, HEAD_DIM)
    return call(
        attn_backward_kernel,
        [d_middle, Late(h), gains]
        + [Late(x) for x in (every, queries, keys, values, attended, totals, *weights, *tables)],
        [((t, D), f32), ((8, D), f32), ((4, 4, 48, 3 * COLS), bf16), ((4, 48, D), bf16)],
        [
            ((SEQ, t, D), bf16), (head, bf16), (head, f32), (head, f32), (head, f32),
            ((SEQ, t, 3 * COLS), bf16), ((2, t, D), bf16), ((2, t, D), bf16), ((t, D), bf16),
            ((t, D), bf16),
        ],
        jobs, shards, cid,
    )


FORWARD_ATTN_FIRST = (
    (AttnFetchHere, 0, (0, 1, 2, 3)),
    (SharedFetch, 0, (2, 3, 6, 9)),
    (ExpertFetch, 0, (4, 8, 9)),
)
FORWARD_FFN_FIRST = (
    (ExpertJoin, 0, (0, 3, 9)),
    (AttnFetch, 1, (0, 1, 3, 9)),
    (ExpertPlane, 1, (3, 9)),
)
FORWARD_ATTN = ((ExpertNear, 1, (1, 9)), (SharedFetch, 1, (1, 2, 5, 9)))
FORWARD_FFN = ((ExpertJoin, 1, (0, 3, 9)),)
BACKWARD_FFN_FIRST = ((SharedAcross, 1, (3, 9)),)
BACKWARD_ATTN = (
    (GateSides, 1, (0, 3, 9)),
    (UpSides, 1, (0, 3, 9)),
    (SecondSides, 1, (0, 4, 9)),
    (SharedReturn, 1, (0, 4, 5, 9)),
)
BACKWARD_FFN = (
    (SharedAcross, 0, (3, 9)),
    (AttnReturn, 1, (0, 2, 5, 8, 9)),
    (GatePlane, 1, (3, 7, 9)),
    (UpPlane, 1, (3, 8, 9)),
    (SecondPlane, 1, (3, 7, 9)),
)
BACKWARD_ATTN_LAST = (
    (GateReturn, 0, (0, 3, 5, 9)),
    (UpReturn, 0, (0, 3, 5, 9)),
    (SecondReturn, 0, (0, 4, 6, 9)),
    (SharedReturn, 0, (0, 4, 5, 9)),
    (AttnReturnHere, 0, (6, 9)),
    (SmallReturnHere, 0, (7, 9)),
)


def local(
    reps, inputs, expert_choice, pair_order, norm_gains, attn_qkv, attn_out, router, shared_in,
    shared_out, expert_in, expert_out, cotangent,
):
    r, s, z = lax.axis_index("rep"), lax.axis_index("seq"), lax.axis_index("fsdp")
    tokens = inputs.shape[1]
    position = jnp.arange(SEQ * tokens, dtype=jnp.int32)
    half = HEAD_DIM // 2
    inverse = jnp.exp(-jnp.log(10000.0) * jnp.arange(half, dtype=f32) * 2.0 / HEAD_DIM)
    angle = position.astype(f32)[:, None] * inverse[None, :]
    cosine, sine = jnp.cos(angle)[:, None, :], jnp.sin(angle)[:, None, :]
    table_cos = jnp.concatenate([cosine, cosine], -1).reshape(SEQ, tokens, HEAD_DIM)
    table_sin = jnp.concatenate([-sine, sine], -1).reshape(SEQ, tokens, HEAD_DIM)
    small = jnp.concatenate([norm_gains, router.transpose(0, 2, 1)], 1).reshape(12, 48)
    shards = {
        "small": jnp.pad(small, ((0, 4), (0, 80))),
        "attn_qkv": attn_qkv.reshape(LAYERS, 48, 3, SEQ, COLS)
        .transpose(0, 3, 1, 2, 4)
        .reshape(LAYERS, SEQ, 48, 3 * COLS),
        "attn_out": attn_out,
        "shared_in": shared_in,
        "shared_out": shared_out,
        "expert_in": expert_in,
        "expert_out": expert_out,
    }
    h = inputs[0].astype(f32)
    kept_layers = []
    _, (small,) = call(prologue_kernel, [], [], [], [(SmallFetch, 0, (0,))], shards, 11)
    small = small.reshape(16, 16, 128)[:, :12, :48].transpose(1, 0, 2).reshape(LAYERS, 6, D)
    gains = small[:, :2].astype(f32)
    routers = small[:, 2:].transpose(0, 2, 1)
    tables = (table_cos, table_sin)
    attn = ()
    for layer in range(LAYERS):
        first = layer == 0
        routes = routing(expert_choice[layer, 0], pair_order[layer, 0, 0])
        onehot = expert_choice[layer, 0].T[..., None] == jnp.arange(128, dtype=jnp.int32)
        onehot = onehot.astype(f32)
        if first:
            jobs = FORWARD_ATTN_FIRST
        else:
            jobs = FORWARD_ATTN
        (middle, second, every_one, queries, keys, values, attended, totals), fetched = attn_forward(
            h, gains[layer], attn, tables, jobs, shards, 12 + layer
        )
        names = ("ax", "ay", "bx", "by")
        if first:
            attn, shared, fetched = fetched[:2], fetched[2:4], fetched[4:]
            names = ("p1", "p2") + names
        else:
            fetched, shared = fetched[:4], fetched[4:]
        shards.update(zip(names, fetched))
        w_in, w_so = shared[0].reshape(2, D, FF_DEV), shared[1].reshape(FF_DEV, D)
        router_pad = jnp.pad(routers[layer], ((0, 0), (0, 124)))
        outs, fetched = ffn_forward(
            second, middle, router_pad, onehot, routes[1], w_in, w_so,
            FORWARD_FFN_FIRST if first else FORWARD_FFN, shards, 14 + layer,
        )
        attn_weights, ffn_weights = attn, (w_in, w_so, fetched[0], fetched[1])
        if first:
            attn = fetched[2:4]
            shards["p1"], shards["p2"] = fetched[4:]
        result, gates, gathered, every_two, joint, hidden, rows, joint_e, hidden_e = outs
        attn_saved = (h, every_one, queries, keys, values, attended, totals)
        ffn_saved = (
            gates, onehot, routes[1], gathered, middle, second, every_two, joint, hidden, rows,
            joint_e, hidden_e,
        )
        h = result
        kept_layers.append((attn_weights, ffn_weights, attn_saved, ffn_saved, router_pad))
    output = h.astype(bf16)[None]
    grad = cotangent[0].astype(f32)
    smalls = [None] * LAYERS
    returned = {}
    grads = {}
    for layer in reversed(range(LAYERS)):
        last = layer == 0
        attn_weights, ffn_weights, attn_saved, ffn_saved, router_pad = kept_layers[layer]
        (d_middle, small, grads["d_w1"], grads["d_w2"]), done = ffn_backward(
            grad, ffn_saved, gains[layer], router_pad, ffn_weights,
            BACKWARD_FFN if last else BACKWARD_FFN_FIRST, grads, 18 + layer,
        )
        grads["r1"], grads["r2"] = done[:2]
        if last:
            returned["d_attn", 1], returned["d_expert", 1] = done[2:4], done[4:]
        smalls[layer] = jnp.concatenate([small[:1], small[8:12]], 0)
        if last:
            rows = jnp.concatenate([jnp.zeros((1, D), f32), smalls[0], d_gain[:1], smalls[1]], 0)
            grads["small_rows"] = jnp.pad(rows, ((0, 4), (0, 0)))
        (grad, d_gain, d_w_qkv, d_w_out), done = attn_backward(
            d_middle, attn_saved, gains[layer], attn_weights, tables,
            BACKWARD_ATTN_LAST if last else BACKWARD_ATTN, grads, 16 + layer,
        )
        if last:
            returned["d_expert", 0], returned["d_shared", 0] = done[:3], done[3:5]
            returned["d_attn", 0], total_small = done[5:7], done[7]
        else:
            grads["q_gate"], grads["q_up"], grads["q_second"] = done[:3]
            returned["d_shared", 1] = done[3:]
            grads["d_w_qkv"], grads["d_w_out"] = d_w_qkv, d_w_out
    total_small = rep_rest(total_small, reps)[:12].reshape(LAYERS, 6, D)
    total_small = lax.dynamic_slice_in_dim(total_small, (s * FSDP + z) * 48, 48, 2)

    def stack(name, k):
        return jnp.stack([rep_rest(returned[name, i][k], reps) for i in range(LAYERS)]).astype(f32)

    d_qkv = stack("d_attn", 0).reshape(LAYERS, SEQ, 48, 3, COLS).transpose(0, 2, 3, 1, 4)
    return (
        output, grad[None], total_small[:, :2], d_qkv.reshape(LAYERS, 48, 3 * D),
        stack("d_attn", 1), total_small[:, 2:].transpose(0, 2, 1), stack("d_shared", 0),
        stack("d_shared", 1), jnp.concatenate([stack("d_expert", 0), stack("d_expert", 1)], -1),
        stack("d_expert", 2),
    )


def solution(mesh):
    tokens = P(("rep", "fsdp"), "seq", None)
    routes = P(None, ("rep", "fsdp"), "seq", None)
    gains = P(None, None, ("seq", "fsdp"))
    dense = P(None, ("seq", "fsdp"), None)
    expert = P(None, None, ("seq", "fsdp"), None)
    in_specs = (
        tokens, routes, routes, gains, dense, dense, dense, dense, dense, expert, expert, tokens,
    )
    out_specs = (tokens, tokens, gains, dense, dense, dense, dense, dense, expert, expert)
    return jax.shard_map(
        functools.partial(local, mesh.shape["rep"]),
        mesh=mesh, in_specs=in_specs, out_specs=out_specs, check_vma=False,
    )
```

```python
import functools

import jax
import jax.numpy as jnp
import numpy as np
from jax import lax
from jax.experimental import pallas as pl
from jax.experimental.pallas import tpu as pltpu
from jax.sharding import PartitionSpec as P

D = 768
HEADS = 12
HEAD_DIM = 64
FF = 2048
EXPERTS = 4
LAYERS = 2
CAP = 144
EPS = 1e-06
MASKED = -1e30
SEQ = 4
FSDP = 4
HEADS_DEV = HEADS // SEQ
COLS = HEADS_DEV * HEAD_DIM
FF_DEV = FF // SEQ
FF_CORE = FF // 2
SLOTS = EXPERTS * CAP
bf16 = jnp.bfloat16
f32 = jnp.float32
MESH = pl.DeviceIdType.MESH


def dot(a, b):
    return jnp.dot(a, b, preferred_element_type=f32)


def dot_nt(a, b):
    return lax.dot_general(a, b, (((1,), (1,)), ((), ())), preferred_element_type=f32)


def dot_tn(a, b):
    return lax.dot_general(a, b, (((0,), (0,)), ((), ())), preferred_element_type=f32)


def rep_rest(x, reps):
    bit = 2
    while bit < reps:
        x = x + lax.ppermute(x, "rep", [(i, i ^ bit) for i in range(reps)])
        bit *= 2
    return x


def routing(choices, order):
    tokens = choices.shape[0]
    pairs = 2 * tokens
    flat = choices.reshape(-1)
    ids = jnp.arange(pairs, dtype=jnp.int32)
    place = (order[:, None] == ids[None, :]).astype(bf16)
    experts = (flat[:, None] == jnp.arange(EXPERTS, dtype=jnp.int32)[None, :]).astype(bf16)
    placed = dot(place, experts).astype(bf16)
    lower = (ids[:, None] > ids[None, :]).astype(bf16)
    slot_placed = jnp.minimum(jnp.sum(dot(lower, placed) * placed.astype(f32), 1), float(CAP))
    slot = dot_tn(place, slot_placed[:, None].astype(bf16))[:, 0].astype(jnp.int32)
    kept = slot < CAP
    target = jnp.where(kept, flat * CAP + slot, SLOTS).reshape(tokens, 2)
    target = target.T.reshape(-1)
    chosen = (target[None, :] == jnp.arange(SLOTS, dtype=jnp.int32)[:, None]).astype(bf16)
    return kept.reshape(tokens, 2).astype(f32), chosen


class Net:
    def __init__(self, send, recv, local_sems):
        self.send, self.recv, self.local_sems = send, recv, local_sems
        self.count = 0
        self.local_count = 0
        self.r, self.s, self.z = (lax.axis_index(a) for a in ("rep", "seq", "fsdp"))
        self.half = lax.rem(self.r, 2)
        self.core = lax.rem(self.s, 2)
        self.far = self.s // 2
        self.partner = self.r + 1 - 2 * self.half

    def seq(self, d):
        core = self.core if d % 2 == 0 else 1 - self.core
        far = self.far if d < 2 else 1 - self.far
        return far * 2 + core

    def plane(self, k):
        return lax.rem(self.z + k, FSDP)

    def copy(self, src, dst, **device):
        k = self.count
        self.count += 1
        out = pltpu.make_async_remote_copy(
            src_ref=src, dst_ref=dst, send_sem=self.send.at[k], recv_sem=self.recv.at[k],
            device_id=device, device_id_type=MESH,
        )
        out.start()
        return out

    def move(self, src, dst):
        k = self.local_count
        self.local_count += 1
        out = pltpu.make_async_copy(src, dst, self.local_sems.at[k])
        out.start()
        return out

    def need(self, *refs):
        for ref in refs:
            self.coming.pop(id(ref)).wait()

    def done(self, *refs):
        for ref in refs:
            self.going.append(self.move(ref, self.there.pop(id(ref))))

    def greet(self, devices):
        self.barrier = pltpu.get_barrier_semaphore()
        for device in devices:
            pl.semaphore_signal(self.barrier, inc=1, device_id=device, device_id_type=MESH)
        self.greeted = len(devices)

    def met(self):
        pl.semaphore_wait(self.barrier, self.greeted)

    def everyone(self):
        seqs = [{"seq": self.seq(d)} for d in (1, 2, 3)]
        planes = [{"fsdp": self.plane(k)} for k in (1, 2, 3)]
        both = [{"seq": self.seq(1), "fsdp": self.plane(k)} for k in (1, 2, 3)]
        return seqs + planes + both + [{"rep": self.partner}]


def columns(start, size):
    return pl.ds(pl.multiple_of(start, 128), size)


def wait_all(copies):
    for copy in copies:
        copy.wait()


class Job:
    space = pl.ANY
    out_space = pl.ANY
    scratch = ()
    kind = bf16

    def __init__(self, net, layer, ins, outs, scratch):
        self.net, self.layer = net, layer
        self.bind(ins, outs, scratch)


class ExpertPlane(Job):
    inputs = ("expert_in", "expert_out")
    shapes = ((2, 2, 4, 48, FF_DEV), (4, 128, 384))

    def bind(self, ins, outs, scratch):
        self.first, self.second = ins
        self.p1, self.p2 = outs

    def stages(self):
        return [self.plane_begin, self.plane_finish]

    def plane_begin(self):
        n = self.net
        self.copies = []
        for k in (2, 1, 3, 0):
            e = n.plane(k)
            for d in (0, 1):
                core = n.core if d == 0 else 1 - n.core
                for gu in (0, 1):
                    src = self.first.at[
                        self.layer, e, :, columns(gu * FF + n.half * FF_CORE + core * FF_DEV, FF_DEV)
                    ]
                    dst = self.p1.at[gu, n.core, n.z]
                    if k == 0 and d == 0:
                        self.copies.append(n.move(src, dst))
                    else:
                        self.copies.append(n.copy(src, dst, seq=n.seq(d), fsdp=e))
            src = self.second.at[self.layer, e, :, columns(n.half * 384, 384)]
            dst = self.p2.at[n.z]
            self.copies.append(n.move(src, dst) if k == 0 else n.copy(src, dst, fsdp=e))

    def plane_finish(self):
        wait_all(self.copies)


class ExpertFetch(ExpertPlane):
    shapes = ExpertPlane.shapes + ((2, 2, 4, 48, FF_DEV), (2, 2, 4, 48, FF_DEV)) + (
        (4, 128, 384), (4, 128, 384),
    )

    def bind(self, ins, outs, scratch):
        ExpertPlane.bind(self, ins, outs[:2], ())
        self.ax, self.ay, self.bx, self.by = outs[2:]

    def stages(self):
        def turn_over():
            self.plane_finish()
            self.near_begin()

        return [self.plane_begin, turn_over, self.near_finish]

    def near_begin(self):
        n = self.net
        self.sides = [
            n.copy(self.p1, self.ax, rep=n.partner), n.copy(self.p1, self.ay, seq=n.seq(2)),
            n.copy(self.p2, self.bx, rep=n.partner), n.copy(self.p2, self.by, seq=n.seq(2)),
        ]

    def near_finish(self):
        wait_all(self.sides)


class ExpertNear(ExpertFetch):
    inputs = ("next_p1", "next_p2")
    shapes = ExpertFetch.shapes[2:]

    def bind(self, ins, outs, scratch):
        self.p1, self.p2 = ins
        self.ax, self.ay, self.bx, self.by = outs

    def stages(self):
        return [self.near_begin, self.near_finish]


class ExpertJoin(Job):
    inputs = ("p1", "p2", "ax", "ay", "bx", "by")
    shapes = ((2, 2, 4, 4, 48, FF_DEV), (2, 4, 128, D))
    scratch = shapes

    def bind(self, ins, outs, scratch):
        self.p1, self.p2, self.ax, self.ay, self.bx, self.by = ins
        self.outs = outs
        self.w1, self.w2 = scratch

    def stages(self):
        return [self.begin, self.finish, self.written]

    def begin(self):
        n = self.net
        here, there = pl.ds(2 * n.far, 2), pl.ds(2 * (1 - n.far), 2)
        mine, rest = columns(n.half * 384, 384), columns((1 - n.half) * 384, 384)
        low, high = pl.ds(0, 2), pl.ds(2, 2)
        w1, w2 = self.w1, self.w2
        self.copies = [
            n.copy(self.ay.at[0], w1.at[n.half, 0, there], rep=n.partner),
            n.copy(self.ax.at[1], w1.at[1 - n.half, 1, here], seq=n.seq(2)),
            n.copy(self.by.at[low], w2.at[1 - n.far, low, :, mine], rep=n.partner),
            n.copy(self.bx.at[high], w2.at[n.far, high, :, rest], seq=n.seq(2)),
            n.move(self.p1, w1.at[n.half, :, here]),
            n.move(self.ax, w1.at[1 - n.half, :, here]),
            n.move(self.ay, w1.at[n.half, :, there]),
            n.move(self.p2, w2.at[n.far, :, :, mine]),
            n.move(self.bx, w2.at[n.far, :, :, rest]),
            n.move(self.by, w2.at[1 - n.far, :, :, mine]),
        ]

    def finish(self):
        wait_all(self.copies)
        self.copies = [
            self.net.move(self.w1, self.outs[0]), self.net.move(self.w2, self.outs[1])
        ]

    def written(self):
        wait_all(self.copies)


class SharedFetch(Job):
    inputs = ("shared_in", "shared_out")
    shapes = ((2, 4, 4, 48, FF_DEV), (4, 128, D))

    def bind(self, ins, outs, scratch):
        self.first, self.second = ins
        self.w_in, self.w_out = outs

    def stages(self):
        return [self.begin, self.second_hop, self.third_hop, self.finish]

    def begin(self):
        n = self.net
        self.firsts = []
        for d in (3, 2, 1, 0):
            src = self.first.at[self.layer, :, columns(n.half * FF + n.seq(d) * FF_DEV, FF_DEV)]
            dst = self.w_in.at[n.half, n.s, n.z]
            self.firsts.append(n.move(src, dst) if d == 0 else n.copy(src, dst, seq=n.seq(d)))
        src = self.second.at[self.layer, :, columns(n.half * 384, 384)]
        self.firsts.append(n.move(src, self.w_out.at[n.z, :, columns(n.half * 384, 384)]))

    def second_hop(self):
        n = self.net
        wait_all(self.firsts)
        part, low = self.w_in.at[n.half, :, n.z], self.w_out.at[n.z, :, columns(n.half * 384, 384)]
        self.sent = {}
        for k in (2, 1, 3):
            self.sent[k] = [n.copy(part, part, fsdp=n.plane(k)), n.copy(low, low, fsdp=n.plane(k))]
        self.across = [n.copy(part, part, rep=n.partner), n.copy(low, low, rep=n.partner)]

    def third_hop(self):
        n = self.net
        for k in (1, 3, 2):
            wait_all(self.sent[k])
            z = n.plane(FSDP - k)
            for part in (self.w_in.at[n.half, :, z], self.w_out.at[z, :, columns(n.half * 384, 384)]):
                self.across.append(n.copy(part, part, rep=n.partner))

    def finish(self):
        wait_all(self.across)


class AttnFetch(Job):
    inputs = ("attn_qkv", "attn_out")
    shapes = ((4, 4, 48, 3 * COLS), (4, 48, D))

    def bind(self, ins, outs, scratch):
        self.qkv, self.out = ins
        self.w_qkv, self.w_out = outs

    def stages(self):
        return [self.begin, self.second_hop, self.third_hop, self.finish]

    def begin(self):
        n = self.net
        self.firsts, self.seconds = [], []
        for d in (3, 2, 1, 0):
            src, dst = self.qkv.at[self.layer, n.seq(d)], self.w_qkv.at[n.s, n.z]
            self.firsts.append(n.move(src, dst) if d == 0 else n.copy(src, dst, seq=n.seq(d)))
        for k in (2, 1, 3, 0):
            src = self.out.at[self.layer, :, columns(n.half * 384, 384)]
            dst = self.w_out.at[n.z, :, columns(n.half * 384, 384)]
            self.seconds.append(n.move(src, dst) if k == 0 else n.copy(src, dst, fsdp=n.plane(k)))

    def second_hop(self):
        n = self.net
        wait_all(self.firsts)
        part = self.w_qkv.at[pl.ds(2 * n.half, 2), n.z]
        self.firsts = [n.copy(part, part, fsdp=n.plane(k)) for k in (2, 1, 3)]
        wait_all(self.seconds)
        part = self.w_out.at[:, :, columns(n.half * 384, 384)]
        self.across = [n.copy(part, part, rep=n.partner)]

    def third_hop(self):
        n = self.net
        for copy, k in zip(self.firsts[1:] + self.firsts[:1], (1, 3, 2)):
            copy.wait()
            part = self.w_qkv.at[pl.ds(2 * n.half, 2), n.plane(FSDP - k)]
            self.across.append(n.copy(part, part, rep=n.partner))

    def finish(self):
        wait_all(self.across)


class AttnFetchHere(AttnFetch):
    out_space = pltpu.VMEM


class SmallFetch(Job):
    out_space = pltpu.VMEM

    inputs = ("small",)
    shapes = ((4, 4, 16, 128),)

    def bind(self, ins, outs, scratch):
        (self.src,), (self.dst,) = ins, outs

    def stages(self):
        return [self.begin, self.second_hop, self.finish]

    def begin(self):
        n = self.net
        dst = self.dst.at[n.s, n.z]
        self.copies = [n.copy(self.src, dst, seq=n.seq(d)) for d in (3, 2, 1)]
        self.copies.append(n.move(self.src, dst))

    def second_hop(self):
        n = self.net
        wait_all(self.copies)
        part = self.dst.at[:, n.z]
        self.copies = [n.copy(part, part, fsdp=n.plane(k)) for k in (2, 1, 3)]

    def finish(self):
        wait_all(self.copies)


def total(*parts):
    out = parts[0].astype(f32)
    for part in parts[1:]:
        out = out + part.astype(f32)
    return out.astype(bf16)


class FirstSides(Job):
    inputs = ("d_w1",)
    out_space = pltpu.VMEM
    shapes = ((2, 4, 48, FF_DEV),)
    scratch = ((2, 2, 4, 48, FF_DEV), (2, 2, 4, 48, FF_DEV))

    def bind(self, ins, outs, scratch):
        (self.d,), (self.q,) = ins, outs
        self.own, self.got = scratch

    def stages(self):
        return [self.sides_begin, self.sides_second, self.sides_finish]

    def sides_begin(self):
        n = self.net
        if self.gu == 0:
            src = [self.d.at[1 - n.half, 0, pl.ds(2 * f, 2)] for f in (0, 1)]
            kept = [self.d.at[n.half, 0, pl.ds(2 * f, 2)] for f in (0, 1)]
            device = {"rep": n.partner}
        else:
            src = [self.d.at[h, 1, pl.ds(2 * (1 - n.far), 2)] for h in (0, 1)]
            kept = [self.d.at[h, 1, pl.ds(2 * n.far, 2)] for h in (0, 1)]
            device = {"seq": n.seq(2)}
        self.sent = [n.copy(src[i], self.got.at[i], **device) for i in (0, 1)]
        self.sent += [n.move(kept[i], self.own.at[i]) for i in (0, 1)]

    def sides_second(self):
        n = self.net
        wait_all(self.sent)
        stays = n.far if self.gu == 0 else n.half
        device = {"seq": n.seq(2)} if self.gu == 0 else {"rep": n.partner}
        goes = 1 - stays
        self.got[goes] = total(self.got[goes], self.own[goes])
        self.sent = [n.copy(self.got.at[goes], self.q, **device)]
        self.got[stays] = total(self.got[stays], self.own[stays])

    def sides_finish(self):
        n = self.net
        wait_all(self.sent)
        self.q[...] = total(self.q[...], self.got[n.far if self.gu == 0 else n.half])


class FirstPlane(Job):
    space = pltpu.VMEM
    shapes = ((EXPERTS, 48, FF),)
    half_only = False

    def bind(self, ins, outs, scratch):
        (self.q,), (self.o,) = ins, outs

    def stages(self):
        return [self.plane_begin, self.plane_second, self.plane_finish]

    def plane_begin(self):
        n = self.net
        self.sent = []
        at = n.core * FF_DEV if self.half_only else n.half * FF_CORE + n.core * FF_DEV
        dst = self.o.at[n.z, :, columns(at, FF_DEV)]
        for k in (2, 1, 3, 0):
            for d in (1, 0):
                core = n.core if d == 0 else 1 - n.core
                src = self.q.at[core, n.plane(k)]
                if k == 0 and d == 0:
                    self.sent.append(n.move(src, dst))
                else:
                    self.sent.append(n.copy(src, dst, seq=n.seq(d), fsdp=n.plane(k)))

    def plane_second(self):
        n = self.net
        wait_all(self.sent)
        part = self.o.at[:, :, columns(n.half * FF_CORE, FF_CORE)]
        self.sent = [n.copy(part, part, rep=n.partner)]

    def plane_finish(self):
        wait_all(self.sent)


class FirstReturn(FirstSides, FirstPlane):
    shapes = FirstPlane.shapes
    scratch = FirstSides.scratch + FirstSides.shapes
    space = pl.ANY
    out_space = pl.ANY

    def bind(self, ins, outs, scratch):
        FirstSides.bind(self, ins, scratch[2:], scratch[:2])
        FirstPlane.bind(self, scratch[2:], outs, ())

    def turn_over(self):
        self.sides_finish()
        self.plane_begin()

    def stages(self):
        return [
            self.sides_begin, self.sides_second, self.turn_over, self.plane_second,
            self.plane_finish,
        ]


class FirstToPlane(FirstReturn):
    shapes = ((EXPERTS, 48, FF_CORE),)
    half_only = True

    def stages(self):
        return [self.sides_begin, self.sides_second, self.turn_over, self.plane_finish]


class FirstFinal(Job):
    shapes = ((EXPERTS, 48, FF),)

    def bind(self, ins, outs, scratch):
        (self.q,), (self.o,) = ins, outs

    def stages(self):
        return [self.begin, self.finish]

    def begin(self):
        n = self.net
        part = self.o.at[:, :, columns(n.half * FF_CORE, FF_CORE)]
        self.sent = [n.copy(self.q, part, rep=n.partner), n.move(self.q, part)]

    def finish(self):
        wait_all(self.sent)


class GateReturn(FirstReturn):
    gu = 0


class UpReturn(FirstReturn):
    gu = 1


class GateToPlane(FirstToPlane):
    gu = 0


class UpToPlane(FirstToPlane):
    gu = 1


class GateFinal(FirstFinal):
    inputs = ("q_gate",)


class UpFinal(FirstFinal):
    inputs = ("q_up",)


class SecondReturn(Job):
    inputs = ("d_w2",)
    shapes = ((EXPERTS, 128, D),)
    scratch = ((2, 4, 128, 384), (2, 4, 128, 384), (4, 128, 384))
    rep_first = True

    def bind(self, ins, outs, scratch):
        (self.d,), (self.o,) = ins, outs
        self.own, self.got, self.q = scratch

    def stages(self):
        return [
            self.sides_begin, self.sides_second, self.turn_over, self.plane_second,
            self.plane_finish,
        ]

    def sides_begin(self):
        n = self.net
        halves = [columns(h * 384, 384) for h in (0, 1)]
        mine, rest = columns(n.half * 384, 384), columns((1 - n.half) * 384, 384)
        if self.rep_first:
            src = [self.d.at[f, :, :, rest] for f in (0, 1)]
            kept = [self.d.at[f, :, :, mine] for f in (0, 1)]
            device = {"rep": n.partner}
        else:
            src = [self.d.at[1 - n.far, :, :, h] for h in halves]
            kept = [self.d.at[n.far, :, :, h] for h in halves]
            device = {"seq": n.seq(2)}
        self.sent = [n.copy(src[i], self.got.at[i], **device) for i in (0, 1)]
        self.sent += [n.move(kept[i], self.own.at[i]) for i in (0, 1)]

    def sides_second(self):
        n = self.net
        wait_all(self.sent)
        self.stays = n.far if self.rep_first else n.half
        device = {"seq": n.seq(2)} if self.rep_first else {"rep": n.partner}
        goes = 1 - self.stays
        self.got[goes] = total(self.got[goes], self.own[goes])
        self.sent = [n.copy(self.got.at[goes], self.q, **device)]
        self.got[self.stays] = total(self.got[self.stays], self.own[self.stays])

    def target(self):
        return columns(self.net.half * 384, 384)

    def turn_over(self):
        n = self.net
        wait_all(self.sent)
        self.q[...] = total(self.q[...], self.got[self.stays])
        self.sent = []
        dst = self.o.at[n.z, :, self.target()]
        for k in (2, 1, 3, 0):
            src = self.q.at[n.plane(k)]
            self.sent.append(n.move(src, dst) if k == 0 else n.copy(src, dst, fsdp=n.plane(k)))

    def plane_second(self):
        n = self.net
        wait_all(self.sent)
        part = self.o.at[:, :, columns(n.half * 384, 384)]
        self.sent = [n.copy(part, part, rep=n.partner)]

    def plane_finish(self):
        wait_all(self.sent)


class SecondToPlane(SecondReturn):
    shapes = ((EXPERTS, 128, 384),)

    def stages(self):
        return [self.sides_begin, self.sides_second, self.turn_over, self.plane_finish]

    def target(self):
        return pl.ds(0, 384)


class SecondFinal(FirstFinal):
    inputs = ("q_second",)
    shapes = ((EXPERTS, 128, D),)

    def begin(self):
        n = self.net
        part = self.o.at[:, :, columns(n.half * 384, 384)]
        self.sent = [n.copy(self.q, part, rep=n.partner), n.move(self.q, part)]


class SharedAcross(Job):
    inputs = ()
    own = (-2, -1)
    out_space = pltpu.VMEM
    shapes = ((4, 4, 48, FF_DEV), (4, 128, 384))

    def bind(self, ins, outs, scratch):
        self.d1, self.d2 = ins
        self.r1, self.r2 = outs

    def stages(self):
        return [self.begin, self.finish]

    def begin(self):
        n = self.net
        part = self.d2.at[:, :, columns((1 - n.half) * 384, 384)]
        self.sent = [
            n.copy(self.d1.at[1 - n.half], self.r1, rep=n.partner),
            n.copy(part, self.r2, rep=n.partner),
        ]

    def finish(self):
        n = self.net
        wait_all(self.sent)
        self.r1[...] = total(self.r1[...], self.d1[n.half])
        self.r2[...] = total(self.r2[...], self.d2[:, :, columns(n.half * 384, 384)])


class SharedReturn(Job):
    space = pltpu.VMEM
    inputs = ("r1", "r2")
    shapes = ((48, 2 * FF), (128, D))
    scratch = ((3, 4, 48, FF_DEV), (4, 48, FF_DEV), (3, 128, 384), (128, 384))

    def bind(self, ins, outs, scratch):
        self.r1, self.r2 = ins
        self.o1, self.o2 = outs
        self.r1z, self.s1, self.r2z, self.s2 = scratch

    def stages(self):
        return [self.second_hop, self.third_hop, self.fourth_hop, self.finish]

    def second_hop(self):
        n = self.net
        self.firsts = [
            n.copy(self.r1.at[:, n.plane(k)], self.r1z.at[k - 1], fsdp=n.plane(k))
            for k in (2, 1, 3)
        ]
        self.seconds = [
            n.copy(self.r2.at[n.plane(k)], self.r2z.at[k - 1], fsdp=n.plane(k)) for k in (2, 1, 3)
        ]

    def third_hop(self):
        n = self.net
        wait_all(self.firsts + self.seconds)
        self.s1[...] = total(self.r1[:, n.z], self.r1z[0], self.r1z[1], self.r1z[2])
        self.firsts = []
        for d in (3, 2, 1, 0):
            src = self.s1.at[n.seq(d)]
            dst = self.o1.at[:, columns(n.half * FF + n.s * FF_DEV, FF_DEV)]
            self.firsts.append(n.move(src, dst) if d == 0 else n.copy(src, dst, seq=n.seq(d)))
        self.s2[...] = total(self.r2[n.z], self.r2z[0], self.r2z[1], self.r2z[2])
        dst = self.o2.at[:, columns(n.half * 384, 384)]
        self.seconds = [n.copy(self.s2, dst, rep=n.partner), n.move(self.s2, dst)]

    def fourth_hop(self):
        n = self.net
        wait_all(self.firsts)
        part = self.o1.at[:, columns(n.half * FF, FF)]
        self.firsts = [n.copy(part, part, rep=n.partner)]

    def finish(self):
        wait_all(self.firsts + self.seconds)


class AttnReturn(Job):
    space = pltpu.VMEM
    inputs = ("d_w_qkv", "d_w_out")
    shapes = ((4, 48, 3 * COLS), (48, D))
    scratch = (
        (2, 4, 48, 3 * COLS), (3, 2, 48, 3 * COLS), (4, 48, 3 * COLS), (4, 48, 384), (3, 48, 384),
        (48, 384),
    )

    def bind(self, ins, outs, scratch):
        self.d1, self.d2 = ins
        self.o1, self.o2 = outs
        self.r1, self.r1z, self.s1, self.r2, self.r2z, self.s2 = scratch

    def stages(self):
        return [self.begin, self.second_hop, self.third_hop, self.fourth_hop, self.finish]

    def begin(self):
        n = self.net
        self.firsts = [n.copy(self.d1.at[pl.ds(2 * (1 - n.half), 2)], self.r1, rep=n.partner)]
        part = self.d2.at[:, :, columns((1 - n.half) * 384, 384)]
        self.seconds = [n.copy(part, self.r2, rep=n.partner)]

    def second_hop(self):
        n = self.net
        wait_all(self.firsts)
        self.r1[...] = total(self.r1[...], self.d1[pl.ds(2 * n.half, 2)])
        self.firsts = [
            n.copy(self.r1.at[:, n.plane(k)], self.r1z.at[k - 1], fsdp=n.plane(k))
            for k in (2, 1, 3)
        ]
        wait_all(self.seconds)
        self.r2[...] = total(self.r2[...], self.d2[:, :, columns(n.half * 384, 384)])
        self.seconds = [
            n.copy(self.r2.at[n.plane(k)], self.r2z.at[k - 1], fsdp=n.plane(k)) for k in (2, 1, 3)
        ]

    def third_hop(self):
        n = self.net
        wait_all(self.firsts + self.seconds)
        pair = pl.ds(2 * n.half, 2)
        self.s1[pair] = total(self.r1[:, n.z], self.r1z[0], self.r1z[1], self.r1z[2])
        self.firsts = [n.copy(self.s1.at[pair], self.s1.at[pair], rep=n.partner)]
        self.s2[...] = total(self.r2[n.z], self.r2z[0], self.r2z[1], self.r2z[2])
        dst = self.o2.at[:, columns(n.half * 384, 384)]
        self.seconds = [n.copy(self.s2, dst, rep=n.partner), n.move(self.s2, dst)]

    def fourth_hop(self):
        n = self.net
        wait_all(self.firsts)
        self.firsts = []
        for d in (3, 2, 1, 0):
            src, dst = self.s1.at[n.seq(d)], self.o1.at[n.s]
            self.firsts.append(n.move(src, dst) if d == 0 else n.copy(src, dst, seq=n.seq(d)))

    def finish(self):
        wait_all(self.firsts + self.seconds)


class AttnReturnHere(AttnReturn):
    inputs = ()
    own = (2, 3)


class SmallReturnHere(Job):
    inputs = ("small_0", "gain_1", "small_1")
    space = pltpu.VMEM
    out_space = pltpu.VMEM
    kind = f32
    own = (1,)
    shapes = ((16, D),)
    scratch = ((16, D), (16, D), (3, 16, D), (3, 16, D))

    def bind(self, ins, outs, scratch):
        self.zero, self.gain_one, self.one, self.gain = ins
        (self.out,) = outs
        self.acc, self.rx, self.rz, self.rs = scratch

    def stages(self):
        return [self.begin, self.second_hop, self.third_hop, self.finish]

    def begin(self):
        n = self.net
        self.acc[12:16] = jnp.zeros((4, D), f32)
        for at, gain, rest in ((0, self.gain, self.zero), (6, self.gain_one, self.one)):
            self.acc[at : at + 1] = gain[0:1]
            self.acc[at + 1 : at + 2] = rest[0:1]
            self.acc[at + 2 : at + 6] = rest[8:12]
        self.copies = [n.copy(self.acc, self.rx, rep=n.partner)]

    def second_hop(self):
        n = self.net
        wait_all(self.copies)
        self.rx[...] = self.acc[...] + self.rx[...]
        self.copies = [n.copy(self.rx, self.rz.at[k - 1], fsdp=n.plane(k)) for k in (2, 1, 3)]

    def third_hop(self):
        n = self.net
        wait_all(self.copies)
        self.acc[...] = self.rx[...] + self.rz[0] + self.rz[1] + self.rz[2]
        self.copies = [n.copy(self.acc, self.rs.at[d - 1], seq=n.seq(d)) for d in (3, 2, 1)]

    def finish(self):
        wait_all(self.copies)
        self.out[...] = self.acc[...] + self.rs[0] + self.rs[1] + self.rs[2]


class Background:
    def __init__(self, net, jobs, ins, own_outs, outs, scratch):
        self.queues, self.made = [], []
        for job, layer, points in jobs:
            a, b, c = len(job.inputs), len(job.shapes), len(job.scratch)
            given = list(ins[:a]) + [own_outs[i] for i in getattr(job, "own", ())]
            made = job(net, layer, given, outs[:b], scratch[:c])
            self.made.append((made, outs[:b]))
            stages = made.stages()
            last = points[-1]
            points = tuple(points) + (last,) * (len(stages) - len(points))
            self.queues.append(list(zip(points, stages)))
            ins, outs, scratch = ins[a:], outs[b:], scratch[c:]

    def at(self, point):
        for queue in self.queues:
            while queue and queue[0][0] <= point:
                queue.pop(0)[1]()

    def drain(self):
        for point in range(9, 30):
            self.at(point)


COPIES = 112


class Late:
    def __init__(self, array):
        self.array = array


def call(kernel, inputs, outputs, scratch, jobs, shards, cid):
    given = [shards[name] for job, *_ in jobs for name in job.inputs]
    results = [
        (jax.ShapeDtypeStruct(shape, job.kind), job.out_space)
        for job, *_ in jobs
        for shape in job.shapes
    ]
    vmem, anywhere = pl.BlockSpec(memory_space=pltpu.VMEM), pl.BlockSpec(memory_space=pl.ANY)
    job_scratch = [pltpu.VMEM(shape, job.kind) for job, *_ in jobs for shape in job.scratch]
    late_in = [i for i, x in enumerate(inputs) if isinstance(x, Late)]
    arrays = [x.array if isinstance(x, Late) else x for x in inputs]
    late_out = [i for i, x in enumerate(outputs) if len(x) == 3]
    late = [pltpu.VMEM(arrays[i].shape, arrays[i].dtype) for i in late_in]
    late += [pltpu.VMEM(outputs[i][0], outputs[i][1]) for i in late_out]

    def body(*refs):
        a = len(inputs)
        b = a + len(given)
        c = b + len(outputs)
        d = c + len(results)
        e = d + len(scratch)
        f = e + len(job_scratch)
        g = f + len(late)
        net = Net(*refs[g:])
        ins, outs = list(refs[:a]), list(refs[b:c])
        net.coming, net.going = {}, []
        for i, ref in zip(late_in, refs[f:]):
            net.coming[id(ref)] = net.move(ins[i], ref)
            ins[i] = ref
        there = {}
        for i, ref in zip(late_out, refs[f + len(late_in) : g]):
            there[id(ref)] = outs[i]
            outs[i] = ref
        net.there = there
        ground = Background(net, jobs, refs[a:b], outs + list(refs[d:e]), refs[c:d], refs[e:f])
        kernel(net, ground, *ins, *outs, *refs[d:e])
        assert not net.coming and not there
        wait_all(net.going)

    made = pl.pallas_call(
        body,
        out_shape=[jax.ShapeDtypeStruct(x[0], x[1]) for x in outputs] + [shape for shape, _ in results],
        in_specs=[anywhere if i in late_in else vmem for i in range(len(inputs))]
        + [pl.BlockSpec(memory_space=job.space) for job, *_ in jobs for _ in job.inputs],
        out_specs=[anywhere if i in late_out else vmem for i in range(len(outputs))]
        + [pl.BlockSpec(memory_space=where) for _, where in results],
        scratch_shapes=[pltpu.VMEM(shape, kind) for shape, kind in scratch]
        + job_scratch
        + late
        + [
            pltpu.SemaphoreType.DMA((COPIES,)),
            pltpu.SemaphoreType.DMA((COPIES,)),
            pltpu.SemaphoreType.DMA((56,)),
        ],
        compiler_params=pltpu.CompilerParams(
            collective_id=cid, has_side_effects=True, vmem_limit_bytes=60 << 20
        ),
        cost_estimate=pl.CostEstimate(flops=0, bytes_accessed=1 << 20, transcendentals=0),
    )(*arrays, *given)
    return made[: len(outputs)], made[len(outputs) :]


def rms_rows(x):
    return lax.rsqrt(jnp.mean(x * x, -1, keepdims=True) + EPS)


def turn(x, cosine, sine):
    half = HEAD_DIM // 2
    return x * cosine + jnp.concatenate([x[:, half:], x[:, :half]], 1) * sine


def spread(small):
    lane = lax.broadcasted_iota(jnp.int32, (128, D), 0)
    col = lax.broadcasted_iota(jnp.int32, (128, D), 1)
    out = jnp.zeros((16, D), f32)
    for i in range(16):
        place = jnp.where((col == lane + 48 * i) & (lane < 48), 1.0, 0.0).astype(bf16)
        out = out + dot(small[i // 4, i % 4], place)
    return out


def attn_forward_kernel(here, net, ground, h, cosine, sine, *refs):
    if here:
        w_qkv, w_out = ground.made[1][1]
        small, *refs = refs
    else:
        gains, w_qkv, w_out, *refs = refs
    (
        middle, second, every, queries, keys, values, attended, totals,
        near_out, near_in, away_out, away_in,
    ) = refs
    net.greet(net.everyone())
    x = h[...].astype(f32)
    factor = rms_rows(x)
    if here:
        net.met()
        for point in (-2, -1, 0):
            ground.at(point)
        small[...] = spread(ground.made[0][1][0])
        gain_one, gain_two = small[0:1, :], small[1:2, :]
    else:
        gain_one, gain_two = gains[0:1, :], gains[1:2, :]
    every[net.s] = (x * factor * gain_one).astype(bf16)
    if not here:
        net.met()
        ground.at(0)
    far = net.copy(every.at[net.s], every.at[net.s], seq=net.seq(2))
    near = net.copy(every.at[net.s], every.at[net.s], seq=net.seq(1))
    ground.at(1)

    def project(b):
        joint = dot(every[b], w_qkv[...].reshape(D, 3 * COLS))
        c, sn = cosine[b], sine[b]
        for i in range(HEADS_DEV):
            at = i * HEAD_DIM
            queries[i, b] = turn(joint[:, at : at + HEAD_DIM], c, sn).astype(bf16)
            at += COLS
            keys[i, b] = turn(joint[:, at : at + HEAD_DIM], c, sn).astype(bf16)
            at += COLS
            values[i, b] = joint[:, at : at + HEAD_DIM].astype(bf16)

    if not here:
        project(net.s)
    near.wait_recv()
    ground.at(2)
    if not here:
        project(net.seq(1))
    far.wait_recv()
    passed = net.copy(every.at[net.seq(2)], every.at[net.seq(2)], seq=net.seq(1))
    ground.at(3)
    if here:
        project(net.s)
        project(net.seq(1))
    project(net.seq(2))
    passed.wait_recv()
    project(net.seq(3))
    net.done(every, queries, keys, values)
    ground.at(4)
    tokens = h.shape[0]

    def head(i):
        for b in range(SEQ):
            size = (b + 1) * tokens
            scores = dot_nt(queries[i, b], keys[i, : b + 1].reshape(size, HEAD_DIM))
            row = lax.broadcasted_iota(jnp.int32, (tokens, size), 0) + b * tokens
            col = lax.broadcasted_iota(jnp.int32, (tokens, size), 1)
            scores = jnp.where(row >= col, scores * HEAD_DIM**-0.5, MASKED)
            top = jnp.max(scores, -1, keepdims=True)
            weights = jnp.exp(scores - top)
            total = jnp.sum(weights, -1, keepdims=True)
            weights = (weights * (1.0 / total)).astype(bf16)
            attended[i, b] = dot(weights, values[i, : b + 1].reshape(size, HEAD_DIM))
            totals[i, b] = jnp.broadcast_to(top + jnp.log(total), (tokens, 128))

    for i in range(HEADS_DEV):
        head(i)
        ground.at(5 + i)
    net.done(attended, totals)

    def part(b):
        low = jnp.concatenate([attended[i, b].astype(bf16) for i in range(HEADS_DEV)], 1)
        return dot(low, w_out[...].reshape(COLS, D))

    near_out[0] = part(net.seq(1)).astype(bf16)
    near_out[1] = part(net.seq(3)).astype(bf16)
    near_sum = net.copy(near_out, near_in, seq=net.seq(1))
    away = part(net.seq(2))
    own = part(net.s)
    near_sum.wait_recv()
    away_out[...] = (away + near_in[1].astype(f32)).astype(bf16)
    away_sum = net.copy(away_out, away_in, seq=net.seq(2))
    own = h[...].astype(f32) + own + near_in[0].astype(f32)
    ground.at(8)
    away_sum.wait_recv()
    own = own + away_in[...].astype(f32)
    middle[...] = own
    second[...] = (own * rms_rows(own) * gain_two).astype(bf16)
    for copy in (far, near, passed, near_sum, away_sum):
        copy.wait_send()
    ground.drain()


def attn_forward(h, gains, weights, tables, jobs, shards, cid):
    t = h.shape[0]
    head = (HEADS_DEV, SEQ, t, HEAD_DIM)
    here = not weights
    return call(
        functools.partial(attn_forward_kernel, here),
        [h, *tables] if here else [h, *tables, gains, *weights],
        ([((16, D), f32)] if here else [])
        + [
            ((t, D), f32), ((t, D), bf16), ((SEQ, t, D), bf16, 1), (head, bf16, 1), (head, bf16, 1),
            (head, bf16, 1), (head, f32, 1), ((HEADS_DEV, SEQ, t, 128), f32, 1),
        ],
        [((2, t, D), bf16), ((2, t, D), bf16), ((t, D), bf16), ((t, D), bf16)],
        jobs, shards, cid,
    )


def silu_gate(g, u):
    return g / (1.0 + jnp.exp(-g)) * u


CHUNKS = ((0, 80), (80, 64))


class SlotTrip:
    def __init__(self, net, out, into):
        self.net, self.into = net, into
        self.sent, self.passed = {}, {}
        for c, (at, size) in enumerate(CHUNKS):
            for k in (2, 1, 3):
                e = net.plane(k)
                self.sent[c, k] = net.copy(
                    out.at[e, pl.ds(at, size)], into.at[net.core, net.z, pl.ds(at, size)], fsdp=e
                )
        into[net.core, net.z] = out[net.z]

    def hand_on(self, c):
        net, (at, size) = self.net, CHUNKS[c]
        self.passed[c] = []
        for k in (0, 1, 3, 2):
            if k:
                self.sent[c, k].wait_recv()
            part = self.into.at[net.core, net.plane(FSDP - k), pl.ds(at, size)]
            self.passed[c].append(net.copy(part, part, seq=net.seq(1)))

    def here(self, c):
        for copy in self.passed[c]:
            copy.wait_recv()

    def close(self):
        for copy in [*self.sent.values(), *self.passed[0], *self.passed[1]]:
            copy.wait_send()


class SlotReturn:
    def __init__(self, net, out, into, own, back, home):
        self.net, self.out, self.into, self.own = net, out, into, own
        self.back, self.home = back, home
        self.near, self.sent = {}, []

    def other(self, c, rows):
        at, size = CHUNKS[c]
        self.out[:, at : at + size] = rows.astype(bf16).reshape(EXPERTS, size, D)
        part = pl.ds(at, size)
        self.near[c] = self.net.copy(self.out.at[:, part], self.into.at[:, part], seq=self.net.seq(1))

    def mine(self, c, rows):
        net, (at, size) = self.net, CHUNKS[c]
        self.own[0 : EXPERTS * size] = rows
        self.near[c].wait_recv()
        got = self.into[:, at : at + size].astype(f32).reshape(EXPERTS * size, D)
        both = (self.own[0 : EXPERTS * size] + got).astype(bf16)
        self.back[:, at : at + size] = both.reshape(EXPERTS, size, D)
        for k in (2, 1, 3):
            e = net.plane(k)
            part = pl.ds(at, size)
            self.sent.append(net.copy(self.back.at[e, part], self.home.at[net.z, part], fsdp=e))
        self.home[net.z, at : at + size] = self.back[net.z, at : at + size]

    def wait(self):
        for copy in self.sent:
            copy.wait_recv()

    def close(self):
        for copy in [*self.sent, *self.near.values()]:
            copy.wait_send()


def ffn_forward_kernel(
    net, ground, second, middle, router, onehot, chosen, w_in, w_so,
    result, gates, gathered, every, joint, hidden, rows, joint_e, hidden_e,
    rows_out, prod_out, prod_in, prod_own, back_out, yields, near_out, near_in, away_out, away_in,
):
    t = second.shape[0]
    w1, w2 = ground.made[0][0].w1, ground.made[0][0].w2
    net.greet(net.everyone())
    picked = chosen[:, :t] + chosen[:, t:]
    rows_out[...] = dot(picked, second[...]).astype(bf16).reshape(EXPERTS, CAP, D)
    every[net.s] = second[...]
    net.met()
    trip = SlotTrip(net, rows_out, rows)
    far = net.copy(every.at[net.s], every.at[net.s], seq=net.seq(2))
    near = net.copy(every.at[net.s], every.at[net.s], seq=net.seq(1))
    ground.at(0)
    logits = dot(second[...], router[...])
    l0 = jnp.sum(onehot[0] * logits, -1, keepdims=True)
    l1 = jnp.sum(onehot[1] * logits, -1, keepdims=True)
    top = jnp.maximum(l0, l1)
    e0, e1 = jnp.exp(l0 - top), jnp.exp(l1 - top)
    g0, g1 = e0 / (e0 + e1), e1 / (e0 + e1)
    lane = lax.broadcasted_iota(jnp.int32, (t, 128), 1)
    gates[...] = jnp.where(lane == 0, g0, jnp.where(lane == 1, g1, 0.0))
    net.need(w_in, w_so)

    def shared(b):
        g, u = dot(every[b], w_in[0]), dot(every[b], w_in[1])
        joint[0, b] = g.astype(bf16)
        joint[1, b] = u.astype(bf16)
        low = silu_gate(g, u).astype(bf16)
        hidden[b] = low
        return dot(low, w_so[...])

    own_part = shared(net.s)
    ground.at(1)
    near.wait_recv()
    near_out[0] = shared(net.seq(1)).astype(bf16)
    far.wait_recv()
    passed_far = net.copy(every.at[net.seq(2)], every.at[net.seq(2)], seq=net.seq(1))
    away_out[...] = shared(net.seq(2)).astype(bf16)
    trip.hand_on(0)
    ground.at(2)
    passed_far.wait_recv()
    near_out[1] = shared(net.seq(3)).astype(bf16)
    near_sum = net.copy(near_out, near_in, seq=net.seq(1))
    net.done(every, joint, hidden)

    def expert(core, c):
        at, size = CHUNKS[c]
        part = slice(at, at + size)
        x = rows[core, :, part].reshape(EXPERTS * size, D)
        total = None
        for half in (0, 1):
            g = dot(x, w1[half, 0].reshape(D, FF_DEV))
            u = dot(x, w1[half, 1].reshape(D, FF_DEV))
            shape = (EXPERTS, size, FF_DEV)
            joint_e[core, half, 0, :, part] = g.astype(bf16).reshape(shape)
            joint_e[core, half, 1, :, part] = u.astype(bf16).reshape(shape)
            low = silu_gate(g, u).astype(bf16)
            hidden_e[core, half, :, part] = low.reshape(shape)
            new = dot(low, w2[half].reshape(FF_DEV, D))
            total = new if total is None else total + new
        return total

    trip.here(0)
    ground.at(3)
    back = SlotReturn(net, prod_out, prod_in, prod_own, back_out, yields)
    back.other(0, expert(1 - net.core, 0))
    trip.hand_on(1)
    near_sum.wait_recv()
    away_out[...] = (away_out[...].astype(f32) + near_in[1].astype(f32)).astype(bf16)
    away_sum = net.copy(away_out, away_in, seq=net.seq(2))
    ground.at(4)
    back.mine(0, expert(net.core, 0))
    ground.at(5)
    trip.here(1)
    back.other(1, expert(1 - net.core, 1))
    back.mine(1, expert(net.core, 1))
    net.done(rows, joint_e, hidden_e)
    ground.at(6)
    net.need(middle)
    away_sum.wait_recv()
    base = middle[...] + own_part + near_in[0].astype(f32) + away_in[...].astype(f32)
    back.wait()
    got = dot_tn(chosen[...], yields[...].reshape(SLOTS, D))
    gathered[...] = got.astype(bf16)
    result[...] = base + g0 * got[:t] + g1 * got[t:]
    for copy in [far, near, passed_far, near_sum, away_sum]:
        copy.wait_send()
    trip.close()
    back.close()
    ground.drain()


def ffn_forward(second, middle, router, onehot, chosen, w_in, w_so, jobs, shards, cid):
    t = second.shape[0]
    slots = (EXPERTS, CAP, FF_DEV)
    return call(
        ffn_forward_kernel,
        [second, Late(middle), router, onehot, chosen, Late(w_in), Late(w_so)],
        [
            ((t, D), f32), ((t, 128), f32), ((2 * t, D), bf16), ((SEQ, t, D), bf16, 1),
            ((2, SEQ, t, FF_DEV), bf16, 1), ((SEQ, t, FF_DEV), bf16, 1),
            ((2, EXPERTS, CAP, D), bf16, 1), ((2, 2, 2, *slots), bf16, 1), ((2, 2, *slots), bf16, 1),
        ],
        [
            ((EXPERTS, CAP, D), bf16), ((EXPERTS, CAP, D), bf16), ((EXPERTS, CAP, D), bf16),
            ((EXPERTS * CHUNKS[0][1], D), f32), ((EXPERTS, CAP, D), bf16),
            ((EXPERTS, CAP, D), bf16), ((2, t, D), bf16), ((2, t, D), bf16), ((t, D), bf16),
            ((t, D), bf16),
        ],
        jobs, shards, cid,
    )


def norm_back(x, gain, gradient):
    factor = rms_rows(x)
    weighted = gradient * gain
    inner = jnp.mean(weighted * x, -1, keepdims=True)
    d_x = factor * weighted - x * (factor * factor * factor) * inner
    return d_x, jnp.sum(gradient * x * factor, 0, keepdims=True)


def gate_back(g, u, gradient):
    sig = 1.0 / (1.0 + jnp.exp(-g))
    d_g = gradient * u * sig * (1.0 + g * (1.0 - sig))
    return d_g.astype(bf16), (gradient * g * sig).astype(bf16)


def ffn_backward_kernel(
    net, ground, grad, gates, onehot, chosen, gathered, middle, second, gains, router, every,
    joint, hidden, rows, joint_e, hidden_e, w_in, w_so, w1, w2,
    d_middle, small, d_w1, d_w2,
    every_g, d_joint, rows_out, d_rows, d_joint_e, prod_out, prod_in, prod_own, back_out, back_in,
    near_out, near_in, away_out, away_in, d_w_in, d_w_so,
):
    t = grad.shape[0]
    net.greet(net.everyone())
    g0, g1 = gates[:, 0:1], gates[:, 1:2]
    up = grad[...].astype(f32)
    pairs = jnp.concatenate([(up * g0).astype(bf16), (up * g1).astype(bf16)], 0)
    rows_out[...] = dot(chosen[...], pairs).astype(bf16).reshape(EXPERTS, CAP, D)
    every_g[net.s] = up.astype(bf16)
    net.met()
    trip = SlotTrip(net, rows_out, d_rows)
    far = net.copy(every_g.at[net.s], every_g.at[net.s], seq=net.seq(2))
    near = net.copy(every_g.at[net.s], every_g.at[net.s], seq=net.seq(1))
    ground.at(0)
    net.need(w_so, joint, w_in)

    def shared(b):
        d_hidden = dot_nt(every_g[b], w_so[...])
        d_g, d_u = gate_back(joint[0, b].astype(f32), joint[1, b].astype(f32), d_hidden)
        d_joint[0, b] = d_g
        d_joint[1, b] = d_u
        return dot_nt(d_g, w_in[0]) + dot_nt(d_u, w_in[1])

    local = shared(net.s)
    ground.at(1)
    near.wait_recv()
    near_out[0] = shared(net.seq(1)).astype(bf16)
    far.wait_recv()
    passed_far = net.copy(every_g.at[net.seq(2)], every_g.at[net.seq(2)], seq=net.seq(1))
    away_out[...] = shared(net.seq(2)).astype(bf16)
    trip.hand_on(0)
    ground.at(2)
    passed_far.wait_recv()
    near_out[1] = shared(net.seq(3)).astype(bf16)
    near_sum = net.copy(near_out, near_in, seq=net.seq(1))
    net.need(every, hidden)
    tokens = every[...].reshape(SEQ * t, D)
    for gu in (0, 1):
        d_w = dot_tn(tokens, d_joint[gu].reshape(SEQ * t, FF_DEV))
        d_w_in[gu] = d_w.astype(bf16).reshape(4, 4, 48, FF_DEV)
    d_w = dot_tn(hidden[...].reshape(SEQ * t, FF_DEV), every_g[...].reshape(SEQ * t, D))
    d_w_so[...] = d_w.astype(bf16).reshape(4, 128, D)
    net.need(w2, w1, joint_e)

    def expert(core, c):
        at, size = CHUNKS[c]
        part = slice(at, at + size)
        x = d_rows[core, :, part].reshape(EXPERTS * size, D)
        out = None
        for half in (0, 1):
            d_hidden = dot_nt(x, w2[half].reshape(FF_DEV, D))
            flat, shape = (EXPERTS * size, FF_DEV), (EXPERTS, size, FF_DEV)
            g = joint_e[core, half, 0, :, part].astype(f32).reshape(flat)
            u = joint_e[core, half, 1, :, part].astype(f32).reshape(flat)
            d_g, d_u = gate_back(g, u, d_hidden)
            d_joint_e[half, 0, core, :, part] = d_g.reshape(shape)
            d_joint_e[half, 1, core, :, part] = d_u.reshape(shape)
            new = dot_nt(d_g, w1[half, 0].reshape(D, FF_DEV))
            new = new + dot_nt(d_u, w1[half, 1].reshape(D, FF_DEV))
            out = new if out is None else out + new
        return out

    trip.here(0)
    ground.at(3)
    back = SlotReturn(net, prod_out, prod_in, prod_own, back_out, back_in)
    back.other(0, expert(1 - net.core, 0))
    trip.hand_on(1)
    near_sum.wait_recv()
    away_out[...] = (away_out[...].astype(f32) + near_in[1].astype(f32)).astype(bf16)
    away_sum = net.copy(away_out, away_in, seq=net.seq(2))
    ground.at(4)
    back.mine(0, expert(net.core, 0))
    ground.at(5)
    trip.here(1)
    back.other(1, expert(1 - net.core, 1))
    back.mine(1, expert(net.core, 1))
    ground.at(6)
    net.need(rows, hidden_e)
    for half in (0, 1):
        d_rows_all = d_rows[...].reshape(2 * SLOTS, D)
        for gu in (0, 1):
            d_w = dot_tn(
                rows[...].reshape(2 * SLOTS, D), d_joint_e[half, gu].reshape(2 * SLOTS, FF_DEV)
            )
            d_w1[half, gu] = d_w.astype(bf16).reshape(4, 4, 48, FF_DEV)
        low = jnp.concatenate(
            [hidden_e[core, half].reshape(SLOTS, FF_DEV) for core in (0, 1)], 0
        )
        d_w2[half] = dot_tn(low, d_rows_all).astype(bf16).reshape(4, 128, D)
        ground.at(7 + half)
    net.done(d_w1, d_w2)
    net.need(gathered, onehot, second, router, middle)
    d0 = jnp.sum(up * gathered[:t].astype(f32), -1, keepdims=True)
    d1 = jnp.sum(up * gathered[t:].astype(f32), -1, keepdims=True)
    mean = g0 * d0 + g1 * d1
    d_logits = (g0 * (d0 - mean) * onehot[0] + g1 * (d1 - mean) * onehot[1]).astype(bf16)
    small[8:16, :] = dot_tn(d_logits, second[...])[:8]
    local = local + dot_nt(d_logits, router[...])
    away_sum.wait_recv()
    local = local + near_in[0].astype(f32) + away_in[...].astype(f32)
    back.wait()
    picked = chosen[:, :t] + chosen[:, t:]
    d_normed = local + dot_tn(picked, back_in[...].reshape(SLOTS, D))
    d_x, d_gain = norm_back(middle[...], gains[1:2, :], d_normed)
    d_middle[...] = up + d_x
    small[0:8, :] = jnp.broadcast_to(d_gain, (8, D))
    for copy in [far, near, passed_far, near_sum, away_sum]:
        copy.wait_send()
    trip.close()
    back.close()
    ground.drain()


def ffn_backward(grad, saved, gains, router, weights, jobs, shards, cid):
    t = grad.shape[0]
    gates, onehot, chosen, gathered, middle, second, every, joint, hidden, rows, joint_e, hidden_e = saved
    w_in, w_so, w1, w2 = weights
    slots = (EXPERTS, CAP, D)
    late = {}
    for name, x in (
        ("w_so", w_so), ("joint", joint), ("w_in", w_in), ("every", every), ("hidden", hidden),
        ("w2", w2), ("joint_e", joint_e), ("w1", w1), ("rows", rows), ("hidden_e", hidden_e),
        ("gathered", gathered), ("onehot", onehot), ("second", second), ("router", router),
        ("middle", middle),
    ):
        late[name] = Late(x)
    return call(
        ffn_backward_kernel,
        [
            grad, gates, late["onehot"], chosen, late["gathered"], late["middle"], late["second"],
            gains, late["router"], late["every"], late["joint"], late["hidden"], late["rows"],
            late["joint_e"], late["hidden_e"], late["w_in"], late["w_so"], late["w1"], late["w2"],
        ],
        [
            ((t, D), f32), ((16, D), f32), ((2, 2, 4, 4, 48, FF_DEV), bf16, 1),
            ((2, 4, 128, D), bf16, 1),
        ],
        [
            ((SEQ, t, D), bf16), ((2, SEQ, t, FF_DEV), bf16), (slots, bf16), ((2, *slots), bf16),
            ((2, 2, 2, EXPERTS, CAP, FF_DEV), bf16), (slots, bf16), (slots, bf16),
            ((EXPERTS * CHUNKS[0][1], D), f32), (slots, bf16), (slots, bf16), ((2, t, D), bf16),
            ((2, t, D), bf16), ((t, D), bf16), ((t, D), bf16), ((2, 4, 4, 48, FF_DEV), bf16),
            ((4, 128, D), bf16),
        ],
        jobs, shards, cid,
    )


def attn_backward_kernel(
    net, ground, d_middle, h, gains, every, queries, keys, values, attended, totals, w_qkv, w_out,
    cosine, sine,
    grad, d_gain, d_w_qkv, d_w_out,
    every_m, d_att, d_q, d_k, d_v, d_joint, near_out, near_in, away_out, away_in,
):
    t = h.shape[0]
    net.greet(net.everyone())
    up = d_middle[...]
    every_m[net.s] = up.astype(bf16)
    net.met()
    far = net.copy(every_m.at[net.s], every_m.at[net.s], seq=net.seq(2))
    near = net.copy(every_m.at[net.s], every_m.at[net.s], seq=net.seq(1))
    ground.at(0)

    net.need(w_out)

    def project(b):
        d = dot_nt(every_m[b], w_out[...].reshape(COLS, D)).astype(bf16)
        for i in range(HEADS_DEV):
            d_att[i, b] = d[:, i * HEAD_DIM : (i + 1) * HEAD_DIM]

    project(net.s)
    near.wait_recv()
    project(net.seq(1))
    far.wait_recv()
    passed = net.copy(every_m.at[net.seq(2)], every_m.at[net.seq(2)], seq=net.seq(1))
    project(net.seq(2))
    passed.wait_recv()
    project(net.seq(3))
    ground.at(1)
    net.need(attended)
    tokens = every_m[...].reshape(SEQ * t, D)
    low = jnp.concatenate(
        [attended[i].reshape(SEQ * t, HEAD_DIM).astype(bf16) for i in range(HEADS_DEV)], 1
    )
    d_w_out[...] = dot_tn(low, tokens).astype(bf16).reshape(SEQ, 48, D)
    scale = HEAD_DIM**-0.5
    net.need(queries, keys, values, totals)

    def head(i):
        d_k[i] = jnp.zeros_like(d_k[i])
        d_v[i] = jnp.zeros_like(d_v[i])
        for b in range(SEQ):
            size = (b + 1) * t
            q, d = queries[i, b], d_att[i, b]
            k = keys[i, : b + 1].reshape(size, HEAD_DIM)
            v = values[i, : b + 1].reshape(size, HEAD_DIM)
            delta = jnp.sum(d.astype(f32) * attended[i, b], -1, keepdims=True)
            row = lax.broadcasted_iota(jnp.int32, (t, size), 0) + b * t
            col = lax.broadcasted_iota(jnp.int32, (t, size), 1)
            scores = jnp.where(row >= col, dot_nt(q, k) * scale, MASKED)
            weights = jnp.exp(scores - totals[i, b][:, 0:1])
            d_scores = (weights * (dot_nt(d, v) - delta)).astype(bf16)
            d_q[i, b] = dot(d_scores, k) * scale
            shape = (b + 1, t, HEAD_DIM)
            d_k[i, : b + 1] += (dot_tn(d_scores, q) * scale).reshape(shape)
            d_v[i, : b + 1] += dot_tn(weights.astype(bf16), d).reshape(shape)

    for i in range(HEADS_DEV):
        head(i)
        ground.at(2 + i)

    net.need(cosine, sine, w_qkv)

    def part(b):
        c, sn = cosine[b], -sine[b]
        pieces = [turn(d_q[i, b], c, sn) for i in range(HEADS_DEV)]
        pieces += [turn(d_k[i, b], c, sn) for i in range(HEADS_DEV)]
        pieces += [d_v[i, b] for i in range(HEADS_DEV)]
        d = jnp.concatenate(pieces, 1).astype(bf16)
        d_joint[b] = d
        return dot_nt(d, w_qkv[...].reshape(D, 3 * COLS))

    near_out[0] = part(net.seq(1)).astype(bf16)
    near_out[1] = part(net.seq(3)).astype(bf16)
    near_sum = net.copy(near_out, near_in, seq=net.seq(1))
    away = part(net.seq(2))
    own = part(net.s)
    near_sum.wait_recv()
    away_out[...] = (away + near_in[1].astype(f32)).astype(bf16)
    away_sum = net.copy(away_out, away_in, seq=net.seq(2))
    own = own + near_in[0].astype(f32)
    ground.at(5)
    net.need(every)
    d_w = dot_tn(every[...].reshape(SEQ * t, D), d_joint[...].reshape(SEQ * t, 3 * COLS))
    d_w_qkv[...] = d_w.astype(bf16).reshape(4, 4, 48, 3 * COLS)
    ground.at(6)
    away_sum.wait_recv()
    net.need(h)
    d_x, gain = norm_back(h[...].astype(f32), gains[0:1, :], own + away_in[...].astype(f32))
    grad[...] = up + d_x
    row = lax.broadcasted_iota(jnp.int32, (8, D), 0)
    d_gain[...] = jnp.where(row == 0, gain, 0.0)
    ground.at(7)
    for copy in (far, near, passed, near_sum, away_sum):
        copy.wait_send()
    ground.drain()


def attn_backward(d_middle, saved, gains, weights, tables, jobs, shards, cid):
    t = d_middle.shape[0]
    h, every, queries, keys, values, attended, totals = saved
    head = (HEADS_DEV, SEQ, t, HEAD_DIM)
    return call(
        attn_backward_kernel,
        [d_middle, Late(h), gains]
        + [Late(x) for x in (every, queries, keys, values, attended, totals, *weights, *tables)],
        [((t, D), f32), ((8, D), f32), ((4, 4, 48, 3 * COLS), bf16), ((4, 48, D), bf16)],
        [
            ((SEQ, t, D), bf16), (head, bf16), (head, f32), (head, f32), (head, f32),
            ((SEQ, t, 3 * COLS), bf16), ((2, t, D), bf16), ((2, t, D), bf16), ((t, D), bf16),
            ((t, D), bf16),
        ],
        jobs, shards, cid,
    )


FORWARD_ATTN_FIRST = (
    (SmallFetch, 0, (-2, -1, 0)),
    (AttnFetchHere, 0, (-2, -1, 2, 3)),
    (ExpertFetch, 0, (-2, 5, 9)),
    (SharedFetch, 0, (1, 4, 8, 10)),
    (ExpertPlane, 1, (8, 11)),
)
FORWARD_FFN_FIRST = (
    (ExpertJoin, 0, (0, 3, 9)),
    (AttnFetch, 1, (0, 3, 6, 9)),
    (ExpertNear, 1, (4, 9)),
)
FORWARD_ATTN = ((SharedFetch, 1, (0, 1, 4, 9)),)
FORWARD_FFN = ((ExpertJoin, 1, (0, 3, 9)),)
BACKWARD_FFN_FIRST = ((SharedAcross, 1, (3, 9)),)
BACKWARD_ATTN = (
    (GateToPlane, 1, (0, 2, 5, 12)),
    (UpToPlane, 1, (0, 2, 5, 12)),
    (SecondToPlane, 1, (2, 8, 10, 12)),
    (SharedReturn, 1, (0, 4, 6, 11)),
)
BACKWARD_FFN = (
    (SharedAcross, 0, (3, 9)),
    (AttnReturn, 1, (0, 3, 6, 8, 9)),
    (GateFinal, 1, (0, 9)),
    (UpFinal, 1, (0, 9)),
    (SecondFinal, 1, (0, 9)),
)
BACKWARD_ATTN_LAST = (
    (GateReturn, 0, (0, 2, 5, 10, 20)),
    (UpReturn, 0, (0, 2, 5, 11, 20)),
    (SharedReturn, 0, (0, 4, 6, 19)),
    (SecondReturn, 0, (2, 8, 12, 15, 20)),
    (AttnReturnHere, 0, (6, 9, 13, 14, 20)),
    (SmallReturnHere, 0, (7, 8, 10, 13)),
)


def local(
    reps, inputs, expert_choice, pair_order, norm_gains, attn_qkv, attn_out, router, shared_in,
    shared_out, expert_in, expert_out, cotangent,
):
    r, s, z = lax.axis_index("rep"), lax.axis_index("seq"), lax.axis_index("fsdp")
    tokens = inputs.shape[1]
    half = HEAD_DIM // 2
    inverse = np.exp(-np.log(np.float32(10000.0)) * np.arange(half, dtype=np.float32) * np.float32(2.0 / HEAD_DIM))
    angle = np.arange(SEQ * tokens, dtype=np.float32)[:, None] * inverse.astype(np.float32)[None, :]
    cosine, sine = np.cos(angle.astype(np.float64)), np.sin(angle.astype(np.float64))
    shape = (SEQ, tokens, HEAD_DIM)
    table_cos = jnp.asarray(np.concatenate([cosine, cosine], -1).reshape(shape), f32)
    table_sin = jnp.asarray(np.concatenate([-sine, sine], -1).reshape(shape), f32)
    small = jnp.concatenate([norm_gains, router.transpose(0, 2, 1)], 1).reshape(12, 48)
    shards = {
        "small": jnp.pad(small, ((0, 4), (0, 80))),
        "attn_qkv": attn_qkv.reshape(LAYERS, 48, 3, SEQ, COLS)
        .transpose(0, 3, 1, 2, 4)
        .reshape(LAYERS, SEQ, 48, 3 * COLS),
        "attn_out": attn_out,
        "shared_in": shared_in,
        "shared_out": shared_out,
        "expert_in": expert_in,
        "expert_out": expert_out,
    }
    h = inputs[0]
    kept_layers = []
    tables = (table_cos, table_sin)
    attn, gains, small = (), [None] * LAYERS, None
    for layer in range(LAYERS):
        first = layer == 0
        routes = routing(expert_choice[layer, 0], pair_order[layer, 0, 0])
        onehot = expert_choice[layer, 0].T[..., None] == jnp.arange(128, dtype=jnp.int32)
        onehot = onehot.astype(f32)
        if first:
            jobs = FORWARD_ATTN_FIRST
        else:
            jobs = FORWARD_ATTN
        outs, fetched = attn_forward(h, gains[layer], attn, tables, jobs, shards, 12 + layer)
        if first:
            small, *outs = outs
            small = small[:12].reshape(LAYERS, 6, D)
            gains = small[:, :2]
            routers = small[:, 2:].astype(bf16).transpose(0, 2, 1)
        middle, second, every_one, queries, keys, values, attended, totals = outs
        names = ("ax", "ay", "bx", "by")
        if first:
            names = ("p1", "p2") + names
            attn, shared, next_plane = fetched[1:3], fetched[9:11], fetched[11:]
            shards.update(zip(names, fetched[3:9]))
        else:
            shared = fetched
        w_in, w_so = shared[0].reshape(2, D, FF_DEV), shared[1].reshape(FF_DEV, D)
        router_pad = jnp.pad(routers[layer], ((0, 0), (0, 124)))
        if first:
            shards["next_p1"], shards["next_p2"] = next_plane
        outs, fetched = ffn_forward(
            second, middle, router_pad, onehot, routes[1], w_in, w_so,
            FORWARD_FFN_FIRST if first else FORWARD_FFN, shards, 14 + layer,
        )
        attn_weights, ffn_weights = attn, (w_in, w_so, fetched[0], fetched[1])
        if first:
            attn = fetched[2:4]
            shards["p1"], shards["p2"] = next_plane
            shards.update(zip(names[2:], fetched[4:]))
        result, gates, gathered, every_two, joint, hidden, rows, joint_e, hidden_e = outs
        attn_saved = (h, every_one, queries, keys, values, attended, totals)
        ffn_saved = (
            gates, onehot, routes[1], gathered, middle, second, every_two, joint, hidden, rows,
            joint_e, hidden_e,
        )
        h = result
        kept_layers.append((attn_weights, ffn_weights, attn_saved, ffn_saved, router_pad))
    output = h.astype(bf16)[None]
    grad = cotangent[0]
    returned = {}
    grads = {}
    for layer in reversed(range(LAYERS)):
        last = layer == 0
        attn_weights, ffn_weights, attn_saved, ffn_saved, router_pad = kept_layers[layer]
        (d_middle, small, grads["d_w1"], grads["d_w2"]), done = ffn_backward(
            grad, ffn_saved, gains[layer], router_pad, ffn_weights,
            BACKWARD_FFN if last else BACKWARD_FFN_FIRST, grads, 18 + layer,
        )
        grads["r1"], grads["r2"] = done[:2]
        if last:
            returned["d_attn", 1], returned["d_expert", 1] = done[2:4], done[4:]
        grads[f"small_{layer}"] = small
        (grad, d_gain, d_w_qkv, d_w_out), done = attn_backward(
            d_middle, attn_saved, gains[layer], attn_weights, tables,
            BACKWARD_ATTN_LAST if last else BACKWARD_ATTN, grads, 16 + layer,
        )
        if last:
            returned["d_expert", 0], returned["d_shared", 0] = [*done[:2], done[4]], done[2:4]
            returned["d_attn", 0], total_small = done[5:7], done[7]
        else:
            grads["q_gate"], grads["q_up"], grads["q_second"] = done[:3]
            returned["d_shared", 1] = done[3:]
            grads["d_w_qkv"], grads["d_w_out"], grads["gain_1"] = d_w_qkv, d_w_out, d_gain
    total_small = rep_rest(total_small, reps)[:12].reshape(LAYERS, 6, D)
    total_small = lax.dynamic_slice_in_dim(total_small, (s * FSDP + z) * 48, 48, 2)

    def stack(name, k):
        return jnp.stack([rep_rest(returned[name, i][k], reps) for i in range(LAYERS)]).astype(f32)

    d_qkv = stack("d_attn", 0).reshape(LAYERS, SEQ, 48, 3, COLS).transpose(0, 2, 3, 1, 4)
    return (
        output, grad[None], total_small[:, :2], d_qkv.reshape(LAYERS, 48, 3 * D),
        stack("d_attn", 1), total_small[:, 2:].transpose(0, 2, 1), stack("d_shared", 0),
        stack("d_shared", 1), jnp.concatenate([stack("d_expert", 0), stack("d_expert", 1)], -1),
        stack("d_expert", 2),
    )


def solution(mesh):
    tokens = P(("rep", "fsdp"), "seq", None)
    routes = P(None, ("rep", "fsdp"), "seq", None)
    gains = P(None, None, ("seq", "fsdp"))
    dense = P(None, ("seq", "fsdp"), None)
    expert = P(None, None, ("seq", "fsdp"), None)
    in_specs = (
        tokens, routes, routes, gains, dense, dense, dense, dense, dense, expert, expert, tokens,
    )
    out_specs = (tokens, tokens, gains, dense, dense, dense, dense, dense, expert, expert)
    return jax.shard_map(
        functools.partial(local, mesh.shape["rep"]),
        mesh=mesh, in_specs=in_specs, out_specs=out_specs, check_vma=False,
    )
```

```python
import functools

import jax
import jax.numpy as jnp
import numpy as np
from jax import lax
from jax.experimental import pallas as pl
from jax.experimental.pallas import tpu as pltpu
from jax.sharding import PartitionSpec as P

D = 768
HEADS = 12
HEAD_DIM = 64
FF = 2048
EXPERTS = 4
LAYERS = 2
CAP = 144
EPS = 1e-06
MASKED = -1e30
SEQ = 4
FSDP = 4
HEADS_DEV = HEADS // SEQ
COLS = HEADS_DEV * HEAD_DIM
FF_DEV = FF // SEQ
FF_CORE = FF // 2
SLOTS = EXPERTS * CAP
bf16 = jnp.bfloat16
f32 = jnp.float32
MESH = pl.DeviceIdType.MESH


def dot(a, b):
    return jnp.dot(a, b, preferred_element_type=f32)


def dot_nt(a, b):
    return lax.dot_general(a, b, (((1,), (1,)), ((), ())), preferred_element_type=f32)


def dot_tn(a, b):
    return lax.dot_general(a, b, (((0,), (0,)), ((), ())), preferred_element_type=f32)


def rep_rest(x, reps):
    bit = 2
    while bit < reps:
        x = x + lax.ppermute(x, "rep", [(i, i ^ bit) for i in range(reps)])
        bit *= 2
    return x


def routing(choices, order):
    tokens = choices.shape[0]
    pairs = 2 * tokens
    flat = choices.reshape(-1)
    ids = jnp.arange(pairs, dtype=jnp.int32)
    place = (order[:, None] == ids[None, :]).astype(bf16)
    experts = (flat[:, None] == jnp.arange(EXPERTS, dtype=jnp.int32)[None, :]).astype(bf16)
    placed = dot(place, experts).astype(bf16)
    lower = (ids[:, None] > ids[None, :]).astype(bf16)
    slot_placed = jnp.minimum(jnp.sum(dot(lower, placed) * placed.astype(f32), 1), float(CAP))
    slot = dot_tn(place, slot_placed[:, None].astype(bf16))[:, 0].astype(jnp.int32)
    kept = slot < CAP
    target = jnp.where(kept, flat * CAP + slot, SLOTS).reshape(tokens, 2)
    target = target.T.reshape(-1)
    chosen = (target[None, :] == jnp.arange(SLOTS, dtype=jnp.int32)[:, None]).astype(bf16)
    return kept.reshape(tokens, 2).astype(f32), chosen


class Net:
    def __init__(self, send, recv, local_sems):
        self.send, self.recv, self.local_sems = send, recv, local_sems
        self.count = 0
        self.local_count = 0
        self.r, self.s, self.z = (lax.axis_index(a) for a in ("rep", "seq", "fsdp"))
        self.half = lax.rem(self.r, 2)
        self.core = lax.rem(self.s, 2)
        self.far = self.s // 2
        self.partner = self.r + 1 - 2 * self.half

    def seq(self, d):
        core = self.core if d % 2 == 0 else 1 - self.core
        far = self.far if d < 2 else 1 - self.far
        return far * 2 + core

    def plane(self, k):
        return lax.rem(self.z + k, FSDP)

    def copy(self, src, dst, **device):
        k = self.count
        self.count += 1
        out = pltpu.make_async_remote_copy(
            src_ref=src, dst_ref=dst, send_sem=self.send.at[k], recv_sem=self.recv.at[k],
            device_id=device, device_id_type=MESH,
        )
        out.start()
        return out

    def move(self, src, dst):
        k = self.local_count
        self.local_count += 1
        out = pltpu.make_async_copy(src, dst, self.local_sems.at[k])
        out.start()
        return out

    def need(self, *refs):
        for ref in refs:
            self.coming.pop(id(ref)).wait()

    def done(self, *refs):
        for ref in refs:
            self.going.append(self.move(ref, self.there.pop(id(ref))))

    def greet(self, devices):
        self.barrier = pltpu.get_barrier_semaphore()
        for device in devices:
            pl.semaphore_signal(self.barrier, inc=1, device_id=device, device_id_type=MESH)
        self.greeted = len(devices)

    def met(self):
        pl.semaphore_wait(self.barrier, self.greeted)

    def everyone(self):
        seqs = [{"seq": self.seq(d)} for d in (1, 2, 3)]
        planes = [{"fsdp": self.plane(k)} for k in (1, 2, 3)]
        both = [{"seq": self.seq(1), "fsdp": self.plane(k)} for k in (1, 2, 3)]
        return seqs + planes + both + [{"rep": self.partner}]


def columns(start, size):
    return pl.ds(pl.multiple_of(start, 128), size)


def wait_all(copies):
    for copy in copies:
        copy.wait()


class Job:
    space = pl.ANY
    out_space = pl.ANY
    scratch = ()
    kind = bf16

    def __init__(self, net, layer, ins, outs, scratch):
        self.net, self.layer = net, layer
        self.bind(ins, outs, scratch)


class ExpertPlane(Job):
    inputs = ("expert_in", "expert_out")
    shapes = ((2, 2, 4, 48, FF_DEV), (4, 128, 384))

    def bind(self, ins, outs, scratch):
        self.first, self.second = ins
        self.p1, self.p2 = outs

    def stages(self):
        return [self.plane_begin, self.plane_finish]

    def plane_begin(self):
        n = self.net
        self.copies = []
        for k in (2, 1, 3, 0):
            e = n.plane(k)
            for d in (0, 1):
                core = n.core if d == 0 else 1 - n.core
                for gu in (0, 1):
                    src = self.first.at[
                        self.layer, e, :, columns(gu * FF + n.half * FF_CORE + core * FF_DEV, FF_DEV)
                    ]
                    dst = self.p1.at[gu, n.core, n.z]
                    if k == 0 and d == 0:
                        self.copies.append(n.move(src, dst))
                    else:
                        self.copies.append(n.copy(src, dst, seq=n.seq(d), fsdp=e))
            src = self.second.at[self.layer, e, :, columns(n.half * 384, 384)]
            dst = self.p2.at[n.z]
            self.copies.append(n.move(src, dst) if k == 0 else n.copy(src, dst, fsdp=e))

    def plane_finish(self):
        wait_all(self.copies)


class ExpertFetch(ExpertPlane):
    shapes = ExpertPlane.shapes + ((2, 2, 4, 48, FF_DEV), (2, 2, 4, 48, FF_DEV)) + (
        (4, 128, 384), (4, 128, 384),
    )

    def bind(self, ins, outs, scratch):
        ExpertPlane.bind(self, ins, outs[:2], ())
        self.ax, self.ay, self.bx, self.by = outs[2:]

    def stages(self):
        def turn_over():
            self.plane_finish()
            self.near_begin()

        return [self.plane_begin, turn_over, self.near_finish]

    def near_begin(self):
        n = self.net
        self.sides = [
            n.copy(self.p1, self.ax, rep=n.partner), n.copy(self.p1, self.ay, seq=n.seq(2)),
            n.copy(self.p2, self.bx, rep=n.partner), n.copy(self.p2, self.by, seq=n.seq(2)),
        ]

    def near_finish(self):
        wait_all(self.sides)


class ExpertNear(ExpertFetch):
    inputs = ("next_p1", "next_p2")
    shapes = ExpertFetch.shapes[2:]

    def bind(self, ins, outs, scratch):
        self.p1, self.p2 = ins
        self.ax, self.ay, self.bx, self.by = outs

    def stages(self):
        return [self.near_begin, self.near_finish]


class ExpertJoin(Job):
    inputs = ("p1", "p2", "ax", "ay", "bx", "by")
    shapes = ((2, 2, 4, 4, 48, FF_DEV), (2, 4, 128, D))
    scratch = shapes

    def bind(self, ins, outs, scratch):
        self.p1, self.p2, self.ax, self.ay, self.bx, self.by = ins
        self.outs = outs
        self.w1, self.w2 = scratch

    def stages(self):
        return [self.begin, self.finish, self.written]

    def begin(self):
        n = self.net
        here, there = pl.ds(2 * n.far, 2), pl.ds(2 * (1 - n.far), 2)
        mine, rest = columns(n.half * 384, 384), columns((1 - n.half) * 384, 384)
        low, high = pl.ds(0, 2), pl.ds(2, 2)
        w1, w2 = self.w1, self.w2
        self.copies = [
            n.copy(self.ay.at[0], w1.at[n.half, 0, there], rep=n.partner),
            n.copy(self.ax.at[1], w1.at[1 - n.half, 1, here], seq=n.seq(2)),
            n.copy(self.by.at[low], w2.at[1 - n.far, low, :, mine], rep=n.partner),
            n.copy(self.bx.at[high], w2.at[n.far, high, :, rest], seq=n.seq(2)),
            n.move(self.p1, w1.at[n.half, :, here]),
            n.move(self.ax, w1.at[1 - n.half, :, here]),
            n.move(self.ay, w1.at[n.half, :, there]),
            n.move(self.p2, w2.at[n.far, :, :, mine]),
            n.move(self.bx, w2.at[n.far, :, :, rest]),
            n.move(self.by, w2.at[1 - n.far, :, :, mine]),
        ]

    def finish(self):
        wait_all(self.copies)
        self.copies = [
            self.net.move(self.w1, self.outs[0]), self.net.move(self.w2, self.outs[1])
        ]

    def written(self):
        wait_all(self.copies)


class JoinFirst(ExpertJoin):
    inputs = ()
    linked = ((2, 0), (2, 1), (2, 2), (2, 3), (2, 4), (2, 5))


class JoinNext(ExpertJoin):
    inputs = ("next_p1", "next_p2")
    linked = ((0, 0), (0, 1), (0, 2), (0, 3))


class SharedFetch(Job):
    inputs = ("shared_in", "shared_out")
    shapes = ((2, 4, 4, 48, FF_DEV), (4, 128, D))

    def bind(self, ins, outs, scratch):
        self.first, self.second = ins
        self.w_in, self.w_out = outs

    def stages(self):
        return [self.begin, self.second_hop, self.third_hop, self.finish]

    def begin(self):
        n = self.net
        self.firsts = []
        for d in (3, 2, 1, 0):
            src = self.first.at[self.layer, :, columns(n.half * FF + n.seq(d) * FF_DEV, FF_DEV)]
            dst = self.w_in.at[n.half, n.s, n.z]
            self.firsts.append(n.move(src, dst) if d == 0 else n.copy(src, dst, seq=n.seq(d)))
        src = self.second.at[self.layer, :, columns(n.half * 384, 384)]
        self.firsts.append(n.move(src, self.w_out.at[n.z, :, columns(n.half * 384, 384)]))

    def second_hop(self):
        n = self.net
        wait_all(self.firsts)
        part, low = self.w_in.at[n.half, :, n.z], self.w_out.at[n.z, :, columns(n.half * 384, 384)]
        self.sent = {}
        for k in (2, 1, 3):
            self.sent[k] = [n.copy(part, part, fsdp=n.plane(k)), n.copy(low, low, fsdp=n.plane(k))]
        self.across = [n.copy(part, part, rep=n.partner), n.copy(low, low, rep=n.partner)]

    def third_hop(self):
        n = self.net
        for k in (1, 3, 2):
            wait_all(self.sent[k])
            z = n.plane(FSDP - k)
            for part in (self.w_in.at[n.half, :, z], self.w_out.at[z, :, columns(n.half * 384, 384)]):
                self.across.append(n.copy(part, part, rep=n.partner))

    def finish(self):
        wait_all(self.across)


class AttnFetch(Job):
    inputs = ("attn_qkv", "attn_out")
    shapes = ((4, 4, 48, 3 * COLS), (4, 48, D))

    def bind(self, ins, outs, scratch):
        self.qkv, self.out = ins
        self.w_qkv, self.w_out = outs

    def stages(self):
        return [self.begin, self.second_hop, self.third_hop, self.finish]

    def begin(self):
        n = self.net
        self.firsts, self.seconds = [], []
        for d in (3, 2, 1, 0):
            src, dst = self.qkv.at[self.layer, n.seq(d)], self.w_qkv.at[n.s, n.z]
            self.firsts.append(n.move(src, dst) if d == 0 else n.copy(src, dst, seq=n.seq(d)))
        for k in (2, 1, 3, 0):
            src = self.out.at[self.layer, :, columns(n.half * 384, 384)]
            dst = self.w_out.at[n.z, :, columns(n.half * 384, 384)]
            self.seconds.append(n.move(src, dst) if k == 0 else n.copy(src, dst, fsdp=n.plane(k)))

    def second_hop(self):
        n = self.net
        wait_all(self.firsts)
        part = self.w_qkv.at[pl.ds(2 * n.half, 2), n.z]
        self.firsts = [n.copy(part, part, fsdp=n.plane(k)) for k in (2, 1, 3)]
        wait_all(self.seconds)
        part = self.w_out.at[:, :, columns(n.half * 384, 384)]
        self.across = [n.copy(part, part, rep=n.partner)]

    def third_hop(self):
        n = self.net
        for copy, k in zip(self.firsts[1:] + self.firsts[:1], (1, 3, 2)):
            copy.wait()
            part = self.w_qkv.at[pl.ds(2 * n.half, 2), n.plane(FSDP - k)]
            self.across.append(n.copy(part, part, rep=n.partner))

    def finish(self):
        wait_all(self.across)


class AttnFetchHere(AttnFetch):
    out_space = pltpu.VMEM


class SmallFetch(Job):
    out_space = pltpu.VMEM

    inputs = ("small",)
    shapes = ((4, 4, 16, 128),)

    def bind(self, ins, outs, scratch):
        (self.src,), (self.dst,) = ins, outs

    def stages(self):
        return [self.begin, self.second_hop, self.finish]

    def begin(self):
        n = self.net
        dst = self.dst.at[n.s, n.z]
        self.copies = [n.copy(self.src, dst, seq=n.seq(d)) for d in (3, 2, 1)]
        self.copies.append(n.move(self.src, dst))

    def second_hop(self):
        n = self.net
        wait_all(self.copies)
        part = self.dst.at[:, n.z]
        self.copies = [n.copy(part, part, fsdp=n.plane(k)) for k in (2, 1, 3)]

    def finish(self):
        wait_all(self.copies)


def total(*parts):
    out = parts[0].astype(f32)
    for part in parts[1:]:
        out = out + part.astype(f32)
    return out.astype(bf16)


class FirstSides(Job):
    inputs = ("d_w1",)
    out_space = pltpu.VMEM
    shapes = ((2, 4, 48, FF_DEV),)
    scratch = ((2, 2, 4, 48, FF_DEV), (2, 2, 4, 48, FF_DEV))

    def bind(self, ins, outs, scratch):
        (self.d,), (self.q,) = ins, outs
        self.own, self.got = scratch

    def stages(self):
        return [self.sides_begin, self.sides_second, self.sides_finish]

    def sides_begin(self):
        n = self.net
        if self.gu == 0:
            src = [self.d.at[1 - n.half, 0, pl.ds(2 * f, 2)] for f in (0, 1)]
            kept = [self.d.at[n.half, 0, pl.ds(2 * f, 2)] for f in (0, 1)]
            device = {"rep": n.partner}
        else:
            src = [self.d.at[h, 1, pl.ds(2 * (1 - n.far), 2)] for h in (0, 1)]
            kept = [self.d.at[h, 1, pl.ds(2 * n.far, 2)] for h in (0, 1)]
            device = {"seq": n.seq(2)}
        self.sent = [n.copy(src[i], self.got.at[i], **device) for i in (0, 1)]
        self.sent += [n.move(kept[i], self.own.at[i]) for i in (0, 1)]

    def sides_second(self):
        n = self.net
        wait_all(self.sent)
        stays = n.far if self.gu == 0 else n.half
        device = {"seq": n.seq(2)} if self.gu == 0 else {"rep": n.partner}
        goes = 1 - stays
        self.got[goes] = total(self.got[goes], self.own[goes])
        self.sent = [n.copy(self.got.at[goes], self.q, **device)]
        self.got[stays] = total(self.got[stays], self.own[stays])

    def sides_finish(self):
        n = self.net
        wait_all(self.sent)
        self.q[...] = total(self.q[...], self.got[n.far if self.gu == 0 else n.half])


class FirstPlane(Job):
    space = pltpu.VMEM
    shapes = ((EXPERTS, 48, FF),)
    half_only = False

    def bind(self, ins, outs, scratch):
        (self.q,), (self.o,) = ins, outs

    def stages(self):
        return [self.plane_begin, self.plane_second, self.plane_finish]

    def plane_begin(self):
        n = self.net
        self.sent = []
        at = n.core * FF_DEV if self.half_only else n.half * FF_CORE + n.core * FF_DEV
        dst = self.o.at[n.z, :, columns(at, FF_DEV)]
        for k in (2, 1, 3, 0):
            for d in (1, 0):
                core = n.core if d == 0 else 1 - n.core
                src = self.q.at[core, n.plane(k)]
                if k == 0 and d == 0:
                    self.sent.append(n.move(src, dst))
                else:
                    self.sent.append(n.copy(src, dst, seq=n.seq(d), fsdp=n.plane(k)))

    def plane_second(self):
        n = self.net
        wait_all(self.sent)
        part = self.o.at[:, :, columns(n.half * FF_CORE, FF_CORE)]
        self.sent = [n.copy(part, part, rep=n.partner)]

    def plane_finish(self):
        wait_all(self.sent)


class FirstReturn(FirstSides, FirstPlane):
    shapes = FirstPlane.shapes
    scratch = FirstSides.scratch + FirstSides.shapes
    space = pl.ANY
    out_space = pl.ANY

    def bind(self, ins, outs, scratch):
        FirstSides.bind(self, ins, scratch[2:], scratch[:2])
        FirstPlane.bind(self, scratch[2:], outs, ())

    def turn_over(self):
        self.sides_finish()
        self.plane_begin()

    def stages(self):
        return [
            self.sides_begin, self.sides_second, self.turn_over, self.plane_second,
            self.plane_finish,
        ]


class FirstToPlane(FirstReturn):
    shapes = ((EXPERTS, 48, FF_CORE),)
    half_only = True

    def stages(self):
        return [self.sides_begin, self.sides_second, self.turn_over, self.plane_finish]


class FirstFinal(Job):
    shapes = ((EXPERTS, 48, FF),)

    def bind(self, ins, outs, scratch):
        (self.q,), (self.o,) = ins, outs

    def stages(self):
        return [self.begin, self.finish]

    def begin(self):
        n = self.net
        part = self.o.at[:, :, columns(n.half * FF_CORE, FF_CORE)]
        self.sent = [n.copy(self.q, part, rep=n.partner), n.move(self.q, part)]

    def finish(self):
        wait_all(self.sent)


class GateReturn(FirstReturn):
    gu = 0


class UpReturn(FirstReturn):
    gu = 1


class GateToPlane(FirstToPlane):
    gu = 0


class UpToPlane(FirstToPlane):
    gu = 1


class GateFinal(FirstFinal):
    inputs = ("q_gate",)


class UpFinal(FirstFinal):
    inputs = ("q_up",)


class SecondReturn(Job):
    inputs = ("d_w2",)
    shapes = ((EXPERTS, 128, D),)
    scratch = ((2, 4, 128, 384), (2, 4, 128, 384), (4, 128, 384))
    rep_first = True

    def bind(self, ins, outs, scratch):
        (self.d,), (self.o,) = ins, outs
        self.own, self.got, self.q = scratch

    def stages(self):
        return [
            self.sides_begin, self.sides_second, self.turn_over, self.plane_second,
            self.plane_finish,
        ]

    def sides_begin(self):
        n = self.net
        halves = [columns(h * 384, 384) for h in (0, 1)]
        mine, rest = columns(n.half * 384, 384), columns((1 - n.half) * 384, 384)
        if self.rep_first:
            src = [self.d.at[f, :, :, rest] for f in (0, 1)]
            kept = [self.d.at[f, :, :, mine] for f in (0, 1)]
            device = {"rep": n.partner}
        else:
            src = [self.d.at[1 - n.far, :, :, h] for h in halves]
            kept = [self.d.at[n.far, :, :, h] for h in halves]
            device = {"seq": n.seq(2)}
        self.sent = [n.copy(src[i], self.got.at[i], **device) for i in (0, 1)]
        self.sent += [n.move(kept[i], self.own.at[i]) for i in (0, 1)]

    def sides_second(self):
        n = self.net
        wait_all(self.sent)
        self.stays = n.far if self.rep_first else n.half
        device = {"seq": n.seq(2)} if self.rep_first else {"rep": n.partner}
        goes = 1 - self.stays
        self.got[goes] = total(self.got[goes], self.own[goes])
        self.sent = [n.copy(self.got.at[goes], self.q, **device)]
        self.got[self.stays] = total(self.got[self.stays], self.own[self.stays])

    def target(self):
        return columns(self.net.half * 384, 384)

    def turn_over(self):
        n = self.net
        wait_all(self.sent)
        self.q[...] = total(self.q[...], self.got[self.stays])
        self.sent = []
        dst = self.o.at[n.z, :, self.target()]
        for k in (2, 1, 3, 0):
            src = self.q.at[n.plane(k)]
            self.sent.append(n.move(src, dst) if k == 0 else n.copy(src, dst, fsdp=n.plane(k)))

    def plane_second(self):
        n = self.net
        wait_all(self.sent)
        part = self.o.at[:, :, columns(n.half * 384, 384)]
        self.sent = [n.copy(part, part, rep=n.partner)]

    def plane_finish(self):
        wait_all(self.sent)


class SecondToPlane(SecondReturn):
    shapes = ((EXPERTS, 128, 384),)

    def stages(self):
        return [self.sides_begin, self.sides_second, self.turn_over, self.plane_finish]

    def target(self):
        return pl.ds(0, 384)


class SecondFinal(FirstFinal):
    inputs = ("q_second",)
    shapes = ((EXPERTS, 128, D),)

    def begin(self):
        n = self.net
        part = self.o.at[:, :, columns(n.half * 384, 384)]
        self.sent = [n.copy(self.q, part, rep=n.partner), n.move(self.q, part)]


class SharedAcross(Job):
    inputs = ()
    own = (-2, -1)
    out_space = pltpu.VMEM
    shapes = ((4, 4, 48, FF_DEV), (4, 128, 384))

    def bind(self, ins, outs, scratch):
        self.d1, self.d2 = ins
        self.r1, self.r2 = outs

    def stages(self):
        return [self.begin, self.finish]

    def begin(self):
        n = self.net
        part = self.d2.at[:, :, columns((1 - n.half) * 384, 384)]
        self.sent = [
            n.copy(self.d1.at[1 - n.half], self.r1, rep=n.partner),
            n.copy(part, self.r2, rep=n.partner),
        ]

    def finish(self):
        n = self.net
        wait_all(self.sent)
        self.r1[...] = total(self.r1[...], self.d1[n.half])
        self.r2[...] = total(self.r2[...], self.d2[:, :, columns(n.half * 384, 384)])


class SharedReturn(Job):
    space = pltpu.VMEM
    inputs = ("r1", "r2")
    shapes = ((48, 2 * FF), (128, D))
    scratch = ((3, 4, 48, FF_DEV), (4, 48, FF_DEV), (3, 128, 384), (128, 384))

    def bind(self, ins, outs, scratch):
        self.r1, self.r2 = ins
        self.o1, self.o2 = outs
        self.r1z, self.s1, self.r2z, self.s2 = scratch

    def stages(self):
        return [self.second_hop, self.third_hop, self.fourth_hop, self.finish]

    def second_hop(self):
        n = self.net
        self.firsts = [
            n.copy(self.r1.at[:, n.plane(k)], self.r1z.at[k - 1], fsdp=n.plane(k))
            for k in (2, 1, 3)
        ]
        self.seconds = [
            n.copy(self.r2.at[n.plane(k)], self.r2z.at[k - 1], fsdp=n.plane(k)) for k in (2, 1, 3)
        ]

    def third_hop(self):
        n = self.net
        wait_all(self.firsts + self.seconds)
        self.s1[...] = total(self.r1[:, n.z], self.r1z[0], self.r1z[1], self.r1z[2])
        self.firsts = []
        for d in (3, 2, 1, 0):
            src = self.s1.at[n.seq(d)]
            dst = self.o1.at[:, columns(n.half * FF + n.s * FF_DEV, FF_DEV)]
            self.firsts.append(n.move(src, dst) if d == 0 else n.copy(src, dst, seq=n.seq(d)))
        self.s2[...] = total(self.r2[n.z], self.r2z[0], self.r2z[1], self.r2z[2])
        dst = self.o2.at[:, columns(n.half * 384, 384)]
        self.seconds = [n.copy(self.s2, dst, rep=n.partner), n.move(self.s2, dst)]

    def fourth_hop(self):
        n = self.net
        wait_all(self.firsts)
        part = self.o1.at[:, columns(n.half * FF, FF)]
        self.firsts = [n.copy(part, part, rep=n.partner)]

    def finish(self):
        wait_all(self.firsts + self.seconds)


class AttnReturn(Job):
    space = pltpu.VMEM
    inputs = ("d_w_qkv", "d_w_out")
    shapes = ((4, 48, 3 * COLS), (48, D))
    scratch = (
        (2, 4, 48, 3 * COLS), (3, 2, 48, 3 * COLS), (4, 48, 3 * COLS), (4, 48, 384), (3, 48, 384),
        (48, 384),
    )

    def bind(self, ins, outs, scratch):
        self.d1, self.d2 = ins
        self.o1, self.o2 = outs
        self.r1, self.r1z, self.s1, self.r2, self.r2z, self.s2 = scratch

    def stages(self):
        return [self.begin, self.second_hop, self.third_hop, self.fourth_hop, self.finish]

    def begin(self):
        n = self.net
        self.firsts = [n.copy(self.d1.at[pl.ds(2 * (1 - n.half), 2)], self.r1, rep=n.partner)]
        part = self.d2.at[:, :, columns((1 - n.half) * 384, 384)]
        self.seconds = [n.copy(part, self.r2, rep=n.partner)]

    def second_hop(self):
        n = self.net
        wait_all(self.firsts)
        self.r1[...] = total(self.r1[...], self.d1[pl.ds(2 * n.half, 2)])
        self.firsts = [
            n.copy(self.r1.at[:, n.plane(k)], self.r1z.at[k - 1], fsdp=n.plane(k))
            for k in (2, 1, 3)
        ]
        wait_all(self.seconds)
        self.r2[...] = total(self.r2[...], self.d2[:, :, columns(n.half * 384, 384)])
        self.seconds = [
            n.copy(self.r2.at[n.plane(k)], self.r2z.at[k - 1], fsdp=n.plane(k)) for k in (2, 1, 3)
        ]

    def third_hop(self):
        n = self.net
        wait_all(self.firsts + self.seconds)
        pair = pl.ds(2 * n.half, 2)
        self.s1[pair] = total(self.r1[:, n.z], self.r1z[0], self.r1z[1], self.r1z[2])
        self.firsts = [n.copy(self.s1.at[pair], self.s1.at[pair], rep=n.partner)]
        self.s2[...] = total(self.r2[n.z], self.r2z[0], self.r2z[1], self.r2z[2])
        dst = self.o2.at[:, columns(n.half * 384, 384)]
        self.seconds = [n.copy(self.s2, dst, rep=n.partner), n.move(self.s2, dst)]

    def fourth_hop(self):
        n = self.net
        wait_all(self.firsts)
        self.firsts = []
        for d in (3, 2, 1, 0):
            src, dst = self.s1.at[n.seq(d)], self.o1.at[n.s]
            self.firsts.append(n.move(src, dst) if d == 0 else n.copy(src, dst, seq=n.seq(d)))

    def finish(self):
        wait_all(self.firsts + self.seconds)


class AttnReturnHere(AttnReturn):
    inputs = ()
    own = (2, 3)


class SmallReturnHere(Job):
    inputs = ("small_0", "gain_1", "small_1")
    space = pltpu.VMEM
    out_space = pltpu.VMEM
    kind = f32
    own = (1,)
    shapes = ((16, D),)
    scratch = ((16, D), (16, D), (3, 16, D), (3, 16, D))

    def bind(self, ins, outs, scratch):
        self.zero, self.gain_one, self.one, self.gain = ins
        (self.out,) = outs
        self.acc, self.rx, self.rz, self.rs = scratch

    def stages(self):
        return [self.begin, self.second_hop, self.third_hop, self.finish]

    def begin(self):
        n = self.net
        self.acc[12:16] = jnp.zeros((4, D), f32)
        for at, gain, rest in ((0, self.gain, self.zero), (6, self.gain_one, self.one)):
            self.acc[at : at + 1] = gain[0:1]
            self.acc[at + 1 : at + 2] = rest[0:1]
            self.acc[at + 2 : at + 6] = rest[8:12]
        self.copies = [n.copy(self.acc, self.rx, rep=n.partner)]

    def second_hop(self):
        n = self.net
        wait_all(self.copies)
        self.rx[...] = self.acc[...] + self.rx[...]
        self.copies = [n.copy(self.rx, self.rz.at[k - 1], fsdp=n.plane(k)) for k in (2, 1, 3)]

    def third_hop(self):
        n = self.net
        wait_all(self.copies)
        self.acc[...] = self.rx[...] + self.rz[0] + self.rz[1] + self.rz[2]
        self.copies = [n.copy(self.acc, self.rs.at[d - 1], seq=n.seq(d)) for d in (3, 2, 1)]

    def finish(self):
        wait_all(self.copies)
        self.out[...] = self.acc[...] + self.rs[0] + self.rs[1] + self.rs[2]


class Background:
    def __init__(self, net, jobs, ins, own_outs, outs, scratch):
        self.queues, self.made = [], []
        for job, layer, points in jobs:
            a, b, c = len(job.inputs), len(job.shapes), len(job.scratch)
            given = list(ins[:a]) + [own_outs[i] for i in getattr(job, "own", ())]
            given += [self.made[i][1][k] for i, k in getattr(job, "linked", ())]
            made = job(net, layer, given, outs[:b], scratch[:c])
            self.made.append((made, outs[:b]))
            stages = made.stages()
            last = points[-1]
            points = tuple(points) + (last,) * (len(stages) - len(points))
            self.queues.append(list(zip(points, stages)))
            ins, outs, scratch = ins[a:], outs[b:], scratch[c:]

    def at(self, point):
        for queue in self.queues:
            while queue and queue[0][0] <= point:
                queue.pop(0)[1]()

    def drain(self):
        for point in range(9, 70):
            self.at(point)


COPIES = 160
MOVES = 64


class Late:
    def __init__(self, array):
        self.array = array


def call(kernel, inputs, outputs, scratch, jobs, shards, cid):
    given = [shards[name] for job, *_ in jobs for name in job.inputs]
    results = [
        (jax.ShapeDtypeStruct(shape, job.kind), job.out_space)
        for job, *_ in jobs
        for shape in job.shapes
    ]
    vmem, anywhere = pl.BlockSpec(memory_space=pltpu.VMEM), pl.BlockSpec(memory_space=pl.ANY)
    job_scratch = [pltpu.VMEM(shape, job.kind) for job, *_ in jobs for shape in job.scratch]
    late_in = [i for i, x in enumerate(inputs) if isinstance(x, Late)]
    arrays = [x.array if isinstance(x, Late) else x for x in inputs]
    late_out = [i for i, x in enumerate(outputs) if len(x) == 3]
    late = [pltpu.VMEM(arrays[i].shape, arrays[i].dtype) for i in late_in]
    late += [pltpu.VMEM(outputs[i][0], outputs[i][1]) for i in late_out]

    def body(*refs):
        a = len(inputs)
        b = a + len(given)
        c = b + len(outputs)
        d = c + len(results)
        e = d + len(scratch)
        f = e + len(job_scratch)
        g = f + len(late)
        net = Net(*refs[g:])
        ins, outs = list(refs[:a]), list(refs[b:c])
        net.coming, net.going = {}, []
        for i, ref in zip(late_in, refs[f:]):
            net.coming[id(ref)] = net.move(ins[i], ref)
            ins[i] = ref
        there = {}
        for i, ref in zip(late_out, refs[f + len(late_in) : g]):
            there[id(ref)] = outs[i]
            outs[i] = ref
        net.there = there
        ground = Background(net, jobs, refs[a:b], outs + list(refs[d:e]), refs[c:d], refs[e:f])
        kernel(net, ground, *ins, *outs, *refs[d:e])
        assert not net.coming and not there
        assert net.count <= COPIES and net.local_count <= MOVES
        wait_all(net.going)

    made = pl.pallas_call(
        body,
        out_shape=[jax.ShapeDtypeStruct(x[0], x[1]) for x in outputs] + [shape for shape, _ in results],
        in_specs=[anywhere if i in late_in else vmem for i in range(len(inputs))]
        + [pl.BlockSpec(memory_space=job.space) for job, *_ in jobs for _ in job.inputs],
        out_specs=[anywhere if i in late_out else vmem for i in range(len(outputs))]
        + [pl.BlockSpec(memory_space=where) for _, where in results],
        scratch_shapes=[pltpu.VMEM(shape, kind) for shape, kind in scratch]
        + job_scratch
        + late
        + [
            pltpu.SemaphoreType.DMA((COPIES,)),
            pltpu.SemaphoreType.DMA((COPIES,)),
            pltpu.SemaphoreType.DMA((MOVES,)),
        ],
        compiler_params=pltpu.CompilerParams(
            collective_id=cid, has_side_effects=True, vmem_limit_bytes=60 << 20
        ),
        cost_estimate=pl.CostEstimate(flops=0, bytes_accessed=1 << 20, transcendentals=0),
    )(*arrays, *given)
    return made[: len(outputs)], made[len(outputs) :]


def rms_rows(x):
    return lax.rsqrt(jnp.mean(x * x, -1, keepdims=True) + EPS)


def turn(x, cosine, sine):
    half = HEAD_DIM // 2
    return x * cosine + jnp.concatenate([x[:, half:], x[:, :half]], 1) * sine


def spread(small):
    lane = lax.broadcasted_iota(jnp.int32, (128, D), 0)
    col = lax.broadcasted_iota(jnp.int32, (128, D), 1)
    out = jnp.zeros((16, D), f32)
    for i in range(16):
        place = jnp.where((col == lane + 48 * i) & (lane < 48), 1.0, 0.0).astype(bf16)
        out = out + dot(small[i // 4, i % 4], place)
    return out


def attn_forward_part(layer, net, ground, h, cosine, sine, small, w_qkv, w_out, refs):
    (
        middle, second, every, queries, keys, values, attended, totals,
        near_out, near_in, away_out, away_in,
    ) = refs
    here = layer == 0
    net.greet(net.everyone())
    x = h[...].astype(f32)
    factor = rms_rows(x)
    if here:
        net.met()
        for point in (-2, -1, 0):
            ground.at(point)
        small[...] = spread(ground.made[0][1][0])
    gain_one, gain_two = small[6 * layer : 6 * layer + 1, :], small[6 * layer + 1 : 6 * layer + 2, :]
    every[net.s] = (x * factor * gain_one).astype(bf16)
    if not here:
        net.met()
        ground.at(0)
    far = net.copy(every.at[net.s], every.at[net.s], seq=net.seq(2))
    near = net.copy(every.at[net.s], every.at[net.s], seq=net.seq(1))
    ground.at(1)

    def project(b):
        joint = dot(every[b], w_qkv[...].reshape(D, 3 * COLS))
        c, sn = cosine[b], sine[b]
        for i in range(HEADS_DEV):
            at = i * HEAD_DIM
            queries[i, b] = turn(joint[:, at : at + HEAD_DIM], c, sn).astype(bf16)
            at += COLS
            keys[i, b] = turn(joint[:, at : at + HEAD_DIM], c, sn).astype(bf16)
            at += COLS
            values[i, b] = joint[:, at : at + HEAD_DIM].astype(bf16)

    if not here:
        project(net.s)
    near.wait_recv()
    ground.at(2)
    if not here:
        project(net.seq(1))
    far.wait_recv()
    passed = net.copy(every.at[net.seq(2)], every.at[net.seq(2)], seq=net.seq(1))
    ground.at(3)
    if here:
        project(net.s)
        project(net.seq(1))
    project(net.seq(2))
    passed.wait_recv()
    project(net.seq(3))
    net.done(every, queries, keys, values)
    ground.at(4)
    tokens = h.shape[0]

    def head(i):
        for b in range(SEQ):
            size = (b + 1) * tokens
            scores = dot_nt(queries[i, b], keys[i, : b + 1].reshape(size, HEAD_DIM))
            row = lax.broadcasted_iota(jnp.int32, (tokens, size), 0) + b * tokens
            col = lax.broadcasted_iota(jnp.int32, (tokens, size), 1)
            scores = jnp.where(row >= col, scores * HEAD_DIM**-0.5, MASKED)
            top = jnp.max(scores, -1, keepdims=True)
            weights = jnp.exp(scores - top)
            total = jnp.sum(weights, -1, keepdims=True)
            weights = (weights * (1.0 / total)).astype(bf16)
            attended[i, b] = dot(weights, values[i, : b + 1].reshape(size, HEAD_DIM))
            totals[i, b] = jnp.broadcast_to(top + jnp.log(total), (tokens, 128))

    for i in range(HEADS_DEV):
        head(i)
        ground.at(5 + i)
    net.done(attended, totals)

    def part(b):
        low = jnp.concatenate([attended[i, b].astype(bf16) for i in range(HEADS_DEV)], 1)
        return dot(low, w_out[...].reshape(COLS, D))

    near_out[0] = part(net.seq(1)).astype(bf16)
    near_out[1] = part(net.seq(3)).astype(bf16)
    near_sum = net.copy(near_out, near_in, seq=net.seq(1))
    away = part(net.seq(2))
    own = part(net.s)
    near_sum.wait_recv()
    away_out[...] = (away + near_in[1].astype(f32)).astype(bf16)
    away_sum = net.copy(away_out, away_in, seq=net.seq(2))
    own = h[...].astype(f32) + own + near_in[0].astype(f32)
    ground.at(8)
    away_sum.wait_recv()
    own = own + away_in[...].astype(f32)
    middle[...] = own
    second[...] = (own * rms_rows(own) * gain_two).astype(bf16)
    for copy in (far, near, passed, near_sum, away_sum):
        copy.wait_send()


def silu_gate(g, u):
    return g / (1.0 + jnp.exp(-g)) * u


CHUNKS = ((0, 80), (80, 64))


class SlotTrip:
    def __init__(self, net, out, into):
        self.net, self.into = net, into
        self.sent, self.passed = {}, {}
        for c, (at, size) in enumerate(CHUNKS):
            for k in (2, 1, 3):
                e = net.plane(k)
                self.sent[c, k] = net.copy(
                    out.at[e, pl.ds(at, size)], into.at[net.core, net.z, pl.ds(at, size)], fsdp=e
                )
        into[net.core, net.z] = out[net.z]

    def hand_on(self, c):
        net, (at, size) = self.net, CHUNKS[c]
        self.passed[c] = []
        for k in (0, 1, 3, 2):
            if k:
                self.sent[c, k].wait_recv()
            part = self.into.at[net.core, net.plane(FSDP - k), pl.ds(at, size)]
            self.passed[c].append(net.copy(part, part, seq=net.seq(1)))

    def here(self, c):
        for copy in self.passed[c]:
            copy.wait_recv()

    def close(self):
        for copy in [*self.sent.values(), *self.passed[0], *self.passed[1]]:
            copy.wait_send()


class SlotReturn:
    def __init__(self, net, out, into, own, back, home):
        self.net, self.out, self.into, self.own = net, out, into, own
        self.back, self.home = back, home
        self.near, self.sent = {}, []

    def other(self, c, rows):
        at, size = CHUNKS[c]
        self.out[:, at : at + size] = rows.astype(bf16).reshape(EXPERTS, size, D)
        part = pl.ds(at, size)
        self.near[c] = self.net.copy(self.out.at[:, part], self.into.at[:, part], seq=self.net.seq(1))

    def mine(self, c, rows):
        net, (at, size) = self.net, CHUNKS[c]
        self.own[0 : EXPERTS * size] = rows
        self.near[c].wait_recv()
        got = self.into[:, at : at + size].astype(f32).reshape(EXPERTS * size, D)
        both = (self.own[0 : EXPERTS * size] + got).astype(bf16)
        self.back[:, at : at + size] = both.reshape(EXPERTS, size, D)
        for k in (2, 1, 3):
            e = net.plane(k)
            part = pl.ds(at, size)
            self.sent.append(net.copy(self.back.at[e, part], self.home.at[net.z, part], fsdp=e))
        self.home[net.z, at : at + size] = self.back[net.z, at : at + size]

    def wait(self):
        for copy in self.sent:
            copy.wait_recv()

    def close(self):
        for copy in [*self.sent, *self.near.values()]:
            copy.wait_send()


def ffn_forward_part(layer, net, ground, second, middle, small, onehot, chosen, jobs, refs):
    (
        result, gates, gathered, every, joint, hidden, rows, joint_e, hidden_e,
        rows_out, prod_out, prod_in, prod_own, back_out, yields, near_out, near_in, away_out,
        away_in, w_in, w_so, router,
    ) = refs
    t = second.shape[0]
    shared_job, join = jobs
    w1, w2 = join.w1, join.w2
    picked = chosen[:, :t] + chosen[:, t:]
    rows_out[...] = dot(picked, second[...]).astype(bf16).reshape(EXPERTS, CAP, D)
    every[net.s] = second[...]
    trip = SlotTrip(net, rows_out, rows)
    far = net.copy(every.at[net.s], every.at[net.s], seq=net.seq(2))
    near = net.copy(every.at[net.s], every.at[net.s], seq=net.seq(1))
    ground.at(30)
    loads = [net.move(shared_job.w_in, w_in), net.move(shared_job.w_out, w_so)]
    router[4:8, :] = jnp.zeros((4, D), f32)
    router[0:4, :] = small[6 * layer + 2 : 6 * layer + 6, :]
    logits = dot_nt(second[...], router[...].astype(bf16))
    l0 = jnp.sum(onehot[0, :, 0:8] * logits, -1, keepdims=True)
    l1 = jnp.sum(onehot[1, :, 0:8] * logits, -1, keepdims=True)
    top = jnp.maximum(l0, l1)
    e0, e1 = jnp.exp(l0 - top), jnp.exp(l1 - top)
    g0, g1 = e0 / (e0 + e1), e1 / (e0 + e1)
    lane = lax.broadcasted_iota(jnp.int32, (t, 128), 1)
    gates[...] = jnp.where(lane == 0, g0, jnp.where(lane == 1, g1, 0.0))
    wait_all(loads)

    def shared(b):
        g, u = dot(every[b], w_in[0].reshape(D, FF_DEV)), dot(every[b], w_in[1].reshape(D, FF_DEV))
        joint[0, b] = g.astype(bf16)
        joint[1, b] = u.astype(bf16)
        low = silu_gate(g, u).astype(bf16)
        hidden[b] = low
        return dot(low, w_so[...].reshape(FF_DEV, D))

    own_part = shared(net.s)
    ground.at(31)
    near.wait_recv()
    near_out[0] = shared(net.seq(1)).astype(bf16)
    far.wait_recv()
    passed_far = net.copy(every.at[net.seq(2)], every.at[net.seq(2)], seq=net.seq(1))
    away_out[...] = shared(net.seq(2)).astype(bf16)
    trip.hand_on(0)
    ground.at(32)
    passed_far.wait_recv()
    near_out[1] = shared(net.seq(3)).astype(bf16)
    near_sum = net.copy(near_out, near_in, seq=net.seq(1))
    net.done(every, joint, hidden)

    def expert(core, c):
        at, size = CHUNKS[c]
        part = slice(at, at + size)
        x = rows[core, :, part].reshape(EXPERTS * size, D)
        total = None
        for half in (0, 1):
            g = dot(x, w1[half, 0].reshape(D, FF_DEV))
            u = dot(x, w1[half, 1].reshape(D, FF_DEV))
            shape = (EXPERTS, size, FF_DEV)
            joint_e[core, half, 0, :, part] = g.astype(bf16).reshape(shape)
            joint_e[core, half, 1, :, part] = u.astype(bf16).reshape(shape)
            low = silu_gate(g, u).astype(bf16)
            hidden_e[core, half, :, part] = low.reshape(shape)
            new = dot(low, w2[half].reshape(FF_DEV, D))
            total = new if total is None else total + new
        return total

    trip.here(0)
    ground.at(33)
    back = SlotReturn(net, prod_out, prod_in, prod_own, back_out, yields)
    back.other(0, expert(1 - net.core, 0))
    trip.hand_on(1)
    near_sum.wait_recv()
    away_out[...] = (away_out[...].astype(f32) + near_in[1].astype(f32)).astype(bf16)
    away_sum = net.copy(away_out, away_in, seq=net.seq(2))
    ground.at(34)
    back.mine(0, expert(net.core, 0))
    ground.at(35)
    trip.here(1)
    back.other(1, expert(1 - net.core, 1))
    back.mine(1, expert(net.core, 1))
    net.done(rows, joint_e, hidden_e)
    ground.at(36)
    away_sum.wait_recv()
    base = middle[...] + own_part + near_in[0].astype(f32) + away_in[...].astype(f32)
    back.wait()
    got = dot_tn(chosen[...], yields[...].reshape(SLOTS, D))
    gathered[...] = got.astype(bf16)
    result[...] = base + g0 * got[:t] + g1 * got[t:]
    for copy in [far, near, passed_far, near_sum, away_sum]:
        copy.wait_send()
    trip.close()
    back.close()


def layer_forward_kernel(layer, places, net, ground, h, cosine, sine, onehot, chosen, *refs):
    if layer == 0:
        small, *refs = refs
        w_qkv, w_out = ground.made[1][1]
    else:
        small, w_qkv, w_out, *refs = refs
    attn, ffn = refs[:8] + refs[17:21], refs[8:17] + refs[21:]
    attn_forward_part(layer, net, ground, h, cosine, sine, small, w_qkv, w_out, attn)
    jobs = [ground.made[i][0] for i in places]
    ffn_forward_part(layer, net, ground, attn[1], attn[0], small, onehot, chosen, jobs, ffn)
    ground.drain()


def layer_forward(layer, h, tables, onehot, chosen, small, weights, jobs, shards, cid):
    t = h.shape[0]
    head = (HEADS_DEV, SEQ, t, HEAD_DIM)
    slots = (EXPERTS, CAP, FF_DEV)
    sums = [((2, t, D), bf16), ((2, t, D), bf16), ((t, D), bf16), ((t, D), bf16)]
    names = [job.__name__ for job, *_ in jobs]
    places = (names.index("SharedFetch"), names.index("JoinNext" if layer else "JoinFirst"))
    return call(
        functools.partial(layer_forward_kernel, layer, places),
        [h, *tables, onehot, chosen] + ([small, *weights] if layer else []),
        ([] if layer else [((16, D), f32)])
        + [
            ((t, D), f32), ((t, D), bf16), ((SEQ, t, D), bf16, 1), (head, bf16, 1), (head, bf16, 1),
            (head, bf16, 1), (head, f32, 1), ((HEADS_DEV, SEQ, t, 128), f32, 1),
        ]
        + [
            ((t, D), f32), ((t, 128), f32), ((2 * t, D), bf16), ((SEQ, t, D), bf16, 1),
            ((2, SEQ, t, FF_DEV), bf16, 1), ((SEQ, t, FF_DEV), bf16, 1),
            ((2, EXPERTS, CAP, D), bf16, 1), ((2, 2, 2, *slots), bf16, 1), ((2, 2, *slots), bf16, 1),
        ],
        sums
        + [
            ((EXPERTS, CAP, D), bf16), ((EXPERTS, CAP, D), bf16), ((EXPERTS, CAP, D), bf16),
            ((EXPERTS * CHUNKS[0][1], D), f32), ((EXPERTS, CAP, D), bf16),
            ((EXPERTS, CAP, D), bf16),
        ]
        + sums
        + [((2, 4, 4, 48, FF_DEV), bf16), ((4, 128, D), bf16), ((8, D), f32)],
        jobs, shards, cid,
    )


def norm_back(x, gain, gradient):
    factor = rms_rows(x)
    weighted = gradient * gain
    inner = jnp.mean(weighted * x, -1, keepdims=True)
    d_x = factor * weighted - x * (factor * factor * factor) * inner
    return d_x, jnp.sum(gradient * x * factor, 0, keepdims=True)


def gate_back(g, u, gradient):
    sig = 1.0 / (1.0 + jnp.exp(-g))
    d_g = gradient * u * sig * (1.0 + g * (1.0 - sig))
    return d_g.astype(bf16), (gradient * g * sig).astype(bf16)


def ffn_backward_kernel(
    net, ground, grad, gates, onehot, chosen, gathered, middle, second, gains, router, every,
    joint, hidden, rows, joint_e, hidden_e, w_in, w_so, w1, w2,
    d_middle, small, d_w1, d_w2,
    every_g, d_joint, rows_out, d_rows, d_joint_e, prod_out, prod_in, prod_own, back_out, back_in,
    near_out, near_in, away_out, away_in, d_w_in, d_w_so,
):
    t = grad.shape[0]
    net.greet(net.everyone())
    g0, g1 = gates[:, 0:1], gates[:, 1:2]
    up = grad[...].astype(f32)
    pairs = jnp.concatenate([(up * g0).astype(bf16), (up * g1).astype(bf16)], 0)
    rows_out[...] = dot(chosen[...], pairs).astype(bf16).reshape(EXPERTS, CAP, D)
    every_g[net.s] = up.astype(bf16)
    net.met()
    trip = SlotTrip(net, rows_out, d_rows)
    far = net.copy(every_g.at[net.s], every_g.at[net.s], seq=net.seq(2))
    near = net.copy(every_g.at[net.s], every_g.at[net.s], seq=net.seq(1))
    ground.at(0)
    net.need(w_so, joint, w_in)

    def shared(b):
        d_hidden = dot_nt(every_g[b], w_so[...])
        d_g, d_u = gate_back(joint[0, b].astype(f32), joint[1, b].astype(f32), d_hidden)
        d_joint[0, b] = d_g
        d_joint[1, b] = d_u
        return dot_nt(d_g, w_in[0]) + dot_nt(d_u, w_in[1])

    local = shared(net.s)
    ground.at(1)
    near.wait_recv()
    near_out[0] = shared(net.seq(1)).astype(bf16)
    far.wait_recv()
    passed_far = net.copy(every_g.at[net.seq(2)], every_g.at[net.seq(2)], seq=net.seq(1))
    away_out[...] = shared(net.seq(2)).astype(bf16)
    trip.hand_on(0)
    ground.at(2)
    passed_far.wait_recv()
    near_out[1] = shared(net.seq(3)).astype(bf16)
    near_sum = net.copy(near_out, near_in, seq=net.seq(1))
    net.need(every, hidden)
    tokens = every[...].reshape(SEQ * t, D)
    for gu in (0, 1):
        d_w = dot_tn(tokens, d_joint[gu].reshape(SEQ * t, FF_DEV))
        d_w_in[gu] = d_w.astype(bf16).reshape(4, 4, 48, FF_DEV)
    d_w = dot_tn(hidden[...].reshape(SEQ * t, FF_DEV), every_g[...].reshape(SEQ * t, D))
    d_w_so[...] = d_w.astype(bf16).reshape(4, 128, D)
    net.need(w2, w1, joint_e)

    def expert(core, c):
        at, size = CHUNKS[c]
        part = slice(at, at + size)
        x = d_rows[core, :, part].reshape(EXPERTS * size, D)
        out = None
        for half in (0, 1):
            d_hidden = dot_nt(x, w2[half].reshape(FF_DEV, D))
            flat, shape = (EXPERTS * size, FF_DEV), (EXPERTS, size, FF_DEV)
            g = joint_e[core, half, 0, :, part].astype(f32).reshape(flat)
            u = joint_e[core, half, 1, :, part].astype(f32).reshape(flat)
            d_g, d_u = gate_back(g, u, d_hidden)
            d_joint_e[half, 0, core, :, part] = d_g.reshape(shape)
            d_joint_e[half, 1, core, :, part] = d_u.reshape(shape)
            new = dot_nt(d_g, w1[half, 0].reshape(D, FF_DEV))
            new = new + dot_nt(d_u, w1[half, 1].reshape(D, FF_DEV))
            out = new if out is None else out + new
        return out

    trip.here(0)
    ground.at(3)
    back = SlotReturn(net, prod_out, prod_in, prod_own, back_out, back_in)
    back.other(0, expert(1 - net.core, 0))
    trip.hand_on(1)
    near_sum.wait_recv()
    away_out[...] = (away_out[...].astype(f32) + near_in[1].astype(f32)).astype(bf16)
    away_sum = net.copy(away_out, away_in, seq=net.seq(2))
    ground.at(4)
    back.mine(0, expert(net.core, 0))
    ground.at(5)
    trip.here(1)
    back.other(1, expert(1 - net.core, 1))
    back.mine(1, expert(net.core, 1))
    ground.at(6)
    net.need(rows, hidden_e)
    for half in (0, 1):
        d_rows_all = d_rows[...].reshape(2 * SLOTS, D)
        for gu in (0, 1):
            d_w = dot_tn(
                rows[...].reshape(2 * SLOTS, D), d_joint_e[half, gu].reshape(2 * SLOTS, FF_DEV)
            )
            d_w1[half, gu] = d_w.astype(bf16).reshape(4, 4, 48, FF_DEV)
        low = jnp.concatenate(
            [hidden_e[core, half].reshape(SLOTS, FF_DEV) for core in (0, 1)], 0
        )
        d_w2[half] = dot_tn(low, d_rows_all).astype(bf16).reshape(4, 128, D)
        ground.at(7 + half)
    net.done(d_w1, d_w2)
    net.need(gathered, onehot, second, router, middle)
    d0 = jnp.sum(up * gathered[:t].astype(f32), -1, keepdims=True)
    d1 = jnp.sum(up * gathered[t:].astype(f32), -1, keepdims=True)
    mean = g0 * d0 + g1 * d1
    d_logits = (g0 * (d0 - mean) * onehot[0] + g1 * (d1 - mean) * onehot[1]).astype(bf16)
    small[8:16, :] = dot_tn(d_logits, second[...])[:8]
    local = local + dot_nt(d_logits, router[...])
    away_sum.wait_recv()
    local = local + near_in[0].astype(f32) + away_in[...].astype(f32)
    back.wait()
    picked = chosen[:, :t] + chosen[:, t:]
    d_normed = local + dot_tn(picked, back_in[...].reshape(SLOTS, D))
    d_x, d_gain = norm_back(middle[...], gains[1:2, :], d_normed)
    d_middle[...] = up + d_x
    small[0:8, :] = jnp.broadcast_to(d_gain, (8, D))
    for copy in [far, near, passed_far, near_sum, away_sum]:
        copy.wait_send()
    trip.close()
    back.close()
    ground.drain()


def ffn_backward(grad, saved, gains, router, weights, jobs, shards, cid):
    t = grad.shape[0]
    gates, onehot, chosen, gathered, middle, second, every, joint, hidden, rows, joint_e, hidden_e = saved
    w_in, w_so, w1, w2 = weights
    slots = (EXPERTS, CAP, D)
    late = {}
    for name, x in (
        ("w_so", w_so), ("joint", joint), ("w_in", w_in), ("every", every), ("hidden", hidden),
        ("w2", w2), ("joint_e", joint_e), ("w1", w1), ("rows", rows), ("hidden_e", hidden_e),
        ("gathered", gathered), ("onehot", onehot), ("second", second), ("router", router),
        ("middle", middle),
    ):
        late[name] = Late(x)
    return call(
        ffn_backward_kernel,
        [
            grad, gates, late["onehot"], chosen, late["gathered"], late["middle"], late["second"],
            gains, late["router"], late["every"], late["joint"], late["hidden"], late["rows"],
            late["joint_e"], late["hidden_e"], late["w_in"], late["w_so"], late["w1"], late["w2"],
        ],
        [
            ((t, D), f32), ((16, D), f32), ((2, 2, 4, 4, 48, FF_DEV), bf16, 1),
            ((2, 4, 128, D), bf16, 1),
        ],
        [
            ((SEQ, t, D), bf16), ((2, SEQ, t, FF_DEV), bf16), (slots, bf16), ((2, *slots), bf16),
            ((2, 2, 2, EXPERTS, CAP, FF_DEV), bf16), (slots, bf16), (slots, bf16),
            ((EXPERTS * CHUNKS[0][1], D), f32), (slots, bf16), (slots, bf16), ((2, t, D), bf16),
            ((2, t, D), bf16), ((t, D), bf16), ((t, D), bf16), ((2, 4, 4, 48, FF_DEV), bf16),
            ((4, 128, D), bf16),
        ],
        jobs, shards, cid,
    )


def attn_backward_kernel(
    net, ground, d_middle, h, gains, every, queries, keys, values, attended, totals, w_qkv, w_out,
    cosine, sine,
    grad, d_gain, d_w_qkv, d_w_out,
    every_m, d_att, d_q, d_k, d_v, d_joint, near_out, near_in, away_out, away_in,
):
    t = h.shape[0]
    net.greet(net.everyone())
    up = d_middle[...]
    every_m[net.s] = up.astype(bf16)
    net.met()
    far = net.copy(every_m.at[net.s], every_m.at[net.s], seq=net.seq(2))
    near = net.copy(every_m.at[net.s], every_m.at[net.s], seq=net.seq(1))
    ground.at(0)

    net.need(w_out)

    def project(b):
        d = dot_nt(every_m[b], w_out[...].reshape(COLS, D)).astype(bf16)
        for i in range(HEADS_DEV):
            d_att[i, b] = d[:, i * HEAD_DIM : (i + 1) * HEAD_DIM]

    project(net.s)
    near.wait_recv()
    project(net.seq(1))
    far.wait_recv()
    passed = net.copy(every_m.at[net.seq(2)], every_m.at[net.seq(2)], seq=net.seq(1))
    project(net.seq(2))
    passed.wait_recv()
    project(net.seq(3))
    ground.at(1)
    net.need(attended)
    tokens = every_m[...].reshape(SEQ * t, D)
    low = jnp.concatenate(
        [attended[i].reshape(SEQ * t, HEAD_DIM).astype(bf16) for i in range(HEADS_DEV)], 1
    )
    d_w_out[...] = dot_tn(low, tokens).astype(bf16).reshape(SEQ, 48, D)
    scale = HEAD_DIM**-0.5
    net.need(queries, keys, values, totals)

    def head(i):
        d_k[i] = jnp.zeros_like(d_k[i])
        d_v[i] = jnp.zeros_like(d_v[i])
        for b in range(SEQ):
            size = (b + 1) * t
            q, d = queries[i, b], d_att[i, b]
            k = keys[i, : b + 1].reshape(size, HEAD_DIM)
            v = values[i, : b + 1].reshape(size, HEAD_DIM)
            delta = jnp.sum(d.astype(f32) * attended[i, b], -1, keepdims=True)
            row = lax.broadcasted_iota(jnp.int32, (t, size), 0) + b * t
            col = lax.broadcasted_iota(jnp.int32, (t, size), 1)
            scores = jnp.where(row >= col, dot_nt(q, k) * scale, MASKED)
            weights = jnp.exp(scores - totals[i, b][:, 0:1])
            d_scores = (weights * (dot_nt(d, v) - delta)).astype(bf16)
            d_q[i, b] = dot(d_scores, k) * scale
            shape = (b + 1, t, HEAD_DIM)
            d_k[i, : b + 1] += (dot_tn(d_scores, q) * scale).reshape(shape)
            d_v[i, : b + 1] += dot_tn(weights.astype(bf16), d).reshape(shape)

    for i in range(HEADS_DEV):
        head(i)
        ground.at(2 + i)

    net.need(cosine, sine, w_qkv)

    def part(b):
        c, sn = cosine[b], -sine[b]
        pieces = [turn(d_q[i, b], c, sn) for i in range(HEADS_DEV)]
        pieces += [turn(d_k[i, b], c, sn) for i in range(HEADS_DEV)]
        pieces += [d_v[i, b] for i in range(HEADS_DEV)]
        d = jnp.concatenate(pieces, 1).astype(bf16)
        d_joint[b] = d
        return dot_nt(d, w_qkv[...].reshape(D, 3 * COLS))

    near_out[0] = part(net.seq(1)).astype(bf16)
    near_out[1] = part(net.seq(3)).astype(bf16)
    near_sum = net.copy(near_out, near_in, seq=net.seq(1))
    away = part(net.seq(2))
    own = part(net.s)
    near_sum.wait_recv()
    away_out[...] = (away + near_in[1].astype(f32)).astype(bf16)
    away_sum = net.copy(away_out, away_in, seq=net.seq(2))
    own = own + near_in[0].astype(f32)
    ground.at(5)
    net.need(every)
    d_w = dot_tn(every[...].reshape(SEQ * t, D), d_joint[...].reshape(SEQ * t, 3 * COLS))
    d_w_qkv[...] = d_w.astype(bf16).reshape(4, 4, 48, 3 * COLS)
    ground.at(6)
    away_sum.wait_recv()
    net.need(h)
    d_x, gain = norm_back(h[...].astype(f32), gains[0:1, :], own + away_in[...].astype(f32))
    grad[...] = up + d_x
    row = lax.broadcasted_iota(jnp.int32, (8, D), 0)
    d_gain[...] = jnp.where(row == 0, gain, 0.0)
    ground.at(7)
    for copy in (far, near, passed, near_sum, away_sum):
        copy.wait_send()
    ground.drain()


def attn_backward(d_middle, saved, gains, weights, tables, jobs, shards, cid):
    t = d_middle.shape[0]
    h, every, queries, keys, values, attended, totals = saved
    head = (HEADS_DEV, SEQ, t, HEAD_DIM)
    return call(
        attn_backward_kernel,
        [d_middle, Late(h), gains]
        + [Late(x) for x in (every, queries, keys, values, attended, totals, *weights, *tables)],
        [((t, D), f32), ((8, D), f32), ((4, 4, 48, 3 * COLS), bf16), ((4, 48, D), bf16)],
        [
            ((SEQ, t, D), bf16), (head, bf16), (head, f32), (head, f32), (head, f32),
            ((SEQ, t, 3 * COLS), bf16), ((2, t, D), bf16), ((2, t, D), bf16), ((t, D), bf16),
            ((t, D), bf16),
        ],
        jobs, shards, cid,
    )


FORWARD_FIRST = (
    (SmallFetch, 0, (-2, -1, 0)),
    (AttnFetchHere, 0, (-2, -1, 2, 3)),
    (ExpertFetch, 0, (-2, 3, 30)),
    (SharedFetch, 0, (1, 3, 7, 30)),
    (JoinFirst, 0, (30, 33, 39)),
    (ExpertPlane, 1, (8, 40)),
    (AttnFetch, 1, (30, 33, 36, 40)),
)
FORWARD_NEXT = (
    (ExpertNear, 1, (2, 30)),
    (SharedFetch, 1, (0, 1, 4, 30)),
    (JoinNext, 1, (30, 33, 39)),
)
BACKWARD_FFN_FIRST = ((SharedAcross, 1, (3, 9)),)
BACKWARD_ATTN = (
    (GateToPlane, 1, (0, 2, 5, 12)),
    (UpToPlane, 1, (0, 2, 5, 12)),
    (SecondToPlane, 1, (2, 8, 10, 12)),
    (SharedReturn, 1, (0, 4, 6, 11)),
)
BACKWARD_FFN = (
    (SharedAcross, 0, (3, 9)),
    (AttnReturn, 1, (0, 3, 6, 8, 9)),
    (GateFinal, 1, (0, 9)),
    (UpFinal, 1, (0, 9)),
    (SecondFinal, 1, (0, 9)),
)
BACKWARD_ATTN_LAST = (
    (GateReturn, 0, (0, 2, 5, 10, 20)),
    (UpReturn, 0, (0, 2, 5, 11, 20)),
    (SharedReturn, 0, (0, 4, 6, 19)),
    (SecondReturn, 0, (2, 8, 12, 15, 20)),
    (AttnReturnHere, 0, (6, 9, 13, 14, 20)),
    (SmallReturnHere, 0, (7, 8, 10, 13)),
)


def local(
    reps, inputs, expert_choice, pair_order, norm_gains, attn_qkv, attn_out, router, shared_in,
    shared_out, expert_in, expert_out, cotangent,
):
    r, s, z = lax.axis_index("rep"), lax.axis_index("seq"), lax.axis_index("fsdp")
    tokens = inputs.shape[1]
    half = HEAD_DIM // 2
    inverse = np.exp(-np.log(np.float32(10000.0)) * np.arange(half, dtype=np.float32) * np.float32(2.0 / HEAD_DIM))
    angle = np.arange(SEQ * tokens, dtype=np.float32)[:, None] * inverse.astype(np.float32)[None, :]
    cosine, sine = np.cos(angle.astype(np.float64)), np.sin(angle.astype(np.float64))
    shape = (SEQ, tokens, HEAD_DIM)
    table_cos = jnp.asarray(np.concatenate([cosine, cosine], -1).reshape(shape), f32)
    table_sin = jnp.asarray(np.concatenate([-sine, sine], -1).reshape(shape), f32)
    small = jnp.concatenate([norm_gains, router.transpose(0, 2, 1)], 1).reshape(12, 48)
    shards = {
        "small": jnp.pad(small, ((0, 4), (0, 80))),
        "attn_qkv": attn_qkv.reshape(LAYERS, 48, 3, SEQ, COLS)
        .transpose(0, 3, 1, 2, 4)
        .reshape(LAYERS, SEQ, 48, 3 * COLS),
        "attn_out": attn_out,
        "shared_in": shared_in,
        "shared_out": shared_out,
        "expert_in": expert_in,
        "expert_out": expert_out,
    }
    h = inputs[0]
    kept_layers = []
    tables = (table_cos, table_sin)
    attn, gains, small = (), [None] * LAYERS, None
    for layer in range(LAYERS):
        first = layer == 0
        routes = routing(expert_choice[layer, 0], pair_order[layer, 0, 0])
        onehot = expert_choice[layer, 0].T[..., None] == jnp.arange(128, dtype=jnp.int32)
        onehot = onehot.astype(f32)
        outs, fetched = layer_forward(
            layer, h, tables, onehot, routes[1], small, attn, FORWARD_FIRST if first else FORWARD_NEXT,
            shards, 12 + layer,
        )
        if first:
            small, *outs = outs
            spread_small = small[:12].reshape(LAYERS, 6, D)
            gains, routers = spread_small[:, :2], spread_small[:, 2:].astype(bf16)
            attn, shared, w1, w2 = fetched[1:3], fetched[9:11], fetched[11], fetched[12]
            shards["next_p1"], shards["next_p2"] = fetched[13:15]
            next_attn = fetched[15:17]
        else:
            shared, w1, w2 = fetched[4:6], fetched[6], fetched[7]
        middle, second, every_one, queries, keys, values, attended, totals = outs[:8]
        result, gates, gathered, every_two, joint, hidden, rows, joint_e, hidden_e = outs[8:]
        w_in, w_so = shared[0].reshape(2, D, FF_DEV), shared[1].reshape(FF_DEV, D)
        router_pad = jnp.pad(routers[layer].T, ((0, 0), (0, 124)))
        attn_weights, ffn_weights = attn, (w_in, w_so, w1, w2)
        if first:
            attn = next_attn
        attn_saved = (h, every_one, queries, keys, values, attended, totals)
        ffn_saved = (
            gates, onehot, routes[1], gathered, middle, second, every_two, joint, hidden, rows,
            joint_e, hidden_e,
        )
        h = result
        kept_layers.append((attn_weights, ffn_weights, attn_saved, ffn_saved, router_pad))
    output = h.astype(bf16)[None]
    grad = cotangent[0]
    returned = {}
    grads = {}
    for layer in reversed(range(LAYERS)):
        last = layer == 0
        attn_weights, ffn_weights, attn_saved, ffn_saved, router_pad = kept_layers[layer]
        (d_middle, small, grads["d_w1"], grads["d_w2"]), done = ffn_backward(
            grad, ffn_saved, gains[layer], router_pad, ffn_weights,
            BACKWARD_FFN if last else BACKWARD_FFN_FIRST, grads, 18 + layer,
        )
        grads["r1"], grads["r2"] = done[:2]
        if last:
            returned["d_attn", 1], returned["d_expert", 1] = done[2:4], done[4:]
        grads[f"small_{layer}"] = small
        (grad, d_gain, d_w_qkv, d_w_out), done = attn_backward(
            d_middle, attn_saved, gains[layer], attn_weights, tables,
            BACKWARD_ATTN_LAST if last else BACKWARD_ATTN, grads, 16 + layer,
        )
        if last:
            returned["d_expert", 0], returned["d_shared", 0] = [*done[:2], done[4]], done[2:4]
            returned["d_attn", 0], total_small = done[5:7], done[7]
        else:
            grads["q_gate"], grads["q_up"], grads["q_second"] = done[:3]
            returned["d_shared", 1] = done[3:]
            grads["d_w_qkv"], grads["d_w_out"], grads["gain_1"] = d_w_qkv, d_w_out, d_gain
    total_small = rep_rest(total_small, reps)[:12].reshape(LAYERS, 6, D)
    total_small = lax.dynamic_slice_in_dim(total_small, (s * FSDP + z) * 48, 48, 2)

    def stack(name, k):
        return jnp.stack([rep_rest(returned[name, i][k], reps) for i in range(LAYERS)]).astype(f32)

    d_qkv = stack("d_attn", 0).reshape(LAYERS, SEQ, 48, 3, COLS).transpose(0, 2, 3, 1, 4)
    return (
        output, grad[None], total_small[:, :2], d_qkv.reshape(LAYERS, 48, 3 * D),
        stack("d_attn", 1), total_small[:, 2:].transpose(0, 2, 1), stack("d_shared", 0),
        stack("d_shared", 1), jnp.concatenate([stack("d_expert", 0), stack("d_expert", 1)], -1),
        stack("d_expert", 2),
    )


def solution(mesh):
    tokens = P(("rep", "fsdp"), "seq", None)
    routes = P(None, ("rep", "fsdp"), "seq", None)
    gains = P(None, None, ("seq", "fsdp"))
    dense = P(None, ("seq", "fsdp"), None)
    expert = P(None, None, ("seq", "fsdp"), None)
    in_specs = (
        tokens, routes, routes, gains, dense, dense, dense, dense, dense, expert, expert, tokens,
    )
    out_specs = (tokens, tokens, gains, dense, dense, dense, dense, dense, expert, expert)
    return jax.shard_map(
        functools.partial(local, mesh.shape["rep"]),
        mesh=mesh, in_specs=in_specs, out_specs=out_specs, check_vma=False,
    )
```

```python
import functools

import jax
import jax.numpy as jnp
import numpy as np
from jax import lax
from jax.experimental import pallas as pl
from jax.experimental.pallas import tpu as pltpu
from jax.sharding import PartitionSpec as P

D = 768
HEADS = 12
HEAD_DIM = 64
FF = 2048
EXPERTS = 4
LAYERS = 2
CAP = 144
EPS = 1e-06
MASKED = -1e30
SEQ = 4
FSDP = 4
HEADS_DEV = HEADS // SEQ
COLS = HEADS_DEV * HEAD_DIM
FF_DEV = FF // SEQ
FF_CORE = FF // 2
SLOTS = EXPERTS * CAP
bf16 = jnp.bfloat16
f32 = jnp.float32
MESH = pl.DeviceIdType.MESH


def dot(a, b):
    return jnp.dot(a, b, preferred_element_type=f32)


def dot_nt(a, b):
    return lax.dot_general(a, b, (((1,), (1,)), ((), ())), preferred_element_type=f32)


def dot_tn(a, b):
    return lax.dot_general(a, b, (((0,), (0,)), ((), ())), preferred_element_type=f32)


def rep_rest(x, reps):
    bit = 2
    while bit < reps:
        x = x + lax.ppermute(x, "rep", [(i, i ^ bit) for i in range(reps)])
        bit *= 2
    return x


def routing(choices, order):
    tokens = choices.shape[0]
    pairs = 2 * tokens
    flat = choices.reshape(-1)
    ids = jnp.arange(pairs, dtype=jnp.int32)
    place = (order[:, None] == ids[None, :]).astype(bf16)
    experts = (flat[:, None] == jnp.arange(EXPERTS, dtype=jnp.int32)[None, :]).astype(bf16)
    placed = dot(place, experts).astype(bf16)
    lower = (ids[:, None] > ids[None, :]).astype(bf16)
    slot_placed = jnp.minimum(jnp.sum(dot(lower, placed) * placed.astype(f32), 1), float(CAP))
    slot = dot_tn(place, slot_placed[:, None].astype(bf16))[:, 0].astype(jnp.int32)
    kept = slot < CAP
    target = jnp.where(kept, flat * CAP + slot, SLOTS).reshape(tokens, 2)
    target = target.T.reshape(-1)
    chosen = (target[None, :] == jnp.arange(SLOTS, dtype=jnp.int32)[:, None]).astype(bf16)
    return kept.reshape(tokens, 2).astype(f32), chosen


class Net:
    def __init__(self, send, recv, local_sems):
        self.send, self.recv, self.local_sems = send, recv, local_sems
        self.count = 0
        self.local_count = 0
        self.r, self.s, self.z = (lax.axis_index(a) for a in ("rep", "seq", "fsdp"))
        self.half = lax.rem(self.r, 2)
        self.core = lax.rem(self.s, 2)
        self.far = self.s // 2
        self.partner = self.r + 1 - 2 * self.half

    def seq(self, d):
        core = self.core if d % 2 == 0 else 1 - self.core
        far = self.far if d < 2 else 1 - self.far
        return far * 2 + core

    def plane(self, k):
        return lax.rem(self.z + k, FSDP)

    def copy(self, src, dst, **device):
        k = self.count
        self.count += 1
        out = pltpu.make_async_remote_copy(
            src_ref=src, dst_ref=dst, send_sem=self.send.at[k], recv_sem=self.recv.at[k],
            device_id=device, device_id_type=MESH,
        )
        out.start()
        return out

    def move(self, src, dst):
        k = self.local_count
        self.local_count += 1
        out = pltpu.make_async_copy(src, dst, self.local_sems.at[k])
        out.start()
        return out

    def need(self, *refs):
        for ref in refs:
            self.coming.pop(id(ref)).wait()

    def done(self, *refs):
        for ref in refs:
            self.going.append(self.move(ref, self.there.pop(id(ref))))

    def greet(self, devices):
        self.barrier = pltpu.get_barrier_semaphore()
        for device in devices:
            pl.semaphore_signal(self.barrier, inc=1, device_id=device, device_id_type=MESH)
        self.greeted = len(devices)

    def met(self):
        pl.semaphore_wait(self.barrier, self.greeted)

    def everyone(self):
        seqs = [{"seq": self.seq(d)} for d in (1, 2, 3)]
        planes = [{"fsdp": self.plane(k)} for k in (1, 2, 3)]
        both = [{"seq": self.seq(1), "fsdp": self.plane(k)} for k in (1, 2, 3)]
        return seqs + planes + both + [{"rep": self.partner}]


def columns(start, size):
    return pl.ds(pl.multiple_of(start, 128), size)


def wait_all(copies):
    for copy in copies:
        copy.wait()


class Job:
    space = pl.ANY
    out_space = pl.ANY
    scratch = ()
    kind = bf16

    def __init__(self, net, layer, ins, outs, scratch):
        self.net, self.layer = net, layer
        self.bind(ins, outs, scratch)


class ExpertPlane(Job):
    inputs = ("expert_in", "expert_out")
    shapes = ((2, 2, 4, 48, FF_DEV), (4, 128, 384))

    def bind(self, ins, outs, scratch):
        self.first, self.second = ins
        self.p1, self.p2 = outs

    def stages(self):
        return [self.plane_begin, self.plane_finish]

    def plane_begin(self):
        n = self.net
        self.copies = []
        for k in (2, 1, 3, 0):
            e = n.plane(k)
            for d in (0, 1):
                core = n.core if d == 0 else 1 - n.core
                for gu in (0, 1):
                    src = self.first.at[
                        self.layer, e, :, columns(gu * FF + n.half * FF_CORE + core * FF_DEV, FF_DEV)
                    ]
                    dst = self.p1.at[gu, n.core, n.z]
                    if k == 0 and d == 0:
                        self.copies.append(n.move(src, dst))
                    else:
                        self.copies.append(n.copy(src, dst, seq=n.seq(d), fsdp=e))
            src = self.second.at[self.layer, e, :, columns(n.half * 384, 384)]
            dst = self.p2.at[n.z]
            self.copies.append(n.move(src, dst) if k == 0 else n.copy(src, dst, fsdp=e))

    def plane_finish(self):
        wait_all(self.copies)


class ExpertFetch(ExpertPlane):
    shapes = ExpertPlane.shapes + ((2, 2, 4, 48, FF_DEV), (2, 2, 4, 48, FF_DEV)) + (
        (4, 128, 384), (4, 128, 384),
    )

    def bind(self, ins, outs, scratch):
        ExpertPlane.bind(self, ins, outs[:2], ())
        self.ax, self.ay, self.bx, self.by = outs[2:]

    def stages(self):
        def turn_over():
            self.plane_finish()
            self.near_begin()

        return [self.plane_begin, turn_over, self.near_finish]

    def near_begin(self):
        n = self.net
        self.sides = [
            n.copy(self.p1, self.ax, rep=n.partner), n.copy(self.p1, self.ay, seq=n.seq(2)),
            n.copy(self.p2, self.bx, rep=n.partner), n.copy(self.p2, self.by, seq=n.seq(2)),
        ]

    def near_finish(self):
        wait_all(self.sides)


class ExpertNear(ExpertFetch):
    inputs = ("next_p1", "next_p2")
    shapes = ExpertFetch.shapes[2:]

    def bind(self, ins, outs, scratch):
        self.p1, self.p2 = ins
        self.ax, self.ay, self.bx, self.by = outs

    def stages(self):
        return [self.near_begin, self.near_finish]


class ExpertJoin(Job):
    inputs = ("p1", "p2", "ax", "ay", "bx", "by")
    shapes = ((2, 2, 4, 4, 48, FF_DEV), (2, 4, 128, D))
    scratch = shapes

    def bind(self, ins, outs, scratch):
        self.p1, self.p2, self.ax, self.ay, self.bx, self.by = ins
        self.outs = outs
        self.w1, self.w2 = scratch

    def stages(self):
        return [self.begin, self.finish, self.written]

    def begin(self):
        n = self.net
        here, there = pl.ds(2 * n.far, 2), pl.ds(2 * (1 - n.far), 2)
        mine, rest = columns(n.half * 384, 384), columns((1 - n.half) * 384, 384)
        low, high = pl.ds(0, 2), pl.ds(2, 2)
        w1, w2 = self.w1, self.w2
        self.copies = [
            n.copy(self.ay.at[0], w1.at[n.half, 0, there], rep=n.partner),
            n.copy(self.ax.at[1], w1.at[1 - n.half, 1, here], seq=n.seq(2)),
            n.copy(self.by.at[low], w2.at[1 - n.far, low, :, mine], rep=n.partner),
            n.copy(self.bx.at[high], w2.at[n.far, high, :, rest], seq=n.seq(2)),
            n.move(self.p1, w1.at[n.half, :, here]),
            n.move(self.ax, w1.at[1 - n.half, :, here]),
            n.move(self.ay, w1.at[n.half, :, there]),
            n.move(self.p2, w2.at[n.far, :, :, mine]),
            n.move(self.bx, w2.at[n.far, :, :, rest]),
            n.move(self.by, w2.at[1 - n.far, :, :, mine]),
        ]

    def finish(self):
        wait_all(self.copies)
        self.copies = [
            self.net.move(self.w1, self.outs[0]), self.net.move(self.w2, self.outs[1])
        ]

    def written(self):
        wait_all(self.copies)


class JoinFirst(ExpertJoin):
    inputs = ()
    linked = ((2, 0), (2, 1), (2, 2), (2, 3), (2, 4), (2, 5))


class JoinNext(ExpertJoin):
    inputs = ("next_p1", "next_p2")
    linked = ((0, 0), (0, 1), (0, 2), (0, 3))


class SharedFetch(Job):
    inputs = ("shared_in", "shared_out")
    shapes = ((2, 4, 4, 48, FF_DEV), (4, 128, D))

    def bind(self, ins, outs, scratch):
        self.first, self.second = ins
        self.w_in, self.w_out = outs

    def stages(self):
        return [self.begin, self.second_hop, self.third_hop, self.finish]

    def begin(self):
        n = self.net
        self.firsts = []
        for d in (3, 2, 1, 0):
            src = self.first.at[self.layer, :, columns(n.half * FF + n.seq(d) * FF_DEV, FF_DEV)]
            dst = self.w_in.at[n.half, n.s, n.z]
            self.firsts.append(n.move(src, dst) if d == 0 else n.copy(src, dst, seq=n.seq(d)))
        src = self.second.at[self.layer, :, columns(n.half * 384, 384)]
        self.firsts.append(n.move(src, self.w_out.at[n.z, :, columns(n.half * 384, 384)]))

    def second_hop(self):
        n = self.net
        wait_all(self.firsts)
        part, low = self.w_in.at[n.half, :, n.z], self.w_out.at[n.z, :, columns(n.half * 384, 384)]
        self.sent = {}
        for k in (2, 1, 3):
            self.sent[k] = [n.copy(part, part, fsdp=n.plane(k)), n.copy(low, low, fsdp=n.plane(k))]
        self.across = [n.copy(part, part, rep=n.partner), n.copy(low, low, rep=n.partner)]

    def third_hop(self):
        n = self.net
        for k in (1, 3, 2):
            wait_all(self.sent[k])
            z = n.plane(FSDP - k)
            for part in (self.w_in.at[n.half, :, z], self.w_out.at[z, :, columns(n.half * 384, 384)]):
                self.across.append(n.copy(part, part, rep=n.partner))

    def finish(self):
        wait_all(self.across)


class AttnFetch(Job):
    inputs = ("attn_qkv", "attn_out")
    shapes = ((4, 4, 48, 3 * COLS), (4, 48, D))

    def bind(self, ins, outs, scratch):
        self.qkv, self.out = ins
        self.w_qkv, self.w_out = outs

    def stages(self):
        return [self.begin, self.second_hop, self.third_hop, self.finish]

    def begin(self):
        n = self.net
        self.firsts, self.seconds = [], []
        for d in (3, 2, 1, 0):
            src, dst = self.qkv.at[self.layer, n.seq(d)], self.w_qkv.at[n.s, n.z]
            self.firsts.append(n.move(src, dst) if d == 0 else n.copy(src, dst, seq=n.seq(d)))
        for k in (2, 1, 3, 0):
            src = self.out.at[self.layer, :, columns(n.half * 384, 384)]
            dst = self.w_out.at[n.z, :, columns(n.half * 384, 384)]
            self.seconds.append(n.move(src, dst) if k == 0 else n.copy(src, dst, fsdp=n.plane(k)))

    def second_hop(self):
        n = self.net
        wait_all(self.firsts)
        part = self.w_qkv.at[pl.ds(2 * n.half, 2), n.z]
        self.firsts = [n.copy(part, part, fsdp=n.plane(k)) for k in (2, 1, 3)]
        wait_all(self.seconds)
        part = self.w_out.at[:, :, columns(n.half * 384, 384)]
        self.across = [n.copy(part, part, rep=n.partner)]

    def third_hop(self):
        n = self.net
        for copy, k in zip(self.firsts[1:] + self.firsts[:1], (1, 3, 2)):
            copy.wait()
            part = self.w_qkv.at[pl.ds(2 * n.half, 2), n.plane(FSDP - k)]
            self.across.append(n.copy(part, part, rep=n.partner))

    def finish(self):
        wait_all(self.across)


class AttnFetchHere(AttnFetch):
    out_space = pltpu.VMEM


class SmallFetch(Job):
    out_space = pltpu.VMEM

    inputs = ("small",)
    shapes = ((4, 4, 16, 128),)

    def bind(self, ins, outs, scratch):
        (self.src,), (self.dst,) = ins, outs

    def stages(self):
        return [self.begin, self.second_hop, self.finish]

    def begin(self):
        n = self.net
        dst = self.dst.at[n.s, n.z]
        self.copies = [n.copy(self.src, dst, seq=n.seq(d)) for d in (3, 2, 1)]
        self.copies.append(n.move(self.src, dst))

    def second_hop(self):
        n = self.net
        wait_all(self.copies)
        part = self.dst.at[:, n.z]
        self.copies = [n.copy(part, part, fsdp=n.plane(k)) for k in (2, 1, 3)]

    def finish(self):
        wait_all(self.copies)


def total(*parts):
    out = parts[0].astype(f32)
    for part in parts[1:]:
        out = out + part.astype(f32)
    return out.astype(bf16)


class FirstSides(Job):
    inputs = ("d_w1",)
    out_space = pltpu.VMEM
    shapes = ((2, 4, 48, FF_DEV),)
    scratch = ((2, 2, 4, 48, FF_DEV), (2, 2, 4, 48, FF_DEV))

    def bind(self, ins, outs, scratch):
        (self.d,), (self.q,) = ins, outs
        self.own, self.got = scratch

    def stages(self):
        return [self.sides_begin, self.sides_second, self.sides_finish]

    def sides_begin(self):
        n = self.net
        if self.gu == 0:
            src = [self.d.at[1 - n.half, 0, pl.ds(2 * f, 2)] for f in (0, 1)]
            kept = [self.d.at[n.half, 0, pl.ds(2 * f, 2)] for f in (0, 1)]
            device = {"rep": n.partner}
        else:
            src = [self.d.at[h, 1, pl.ds(2 * (1 - n.far), 2)] for h in (0, 1)]
            kept = [self.d.at[h, 1, pl.ds(2 * n.far, 2)] for h in (0, 1)]
            device = {"seq": n.seq(2)}
        self.sent = [n.copy(src[i], self.got.at[i], **device) for i in (0, 1)]
        self.sent += [n.move(kept[i], self.own.at[i]) for i in (0, 1)]

    def sides_second(self):
        n = self.net
        wait_all(self.sent)
        stays = n.far if self.gu == 0 else n.half
        device = {"seq": n.seq(2)} if self.gu == 0 else {"rep": n.partner}
        goes = 1 - stays
        self.got[goes] = total(self.got[goes], self.own[goes])
        self.sent = [n.copy(self.got.at[goes], self.q, **device)]
        self.got[stays] = total(self.got[stays], self.own[stays])

    def sides_finish(self):
        n = self.net
        wait_all(self.sent)
        self.q[...] = total(self.q[...], self.got[n.far if self.gu == 0 else n.half])


class FirstPlane(Job):
    space = pltpu.VMEM
    shapes = ((EXPERTS, 48, FF),)
    half_only = False

    def bind(self, ins, outs, scratch):
        (self.q,), (self.o,) = ins, outs

    def stages(self):
        return [self.plane_begin, self.plane_second, self.plane_finish]

    def plane_begin(self):
        n = self.net
        self.sent = []
        at = n.core * FF_DEV if self.half_only else n.half * FF_CORE + n.core * FF_DEV
        dst = self.o.at[n.z, :, columns(at, FF_DEV)]
        for k in (2, 1, 3, 0):
            for d in (1, 0):
                core = n.core if d == 0 else 1 - n.core
                src = self.q.at[core, n.plane(k)]
                if k == 0 and d == 0:
                    self.sent.append(n.move(src, dst))
                else:
                    self.sent.append(n.copy(src, dst, seq=n.seq(d), fsdp=n.plane(k)))

    def plane_second(self):
        n = self.net
        wait_all(self.sent)
        part = self.o.at[:, :, columns(n.half * FF_CORE, FF_CORE)]
        self.sent = [n.copy(part, part, rep=n.partner)]

    def plane_finish(self):
        wait_all(self.sent)


class FirstReturn(FirstSides, FirstPlane):
    shapes = FirstPlane.shapes
    scratch = FirstSides.scratch + FirstSides.shapes
    space = pl.ANY
    out_space = pl.ANY

    def bind(self, ins, outs, scratch):
        FirstSides.bind(self, ins, scratch[2:], scratch[:2])
        FirstPlane.bind(self, scratch[2:], outs, ())

    def turn_over(self):
        self.sides_finish()
        self.plane_begin()

    def stages(self):
        return [
            self.sides_begin, self.sides_second, self.turn_over, self.plane_second,
            self.plane_finish,
        ]


class FirstToPlane(FirstReturn):
    shapes = ((EXPERTS, 48, FF_CORE),)
    half_only = True

    def stages(self):
        return [self.sides_begin, self.sides_second, self.turn_over, self.plane_finish]


class FirstFinal(Job):
    shapes = ((EXPERTS, 48, FF),)

    def bind(self, ins, outs, scratch):
        (self.q,), (self.o,) = ins, outs

    def stages(self):
        return [self.begin, self.finish]

    def begin(self):
        n = self.net
        part = self.o.at[:, :, columns(n.half * FF_CORE, FF_CORE)]
        self.sent = [n.copy(self.q, part, rep=n.partner), n.move(self.q, part)]

    def finish(self):
        wait_all(self.sent)


class GateReturn(FirstReturn):
    gu = 0


class UpReturn(FirstReturn):
    gu = 1


class GateToPlane(FirstToPlane):
    gu = 0


class UpToPlane(FirstToPlane):
    gu = 1


class GateFinal(FirstFinal):
    inputs = ("q_gate",)


class UpFinal(FirstFinal):
    inputs = ("q_up",)


class SecondReturn(Job):
    inputs = ("d_w2",)
    shapes = ((EXPERTS, 128, D),)
    scratch = ((2, 4, 128, 384), (2, 4, 128, 384), (4, 128, 384))
    rep_first = True

    def bind(self, ins, outs, scratch):
        (self.d,), (self.o,) = ins, outs
        self.own, self.got, self.q = scratch

    def stages(self):
        return [
            self.sides_begin, self.sides_second, self.turn_over, self.plane_second,
            self.plane_finish,
        ]

    def sides_begin(self):
        n = self.net
        halves = [columns(h * 384, 384) for h in (0, 1)]
        mine, rest = columns(n.half * 384, 384), columns((1 - n.half) * 384, 384)
        if self.rep_first:
            src = [self.d.at[f, :, :, rest] for f in (0, 1)]
            kept = [self.d.at[f, :, :, mine] for f in (0, 1)]
            device = {"rep": n.partner}
        else:
            src = [self.d.at[1 - n.far, :, :, h] for h in halves]
            kept = [self.d.at[n.far, :, :, h] for h in halves]
            device = {"seq": n.seq(2)}
        self.sent = [n.copy(src[i], self.got.at[i], **device) for i in (0, 1)]
        self.sent += [n.move(kept[i], self.own.at[i]) for i in (0, 1)]

    def sides_second(self):
        n = self.net
        wait_all(self.sent)
        self.stays = n.far if self.rep_first else n.half
        device = {"seq": n.seq(2)} if self.rep_first else {"rep": n.partner}
        goes = 1 - self.stays
        self.got[goes] = total(self.got[goes], self.own[goes])
        self.sent = [n.copy(self.got.at[goes], self.q, **device)]
        self.got[self.stays] = total(self.got[self.stays], self.own[self.stays])

    def target(self):
        return columns(self.net.half * 384, 384)

    def turn_over(self):
        n = self.net
        wait_all(self.sent)
        self.q[...] = total(self.q[...], self.got[self.stays])
        self.sent = []
        dst = self.o.at[n.z, :, self.target()]
        for k in (2, 1, 3, 0):
            src = self.q.at[n.plane(k)]
            self.sent.append(n.move(src, dst) if k == 0 else n.copy(src, dst, fsdp=n.plane(k)))

    def plane_second(self):
        n = self.net
        wait_all(self.sent)
        part = self.o.at[:, :, columns(n.half * 384, 384)]
        self.sent = [n.copy(part, part, rep=n.partner)]

    def plane_finish(self):
        wait_all(self.sent)


class SecondToPlane(SecondReturn):
    shapes = ((EXPERTS, 128, 384),)

    def stages(self):
        return [self.sides_begin, self.sides_second, self.turn_over, self.plane_finish]

    def target(self):
        return pl.ds(0, 384)


class SecondFinal(FirstFinal):
    inputs = ("q_second",)
    shapes = ((EXPERTS, 128, D),)

    def begin(self):
        n = self.net
        part = self.o.at[:, :, columns(n.half * 384, 384)]
        self.sent = [n.copy(self.q, part, rep=n.partner), n.move(self.q, part)]


class SharedAcross(Job):
    inputs = ()
    own = (-2, -1)
    out_space = pltpu.VMEM
    shapes = ((4, 4, 48, FF_DEV), (4, 128, 384))

    def bind(self, ins, outs, scratch):
        self.d1, self.d2 = ins
        self.r1, self.r2 = outs

    def stages(self):
        return [self.begin, self.finish]

    def begin(self):
        n = self.net
        part = self.d2.at[:, :, columns((1 - n.half) * 384, 384)]
        self.sent = [
            n.copy(self.d1.at[1 - n.half], self.r1, rep=n.partner),
            n.copy(part, self.r2, rep=n.partner),
        ]

    def finish(self):
        n = self.net
        wait_all(self.sent)
        self.r1[...] = total(self.r1[...], self.d1[n.half])
        self.r2[...] = total(self.r2[...], self.d2[:, :, columns(n.half * 384, 384)])


class SharedReturn(Job):
    space = pltpu.VMEM
    inputs = ("r1", "r2")
    shapes = ((48, 2 * FF), (128, D))
    scratch = ((3, 4, 48, FF_DEV), (4, 48, FF_DEV), (3, 128, 384), (128, 384))

    def bind(self, ins, outs, scratch):
        self.r1, self.r2 = ins
        self.o1, self.o2 = outs
        self.r1z, self.s1, self.r2z, self.s2 = scratch

    def stages(self):
        return [self.second_hop, self.third_hop, self.fourth_hop, self.finish]

    def second_hop(self):
        n = self.net
        self.firsts = [
            n.copy(self.r1.at[:, n.plane(k)], self.r1z.at[k - 1], fsdp=n.plane(k))
            for k in (2, 1, 3)
        ]
        self.seconds = [
            n.copy(self.r2.at[n.plane(k)], self.r2z.at[k - 1], fsdp=n.plane(k)) for k in (2, 1, 3)
        ]

    def third_hop(self):
        n = self.net
        wait_all(self.firsts + self.seconds)
        self.s1[...] = total(self.r1[:, n.z], self.r1z[0], self.r1z[1], self.r1z[2])
        self.firsts = []
        for d in (3, 2, 1, 0):
            src = self.s1.at[n.seq(d)]
            dst = self.o1.at[:, columns(n.half * FF + n.s * FF_DEV, FF_DEV)]
            self.firsts.append(n.move(src, dst) if d == 0 else n.copy(src, dst, seq=n.seq(d)))
        self.s2[...] = total(self.r2[n.z], self.r2z[0], self.r2z[1], self.r2z[2])
        dst = self.o2.at[:, columns(n.half * 384, 384)]
        self.seconds = [n.copy(self.s2, dst, rep=n.partner), n.move(self.s2, dst)]

    def fourth_hop(self):
        n = self.net
        wait_all(self.firsts)
        part = self.o1.at[:, columns(n.half * FF, FF)]
        self.firsts = [n.copy(part, part, rep=n.partner)]

    def finish(self):
        wait_all(self.firsts + self.seconds)


class AttnReturn(Job):
    space = pltpu.VMEM
    inputs = ("d_w_qkv", "d_w_out")
    shapes = ((4, 48, 3 * COLS), (48, D))
    scratch = (
        (2, 4, 48, 3 * COLS), (3, 2, 48, 3 * COLS), (4, 48, 3 * COLS), (4, 48, 384), (3, 48, 384),
        (48, 384),
    )

    def bind(self, ins, outs, scratch):
        self.d1, self.d2 = ins
        self.o1, self.o2 = outs
        self.r1, self.r1z, self.s1, self.r2, self.r2z, self.s2 = scratch

    def stages(self):
        return [self.begin, self.second_hop, self.third_hop, self.fourth_hop, self.finish]

    def begin(self):
        n = self.net
        self.firsts = [n.copy(self.d1.at[pl.ds(2 * (1 - n.half), 2)], self.r1, rep=n.partner)]
        part = self.d2.at[:, :, columns((1 - n.half) * 384, 384)]
        self.seconds = [n.copy(part, self.r2, rep=n.partner)]

    def second_hop(self):
        n = self.net
        wait_all(self.firsts)
        self.r1[...] = total(self.r1[...], self.d1[pl.ds(2 * n.half, 2)])
        self.firsts = [
            n.copy(self.r1.at[:, n.plane(k)], self.r1z.at[k - 1], fsdp=n.plane(k))
            for k in (2, 1, 3)
        ]
        wait_all(self.seconds)
        self.r2[...] = total(self.r2[...], self.d2[:, :, columns(n.half * 384, 384)])
        self.seconds = [
            n.copy(self.r2.at[n.plane(k)], self.r2z.at[k - 1], fsdp=n.plane(k)) for k in (2, 1, 3)
        ]

    def third_hop(self):
        n = self.net
        wait_all(self.firsts + self.seconds)
        pair = pl.ds(2 * n.half, 2)
        self.s1[pair] = total(self.r1[:, n.z], self.r1z[0], self.r1z[1], self.r1z[2])
        self.firsts = [n.copy(self.s1.at[pair], self.s1.at[pair], rep=n.partner)]
        self.s2[...] = total(self.r2[n.z], self.r2z[0], self.r2z[1], self.r2z[2])
        dst = self.o2.at[:, columns(n.half * 384, 384)]
        self.seconds = [n.copy(self.s2, dst, rep=n.partner), n.move(self.s2, dst)]

    def fourth_hop(self):
        n = self.net
        wait_all(self.firsts)
        self.firsts = []
        for d in (3, 2, 1, 0):
            src, dst = self.s1.at[n.seq(d)], self.o1.at[n.s]
            self.firsts.append(n.move(src, dst) if d == 0 else n.copy(src, dst, seq=n.seq(d)))

    def finish(self):
        wait_all(self.firsts + self.seconds)


class AttnReturnHere(AttnReturn):
    inputs = ()
    own = (2, 3)


class SmallReturnHere(Job):
    inputs = ("small_0", "gain_1", "small_1")
    space = pltpu.VMEM
    out_space = pltpu.VMEM
    kind = f32
    own = (1,)
    shapes = ((16, D),)
    scratch = ((16, D), (16, D), (3, 16, D), (3, 16, D))

    def bind(self, ins, outs, scratch):
        self.zero, self.gain_one, self.one, self.gain = ins
        (self.out,) = outs
        self.acc, self.rx, self.rz, self.rs = scratch

    def stages(self):
        return [self.begin, self.second_hop, self.third_hop, self.finish]

    def begin(self):
        n = self.net
        self.acc[12:16] = jnp.zeros((4, D), f32)
        for at, gain, rest in ((0, self.gain, self.zero), (6, self.gain_one, self.one)):
            self.acc[at : at + 1] = gain[0:1]
            self.acc[at + 1 : at + 2] = rest[0:1]
            self.acc[at + 2 : at + 6] = rest[8:12]
        self.copies = [n.copy(self.acc, self.rx, rep=n.partner)]

    def second_hop(self):
        n = self.net
        wait_all(self.copies)
        self.rx[...] = self.acc[...] + self.rx[...]
        self.copies = [n.copy(self.rx, self.rz.at[k - 1], fsdp=n.plane(k)) for k in (2, 1, 3)]

    def third_hop(self):
        n = self.net
        wait_all(self.copies)
        self.acc[...] = self.rx[...] + self.rz[0] + self.rz[1] + self.rz[2]
        self.copies = [n.copy(self.acc, self.rs.at[d - 1], seq=n.seq(d)) for d in (3, 2, 1)]

    def finish(self):
        wait_all(self.copies)
        self.out[...] = self.acc[...] + self.rs[0] + self.rs[1] + self.rs[2]


class Background:
    def __init__(self, net, jobs, ins, own_outs, outs, scratch):
        self.queues, self.made = [], []
        for job, layer, points in jobs:
            a, b, c = len(job.inputs), len(job.shapes), len(job.scratch)
            given = list(ins[:a]) + [own_outs[i] for i in getattr(job, "own", ())]
            given += [self.made[i][1][k] for i, k in getattr(job, "linked", ())]
            made = job(net, layer, given, outs[:b], scratch[:c])
            self.made.append((made, outs[:b]))
            stages = made.stages()
            last = points[-1]
            points = tuple(points) + (last,) * (len(stages) - len(points))
            self.queues.append(list(zip(points, stages)))
            ins, outs, scratch = ins[a:], outs[b:], scratch[c:]

    def at(self, point):
        for queue in self.queues:
            while queue and queue[0][0] <= point:
                queue.pop(0)[1]()

    def drain(self):
        for point in range(9, 70):
            self.at(point)


COPIES = 160
MOVES = 64


class Late:
    def __init__(self, array):
        self.array = array


def call(kernel, inputs, outputs, scratch, jobs, shards, cid):
    given = [shards[name] for job, *_ in jobs for name in job.inputs]
    results = [
        (jax.ShapeDtypeStruct(shape, job.kind), job.out_space)
        for job, *_ in jobs
        for shape in job.shapes
    ]
    vmem, anywhere = pl.BlockSpec(memory_space=pltpu.VMEM), pl.BlockSpec(memory_space=pl.ANY)
    job_scratch = [pltpu.VMEM(shape, job.kind) for job, *_ in jobs for shape in job.scratch]
    late_in = [i for i, x in enumerate(inputs) if isinstance(x, Late)]
    arrays = [x.array if isinstance(x, Late) else x for x in inputs]
    late_out = [i for i, x in enumerate(outputs) if len(x) == 3]
    late = [pltpu.VMEM(arrays[i].shape, arrays[i].dtype) for i in late_in]
    late += [pltpu.VMEM(outputs[i][0], outputs[i][1]) for i in late_out]

    def body(*refs):
        a = len(inputs)
        b = a + len(given)
        c = b + len(outputs)
        d = c + len(results)
        e = d + len(scratch)
        f = e + len(job_scratch)
        g = f + len(late)
        net = Net(*refs[g:])
        ins, outs = list(refs[:a]), list(refs[b:c])
        net.coming, net.going = {}, []
        for i, ref in zip(late_in, refs[f:]):
            net.coming[id(ref)] = net.move(ins[i], ref)
            ins[i] = ref
        there = {}
        for i, ref in zip(late_out, refs[f + len(late_in) : g]):
            there[id(ref)] = outs[i]
            outs[i] = ref
        net.there = there
        ground = Background(net, jobs, refs[a:b], outs + list(refs[d:e]), refs[c:d], refs[e:f])
        kernel(net, ground, *ins, *outs, *refs[d:e])
        assert not net.coming and not there
        assert net.count <= COPIES and net.local_count <= MOVES
        wait_all(net.going)

    made = pl.pallas_call(
        body,
        out_shape=[jax.ShapeDtypeStruct(x[0], x[1]) for x in outputs] + [shape for shape, _ in results],
        in_specs=[anywhere if i in late_in else vmem for i in range(len(inputs))]
        + [pl.BlockSpec(memory_space=job.space) for job, *_ in jobs for _ in job.inputs],
        out_specs=[anywhere if i in late_out else vmem for i in range(len(outputs))]
        + [pl.BlockSpec(memory_space=where) for _, where in results],
        scratch_shapes=[pltpu.VMEM(shape, kind) for shape, kind in scratch]
        + job_scratch
        + late
        + [
            pltpu.SemaphoreType.DMA((COPIES,)),
            pltpu.SemaphoreType.DMA((COPIES,)),
            pltpu.SemaphoreType.DMA((MOVES,)),
        ],
        compiler_params=pltpu.CompilerParams(
            collective_id=cid, has_side_effects=True, vmem_limit_bytes=60 << 20
        ),
        cost_estimate=pl.CostEstimate(flops=0, bytes_accessed=1 << 20, transcendentals=0),
    )(*arrays, *given)
    return made[: len(outputs)], made[len(outputs) :]


def rms_rows(x):
    return lax.rsqrt(jnp.mean(x * x, -1, keepdims=True) + EPS)


def turn(x, cosine, sine):
    half = HEAD_DIM // 2
    return x * cosine + jnp.concatenate([x[:, half:], x[:, :half]], 1) * sine


def spread(small):
    lane = lax.broadcasted_iota(jnp.int32, (128, D), 0)
    col = lax.broadcasted_iota(jnp.int32, (128, D), 1)
    out = jnp.zeros((16, D), f32)
    for i in range(16):
        place = jnp.where((col == lane + 48 * i) & (lane < 48), 1.0, 0.0).astype(bf16)
        out = out + dot(small[i // 4, i % 4], place)
    return out


def attn_forward_part(layer, net, ground, h, cosine, sine, small, w_qkv, w_out, refs):
    (
        middle, second, every, queries, keys, values, attended, totals,
        near_out, near_in, away_out, away_in,
    ) = refs
    here = layer == 0
    net.greet(net.everyone())
    x = h[...].astype(f32)
    factor = rms_rows(x)
    if here:
        net.met()
        for point in (-2, -1, 0):
            ground.at(point)
        small[...] = spread(ground.made[0][1][0])
    gain_one, gain_two = small[6 * layer : 6 * layer + 1, :], small[6 * layer + 1 : 6 * layer + 2, :]
    every[net.s] = (x * factor * gain_one).astype(bf16)
    if not here:
        net.met()
        ground.at(0)
    far = net.copy(every.at[net.s], every.at[net.s], seq=net.seq(2))
    near = net.copy(every.at[net.s], every.at[net.s], seq=net.seq(1))
    ground.at(1)

    def project(b):
        joint = dot(every[b], w_qkv[...].reshape(D, 3 * COLS))
        c, sn = cosine[b], sine[b]
        for i in range(HEADS_DEV):
            at = i * HEAD_DIM
            queries[i, b] = turn(joint[:, at : at + HEAD_DIM], c, sn).astype(bf16)
            at += COLS
            keys[i, b] = turn(joint[:, at : at + HEAD_DIM], c, sn).astype(bf16)
            at += COLS
            values[i, b] = joint[:, at : at + HEAD_DIM].astype(bf16)

    if not here:
        project(net.s)
    near.wait_recv()
    ground.at(2)
    if not here:
        project(net.seq(1))
    far.wait_recv()
    passed = net.copy(every.at[net.seq(2)], every.at[net.seq(2)], seq=net.seq(1))
    ground.at(3)
    if here:
        project(net.s)
        project(net.seq(1))
    project(net.seq(2))
    passed.wait_recv()
    project(net.seq(3))
    net.done(every, queries, keys, values)
    ground.at(4)
    tokens = h.shape[0]

    def head(i):
        for b in range(SEQ):
            size = (b + 1) * tokens
            scores = dot_nt(queries[i, b], keys[i, : b + 1].reshape(size, HEAD_DIM))
            row = lax.broadcasted_iota(jnp.int32, (tokens, size), 0) + b * tokens
            col = lax.broadcasted_iota(jnp.int32, (tokens, size), 1)
            scores = jnp.where(row >= col, scores * HEAD_DIM**-0.5, MASKED)
            top = jnp.max(scores, -1, keepdims=True)
            weights = jnp.exp(scores - top)
            total = jnp.sum(weights, -1, keepdims=True)
            weights = (weights * (1.0 / total)).astype(bf16)
            attended[i, b] = dot(weights, values[i, : b + 1].reshape(size, HEAD_DIM))
            totals[i, b] = jnp.broadcast_to(top + jnp.log(total), (tokens, 128))

    for i in range(HEADS_DEV):
        head(i)
        ground.at(5 + i)
    net.done(attended, totals)

    def part(b):
        low = jnp.concatenate([attended[i, b].astype(bf16) for i in range(HEADS_DEV)], 1)
        return dot(low, w_out[...].reshape(COLS, D))

    near_out[0] = part(net.seq(1)).astype(bf16)
    near_out[1] = part(net.seq(3)).astype(bf16)
    near_sum = net.copy(near_out, near_in, seq=net.seq(1))
    away = part(net.seq(2))
    own = part(net.s)
    near_sum.wait_recv()
    away_out[...] = (away + near_in[1].astype(f32)).astype(bf16)
    away_sum = net.copy(away_out, away_in, seq=net.seq(2))
    own = h[...].astype(f32) + own + near_in[0].astype(f32)
    ground.at(8)
    away_sum.wait_recv()
    own = own + away_in[...].astype(f32)
    middle[...] = own
    second[...] = (own * rms_rows(own) * gain_two).astype(bf16)
    for copy in (far, near, passed, near_sum, away_sum):
        copy.wait_send()


def silu_gate(g, u):
    return g / (1.0 + jnp.exp(-g)) * u


CHUNKS = ((0, 80), (80, 64))


class SlotTrip:
    def __init__(self, net, out, into):
        self.net, self.into = net, into
        self.sent, self.passed = {}, {}
        for c, (at, size) in enumerate(CHUNKS):
            for k in (2, 1, 3):
                e = net.plane(k)
                self.sent[c, k] = net.copy(
                    out.at[e, pl.ds(at, size)], into.at[net.core, net.z, pl.ds(at, size)], fsdp=e
                )
        into[net.core, net.z] = out[net.z]

    def hand_on(self, c):
        net, (at, size) = self.net, CHUNKS[c]
        self.passed[c] = []
        for k in (0, 1, 3, 2):
            if k:
                self.sent[c, k].wait_recv()
            part = self.into.at[net.core, net.plane(FSDP - k), pl.ds(at, size)]
            self.passed[c].append(net.copy(part, part, seq=net.seq(1)))

    def here(self, c):
        for copy in self.passed[c]:
            copy.wait_recv()

    def close(self):
        for copy in [*self.sent.values(), *self.passed[0], *self.passed[1]]:
            copy.wait_send()


class SlotReturn:
    def __init__(self, net, out, into, own, back, home):
        self.net, self.out, self.into, self.own = net, out, into, own
        self.back, self.home = back, home
        self.near, self.sent = {}, []

    def other(self, c, rows):
        at, size = CHUNKS[c]
        self.out[:, at : at + size] = rows.astype(bf16).reshape(EXPERTS, size, D)
        part = pl.ds(at, size)
        self.near[c] = self.net.copy(self.out.at[:, part], self.into.at[:, part], seq=self.net.seq(1))

    def mine(self, c, rows):
        net, (at, size) = self.net, CHUNKS[c]
        self.own[0 : EXPERTS * size] = rows
        self.near[c].wait_recv()
        got = self.into[:, at : at + size].astype(f32).reshape(EXPERTS * size, D)
        both = (self.own[0 : EXPERTS * size] + got).astype(bf16)
        self.back[:, at : at + size] = both.reshape(EXPERTS, size, D)
        for k in (2, 1, 3):
            e = net.plane(k)
            part = pl.ds(at, size)
            self.sent.append(net.copy(self.back.at[e, part], self.home.at[net.z, part], fsdp=e))
        self.home[net.z, at : at + size] = self.back[net.z, at : at + size]

    def wait(self):
        for copy in self.sent:
            copy.wait_recv()

    def close(self):
        for copy in [*self.sent, *self.near.values()]:
            copy.wait_send()


def ffn_forward_part(layer, net, ground, second, middle, small, onehot, chosen, jobs, refs):
    (
        result, gates, gathered, every, joint, hidden, rows, joint_e, hidden_e,
        rows_out, prod_out, prod_in, prod_own, back_out, yields, near_out, near_in, away_out,
        away_in, w_in, w_so, router,
    ) = refs
    t = second.shape[0]
    shared_job, join = jobs
    w1, w2 = join.w1, join.w2
    picked = chosen[:, :t] + chosen[:, t:]
    rows_out[...] = dot(picked, second[...]).astype(bf16).reshape(EXPERTS, CAP, D)
    every[net.s] = second[...]
    trip = SlotTrip(net, rows_out, rows)
    far = net.copy(every.at[net.s], every.at[net.s], seq=net.seq(2))
    near = net.copy(every.at[net.s], every.at[net.s], seq=net.seq(1))
    ground.at(30)
    loads = [net.move(shared_job.w_in, w_in), net.move(shared_job.w_out, w_so)]
    router[4:8, :] = jnp.zeros((4, D), f32)
    router[0:4, :] = small[6 * layer + 2 : 6 * layer + 6, :]
    logits = dot_nt(second[...], router[...].astype(bf16))
    l0 = jnp.sum(onehot[0, :, 0:8] * logits, -1, keepdims=True)
    l1 = jnp.sum(onehot[1, :, 0:8] * logits, -1, keepdims=True)
    top = jnp.maximum(l0, l1)
    e0, e1 = jnp.exp(l0 - top), jnp.exp(l1 - top)
    g0, g1 = e0 / (e0 + e1), e1 / (e0 + e1)
    lane = lax.broadcasted_iota(jnp.int32, (t, 128), 1)
    gates[...] = jnp.where(lane == 0, g0, jnp.where(lane == 1, g1, 0.0))
    wait_all(loads)

    def shared(b):
        g, u = dot(every[b], w_in[0].reshape(D, FF_DEV)), dot(every[b], w_in[1].reshape(D, FF_DEV))
        joint[0, b] = g.astype(bf16)
        joint[1, b] = u.astype(bf16)
        low = silu_gate(g, u).astype(bf16)
        hidden[b] = low
        return dot(low, w_so[...].reshape(FF_DEV, D))

    own_part = shared(net.s)
    ground.at(31)
    near.wait_recv()
    near_out[0] = shared(net.seq(1)).astype(bf16)
    far.wait_recv()
    passed_far = net.copy(every.at[net.seq(2)], every.at[net.seq(2)], seq=net.seq(1))
    away_out[...] = shared(net.seq(2)).astype(bf16)
    trip.hand_on(0)
    ground.at(32)
    passed_far.wait_recv()
    near_out[1] = shared(net.seq(3)).astype(bf16)
    near_sum = net.copy(near_out, near_in, seq=net.seq(1))
    net.done(every, joint, hidden)

    def expert(core, c):
        at, size = CHUNKS[c]
        part = slice(at, at + size)
        x = rows[core, :, part].reshape(EXPERTS * size, D)
        total = None
        for half in (0, 1):
            g = dot(x, w1[half, 0].reshape(D, FF_DEV))
            u = dot(x, w1[half, 1].reshape(D, FF_DEV))
            shape = (EXPERTS, size, FF_DEV)
            joint_e[core, half, 0, :, part] = g.astype(bf16).reshape(shape)
            joint_e[core, half, 1, :, part] = u.astype(bf16).reshape(shape)
            low = silu_gate(g, u).astype(bf16)
            hidden_e[core, half, :, part] = low.reshape(shape)
            new = dot(low, w2[half].reshape(FF_DEV, D))
            total = new if total is None else total + new
        return total

    trip.here(0)
    ground.at(33)
    back = SlotReturn(net, prod_out, prod_in, prod_own, back_out, yields)
    back.other(0, expert(1 - net.core, 0))
    trip.hand_on(1)
    near_sum.wait_recv()
    away_out[...] = (away_out[...].astype(f32) + near_in[1].astype(f32)).astype(bf16)
    away_sum = net.copy(away_out, away_in, seq=net.seq(2))
    ground.at(34)
    back.mine(0, expert(net.core, 0))
    ground.at(35)
    trip.here(1)
    back.other(1, expert(1 - net.core, 1))
    back.mine(1, expert(net.core, 1))
    net.done(rows, joint_e, hidden_e)
    ground.at(36)
    away_sum.wait_recv()
    base = middle[...] + own_part + near_in[0].astype(f32) + away_in[...].astype(f32)
    back.wait()
    got = dot_tn(chosen[...], yields[...].reshape(SLOTS, D))
    gathered[...] = got.astype(bf16)
    result[...] = base + g0 * got[:t] + g1 * got[t:]
    for copy in [far, near, passed_far, near_sum, away_sum]:
        copy.wait_send()
    trip.close()
    back.close()


def layer_forward_kernel(layer, places, net, ground, h, cosine, sine, onehot, chosen, *refs):
    if layer == 0:
        small, *refs = refs
        w_qkv, w_out = ground.made[1][1]
    else:
        small, w_qkv, w_out, *refs = refs
    attn, ffn = refs[:8] + refs[17:21], refs[8:17] + refs[21:]
    attn_forward_part(layer, net, ground, h, cosine, sine, small, w_qkv, w_out, attn)
    jobs = [ground.made[i][0] for i in places]
    ffn_forward_part(layer, net, ground, attn[1], attn[0], small, onehot, chosen, jobs, ffn)
    ground.drain()


def layer_forward(layer, h, tables, onehot, chosen, small, weights, jobs, shards, cid):
    t = h.shape[0]
    head = (HEADS_DEV, SEQ, t, HEAD_DIM)
    slots = (EXPERTS, CAP, FF_DEV)
    sums = [((2, t, D), bf16), ((2, t, D), bf16), ((t, D), bf16), ((t, D), bf16)]
    names = [job.__name__ for job, *_ in jobs]
    places = (names.index("SharedFetch"), names.index("JoinNext" if layer else "JoinFirst"))
    return call(
        functools.partial(layer_forward_kernel, layer, places),
        [h, *tables, onehot, chosen] + ([small, *weights] if layer else []),
        ([] if layer else [((16, D), f32)])
        + [
            ((t, D), f32), ((t, D), bf16), ((SEQ, t, D), bf16, 1), (head, bf16, 1), (head, bf16, 1),
            (head, bf16, 1), (head, f32, 1), ((HEADS_DEV, SEQ, t, 128), f32, 1),
        ]
        + [
            ((t, D), f32), ((t, 128), f32), ((2 * t, D), bf16), ((SEQ, t, D), bf16, 1),
            ((2, SEQ, t, FF_DEV), bf16, 1), ((SEQ, t, FF_DEV), bf16, 1),
            ((2, EXPERTS, CAP, D), bf16, 1), ((2, 2, 2, *slots), bf16, 1), ((2, 2, *slots), bf16, 1),
        ],
        sums
        + [
            ((EXPERTS, CAP, D), bf16), ((EXPERTS, CAP, D), bf16), ((EXPERTS, CAP, D), bf16),
            ((EXPERTS * CHUNKS[0][1], D), f32), ((EXPERTS, CAP, D), bf16),
            ((EXPERTS, CAP, D), bf16),
        ]
        + sums
        + [((2, 4, 4, 48, FF_DEV), bf16), ((4, 128, D), bf16), ((8, D), f32)],
        jobs, shards, cid,
    )


def norm_back(x, gain, gradient):
    factor = rms_rows(x)
    weighted = gradient * gain
    inner = jnp.mean(weighted * x, -1, keepdims=True)
    d_x = factor * weighted - x * (factor * factor * factor) * inner
    return d_x, jnp.sum(gradient * x * factor, 0, keepdims=True)


def gate_back(g, u, gradient):
    sig = 1.0 / (1.0 + jnp.exp(-g))
    d_g = gradient * u * sig * (1.0 + g * (1.0 - sig))
    return d_g.astype(bf16), (gradient * g * sig).astype(bf16)


def ffn_backward_kernel(
    net, ground, grad, gates, onehot, chosen, gathered, middle, second, gains, router, every,
    joint, hidden, rows, joint_e, hidden_e, w_in, w_so, w1, w2,
    d_middle, small, d_w1, d_w2,
    every_g, d_joint, rows_out, d_rows, d_joint_e, prod_out, prod_in, prod_own, back_out, back_in,
    near_out, near_in, away_out, away_in, d_w_in, d_w_so,
):
    t = grad.shape[0]
    net.greet(net.everyone())
    g0, g1 = gates[:, 0:1], gates[:, 1:2]
    up = grad[...].astype(f32)
    pairs = jnp.concatenate([(up * g0).astype(bf16), (up * g1).astype(bf16)], 0)
    rows_out[...] = dot(chosen[...], pairs).astype(bf16).reshape(EXPERTS, CAP, D)
    every_g[net.s] = up.astype(bf16)
    net.met()
    trip = SlotTrip(net, rows_out, d_rows)
    far = net.copy(every_g.at[net.s], every_g.at[net.s], seq=net.seq(2))
    near = net.copy(every_g.at[net.s], every_g.at[net.s], seq=net.seq(1))
    ground.at(0)
    net.need(w_so, joint, w_in)

    def shared(b):
        d_hidden = dot_nt(every_g[b], w_so[...])
        d_g, d_u = gate_back(joint[0, b].astype(f32), joint[1, b].astype(f32), d_hidden)
        d_joint[0, b] = d_g
        d_joint[1, b] = d_u
        return dot_nt(d_g, w_in[0]) + dot_nt(d_u, w_in[1])

    local = shared(net.s)
    ground.at(1)
    near.wait_recv()
    near_out[0] = shared(net.seq(1)).astype(bf16)
    far.wait_recv()
    passed_far = net.copy(every_g.at[net.seq(2)], every_g.at[net.seq(2)], seq=net.seq(1))
    away_out[...] = shared(net.seq(2)).astype(bf16)
    trip.hand_on(0)
    ground.at(2)
    passed_far.wait_recv()
    near_out[1] = shared(net.seq(3)).astype(bf16)
    near_sum = net.copy(near_out, near_in, seq=net.seq(1))
    net.need(every, hidden)
    tokens = every[...].reshape(SEQ * t, D)
    for gu in (0, 1):
        d_w = dot_tn(tokens, d_joint[gu].reshape(SEQ * t, FF_DEV))
        d_w_in[gu] = d_w.astype(bf16).reshape(4, 4, 48, FF_DEV)
    d_w = dot_tn(hidden[...].reshape(SEQ * t, FF_DEV), every_g[...].reshape(SEQ * t, D))
    d_w_so[...] = d_w.astype(bf16).reshape(4, 128, D)
    net.need(w2, w1, joint_e)

    def expert(core, c):
        at, size = CHUNKS[c]
        part = slice(at, at + size)
        x = d_rows[core, :, part].reshape(EXPERTS * size, D)
        out = None
        for half in (0, 1):
            d_hidden = dot_nt(x, w2[half].reshape(FF_DEV, D))
            flat, shape = (EXPERTS * size, FF_DEV), (EXPERTS, size, FF_DEV)
            g = joint_e[core, half, 0, :, part].astype(f32).reshape(flat)
            u = joint_e[core, half, 1, :, part].astype(f32).reshape(flat)
            d_g, d_u = gate_back(g, u, d_hidden)
            d_joint_e[half, 0, core, :, part] = d_g.reshape(shape)
            d_joint_e[half, 1, core, :, part] = d_u.reshape(shape)
            new = dot_nt(d_g, w1[half, 0].reshape(D, FF_DEV))
            new = new + dot_nt(d_u, w1[half, 1].reshape(D, FF_DEV))
            out = new if out is None else out + new
        return out

    trip.here(0)
    ground.at(3)
    back = SlotReturn(net, prod_out, prod_in, prod_own, back_out, back_in)
    back.other(0, expert(1 - net.core, 0))
    trip.hand_on(1)
    near_sum.wait_recv()
    away_out[...] = (away_out[...].astype(f32) + near_in[1].astype(f32)).astype(bf16)
    away_sum = net.copy(away_out, away_in, seq=net.seq(2))
    ground.at(4)
    back.mine(0, expert(net.core, 0))
    ground.at(5)
    trip.here(1)
    back.other(1, expert(1 - net.core, 1))
    back.mine(1, expert(net.core, 1))
    ground.at(6)
    net.need(rows, hidden_e)
    for half in (0, 1):
        d_rows_all = d_rows[...].reshape(2 * SLOTS, D)
        for gu in (0, 1):
            d_w = dot_tn(
                rows[...].reshape(2 * SLOTS, D), d_joint_e[half, gu].reshape(2 * SLOTS, FF_DEV)
            )
            d_w1[half, gu] = d_w.astype(bf16).reshape(4, 4, 48, FF_DEV)
        low = jnp.concatenate(
            [hidden_e[core, half].reshape(SLOTS, FF_DEV) for core in (0, 1)], 0
        )
        d_w2[half] = dot_tn(low, d_rows_all).astype(bf16).reshape(4, 128, D)
        ground.at(7 + half)
    net.done(d_w1, d_w2)
    net.need(gathered, onehot, second, router, middle)
    d0 = jnp.sum(up * gathered[:t].astype(f32), -1, keepdims=True)
    d1 = jnp.sum(up * gathered[t:].astype(f32), -1, keepdims=True)
    mean = g0 * d0 + g1 * d1
    d_logits = (g0 * (d0 - mean) * onehot[0] + g1 * (d1 - mean) * onehot[1]).astype(bf16)
    small[8:16, :] = dot_tn(d_logits, second[...])[:8]
    local = local + dot_nt(d_logits, router[...])
    away_sum.wait_recv()
    local = local + near_in[0].astype(f32) + away_in[...].astype(f32)
    back.wait()
    picked = chosen[:, :t] + chosen[:, t:]
    d_normed = local + dot_tn(picked, back_in[...].reshape(SLOTS, D))
    d_x, d_gain = norm_back(middle[...], gains[1:2, :], d_normed)
    d_middle[...] = up + d_x
    small[0:8, :] = jnp.broadcast_to(d_gain, (8, D))
    for copy in [far, near, passed_far, near_sum, away_sum]:
        copy.wait_send()
    trip.close()
    back.close()
    ground.drain()


def ffn_backward(grad, saved, gains, router, weights, jobs, shards, cid):
    t = grad.shape[0]
    gates, onehot, chosen, gathered, middle, second, every, joint, hidden, rows, joint_e, hidden_e = saved
    w_in, w_so, w1, w2 = weights
    slots = (EXPERTS, CAP, D)
    late = {}
    for name, x in (
        ("w_so", w_so), ("joint", joint), ("w_in", w_in), ("every", every), ("hidden", hidden),
        ("w2", w2), ("joint_e", joint_e), ("w1", w1), ("rows", rows), ("hidden_e", hidden_e),
        ("gathered", gathered), ("onehot", onehot), ("second", second), ("router", router),
        ("middle", middle),
    ):
        late[name] = Late(x)
    return call(
        ffn_backward_kernel,
        [
            grad, gates, late["onehot"], chosen, late["gathered"], late["middle"], late["second"],
            gains, late["router"], late["every"], late["joint"], late["hidden"], late["rows"],
            late["joint_e"], late["hidden_e"], late["w_in"], late["w_so"], late["w1"], late["w2"],
        ],
        [
            ((t, D), f32), ((16, D), f32), ((2, 2, 4, 4, 48, FF_DEV), bf16, 1),
            ((2, 4, 128, D), bf16, 1),
        ],
        [
            ((SEQ, t, D), bf16), ((2, SEQ, t, FF_DEV), bf16), (slots, bf16), ((2, *slots), bf16),
            ((2, 2, 2, EXPERTS, CAP, FF_DEV), bf16), (slots, bf16), (slots, bf16),
            ((EXPERTS * CHUNKS[0][1], D), f32), (slots, bf16), (slots, bf16), ((2, t, D), bf16),
            ((2, t, D), bf16), ((t, D), bf16), ((t, D), bf16), ((2, 4, 4, 48, FF_DEV), bf16),
            ((4, 128, D), bf16),
        ],
        jobs, shards, cid,
    )


def attn_backward_kernel(
    net, ground, d_middle, h, gains, every, queries, keys, values, attended, totals, w_qkv, w_out,
    cosine, sine,
    grad, d_gain, d_w_qkv, d_w_out,
    every_m, d_att, d_q, d_k, d_v, d_joint, near_out, near_in, away_out, away_in,
):
    t = h.shape[0]
    net.greet(net.everyone())
    up = d_middle[...]
    every_m[net.s] = up.astype(bf16)
    net.met()
    far = net.copy(every_m.at[net.s], every_m.at[net.s], seq=net.seq(2))
    near = net.copy(every_m.at[net.s], every_m.at[net.s], seq=net.seq(1))
    ground.at(0)

    net.need(w_out)

    def project(b):
        d = dot_nt(every_m[b], w_out[...].reshape(COLS, D)).astype(bf16)
        for i in range(HEADS_DEV):
            d_att[i, b] = d[:, i * HEAD_DIM : (i + 1) * HEAD_DIM]

    project(net.s)
    near.wait_recv()
    project(net.seq(1))
    far.wait_recv()
    passed = net.copy(every_m.at[net.seq(2)], every_m.at[net.seq(2)], seq=net.seq(1))
    project(net.seq(2))
    passed.wait_recv()
    project(net.seq(3))
    ground.at(1)
    net.need(attended)
    tokens = every_m[...].reshape(SEQ * t, D)
    low = jnp.concatenate(
        [attended[i].reshape(SEQ * t, HEAD_DIM).astype(bf16) for i in range(HEADS_DEV)], 1
    )
    d_w_out[...] = dot_tn(low, tokens).astype(bf16).reshape(SEQ, 48, D)
    scale = HEAD_DIM**-0.5
    net.need(queries, keys, values, totals)

    def head(i):
        d_k[i] = jnp.zeros_like(d_k[i])
        d_v[i] = jnp.zeros_like(d_v[i])
        for b in range(SEQ):
            size = (b + 1) * t
            q, d = queries[i, b], d_att[i, b]
            k = keys[i, : b + 1].reshape(size, HEAD_DIM)
            v = values[i, : b + 1].reshape(size, HEAD_DIM)
            delta = jnp.sum(d.astype(f32) * attended[i, b], -1, keepdims=True)
            row = lax.broadcasted_iota(jnp.int32, (t, size), 0) + b * t
            col = lax.broadcasted_iota(jnp.int32, (t, size), 1)
            scores = jnp.where(row >= col, dot_nt(q, k) * scale, MASKED)
            weights = jnp.exp(scores - totals[i, b][:, 0:1])
            d_scores = (weights * (dot_nt(d, v) - delta)).astype(bf16)
            d_q[i, b] = dot(d_scores, k) * scale
            shape = (b + 1, t, HEAD_DIM)
            d_k[i, : b + 1] += (dot_tn(d_scores, q) * scale).reshape(shape)
            d_v[i, : b + 1] += dot_tn(weights.astype(bf16), d).reshape(shape)

    for i in range(HEADS_DEV):
        head(i)
        ground.at(2 + i)

    net.need(cosine, sine, w_qkv)

    def part(b):
        c, sn = cosine[b], -sine[b]
        pieces = [turn(d_q[i, b], c, sn) for i in range(HEADS_DEV)]
        pieces += [turn(d_k[i, b], c, sn) for i in range(HEADS_DEV)]
        pieces += [d_v[i, b] for i in range(HEADS_DEV)]
        d = jnp.concatenate(pieces, 1).astype(bf16)
        d_joint[b] = d
        return dot_nt(d, w_qkv[...].reshape(D, 3 * COLS))

    near_out[0] = part(net.seq(1)).astype(bf16)
    near_out[1] = part(net.seq(3)).astype(bf16)
    near_sum = net.copy(near_out, near_in, seq=net.seq(1))
    away = part(net.seq(2))
    own = part(net.s)
    near_sum.wait_recv()
    away_out[...] = (away + near_in[1].astype(f32)).astype(bf16)
    away_sum = net.copy(away_out, away_in, seq=net.seq(2))
    own = own + near_in[0].astype(f32)
    ground.at(5)
    net.need(every)
    d_w = dot_tn(every[...].reshape(SEQ * t, D), d_joint[...].reshape(SEQ * t, 3 * COLS))
    d_w_qkv[...] = d_w.astype(bf16).reshape(4, 4, 48, 3 * COLS)
    ground.at(6)
    away_sum.wait_recv()
    net.need(h)
    d_x, gain = norm_back(h[...].astype(f32), gains[0:1, :], own + away_in[...].astype(f32))
    grad[...] = up + d_x
    row = lax.broadcasted_iota(jnp.int32, (8, D), 0)
    d_gain[...] = jnp.where(row == 0, gain, 0.0)
    ground.at(7)
    for copy in (far, near, passed, near_sum, away_sum):
        copy.wait_send()
    ground.drain()


def attn_backward(d_middle, saved, gains, weights, tables, jobs, shards, cid):
    t = d_middle.shape[0]
    h, every, queries, keys, values, attended, totals = saved
    head = (HEADS_DEV, SEQ, t, HEAD_DIM)
    return call(
        attn_backward_kernel,
        [d_middle, Late(h), gains]
        + [Late(x) for x in (every, queries, keys, values, attended, totals, *weights, *tables)],
        [((t, D), f32), ((8, D), f32), ((4, 4, 48, 3 * COLS), bf16), ((4, 48, D), bf16)],
        [
            ((SEQ, t, D), bf16), (head, bf16), (head, f32), (head, f32), (head, f32),
            ((SEQ, t, 3 * COLS), bf16), ((2, t, D), bf16), ((2, t, D), bf16), ((t, D), bf16),
            ((t, D), bf16),
        ],
        jobs, shards, cid,
    )


FORWARD_FIRST = (
    (SmallFetch, 0, (-2, -1, 0)),
    (AttnFetchHere, 0, (-2, -1, 2, 3)),
    (ExpertFetch, 0, (-2, 3, 30)),
    (SharedFetch, 0, (1, 3, 7, 30)),
    (JoinFirst, 0, (30, 33, 39)),
    (ExpertPlane, 1, (8, 40)),
    (AttnFetch, 1, (30, 33, 36, 40)),
)
FORWARD_NEXT = (
    (ExpertNear, 1, (2, 30)),
    (SharedFetch, 1, (0, 1, 4, 30)),
    (JoinNext, 1, (30, 33, 39)),
)
BACKWARD_FFN_FIRST = ((SharedAcross, 1, (3, 9)),)
BACKWARD_ATTN = (
    (GateToPlane, 1, (0, 2, 5, 12)),
    (UpToPlane, 1, (0, 2, 5, 12)),
    (SecondToPlane, 1, (2, 8, 10, 12)),
    (SharedReturn, 1, (0, 4, 6, 11)),
)
BACKWARD_FFN = (
    (SharedAcross, 0, (3, 9)),
    (AttnReturn, 1, (0, 3, 6, 8, 9)),
    (GateFinal, 1, (0, 9)),
    (UpFinal, 1, (0, 9)),
    (SecondFinal, 1, (0, 9)),
)
BACKWARD_ATTN_LAST = (
    (GateReturn, 0, (0, 3, 5, 9, 11)),
    (UpReturn, 0, (0, 3, 5, 9, 11)),
    (SharedReturn, 0, (0, 4, 5, 11)),
    (SecondReturn, 0, (0, 4, 6, 9, 11)),
    (AttnReturnHere, 0, (6, 9, 10, 11, 12)),
    (SmallReturnHere, 0, (7, 8, 9, 10)),
)


def local(
    reps, inputs, expert_choice, pair_order, norm_gains, attn_qkv, attn_out, router, shared_in,
    shared_out, expert_in, expert_out, cotangent,
):
    r, s, z = lax.axis_index("rep"), lax.axis_index("seq"), lax.axis_index("fsdp")
    tokens = inputs.shape[1]
    half = HEAD_DIM // 2
    inverse = np.exp(-np.log(np.float32(10000.0)) * np.arange(half, dtype=np.float32) * np.float32(2.0 / HEAD_DIM))
    angle = np.arange(SEQ * tokens, dtype=np.float32)[:, None] * inverse.astype(np.float32)[None, :]
    cosine, sine = np.cos(angle.astype(np.float64)), np.sin(angle.astype(np.float64))
    shape = (SEQ, tokens, HEAD_DIM)
    table_cos = jnp.asarray(np.concatenate([cosine, cosine], -1).reshape(shape), f32)
    table_sin = jnp.asarray(np.concatenate([-sine, sine], -1).reshape(shape), f32)
    small = jnp.concatenate([norm_gains, router.transpose(0, 2, 1)], 1).reshape(12, 48)
    shards = {
        "small": jnp.pad(small, ((0, 4), (0, 80))),
        "attn_qkv": attn_qkv.reshape(LAYERS, 48, 3, SEQ, COLS)
        .transpose(0, 3, 1, 2, 4)
        .reshape(LAYERS, SEQ, 48, 3 * COLS),
        "attn_out": attn_out,
        "shared_in": shared_in,
        "shared_out": shared_out,
        "expert_in": expert_in,
        "expert_out": expert_out,
    }
    h = inputs[0]
    kept_layers = []
    tables = (table_cos, table_sin)
    attn, gains, small = (), [None] * LAYERS, None
    for layer in range(LAYERS):
        first = layer == 0
        routes = routing(expert_choice[layer, 0], pair_order[layer, 0, 0])
        onehot = expert_choice[layer, 0].T[..., None] == jnp.arange(128, dtype=jnp.int32)
        onehot = onehot.astype(f32)
        outs, fetched = layer_forward(
            layer, h, tables, onehot, routes[1], small, attn, FORWARD_FIRST if first else FORWARD_NEXT,
            shards, 12 + layer,
        )
        if first:
            small, *outs = outs
            spread_small = small[:12].reshape(LAYERS, 6, D)
            gains, routers = spread_small[:, :2], spread_small[:, 2:].astype(bf16)
            attn, shared, w1, w2 = fetched[1:3], fetched[9:11], fetched[11], fetched[12]
            shards["next_p1"], shards["next_p2"] = fetched[13:15]
            next_attn = fetched[15:17]
        else:
            shared, w1, w2 = fetched[4:6], fetched[6], fetched[7]
        middle, second, every_one, queries, keys, values, attended, totals = outs[:8]
        result, gates, gathered, every_two, joint, hidden, rows, joint_e, hidden_e = outs[8:]
        w_in, w_so = shared[0].reshape(2, D, FF_DEV), shared[1].reshape(FF_DEV, D)
        router_pad = jnp.pad(routers[layer].T, ((0, 0), (0, 124)))
        attn_weights, ffn_weights = attn, (w_in, w_so, w1, w2)
        if first:
            attn = next_attn
        attn_saved = (h, every_one, queries, keys, values, attended, totals)
        ffn_saved = (
            gates, onehot, routes[1], gathered, middle, second, every_two, joint, hidden, rows,
            joint_e, hidden_e,
        )
        h = result
        kept_layers.append((attn_weights, ffn_weights, attn_saved, ffn_saved, router_pad))
    output = h.astype(bf16)[None]
    grad = cotangent[0]
    returned = {}
    grads = {}
    for layer in reversed(range(LAYERS)):
        last = layer == 0
        attn_weights, ffn_weights, attn_saved, ffn_saved, router_pad = kept_layers[layer]
        (d_middle, small, grads["d_w1"], grads["d_w2"]), done = ffn_backward(
            grad, ffn_saved, gains[layer], router_pad, ffn_weights,
            BACKWARD_FFN if last else BACKWARD_FFN_FIRST, grads, 18 + layer,
        )
        grads["r1"], grads["r2"] = done[:2]
        if last:
            returned["d_attn", 1], returned["d_expert", 1] = done[2:4], done[4:]
        grads[f"small_{layer}"] = small
        (grad, d_gain, d_w_qkv, d_w_out), done = attn_backward(
            d_middle, attn_saved, gains[layer], attn_weights, tables,
            BACKWARD_ATTN_LAST if last else BACKWARD_ATTN, grads, 16 + layer,
        )
        if last:
            returned["d_expert", 0], returned["d_shared", 0] = [*done[:2], done[4]], done[2:4]
            returned["d_attn", 0], total_small = done[5:7], done[7]
        else:
            grads["q_gate"], grads["q_up"], grads["q_second"] = done[:3]
            returned["d_shared", 1] = done[3:]
            grads["d_w_qkv"], grads["d_w_out"], grads["gain_1"] = d_w_qkv, d_w_out, d_gain
    total_small = rep_rest(total_small, reps)[:12].reshape(LAYERS, 6, D)
    total_small = lax.dynamic_slice_in_dim(total_small, (s * FSDP + z) * 48, 48, 2)

    def stack(name, k):
        return jnp.stack([rep_rest(returned[name, i][k], reps) for i in range(LAYERS)]).astype(f32)

    d_qkv = stack("d_attn", 0).reshape(LAYERS, SEQ, 48, 3, COLS).transpose(0, 2, 3, 1, 4)
    return (
        output, grad[None], total_small[:, :2], d_qkv.reshape(LAYERS, 48, 3 * D),
        stack("d_attn", 1), total_small[:, 2:].transpose(0, 2, 1), stack("d_shared", 0),
        stack("d_shared", 1), jnp.concatenate([stack("d_expert", 0), stack("d_expert", 1)], -1),
        stack("d_expert", 2),
    )


def solution(mesh):
    tokens = P(("rep", "fsdp"), "seq", None)
    routes = P(None, ("rep", "fsdp"), "seq", None)
    gains = P(None, None, ("seq", "fsdp"))
    dense = P(None, ("seq", "fsdp"), None)
    expert = P(None, None, ("seq", "fsdp"), None)
    in_specs = (
        tokens, routes, routes, gains, dense, dense, dense, dense, dense, expert, expert, tokens,
    )
    out_specs = (tokens, tokens, gains, dense, dense, dense, dense, dense, expert, expert)
    return jax.shard_map(
        functools.partial(local, mesh.shape["rep"]),
        mesh=mesh, in_specs=in_specs, out_specs=out_specs, check_vma=False,
    )
```

```python
import functools

import jax
import jax.numpy as jnp
import numpy as np
from jax import lax
from jax.experimental import pallas as pl
from jax.experimental.pallas import tpu as pltpu
from jax.sharding import PartitionSpec as P

D = 768
HEADS = 12
HEAD_DIM = 64
FF = 2048
EXPERTS = 4
LAYERS = 2
CAP = 144
EPS = 1e-06
MASKED = -1e30
SEQ = 4
FSDP = 4
HEADS_DEV = HEADS // SEQ
COLS = HEADS_DEV * HEAD_DIM
FF_DEV = FF // SEQ
FF_CORE = FF // 2
SLOTS = EXPERTS * CAP
bf16 = jnp.bfloat16
f32 = jnp.float32
MESH = pl.DeviceIdType.MESH


def dot(a, b):
    return jnp.dot(a, b, preferred_element_type=f32)


def dot_nt(a, b):
    return lax.dot_general(a, b, (((1,), (1,)), ((), ())), preferred_element_type=f32)


def dot_tn(a, b):
    return lax.dot_general(a, b, (((0,), (0,)), ((), ())), preferred_element_type=f32)


def rep_rest(x, reps):
    bit = 2
    while bit < reps:
        x = x + lax.ppermute(x, "rep", [(i, i ^ bit) for i in range(reps)])
        bit *= 2
    return x


def routing(choices, order):
    tokens = choices.shape[0]
    pairs = 2 * tokens
    flat = choices.reshape(-1)
    ids = jnp.arange(pairs, dtype=jnp.int32)
    place = (order[:, None] == ids[None, :]).astype(bf16)
    experts = (flat[:, None] == jnp.arange(EXPERTS, dtype=jnp.int32)[None, :]).astype(bf16)
    placed = dot(place, experts).astype(bf16)
    lower = (ids[:, None] > ids[None, :]).astype(bf16)
    slot_placed = jnp.minimum(jnp.sum(dot(lower, placed) * placed.astype(f32), 1), float(CAP))
    slot = dot_tn(place, slot_placed[:, None].astype(bf16))[:, 0].astype(jnp.int32)
    kept = slot < CAP
    target = jnp.where(kept, flat * CAP + slot, SLOTS).reshape(tokens, 2)
    target = target.T.reshape(-1)
    chosen = (target[None, :] == jnp.arange(SLOTS, dtype=jnp.int32)[:, None]).astype(bf16)
    return kept.reshape(tokens, 2).astype(f32), chosen


class Net:
    def __init__(self, send, recv, local_sems):
        self.send, self.recv, self.local_sems = send, recv, local_sems
        self.count = 0
        self.local_count = 0
        self.r, self.s, self.z = (lax.axis_index(a) for a in ("rep", "seq", "fsdp"))
        self.half = lax.rem(self.r, 2)
        self.core = lax.rem(self.s, 2)
        self.far = self.s // 2
        self.partner = self.r + 1 - 2 * self.half

    def seq(self, d):
        core = self.core if d % 2 == 0 else 1 - self.core
        far = self.far if d < 2 else 1 - self.far
        return far * 2 + core

    def plane(self, k):
        return lax.rem(self.z + k, FSDP)

    def copy(self, src, dst, **device):
        k = self.count
        self.count += 1
        out = pltpu.make_async_remote_copy(
            src_ref=src, dst_ref=dst, send_sem=self.send.at[k], recv_sem=self.recv.at[k],
            device_id=device, device_id_type=MESH,
        )
        out.start()
        return out

    def move(self, src, dst):
        k = self.local_count
        self.local_count += 1
        out = pltpu.make_async_copy(src, dst, self.local_sems.at[k])
        out.start()
        return out

    def need(self, *refs):
        for ref in refs:
            self.coming.pop(id(ref)).wait()

    def done(self, *refs):
        for ref in refs:
            self.going.append(self.move(ref, self.there.pop(id(ref))))

    def greet(self, devices):
        self.barrier = pltpu.get_barrier_semaphore()
        for device in devices:
            pl.semaphore_signal(self.barrier, inc=1, device_id=device, device_id_type=MESH)
        self.greeted = len(devices)

    def met(self):
        pl.semaphore_wait(self.barrier, self.greeted)

    def everyone(self):
        seqs = [{"seq": self.seq(d)} for d in (1, 2, 3)]
        planes = [{"fsdp": self.plane(k)} for k in (1, 2, 3)]
        both = [{"seq": self.seq(1), "fsdp": self.plane(k)} for k in (1, 2, 3)]
        return seqs + planes + both + [{"rep": self.partner}]


def columns(start, size):
    return pl.ds(pl.multiple_of(start, 128), size)


def wait_all(copies):
    for copy in copies:
        copy.wait()


class Job:
    space = pl.ANY
    out_space = pl.ANY
    scratch = ()
    kind = bf16

    def __init__(self, net, layer, ins, outs, scratch):
        self.net, self.layer = net, layer
        self.bind(ins, outs, scratch)


class ExpertPlane(Job):
    inputs = ("expert_in", "expert_out")
    shapes = ((2, 2, 4, 48, FF_DEV), (4, 128, 384))

    def bind(self, ins, outs, scratch):
        self.first, self.second = ins
        self.p1, self.p2 = outs

    def stages(self):
        return [self.plane_begin, self.plane_finish]

    def plane_begin(self):
        n = self.net
        self.copies = []
        for k in (2, 1, 3, 0):
            e = n.plane(k)
            for d in (0, 1):
                core = n.core if d == 0 else 1 - n.core
                for gu in (0, 1):
                    src = self.first.at[
                        self.layer, e, :, columns(gu * FF + n.half * FF_CORE + core * FF_DEV, FF_DEV)
                    ]
                    dst = self.p1.at[gu, n.core, n.z]
                    if k == 0 and d == 0:
                        self.copies.append(n.move(src, dst))
                    else:
                        self.copies.append(n.copy(src, dst, seq=n.seq(d), fsdp=e))
            src = self.second.at[self.layer, e, :, columns(n.half * 384, 384)]
            dst = self.p2.at[n.z]
            self.copies.append(n.move(src, dst) if k == 0 else n.copy(src, dst, fsdp=e))

    def plane_finish(self):
        wait_all(self.copies)


class ExpertFetch(ExpertPlane):
    shapes = ExpertPlane.shapes + ((2, 2, 4, 48, FF_DEV), (2, 2, 4, 48, FF_DEV)) + (
        (4, 128, 384), (4, 128, 384),
    )

    def bind(self, ins, outs, scratch):
        ExpertPlane.bind(self, ins, outs[:2], ())
        self.ax, self.ay, self.bx, self.by = outs[2:]

    def stages(self):
        def turn_over():
            self.plane_finish()
            self.near_begin()

        return [self.plane_begin, turn_over, self.near_finish]

    def near_begin(self):
        n = self.net
        self.sides = [
            n.copy(self.p1, self.ax, rep=n.partner), n.copy(self.p1, self.ay, seq=n.seq(2)),
            n.copy(self.p2, self.bx, rep=n.partner), n.copy(self.p2, self.by, seq=n.seq(2)),
        ]

    def near_finish(self):
        wait_all(self.sides)


class ExpertNear(ExpertFetch):
    inputs = ("next_p1", "next_p2")
    shapes = ExpertFetch.shapes[2:]

    def bind(self, ins, outs, scratch):
        self.p1, self.p2 = ins
        self.ax, self.ay, self.bx, self.by = outs

    def stages(self):
        return [self.near_begin, self.near_finish]


class ExpertJoin(Job):
    inputs = ("p1", "p2", "ax", "ay", "bx", "by")
    shapes = ((2, 2, 4, 4, 48, FF_DEV), (2, 4, 128, D))
    scratch = shapes

    def bind(self, ins, outs, scratch):
        self.p1, self.p2, self.ax, self.ay, self.bx, self.by = ins
        self.outs = outs
        self.w1, self.w2 = scratch

    def stages(self):
        return [self.begin, self.finish, self.written]

    def begin(self):
        n = self.net
        here, there = pl.ds(2 * n.far, 2), pl.ds(2 * (1 - n.far), 2)
        mine, rest = columns(n.half * 384, 384), columns((1 - n.half) * 384, 384)
        low, high = pl.ds(0, 2), pl.ds(2, 2)
        w1, w2 = self.w1, self.w2
        self.copies = [
            n.copy(self.ay.at[0], w1.at[n.half, 0, there], rep=n.partner),
            n.copy(self.ax.at[1], w1.at[1 - n.half, 1, here], seq=n.seq(2)),
            n.copy(self.by.at[low], w2.at[1 - n.far, low, :, mine], rep=n.partner),
            n.copy(self.bx.at[high], w2.at[n.far, high, :, rest], seq=n.seq(2)),
            n.move(self.p1, w1.at[n.half, :, here]),
            n.move(self.ax, w1.at[1 - n.half, :, here]),
            n.move(self.ay, w1.at[n.half, :, there]),
            n.move(self.p2, w2.at[n.far, :, :, mine]),
            n.move(self.bx, w2.at[n.far, :, :, rest]),
            n.move(self.by, w2.at[1 - n.far, :, :, mine]),
        ]

    def finish(self):
        wait_all(self.copies)
        self.copies = [
            self.net.move(self.w1, self.outs[0]), self.net.move(self.w2, self.outs[1])
        ]

    def written(self):
        wait_all(self.copies)


class JoinFirst(ExpertJoin):
    inputs = ()
    linked = ((2, 0), (2, 1), (2, 2), (2, 3), (2, 4), (2, 5))


class JoinNext(ExpertJoin):
    inputs = ("next_p1", "next_p2")
    linked = ((0, 0), (0, 1), (0, 2), (0, 3))


class SharedFetch(Job):
    inputs = ("shared_in", "shared_out")
    shapes = ((2, 4, 4, 48, FF_DEV), (4, 128, D))

    def bind(self, ins, outs, scratch):
        self.first, self.second = ins
        self.w_in, self.w_out = outs

    def stages(self):
        return [self.begin, self.second_hop, self.third_hop, self.finish]

    def begin(self):
        n = self.net
        self.firsts = []
        for d in (3, 2, 1, 0):
            src = self.first.at[self.layer, :, columns(n.half * FF + n.seq(d) * FF_DEV, FF_DEV)]
            dst = self.w_in.at[n.half, n.s, n.z]
            self.firsts.append(n.move(src, dst) if d == 0 else n.copy(src, dst, seq=n.seq(d)))
        src = self.second.at[self.layer, :, columns(n.half * 384, 384)]
        self.firsts.append(n.move(src, self.w_out.at[n.z, :, columns(n.half * 384, 384)]))

    def second_hop(self):
        n = self.net
        wait_all(self.firsts)
        part, low = self.w_in.at[n.half, :, n.z], self.w_out.at[n.z, :, columns(n.half * 384, 384)]
        self.sent = {}
        for k in (2, 1, 3):
            self.sent[k] = [n.copy(part, part, fsdp=n.plane(k)), n.copy(low, low, fsdp=n.plane(k))]
        self.across = [n.copy(part, part, rep=n.partner), n.copy(low, low, rep=n.partner)]

    def third_hop(self):
        n = self.net
        for k in (1, 3, 2):
            wait_all(self.sent[k])
            z = n.plane(FSDP - k)
            for part in (self.w_in.at[n.half, :, z], self.w_out.at[z, :, columns(n.half * 384, 384)]):
                self.across.append(n.copy(part, part, rep=n.partner))

    def finish(self):
        wait_all(self.across)


class AttnFetch(Job):
    inputs = ("attn_qkv", "attn_out")
    shapes = ((4, 4, 48, 3 * COLS), (4, 48, D))

    def bind(self, ins, outs, scratch):
        self.qkv, self.out = ins
        self.w_qkv, self.w_out = outs

    def stages(self):
        return [self.begin, self.second_hop, self.third_hop, self.finish]

    def begin(self):
        n = self.net
        self.firsts, self.seconds = [], []
        for d in (3, 2, 1, 0):
            src, dst = self.qkv.at[self.layer, n.seq(d)], self.w_qkv.at[n.s, n.z]
            self.firsts.append(n.move(src, dst) if d == 0 else n.copy(src, dst, seq=n.seq(d)))
        for k in (2, 1, 3, 0):
            src = self.out.at[self.layer, :, columns(n.half * 384, 384)]
            dst = self.w_out.at[n.z, :, columns(n.half * 384, 384)]
            self.seconds.append(n.move(src, dst) if k == 0 else n.copy(src, dst, fsdp=n.plane(k)))

    def second_hop(self):
        n = self.net
        wait_all(self.firsts)
        part = self.w_qkv.at[pl.ds(2 * n.half, 2), n.z]
        self.firsts = [n.copy(part, part, fsdp=n.plane(k)) for k in (2, 1, 3)]
        wait_all(self.seconds)
        part = self.w_out.at[:, :, columns(n.half * 384, 384)]
        self.across = [n.copy(part, part, rep=n.partner)]

    def third_hop(self):
        n = self.net
        for copy, k in zip(self.firsts[1:] + self.firsts[:1], (1, 3, 2)):
            copy.wait()
            part = self.w_qkv.at[pl.ds(2 * n.half, 2), n.plane(FSDP - k)]
            self.across.append(n.copy(part, part, rep=n.partner))

    def finish(self):
        wait_all(self.across)


class AttnFetchHere(AttnFetch):
    out_space = pltpu.VMEM


class SmallFetch(Job):
    out_space = pltpu.VMEM

    inputs = ("small",)
    shapes = ((4, 4, 16, 128),)

    def bind(self, ins, outs, scratch):
        (self.src,), (self.dst,) = ins, outs

    def stages(self):
        return [self.begin, self.second_hop, self.finish]

    def begin(self):
        n = self.net
        dst = self.dst.at[n.s, n.z]
        self.copies = [n.copy(self.src, dst, seq=n.seq(d)) for d in (3, 2, 1)]
        self.copies.append(n.move(self.src, dst))

    def second_hop(self):
        n = self.net
        wait_all(self.copies)
        part = self.dst.at[:, n.z]
        self.copies = [n.copy(part, part, fsdp=n.plane(k)) for k in (2, 1, 3)]

    def finish(self):
        wait_all(self.copies)


def total(*parts):
    out = parts[0].astype(f32)
    for part in parts[1:]:
        out = out + part.astype(f32)
    return out.astype(bf16)


class FirstSides(Job):
    inputs = ("d_w1",)
    out_space = pltpu.VMEM
    shapes = ((2, 4, 48, FF_DEV),)
    scratch = ((2, 2, 4, 48, FF_DEV), (2, 2, 4, 48, FF_DEV))

    def bind(self, ins, outs, scratch):
        (self.d,), (self.q,) = ins, outs
        self.own, self.got = scratch

    def stages(self):
        return [self.sides_begin, self.sides_second, self.sides_finish]

    def sides_begin(self):
        n = self.net
        if self.gu == 0:
            src = [self.d.at[1 - n.half, 0, pl.ds(2 * f, 2)] for f in (0, 1)]
            kept = [self.d.at[n.half, 0, pl.ds(2 * f, 2)] for f in (0, 1)]
            device = {"rep": n.partner}
        else:
            src = [self.d.at[h, 1, pl.ds(2 * (1 - n.far), 2)] for h in (0, 1)]
            kept = [self.d.at[h, 1, pl.ds(2 * n.far, 2)] for h in (0, 1)]
            device = {"seq": n.seq(2)}
        self.sent = [n.copy(src[i], self.got.at[i], **device) for i in (0, 1)]
        self.sent += [n.move(kept[i], self.own.at[i]) for i in (0, 1)]

    def sides_second(self):
        n = self.net
        wait_all(self.sent)
        stays = n.far if self.gu == 0 else n.half
        device = {"seq": n.seq(2)} if self.gu == 0 else {"rep": n.partner}
        goes = 1 - stays
        self.got[goes] = total(self.got[goes], self.own[goes])
        self.sent = [n.copy(self.got.at[goes], self.q, **device)]
        self.got[stays] = total(self.got[stays], self.own[stays])

    def sides_finish(self):
        n = self.net
        wait_all(self.sent)
        self.q[...] = total(self.q[...], self.got[n.far if self.gu == 0 else n.half])


class FirstPlane(Job):
    space = pltpu.VMEM
    shapes = ((EXPERTS, 48, FF),)
    half_only = False

    def bind(self, ins, outs, scratch):
        (self.q,), (self.o,) = ins, outs

    def stages(self):
        return [self.plane_begin, self.plane_second, self.plane_finish]

    def plane_begin(self):
        n = self.net
        self.sent = []
        at = n.core * FF_DEV if self.half_only else n.half * FF_CORE + n.core * FF_DEV
        dst = self.o.at[n.z, :, columns(at, FF_DEV)]
        for k in (2, 1, 3, 0):
            for d in (1, 0):
                core = n.core if d == 0 else 1 - n.core
                src = self.q.at[core, n.plane(k)]
                if k == 0 and d == 0:
                    self.sent.append(n.move(src, dst))
                else:
                    self.sent.append(n.copy(src, dst, seq=n.seq(d), fsdp=n.plane(k)))

    def plane_second(self):
        n = self.net
        wait_all(self.sent)
        part = self.o.at[:, :, columns(n.half * FF_CORE, FF_CORE)]
        self.sent = [n.copy(part, part, rep=n.partner)]

    def plane_finish(self):
        wait_all(self.sent)


class FirstReturn(FirstSides, FirstPlane):
    shapes = FirstPlane.shapes
    scratch = FirstSides.scratch + FirstSides.shapes
    space = pl.ANY
    out_space = pl.ANY

    def bind(self, ins, outs, scratch):
        FirstSides.bind(self, ins, scratch[2:], scratch[:2])
        FirstPlane.bind(self, scratch[2:], outs, ())

    def turn_over(self):
        self.sides_finish()
        self.plane_begin()

    def stages(self):
        return [
            self.sides_begin, self.sides_second, self.turn_over, self.plane_second,
            self.plane_finish,
        ]


class FirstToPlane(FirstReturn):
    shapes = ((EXPERTS, 48, FF_CORE),)
    half_only = True

    def stages(self):
        return [self.sides_begin, self.sides_second, self.turn_over, self.plane_finish]


class FirstFinal(Job):
    shapes = ((EXPERTS, 48, FF),)

    def bind(self, ins, outs, scratch):
        (self.q,), (self.o,) = ins, outs

    def stages(self):
        return [self.begin, self.finish]

    def begin(self):
        n = self.net
        part = self.o.at[:, :, columns(n.half * FF_CORE, FF_CORE)]
        self.sent = [n.copy(self.q, part, rep=n.partner), n.move(self.q, part)]

    def finish(self):
        wait_all(self.sent)


class GateReturn(FirstReturn):
    gu = 0


class UpReturn(FirstReturn):
    gu = 1


class GateToPlane(FirstToPlane):
    gu = 0


class UpToPlane(FirstToPlane):
    gu = 1


class GateFinal(FirstFinal):
    inputs = ("q_gate",)


class UpFinal(FirstFinal):
    inputs = ("q_up",)


class SecondReturn(Job):
    inputs = ("d_w2",)
    shapes = ((EXPERTS, 128, D),)
    scratch = ((2, 4, 128, 384), (2, 4, 128, 384), (4, 128, 384))
    rep_first = True

    def bind(self, ins, outs, scratch):
        (self.d,), (self.o,) = ins, outs
        self.own, self.got, self.q = scratch

    def stages(self):
        return [
            self.sides_begin, self.sides_second, self.turn_over, self.plane_second,
            self.plane_finish,
        ]

    def sides_begin(self):
        n = self.net
        halves = [columns(h * 384, 384) for h in (0, 1)]
        mine, rest = columns(n.half * 384, 384), columns((1 - n.half) * 384, 384)
        if self.rep_first:
            src = [self.d.at[f, :, :, rest] for f in (0, 1)]
            kept = [self.d.at[f, :, :, mine] for f in (0, 1)]
            device = {"rep": n.partner}
        else:
            src = [self.d.at[1 - n.far, :, :, h] for h in halves]
            kept = [self.d.at[n.far, :, :, h] for h in halves]
            device = {"seq": n.seq(2)}
        self.sent = [n.copy(src[i], self.got.at[i], **device) for i in (0, 1)]
        self.sent += [n.move(kept[i], self.own.at[i]) for i in (0, 1)]

    def sides_second(self):
        n = self.net
        wait_all(self.sent)
        self.stays = n.far if self.rep_first else n.half
        device = {"seq": n.seq(2)} if self.rep_first else {"rep": n.partner}
        goes = 1 - self.stays
        self.got[goes] = total(self.got[goes], self.own[goes])
        self.sent = [n.copy(self.got.at[goes], self.q, **device)]
        self.got[self.stays] = total(self.got[self.stays], self.own[self.stays])

    def target(self):
        return columns(self.net.half * 384, 384)

    def turn_over(self):
        n = self.net
        wait_all(self.sent)
        self.q[...] = total(self.q[...], self.got[self.stays])
        self.sent = []
        dst = self.o.at[n.z, :, self.target()]
        for k in (2, 1, 3, 0):
            src = self.q.at[n.plane(k)]
            self.sent.append(n.move(src, dst) if k == 0 else n.copy(src, dst, fsdp=n.plane(k)))

    def plane_second(self):
        n = self.net
        wait_all(self.sent)
        part = self.o.at[:, :, columns(n.half * 384, 384)]
        self.sent = [n.copy(part, part, rep=n.partner)]

    def plane_finish(self):
        wait_all(self.sent)


class SecondToPlane(SecondReturn):
    shapes = ((EXPERTS, 128, 384),)

    def stages(self):
        return [self.sides_begin, self.sides_second, self.turn_over, self.plane_finish]

    def target(self):
        return pl.ds(0, 384)


class SecondFinal(FirstFinal):
    inputs = ("q_second",)
    shapes = ((EXPERTS, 128, D),)

    def begin(self):
        n = self.net
        part = self.o.at[:, :, columns(n.half * 384, 384)]
        self.sent = [n.copy(self.q, part, rep=n.partner), n.move(self.q, part)]


class SharedAcross(Job):
    inputs = ()
    own = (-2, -1)
    out_space = pltpu.VMEM
    shapes = ((4, 4, 48, FF_DEV), (4, 128, 384))

    def bind(self, ins, outs, scratch):
        self.d1, self.d2 = ins
        self.r1, self.r2 = outs

    def stages(self):
        return [self.begin, self.finish]

    def begin(self):
        n = self.net
        part = self.d2.at[:, :, columns((1 - n.half) * 384, 384)]
        self.sent = [
            n.copy(self.d1.at[1 - n.half], self.r1, rep=n.partner),
            n.copy(part, self.r2, rep=n.partner),
        ]

    def finish(self):
        n = self.net
        wait_all(self.sent)
        self.r1[...] = total(self.r1[...], self.d1[n.half])
        self.r2[...] = total(self.r2[...], self.d2[:, :, columns(n.half * 384, 384)])


class SharedReturn(Job):
    space = pltpu.VMEM
    inputs = ("r1", "r2")
    shapes = ((48, 2 * FF), (128, D))
    scratch = ((3, 4, 48, FF_DEV), (4, 48, FF_DEV), (3, 128, 384), (128, 384))

    def bind(self, ins, outs, scratch):
        self.r1, self.r2 = ins
        self.o1, self.o2 = outs
        self.r1z, self.s1, self.r2z, self.s2 = scratch

    def stages(self):
        return [self.second_hop, self.third_hop, self.fourth_hop, self.finish]

    def second_hop(self):
        n = self.net
        self.firsts = [
            n.copy(self.r1.at[:, n.plane(k)], self.r1z.at[k - 1], fsdp=n.plane(k))
            for k in (2, 1, 3)
        ]
        self.seconds = [
            n.copy(self.r2.at[n.plane(k)], self.r2z.at[k - 1], fsdp=n.plane(k)) for k in (2, 1, 3)
        ]

    def third_hop(self):
        n = self.net
        wait_all(self.firsts + self.seconds)
        self.s1[...] = total(self.r1[:, n.z], self.r1z[0], self.r1z[1], self.r1z[2])
        self.firsts = []
        for d in (3, 2, 1, 0):
            src = self.s1.at[n.seq(d)]
            dst = self.o1.at[:, columns(n.half * FF + n.s * FF_DEV, FF_DEV)]
            self.firsts.append(n.move(src, dst) if d == 0 else n.copy(src, dst, seq=n.seq(d)))
        self.s2[...] = total(self.r2[n.z], self.r2z[0], self.r2z[1], self.r2z[2])
        dst = self.o2.at[:, columns(n.half * 384, 384)]
        self.seconds = [n.copy(self.s2, dst, rep=n.partner), n.move(self.s2, dst)]

    def fourth_hop(self):
        n = self.net
        wait_all(self.firsts)
        part = self.o1.at[:, columns(n.half * FF, FF)]
        self.firsts = [n.copy(part, part, rep=n.partner)]

    def finish(self):
        wait_all(self.firsts + self.seconds)


class AttnReturn(Job):
    space = pltpu.VMEM
    inputs = ("d_w_qkv", "d_w_out")
    shapes = ((4, 48, 3 * COLS), (48, D))
    scratch = (
        (2, 4, 48, 3 * COLS), (3, 2, 48, 3 * COLS), (4, 48, 3 * COLS), (4, 48, 384), (3, 48, 384),
        (48, 384),
    )

    def bind(self, ins, outs, scratch):
        self.d1, self.d2 = ins
        self.o1, self.o2 = outs
        self.r1, self.r1z, self.s1, self.r2, self.r2z, self.s2 = scratch

    def stages(self):
        return [self.begin, self.second_hop, self.third_hop, self.fourth_hop, self.finish]

    def begin(self):
        n = self.net
        self.firsts = [n.copy(self.d1.at[pl.ds(2 * (1 - n.half), 2)], self.r1, rep=n.partner)]
        part = self.d2.at[:, :, columns((1 - n.half) * 384, 384)]
        self.seconds = [n.copy(part, self.r2, rep=n.partner)]

    def second_hop(self):
        n = self.net
        wait_all(self.firsts)
        self.r1[...] = total(self.r1[...], self.d1[pl.ds(2 * n.half, 2)])
        self.firsts = [
            n.copy(self.r1.at[:, n.plane(k)], self.r1z.at[k - 1], fsdp=n.plane(k))
            for k in (2, 1, 3)
        ]
        wait_all(self.seconds)
        self.r2[...] = total(self.r2[...], self.d2[:, :, columns(n.half * 384, 384)])
        self.seconds = [
            n.copy(self.r2.at[n.plane(k)], self.r2z.at[k - 1], fsdp=n.plane(k)) for k in (2, 1, 3)
        ]

    def third_hop(self):
        n = self.net
        wait_all(self.firsts + self.seconds)
        pair = pl.ds(2 * n.half, 2)
        self.s1[pair] = total(self.r1[:, n.z], self.r1z[0], self.r1z[1], self.r1z[2])
        self.firsts = [n.copy(self.s1.at[pair], self.s1.at[pair], rep=n.partner)]
        self.s2[...] = total(self.r2[n.z], self.r2z[0], self.r2z[1], self.r2z[2])
        dst = self.o2.at[:, columns(n.half * 384, 384)]
        self.seconds = [n.copy(self.s2, dst, rep=n.partner), n.move(self.s2, dst)]

    def fourth_hop(self):
        n = self.net
        wait_all(self.firsts)
        self.firsts = []
        for d in (3, 2, 1, 0):
            src, dst = self.s1.at[n.seq(d)], self.o1.at[n.s]
            self.firsts.append(n.move(src, dst) if d == 0 else n.copy(src, dst, seq=n.seq(d)))

    def finish(self):
        wait_all(self.firsts + self.seconds)


class AttnReturnHere(AttnReturn):
    inputs = ()
    own = (2, 3)


class SmallReturnHere(Job):
    inputs = ("small_0", "gain_1", "small_1")
    space = pltpu.VMEM
    out_space = pltpu.VMEM
    kind = f32
    own = (1,)
    shapes = ((16, D),)
    scratch = ((16, D), (16, D), (3, 16, D), (3, 16, D))

    def bind(self, ins, outs, scratch):
        self.zero, self.gain_one, self.one, self.gain = ins
        (self.out,) = outs
        self.acc, self.rx, self.rz, self.rs = scratch

    def stages(self):
        return [self.begin, self.second_hop, self.third_hop, self.finish]

    def begin(self):
        n = self.net
        self.acc[12:16] = jnp.zeros((4, D), f32)
        for at, gain, rest in ((0, self.gain, self.zero), (6, self.gain_one, self.one)):
            self.acc[at : at + 1] = gain[0:1]
            self.acc[at + 1 : at + 2] = rest[0:1]
            self.acc[at + 2 : at + 6] = rest[8:12]
        self.copies = [n.copy(self.acc, self.rx, rep=n.partner)]

    def second_hop(self):
        n = self.net
        wait_all(self.copies)
        self.rx[...] = self.acc[...] + self.rx[...]
        self.copies = [n.copy(self.rx, self.rz.at[k - 1], fsdp=n.plane(k)) for k in (2, 1, 3)]

    def third_hop(self):
        n = self.net
        wait_all(self.copies)
        self.acc[...] = self.rx[...] + self.rz[0] + self.rz[1] + self.rz[2]
        self.copies = [n.copy(self.acc, self.rs.at[d - 1], seq=n.seq(d)) for d in (3, 2, 1)]

    def finish(self):
        wait_all(self.copies)
        self.out[...] = self.acc[...] + self.rs[0] + self.rs[1] + self.rs[2]


class Background:
    def __init__(self, net, jobs, ins, own_outs, outs, scratch):
        self.queues, self.made = [], []
        for job, layer, points in jobs:
            a, b, c = len(job.inputs), len(job.shapes), len(job.scratch)
            given = list(ins[:a]) + [own_outs[i] for i in getattr(job, "own", ())]
            given += [self.made[i][1][k] for i, k in getattr(job, "linked", ())]
            made = job(net, layer, given, outs[:b], scratch[:c])
            self.made.append((made, outs[:b]))
            stages = made.stages()
            last = points[-1]
            points = tuple(points) + (last,) * (len(stages) - len(points))
            self.queues.append(list(zip(points, stages)))
            ins, outs, scratch = ins[a:], outs[b:], scratch[c:]

    def at(self, point):
        for queue in self.queues:
            while queue and queue[0][0] <= point:
                queue.pop(0)[1]()

    def drain(self):
        for point in range(9, 70):
            self.at(point)


COPIES = 160
MOVES = 64


class Late:
    def __init__(self, array):
        self.array = array


def call(kernel, inputs, outputs, scratch, jobs, shards, cid):
    given = [shards[name] for job, *_ in jobs for name in job.inputs]
    results = [
        (jax.ShapeDtypeStruct(shape, job.kind), job.out_space)
        for job, *_ in jobs
        for shape in job.shapes
    ]
    vmem, anywhere = pl.BlockSpec(memory_space=pltpu.VMEM), pl.BlockSpec(memory_space=pl.ANY)
    job_scratch = [pltpu.VMEM(shape, job.kind) for job, *_ in jobs for shape in job.scratch]
    late_in = [i for i, x in enumerate(inputs) if isinstance(x, Late)]
    arrays = [x.array if isinstance(x, Late) else x for x in inputs]
    late_out = [i for i, x in enumerate(outputs) if len(x) == 3]
    late = [pltpu.VMEM(arrays[i].shape, arrays[i].dtype) for i in late_in]
    late += [pltpu.VMEM(outputs[i][0], outputs[i][1]) for i in late_out]

    def body(*refs):
        a = len(inputs)
        b = a + len(given)
        c = b + len(outputs)
        d = c + len(results)
        e = d + len(scratch)
        f = e + len(job_scratch)
        g = f + len(late)
        net = Net(*refs[g:])
        ins, outs = list(refs[:a]), list(refs[b:c])
        net.coming, net.going = {}, []
        for i, ref in zip(late_in, refs[f:]):
            net.coming[id(ref)] = net.move(ins[i], ref)
            ins[i] = ref
        there = {}
        for i, ref in zip(late_out, refs[f + len(late_in) : g]):
            there[id(ref)] = outs[i]
            outs[i] = ref
        net.there = there
        ground = Background(net, jobs, refs[a:b], outs + list(refs[d:e]), refs[c:d], refs[e:f])
        kernel(net, ground, *ins, *outs, *refs[d:e])
        assert not net.coming and not there
        assert net.count <= COPIES and net.local_count <= MOVES
        wait_all(net.going)

    made = pl.pallas_call(
        body,
        out_shape=[jax.ShapeDtypeStruct(x[0], x[1]) for x in outputs] + [shape for shape, _ in results],
        in_specs=[anywhere if i in late_in else vmem for i in range(len(inputs))]
        + [pl.BlockSpec(memory_space=job.space) for job, *_ in jobs for _ in job.inputs],
        out_specs=[anywhere if i in late_out else vmem for i in range(len(outputs))]
        + [pl.BlockSpec(memory_space=where) for _, where in results],
        scratch_shapes=[pltpu.VMEM(shape, kind) for shape, kind in scratch]
        + job_scratch
        + late
        + [
            pltpu.SemaphoreType.DMA((COPIES,)),
            pltpu.SemaphoreType.DMA((COPIES,)),
            pltpu.SemaphoreType.DMA((MOVES,)),
        ],
        compiler_params=pltpu.CompilerParams(
            collective_id=cid, has_side_effects=True, vmem_limit_bytes=60 << 20
        ),
        cost_estimate=pl.CostEstimate(flops=0, bytes_accessed=1 << 20, transcendentals=0),
    )(*arrays, *given)
    return made[: len(outputs)], made[len(outputs) :]


def rms_rows(x):
    return lax.rsqrt(jnp.mean(x * x, -1, keepdims=True) + EPS)


def turn(x, cosine, sine):
    half = HEAD_DIM // 2
    return x * cosine + jnp.concatenate([x[:, half:], x[:, :half]], 1) * sine


def spread(small):
    lane = lax.broadcasted_iota(jnp.int32, (128, D), 0)
    col = lax.broadcasted_iota(jnp.int32, (128, D), 1)
    out = jnp.zeros((16, D), f32)
    for i in range(16):
        place = jnp.where((col == lane + 48 * i) & (lane < 48), 1.0, 0.0).astype(bf16)
        out = out + dot(small[i // 4, i % 4], place)
    return out


def attn_forward_part(layer, net, ground, h, cosine, sine, small, w_qkv, w_out, refs):
    (
        middle, second, every, queries, keys, values, attended, totals,
        near_out, near_in, away_out, away_in,
    ) = refs
    here = layer == 0
    net.greet(net.everyone())
    x = h[...].astype(f32)
    factor = rms_rows(x)
    if here:
        net.met()
        for point in (-2, -1, 0):
            ground.at(point)
        small[...] = spread(ground.made[0][1][0])
    gain_one, gain_two = small[6 * layer : 6 * layer + 1, :], small[6 * layer + 1 : 6 * layer + 2, :]
    every[net.s] = (x * factor * gain_one).astype(bf16)
    if not here:
        net.met()
        ground.at(0)
    far = net.copy(every.at[net.s], every.at[net.s], seq=net.seq(2))
    near = net.copy(every.at[net.s], every.at[net.s], seq=net.seq(1))
    ground.at(1)

    def project(b):
        joint = dot(every[b], w_qkv[...].reshape(D, 3 * COLS))
        c, sn = cosine[b], sine[b]
        for i in range(HEADS_DEV):
            at = i * HEAD_DIM
            queries[i, b] = turn(joint[:, at : at + HEAD_DIM], c, sn).astype(bf16)
            at += COLS
            keys[i, b] = turn(joint[:, at : at + HEAD_DIM], c, sn).astype(bf16)
            at += COLS
            values[i, b] = joint[:, at : at + HEAD_DIM].astype(bf16)

    if not here:
        project(net.s)
    near.wait_recv()
    ground.at(2)
    if not here:
        project(net.seq(1))
    far.wait_recv()
    passed = net.copy(every.at[net.seq(2)], every.at[net.seq(2)], seq=net.seq(1))
    ground.at(3)
    if here:
        project(net.s)
        project(net.seq(1))
    project(net.seq(2))
    passed.wait_recv()
    project(net.seq(3))
    net.done(every, queries, keys, values)
    ground.at(4)
    tokens = h.shape[0]

    def head(i):
        for b in range(SEQ):
            size = (b + 1) * tokens
            scores = dot_nt(queries[i, b], keys[i, : b + 1].reshape(size, HEAD_DIM))
            row = lax.broadcasted_iota(jnp.int32, (tokens, size), 0) + b * tokens
            col = lax.broadcasted_iota(jnp.int32, (tokens, size), 1)
            scores = jnp.where(row >= col, scores * HEAD_DIM**-0.5, MASKED)
            top = jnp.max(scores, -1, keepdims=True)
            weights = jnp.exp(scores - top)
            total = jnp.sum(weights, -1, keepdims=True)
            weights = (weights * (1.0 / total)).astype(bf16)
            attended[i, b] = dot(weights, values[i, : b + 1].reshape(size, HEAD_DIM))
            totals[i, b] = jnp.broadcast_to(top + jnp.log(total), (tokens, 128))

    for i in range(HEADS_DEV):
        head(i)
        ground.at(5 + i)
    net.done(attended, totals)

    def part(b):
        low = jnp.concatenate([attended[i, b].astype(bf16) for i in range(HEADS_DEV)], 1)
        return dot(low, w_out[...].reshape(COLS, D))

    near_out[0] = part(net.seq(1)).astype(bf16)
    near_out[1] = part(net.seq(3)).astype(bf16)
    near_sum = net.copy(near_out, near_in, seq=net.seq(1))
    away = part(net.seq(2))
    own = part(net.s)
    near_sum.wait_recv()
    away_out[...] = (away + near_in[1].astype(f32)).astype(bf16)
    away_sum = net.copy(away_out, away_in, seq=net.seq(2))
    own = h[...].astype(f32) + own + near_in[0].astype(f32)
    ground.at(8)
    away_sum.wait_recv()
    own = own + away_in[...].astype(f32)
    middle[...] = own
    second[...] = (own * rms_rows(own) * gain_two).astype(bf16)
    for copy in (far, near, passed, near_sum, away_sum):
        copy.wait_send()


def silu_gate(g, u):
    return g / (1.0 + jnp.exp(-g)) * u


CHUNKS = ((0, 80), (80, 64))


class SlotTrip:
    def __init__(self, net, out, into):
        self.net, self.into = net, into
        self.sent, self.passed = {}, {}
        for c, (at, size) in enumerate(CHUNKS):
            for k in (2, 1, 3):
                e = net.plane(k)
                self.sent[c, k] = net.copy(
                    out.at[e, pl.ds(at, size)], into.at[net.core, net.z, pl.ds(at, size)], fsdp=e
                )
        into[net.core, net.z] = out[net.z]

    def hand_on(self, c):
        net, (at, size) = self.net, CHUNKS[c]
        self.passed[c] = []
        for k in (0, 1, 3, 2):
            if k:
                self.sent[c, k].wait_recv()
            part = self.into.at[net.core, net.plane(FSDP - k), pl.ds(at, size)]
            self.passed[c].append(net.copy(part, part, seq=net.seq(1)))

    def here(self, c):
        for copy in self.passed[c]:
            copy.wait_recv()

    def close(self):
        for copy in [*self.sent.values(), *self.passed[0], *self.passed[1]]:
            copy.wait_send()


class SlotReturn:
    def __init__(self, net, out, into, own, back, home):
        self.net, self.out, self.into, self.own = net, out, into, own
        self.back, self.home = back, home
        self.near, self.sent = {}, []

    def other(self, c, rows):
        at, size = CHUNKS[c]
        self.out[:, at : at + size] = rows.astype(bf16).reshape(EXPERTS, size, D)
        part = pl.ds(at, size)
        self.near[c] = self.net.copy(self.out.at[:, part], self.into.at[:, part], seq=self.net.seq(1))

    def mine(self, c, rows):
        net, (at, size) = self.net, CHUNKS[c]
        self.own[0 : EXPERTS * size] = rows
        self.near[c].wait_recv()
        got = self.into[:, at : at + size].astype(f32).reshape(EXPERTS * size, D)
        both = (self.own[0 : EXPERTS * size] + got).astype(bf16)
        self.back[:, at : at + size] = both.reshape(EXPERTS, size, D)
        for k in (2, 1, 3):
            e = net.plane(k)
            part = pl.ds(at, size)
            self.sent.append(net.copy(self.back.at[e, part], self.home.at[net.z, part], fsdp=e))
        self.home[net.z, at : at + size] = self.back[net.z, at : at + size]

    def wait(self):
        for copy in self.sent:
            copy.wait_recv()

    def close(self):
        for copy in [*self.sent, *self.near.values()]:
            copy.wait_send()


def ffn_forward_part(layer, net, ground, second, middle, small, onehot, chosen, jobs, refs):
    (
        result, gates, gathered, every, joint, hidden, rows, joint_e, hidden_e,
        rows_out, prod_out, prod_in, prod_own, back_out, yields, near_out, near_in, away_out,
        away_in, w_in, w_so, router,
    ) = refs
    t = second.shape[0]
    shared_job, join = jobs
    w1, w2 = join.w1, join.w2
    picked = chosen[:, :t] + chosen[:, t:]
    rows_out[...] = dot(picked, second[...]).astype(bf16).reshape(EXPERTS, CAP, D)
    every[net.s] = second[...]
    trip = SlotTrip(net, rows_out, rows)
    far = net.copy(every.at[net.s], every.at[net.s], seq=net.seq(2))
    near = net.copy(every.at[net.s], every.at[net.s], seq=net.seq(1))
    ground.at(30)
    loads = [net.move(shared_job.w_in, w_in), net.move(shared_job.w_out, w_so)]
    router[4:8, :] = jnp.zeros((4, D), f32)
    router[0:4, :] = small[6 * layer + 2 : 6 * layer + 6, :]
    logits = dot_nt(second[...], router[...].astype(bf16))
    l0 = jnp.sum(onehot[0, :, 0:8] * logits, -1, keepdims=True)
    l1 = jnp.sum(onehot[1, :, 0:8] * logits, -1, keepdims=True)
    top = jnp.maximum(l0, l1)
    e0, e1 = jnp.exp(l0 - top), jnp.exp(l1 - top)
    g0, g1 = e0 / (e0 + e1), e1 / (e0 + e1)
    lane = lax.broadcasted_iota(jnp.int32, (t, 128), 1)
    gates[...] = jnp.where(lane == 0, g0, jnp.where(lane == 1, g1, 0.0))
    wait_all(loads)

    def shared(b):
        g, u = dot(every[b], w_in[0].reshape(D, FF_DEV)), dot(every[b], w_in[1].reshape(D, FF_DEV))
        joint[0, b] = g.astype(bf16)
        joint[1, b] = u.astype(bf16)
        low = silu_gate(g, u).astype(bf16)
        hidden[b] = low
        return dot(low, w_so[...].reshape(FF_DEV, D))

    own_part = shared(net.s)
    ground.at(31)
    near.wait_recv()
    near_out[0] = shared(net.seq(1)).astype(bf16)
    far.wait_recv()
    passed_far = net.copy(every.at[net.seq(2)], every.at[net.seq(2)], seq=net.seq(1))
    away_out[...] = shared(net.seq(2)).astype(bf16)
    trip.hand_on(0)
    ground.at(32)
    passed_far.wait_recv()
    near_out[1] = shared(net.seq(3)).astype(bf16)
    near_sum = net.copy(near_out, near_in, seq=net.seq(1))
    net.done(every, joint, hidden)

    def expert(core, c):
        at, size = CHUNKS[c]
        part = slice(at, at + size)
        x = rows[core, :, part].reshape(EXPERTS * size, D)
        total = None
        for half in (0, 1):
            g = dot(x, w1[half, 0].reshape(D, FF_DEV))
            u = dot(x, w1[half, 1].reshape(D, FF_DEV))
            shape = (EXPERTS, size, FF_DEV)
            joint_e[core, half, 0, :, part] = g.astype(bf16).reshape(shape)
            joint_e[core, half, 1, :, part] = u.astype(bf16).reshape(shape)
            low = silu_gate(g, u).astype(bf16)
            hidden_e[core, half, :, part] = low.reshape(shape)
            new = dot(low, w2[half].reshape(FF_DEV, D))
            total = new if total is None else total + new
        return total

    trip.here(0)
    ground.at(33)
    back = SlotReturn(net, prod_out, prod_in, prod_own, back_out, yields)
    back.other(0, expert(1 - net.core, 0))
    trip.hand_on(1)
    near_sum.wait_recv()
    away_out[...] = (away_out[...].astype(f32) + near_in[1].astype(f32)).astype(bf16)
    away_sum = net.copy(away_out, away_in, seq=net.seq(2))
    ground.at(34)
    back.mine(0, expert(net.core, 0))
    ground.at(35)
    trip.here(1)
    back.other(1, expert(1 - net.core, 1))
    back.mine(1, expert(net.core, 1))
    net.done(rows, joint_e, hidden_e)
    ground.at(36)
    away_sum.wait_recv()
    base = middle[...] + own_part + near_in[0].astype(f32) + away_in[...].astype(f32)
    back.wait()
    got = dot_tn(chosen[...], yields[...].reshape(SLOTS, D))
    gathered[...] = got.astype(bf16)
    result[...] = base + g0 * got[:t] + g1 * got[t:]
    for copy in [far, near, passed_far, near_sum, away_sum]:
        copy.wait_send()
    trip.close()
    back.close()


def layer_forward_kernel(layer, places, net, ground, h, cosine, sine, onehot, chosen, *refs):
    if layer == 0:
        small, *refs = refs
        w_qkv, w_out = ground.made[1][1]
    else:
        small, w_qkv, w_out, *refs = refs
    attn, ffn = refs[:8] + refs[17:21], refs[8:17] + refs[21:]
    attn_forward_part(layer, net, ground, h, cosine, sine, small, w_qkv, w_out, attn)
    jobs = [ground.made[i][0] for i in places]
    ffn_forward_part(layer, net, ground, attn[1], attn[0], small, onehot, chosen, jobs, ffn)
    ground.drain()


def layer_forward(layer, h, tables, onehot, chosen, small, weights, jobs, shards, cid):
    t = h.shape[0]
    head = (HEADS_DEV, SEQ, t, HEAD_DIM)
    slots = (EXPERTS, CAP, FF_DEV)
    sums = [((2, t, D), bf16), ((2, t, D), bf16), ((t, D), bf16), ((t, D), bf16)]
    names = [job.__name__ for job, *_ in jobs]
    places = (names.index("SharedFetch"), names.index("JoinNext" if layer else "JoinFirst"))
    return call(
        functools.partial(layer_forward_kernel, layer, places),
        [h, *tables, onehot, chosen] + ([small, *weights] if layer else []),
        ([] if layer else [((16, D), f32)])
        + [
            ((t, D), f32), ((t, D), bf16), ((SEQ, t, D), bf16, 1), (head, bf16, 1), (head, bf16, 1),
            (head, bf16, 1), (head, f32, 1), ((HEADS_DEV, SEQ, t, 128), f32, 1),
        ]
        + [
            ((t, D), f32), ((t, 128), f32), ((2 * t, D), bf16), ((SEQ, t, D), bf16, 1),
            ((2, SEQ, t, FF_DEV), bf16, 1), ((SEQ, t, FF_DEV), bf16, 1),
            ((2, EXPERTS, CAP, D), bf16, 1), ((2, 2, 2, *slots), bf16, 1), ((2, 2, *slots), bf16, 1),
        ],
        sums
        + [
            ((EXPERTS, CAP, D), bf16), ((EXPERTS, CAP, D), bf16), ((EXPERTS, CAP, D), bf16),
            ((EXPERTS * CHUNKS[0][1], D), f32), ((EXPERTS, CAP, D), bf16),
            ((EXPERTS, CAP, D), bf16),
        ]
        + sums
        + [((2, 4, 4, 48, FF_DEV), bf16), ((4, 128, D), bf16), ((8, D), f32)],
        jobs, shards, cid,
    )


def norm_back(x, gain, gradient):
    factor = rms_rows(x)
    weighted = gradient * gain
    inner = jnp.mean(weighted * x, -1, keepdims=True)
    d_x = factor * weighted - x * (factor * factor * factor) * inner
    return d_x, jnp.sum(gradient * x * factor, 0, keepdims=True)


def gate_back(g, u, gradient):
    sig = 1.0 / (1.0 + jnp.exp(-g))
    d_g = gradient * u * sig * (1.0 + g * (1.0 - sig))
    return d_g.astype(bf16), (gradient * g * sig).astype(bf16)


def ffn_backward_kernel(
    net, ground, grad, gates, onehot, chosen, gathered, middle, second, gains, router, every,
    joint, hidden, rows, joint_e, hidden_e, w_in, w_so, w1, w2,
    d_middle, small, d_w1, d_w2,
    every_g, d_joint, rows_out, d_rows, d_joint_e, prod_out, prod_in, prod_own, back_out, back_in,
    near_out, near_in, away_out, away_in, d_w_in, d_w_so,
):
    t = grad.shape[0]
    net.greet(net.everyone())
    g0, g1 = gates[:, 0:1], gates[:, 1:2]
    up = grad[...].astype(f32)
    pairs = jnp.concatenate([(up * g0).astype(bf16), (up * g1).astype(bf16)], 0)
    rows_out[...] = dot(chosen[...], pairs).astype(bf16).reshape(EXPERTS, CAP, D)
    every_g[net.s] = up.astype(bf16)
    net.met()
    trip = SlotTrip(net, rows_out, d_rows)
    far = net.copy(every_g.at[net.s], every_g.at[net.s], seq=net.seq(2))
    near = net.copy(every_g.at[net.s], every_g.at[net.s], seq=net.seq(1))
    ground.at(0)
    net.need(w_so, joint, w_in)

    def shared(b):
        d_hidden = dot_nt(every_g[b], w_so[...])
        d_g, d_u = gate_back(joint[0, b].astype(f32), joint[1, b].astype(f32), d_hidden)
        d_joint[0, b] = d_g
        d_joint[1, b] = d_u
        return dot_nt(d_g, w_in[0]) + dot_nt(d_u, w_in[1])

    local = shared(net.s)
    ground.at(1)
    near.wait_recv()
    near_out[0] = shared(net.seq(1)).astype(bf16)
    far.wait_recv()
    passed_far = net.copy(every_g.at[net.seq(2)], every_g.at[net.seq(2)], seq=net.seq(1))
    away_out[...] = shared(net.seq(2)).astype(bf16)
    trip.hand_on(0)
    ground.at(2)
    passed_far.wait_recv()
    near_out[1] = shared(net.seq(3)).astype(bf16)
    near_sum = net.copy(near_out, near_in, seq=net.seq(1))
    net.need(every, hidden)
    tokens = every[...].reshape(SEQ * t, D)
    for gu in (0, 1):
        d_w = dot_tn(tokens, d_joint[gu].reshape(SEQ * t, FF_DEV))
        d_w_in[gu] = d_w.astype(bf16).reshape(4, 4, 48, FF_DEV)
    d_w = dot_tn(hidden[...].reshape(SEQ * t, FF_DEV), every_g[...].reshape(SEQ * t, D))
    d_w_so[...] = d_w.astype(bf16).reshape(4, 128, D)
    net.need(w2, w1, joint_e)

    def expert(core, c):
        at, size = CHUNKS[c]
        part = slice(at, at + size)
        x = d_rows[core, :, part].reshape(EXPERTS * size, D)
        out = None
        for half in (0, 1):
            d_hidden = dot_nt(x, w2[half].reshape(FF_DEV, D))
            flat, shape = (EXPERTS * size, FF_DEV), (EXPERTS, size, FF_DEV)
            g = joint_e[core, half, 0, :, part].astype(f32).reshape(flat)
            u = joint_e[core, half, 1, :, part].astype(f32).reshape(flat)
            d_g, d_u = gate_back(g, u, d_hidden)
            d_joint_e[half, 0, core, :, part] = d_g.reshape(shape)
            d_joint_e[half, 1, core, :, part] = d_u.reshape(shape)
            new = dot_nt(d_g, w1[half, 0].reshape(D, FF_DEV))
            new = new + dot_nt(d_u, w1[half, 1].reshape(D, FF_DEV))
            out = new if out is None else out + new
        return out

    trip.here(0)
    ground.at(3)
    back = SlotReturn(net, prod_out, prod_in, prod_own, back_out, back_in)
    back.other(0, expert(1 - net.core, 0))
    trip.hand_on(1)
    near_sum.wait_recv()
    away_out[...] = (away_out[...].astype(f32) + near_in[1].astype(f32)).astype(bf16)
    away_sum = net.copy(away_out, away_in, seq=net.seq(2))
    ground.at(4)
    back.mine(0, expert(net.core, 0))
    ground.at(5)
    trip.here(1)
    back.other(1, expert(1 - net.core, 1))
    back.mine(1, expert(net.core, 1))
    ground.at(6)
    net.need(rows, hidden_e)
    for half in (0, 1):
        d_rows_all = d_rows[...].reshape(2 * SLOTS, D)
        for gu in (0, 1):
            d_w = dot_tn(
                rows[...].reshape(2 * SLOTS, D), d_joint_e[half, gu].reshape(2 * SLOTS, FF_DEV)
            )
            d_w1[half, gu] = d_w.astype(bf16).reshape(4, 4, 48, FF_DEV)
        low = jnp.concatenate(
            [hidden_e[core, half].reshape(SLOTS, FF_DEV) for core in (0, 1)], 0
        )
        d_w2[half] = dot_tn(low, d_rows_all).astype(bf16).reshape(4, 128, D)
        ground.at(7 + half)
    net.done(d_w1, d_w2)
    net.need(gathered, onehot, second, router, middle)
    d0 = jnp.sum(up * gathered[:t].astype(f32), -1, keepdims=True)
    d1 = jnp.sum(up * gathered[t:].astype(f32), -1, keepdims=True)
    mean = g0 * d0 + g1 * d1
    d_logits = (g0 * (d0 - mean) * onehot[0] + g1 * (d1 - mean) * onehot[1]).astype(bf16)
    small[8:16, :] = dot_tn(d_logits, second[...])[:8]
    local = local + dot_nt(d_logits, router[...])
    away_sum.wait_recv()
    local = local + near_in[0].astype(f32) + away_in[...].astype(f32)
    back.wait()
    picked = chosen[:, :t] + chosen[:, t:]
    d_normed = local + dot_tn(picked, back_in[...].reshape(SLOTS, D))
    d_x, d_gain = norm_back(middle[...], gains[1:2, :], d_normed)
    d_middle[...] = up + d_x
    small[0:8, :] = jnp.broadcast_to(d_gain, (8, D))
    for copy in [far, near, passed_far, near_sum, away_sum]:
        copy.wait_send()
    trip.close()
    back.close()
    ground.drain()


def ffn_backward(grad, saved, gains, router, weights, jobs, shards, cid):
    t = grad.shape[0]
    gates, onehot, chosen, gathered, middle, second, every, joint, hidden, rows, joint_e, hidden_e = saved
    w_in, w_so, w1, w2 = weights
    slots = (EXPERTS, CAP, D)
    late = {}
    for name, x in (
        ("w_so", w_so), ("joint", joint), ("w_in", w_in), ("every", every), ("hidden", hidden),
        ("w2", w2), ("joint_e", joint_e), ("w1", w1), ("rows", rows), ("hidden_e", hidden_e),
        ("gathered", gathered), ("onehot", onehot), ("second", second), ("router", router),
        ("middle", middle),
    ):
        late[name] = Late(x)
    return call(
        ffn_backward_kernel,
        [
            grad, gates, late["onehot"], chosen, late["gathered"], late["middle"], late["second"],
            gains, late["router"], late["every"], late["joint"], late["hidden"], late["rows"],
            late["joint_e"], late["hidden_e"], late["w_in"], late["w_so"], late["w1"], late["w2"],
        ],
        [
            ((t, D), f32), ((16, D), f32), ((2, 2, 4, 4, 48, FF_DEV), bf16, 1),
            ((2, 4, 128, D), bf16, 1),
        ],
        [
            ((SEQ, t, D), bf16), ((2, SEQ, t, FF_DEV), bf16), (slots, bf16), ((2, *slots), bf16),
            ((2, 2, 2, EXPERTS, CAP, FF_DEV), bf16), (slots, bf16), (slots, bf16),
            ((EXPERTS * CHUNKS[0][1], D), f32), (slots, bf16), (slots, bf16), ((2, t, D), bf16),
            ((2, t, D), bf16), ((t, D), bf16), ((t, D), bf16), ((2, 4, 4, 48, FF_DEV), bf16),
            ((4, 128, D), bf16),
        ],
        jobs, shards, cid,
    )


def attn_backward_kernel(
    net, ground, d_middle, h, gains, every, queries, keys, values, attended, totals, w_qkv, w_out,
    cosine, sine,
    grad, d_gain, d_w_qkv, d_w_out,
    every_m, d_att, d_q, d_k, d_v, d_joint, near_out, near_in, away_out, away_in,
):
    t = h.shape[0]
    net.greet(net.everyone())
    up = d_middle[...]
    every_m[net.s] = up.astype(bf16)
    net.met()
    far = net.copy(every_m.at[net.s], every_m.at[net.s], seq=net.seq(2))
    near = net.copy(every_m.at[net.s], every_m.at[net.s], seq=net.seq(1))
    ground.at(0)

    net.need(w_out)

    def project(b):
        d = dot_nt(every_m[b], w_out[...].reshape(COLS, D)).astype(bf16)
        for i in range(HEADS_DEV):
            d_att[i, b] = d[:, i * HEAD_DIM : (i + 1) * HEAD_DIM]

    project(net.s)
    near.wait_recv()
    project(net.seq(1))
    far.wait_recv()
    passed = net.copy(every_m.at[net.seq(2)], every_m.at[net.seq(2)], seq=net.seq(1))
    project(net.seq(2))
    passed.wait_recv()
    project(net.seq(3))
    ground.at(1)
    net.need(attended)
    tokens = every_m[...].reshape(SEQ * t, D)
    low = jnp.concatenate(
        [attended[i].reshape(SEQ * t, HEAD_DIM).astype(bf16) for i in range(HEADS_DEV)], 1
    )
    d_w_out[...] = dot_tn(low, tokens).astype(bf16).reshape(SEQ, 48, D)
    scale = HEAD_DIM**-0.5
    net.need(queries, keys, values, totals)

    def head(i):
        d_k[i] = jnp.zeros_like(d_k[i])
        d_v[i] = jnp.zeros_like(d_v[i])
        for b in range(SEQ):
            size = (b + 1) * t
            q, d = queries[i, b], d_att[i, b]
            k = keys[i, : b + 1].reshape(size, HEAD_DIM)
            v = values[i, : b + 1].reshape(size, HEAD_DIM)
            delta = jnp.sum(d.astype(f32) * attended[i, b], -1, keepdims=True)
            row = lax.broadcasted_iota(jnp.int32, (t, size), 0) + b * t
            col = lax.broadcasted_iota(jnp.int32, (t, size), 1)
            scores = jnp.where(row >= col, dot_nt(q, k) * scale, MASKED)
            weights = jnp.exp(scores - totals[i, b][:, 0:1])
            d_scores = (weights * (dot_nt(d, v) - delta)).astype(bf16)
            d_q[i, b] = dot(d_scores, k) * scale
            shape = (b + 1, t, HEAD_DIM)
            d_k[i, : b + 1] += (dot_tn(d_scores, q) * scale).reshape(shape)
            d_v[i, : b + 1] += dot_tn(weights.astype(bf16), d).reshape(shape)

    for i in range(HEADS_DEV):
        head(i)
        ground.at(2 + i)

    net.need(cosine, sine, w_qkv)

    def part(b):
        c, sn = cosine[b], -sine[b]
        pieces = [turn(d_q[i, b], c, sn) for i in range(HEADS_DEV)]
        pieces += [turn(d_k[i, b], c, sn) for i in range(HEADS_DEV)]
        pieces += [d_v[i, b] for i in range(HEADS_DEV)]
        d = jnp.concatenate(pieces, 1).astype(bf16)
        d_joint[b] = d
        return dot_nt(d, w_qkv[...].reshape(D, 3 * COLS))

    near_out[0] = part(net.seq(1)).astype(bf16)
    near_out[1] = part(net.seq(3)).astype(bf16)
    near_sum = net.copy(near_out, near_in, seq=net.seq(1))
    away = part(net.seq(2))
    own = part(net.s)
    near_sum.wait_recv()
    away_out[...] = (away + near_in[1].astype(f32)).astype(bf16)
    away_sum = net.copy(away_out, away_in, seq=net.seq(2))
    own = own + near_in[0].astype(f32)
    ground.at(5)
    net.need(every)
    d_w = dot_tn(every[...].reshape(SEQ * t, D), d_joint[...].reshape(SEQ * t, 3 * COLS))
    d_w_qkv[...] = d_w.astype(bf16).reshape(4, 4, 48, 3 * COLS)
    ground.at(6)
    away_sum.wait_recv()
    net.need(h)
    d_x, gain = norm_back(h[...].astype(f32), gains[0:1, :], own + away_in[...].astype(f32))
    grad[...] = up + d_x
    row = lax.broadcasted_iota(jnp.int32, (8, D), 0)
    d_gain[...] = jnp.where(row == 0, gain, 0.0)
    ground.at(7)
    for copy in (far, near, passed, near_sum, away_sum):
        copy.wait_send()
    ground.drain()


def attn_backward(d_middle, saved, gains, weights, tables, jobs, shards, cid):
    t = d_middle.shape[0]
    h, every, queries, keys, values, attended, totals = saved
    head = (HEADS_DEV, SEQ, t, HEAD_DIM)
    return call(
        attn_backward_kernel,
        [d_middle, Late(h), gains]
        + [Late(x) for x in (every, queries, keys, values, attended, totals, *weights, *tables)],
        [((t, D), f32), ((8, D), f32), ((4, 4, 48, 3 * COLS), bf16), ((4, 48, D), bf16)],
        [
            ((SEQ, t, D), bf16), (head, bf16), (head, f32), (head, f32), (head, f32),
            ((SEQ, t, 3 * COLS), bf16), ((2, t, D), bf16), ((2, t, D), bf16), ((t, D), bf16),
            ((t, D), bf16),
        ],
        jobs, shards, cid,
    )


FORWARD_FIRST = (
    (SmallFetch, 0, (-2, -1, 0)),
    (AttnFetchHere, 0, (-2, -1, 2, 3)),
    (ExpertFetch, 0, (-2, 3, 30)),
    (SharedFetch, 0, (1, 3, 7, 30)),
    (JoinFirst, 0, (30, 33, 39)),
    (ExpertPlane, 1, (8, 40)),
    (AttnFetch, 1, (30, 33, 36, 40)),
)
FORWARD_NEXT = (
    (ExpertNear, 1, (2, 30)),
    (SharedFetch, 1, (0, 1, 4, 30)),
    (JoinNext, 1, (30, 33, 39)),
)
BACKWARD_FFN_FIRST = ((SharedAcross, 1, (3, 9)),)
BACKWARD_ATTN = (
    (GateToPlane, 1, (0, 3, 5, 9)),
    (UpToPlane, 1, (0, 3, 5, 9)),
    (SecondToPlane, 1, (0, 4, 6, 9)),
    (SharedReturn, 1, (0, 4, 5, 9)),
)
BACKWARD_FFN = (
    (SharedAcross, 0, (3, 9)),
    (AttnReturn, 1, (0, 3, 6, 8, 9)),
    (GateFinal, 1, (0, 9)),
    (UpFinal, 1, (0, 9)),
    (SecondFinal, 1, (0, 9)),
)
BACKWARD_ATTN_LAST = (
    (GateReturn, 0, (0, 3, 5, 9, 11)),
    (UpReturn, 0, (0, 3, 5, 9, 11)),
    (SharedReturn, 0, (0, 4, 5, 11)),
    (SecondReturn, 0, (0, 4, 6, 9, 11)),
    (AttnReturnHere, 0, (6, 9, 10, 11, 12)),
    (SmallReturnHere, 0, (7, 8, 9, 10)),
)


def local(
    reps, inputs, expert_choice, pair_order, norm_gains, attn_qkv, attn_out, router, shared_in,
    shared_out, expert_in, expert_out, cotangent,
):
    r, s, z = lax.axis_index("rep"), lax.axis_index("seq"), lax.axis_index("fsdp")
    tokens = inputs.shape[1]
    half = HEAD_DIM // 2
    inverse = np.exp(-np.log(np.float32(10000.0)) * np.arange(half, dtype=np.float32) * np.float32(2.0 / HEAD_DIM))
    angle = np.arange(SEQ * tokens, dtype=np.float32)[:, None] * inverse.astype(np.float32)[None, :]
    cosine, sine = np.cos(angle.astype(np.float64)), np.sin(angle.astype(np.float64))
    shape = (SEQ, tokens, HEAD_DIM)
    table_cos = jnp.asarray(np.concatenate([cosine, cosine], -1).reshape(shape), f32)
    table_sin = jnp.asarray(np.concatenate([-sine, sine], -1).reshape(shape), f32)
    small = jnp.concatenate([norm_gains, router.transpose(0, 2, 1)], 1).reshape(12, 48)
    shards = {
        "small": jnp.pad(small, ((0, 4), (0, 80))),
        "attn_qkv": attn_qkv.reshape(LAYERS, 48, 3, SEQ, COLS)
        .transpose(0, 3, 1, 2, 4)
        .reshape(LAYERS, SEQ, 48, 3 * COLS),
        "attn_out": attn_out,
        "shared_in": shared_in,
        "shared_out": shared_out,
        "expert_in": expert_in,
        "expert_out": expert_out,
    }
    h = inputs[0]
    kept_layers = []
    tables = (table_cos, table_sin)
    attn, gains, small = (), [None] * LAYERS, None
    for layer in range(LAYERS):
        first = layer == 0
        routes = routing(expert_choice[layer, 0], pair_order[layer, 0, 0])
        onehot = expert_choice[layer, 0].T[..., None] == jnp.arange(128, dtype=jnp.int32)
        onehot = onehot.astype(f32)
        outs, fetched = layer_forward(
            layer, h, tables, onehot, routes[1], small, attn, FORWARD_FIRST if first else FORWARD_NEXT,
            shards, 12 + layer,
        )
        if first:
            small, *outs = outs
            spread_small = small[:12].reshape(LAYERS, 6, D)
            gains, routers = spread_small[:, :2], spread_small[:, 2:].astype(bf16)
            attn, shared, w1, w2 = fetched[1:3], fetched[9:11], fetched[11], fetched[12]
            shards["next_p1"], shards["next_p2"] = fetched[13:15]
            next_attn = fetched[15:17]
        else:
            shared, w1, w2 = fetched[4:6], fetched[6], fetched[7]
        middle, second, every_one, queries, keys, values, attended, totals = outs[:8]
        result, gates, gathered, every_two, joint, hidden, rows, joint_e, hidden_e = outs[8:]
        w_in, w_so = shared[0].reshape(2, D, FF_DEV), shared[1].reshape(FF_DEV, D)
        router_pad = jnp.pad(routers[layer].T, ((0, 0), (0, 124)))
        attn_weights, ffn_weights = attn, (w_in, w_so, w1, w2)
        if first:
            attn = next_attn
        attn_saved = (h, every_one, queries, keys, values, attended, totals)
        ffn_saved = (
            gates, onehot, routes[1], gathered, middle, second, every_two, joint, hidden, rows,
            joint_e, hidden_e,
        )
        h = result
        kept_layers.append((attn_weights, ffn_weights, attn_saved, ffn_saved, router_pad))
    output = h.astype(bf16)[None]
    grad = cotangent[0]
    returned = {}
    grads = {}
    for layer in reversed(range(LAYERS)):
        last = layer == 0
        attn_weights, ffn_weights, attn_saved, ffn_saved, router_pad = kept_layers[layer]
        (d_middle, small, grads["d_w1"], grads["d_w2"]), done = ffn_backward(
            grad, ffn_saved, gains[layer], router_pad, ffn_weights,
            BACKWARD_FFN if last else BACKWARD_FFN_FIRST, grads, 18 + layer,
        )
        grads["r1"], grads["r2"] = done[:2]
        if last:
            returned["d_attn", 1], returned["d_expert", 1] = done[2:4], done[4:]
        grads[f"small_{layer}"] = small
        (grad, d_gain, d_w_qkv, d_w_out), done = attn_backward(
            d_middle, attn_saved, gains[layer], attn_weights, tables,
            BACKWARD_ATTN_LAST if last else BACKWARD_ATTN, grads, 16 + layer,
        )
        if last:
            returned["d_expert", 0], returned["d_shared", 0] = [*done[:2], done[4]], done[2:4]
            returned["d_attn", 0], total_small = done[5:7], done[7]
        else:
            grads["q_gate"], grads["q_up"], grads["q_second"] = done[:3]
            returned["d_shared", 1] = done[3:]
            grads["d_w_qkv"], grads["d_w_out"], grads["gain_1"] = d_w_qkv, d_w_out, d_gain
    total_small = rep_rest(total_small, reps)[:12].reshape(LAYERS, 6, D)
    total_small = lax.dynamic_slice_in_dim(total_small, (s * FSDP + z) * 48, 48, 2)

    def stack(name, k):
        return jnp.stack([rep_rest(returned[name, i][k], reps) for i in range(LAYERS)]).astype(f32)

    d_qkv = stack("d_attn", 0).reshape(LAYERS, SEQ, 48, 3, COLS).transpose(0, 2, 3, 1, 4)
    return (
        output, grad[None], total_small[:, :2], d_qkv.reshape(LAYERS, 48, 3 * D),
        stack("d_attn", 1), total_small[:, 2:].transpose(0, 2, 1), stack("d_shared", 0),
        stack("d_shared", 1), jnp.concatenate([stack("d_expert", 0), stack("d_expert", 1)], -1),
        stack("d_expert", 2),
    )


def solution(mesh):
    tokens = P(("rep", "fsdp"), "seq", None)
    routes = P(None, ("rep", "fsdp"), "seq", None)
    gains = P(None, None, ("seq", "fsdp"))
    dense = P(None, ("seq", "fsdp"), None)
    expert = P(None, None, ("seq", "fsdp"), None)
    in_specs = (
        tokens, routes, routes, gains, dense, dense, dense, dense, dense, expert, expert, tokens,
    )
    out_specs = (tokens, tokens, gains, dense, dense, dense, dense, dense, expert, expert)
    return jax.shard_map(
        functools.partial(local, mesh.shape["rep"]),
        mesh=mesh, in_specs=in_specs, out_specs=out_specs, check_vma=False,
    )
```

```python
import functools

import jax
import jax.numpy as jnp
import numpy as np
from jax import lax
from jax.experimental import pallas as pl
from jax.experimental.pallas import tpu as pltpu
from jax.sharding import PartitionSpec as P

D = 768
HEADS = 12
HEAD_DIM = 64
FF = 2048
EXPERTS = 4
LAYERS = 2
CAP = 144
EPS = 1e-06
MASKED = -1e30
SEQ = 4
FSDP = 4
HEADS_DEV = HEADS // SEQ
COLS = HEADS_DEV * HEAD_DIM
FF_DEV = FF // SEQ
FF_CORE = FF // 2
SLOTS = EXPERTS * CAP
bf16 = jnp.bfloat16
f32 = jnp.float32
MESH = pl.DeviceIdType.MESH


def dot(a, b):
    return jnp.dot(a, b, preferred_element_type=f32)


def dot_nt(a, b):
    return lax.dot_general(a, b, (((1,), (1,)), ((), ())), preferred_element_type=f32)


def dot_tn(a, b):
    return lax.dot_general(a, b, (((0,), (0,)), ((), ())), preferred_element_type=f32)


def rep_rest(x, reps):
    bit = 2
    while bit < reps:
        x = x + lax.ppermute(x, "rep", [(i, i ^ bit) for i in range(reps)])
        bit *= 2
    return x


def routing(choices, order):
    tokens = choices.shape[0]
    pairs = 2 * tokens
    flat = choices.reshape(-1)
    ids = jnp.arange(pairs, dtype=jnp.int32)
    place = (order[:, None] == ids[None, :]).astype(bf16)
    experts = (flat[:, None] == jnp.arange(EXPERTS, dtype=jnp.int32)[None, :]).astype(bf16)
    placed = dot(place, experts).astype(bf16)
    lower = (ids[:, None] > ids[None, :]).astype(bf16)
    slot_placed = jnp.minimum(jnp.sum(dot(lower, placed) * placed.astype(f32), 1), float(CAP))
    slot = dot_tn(place, slot_placed[:, None].astype(bf16))[:, 0].astype(jnp.int32)
    kept = slot < CAP
    target = jnp.where(kept, flat * CAP + slot, SLOTS).reshape(tokens, 2)
    target = target.T.reshape(-1)
    chosen = (target[None, :] == jnp.arange(SLOTS, dtype=jnp.int32)[:, None]).astype(bf16)
    return kept.reshape(tokens, 2).astype(f32), chosen


class Net:
    def __init__(self, send, recv, local_sems):
        self.send, self.recv, self.local_sems = send, recv, local_sems
        self.count = 0
        self.local_count = 0
        self.r, self.s, self.z = (lax.axis_index(a) for a in ("rep", "seq", "fsdp"))
        self.half = lax.rem(self.r, 2)
        self.core = lax.rem(self.s, 2)
        self.far = self.s // 2
        self.partner = self.r + 1 - 2 * self.half

    def seq(self, d):
        core = self.core if d % 2 == 0 else 1 - self.core
        far = self.far if d < 2 else 1 - self.far
        return far * 2 + core

    def plane(self, k):
        return lax.rem(self.z + k, FSDP)

    def copy(self, src, dst, **device):
        k = self.count
        self.count += 1
        out = pltpu.make_async_remote_copy(
            src_ref=src, dst_ref=dst, send_sem=self.send.at[k], recv_sem=self.recv.at[k],
            device_id=device, device_id_type=MESH,
        )
        out.start()
        return out

    def move(self, src, dst):
        k = self.local_count
        self.local_count += 1
        out = pltpu.make_async_copy(src, dst, self.local_sems.at[k])
        out.start()
        return out

    def need(self, *refs):
        for ref in refs:
            self.coming.pop(id(ref)).wait()

    def done(self, *refs):
        for ref in refs:
            self.going.append(self.move(ref, self.there.pop(id(ref))))

    def greet(self, devices):
        self.barrier = pltpu.get_barrier_semaphore()
        for device in devices:
            pl.semaphore_signal(self.barrier, inc=1, device_id=device, device_id_type=MESH)
        self.greeted = len(devices)

    def met(self):
        pl.semaphore_wait(self.barrier, self.greeted)

    def everyone(self):
        seqs = [{"seq": self.seq(d)} for d in (1, 2, 3)]
        planes = [{"fsdp": self.plane(k)} for k in (1, 2, 3)]
        both = [{"seq": self.seq(1), "fsdp": self.plane(k)} for k in (1, 2, 3)]
        return seqs + planes + both + [{"rep": self.partner}]


def columns(start, size):
    return pl.ds(pl.multiple_of(start, 128), size)


def wait_all(copies):
    for copy in copies:
        copy.wait()


class Job:
    space = pl.ANY
    out_space = pl.ANY
    scratch = ()
    kind = bf16

    def __init__(self, net, layer, ins, outs, scratch):
        self.net, self.layer = net, layer
        self.bind(ins, outs, scratch)


class ExpertPlane(Job):
    inputs = ("expert_in", "expert_out")
    shapes = ((2, 2, 4, 48, FF_DEV), (4, 128, 384))

    def bind(self, ins, outs, scratch):
        self.first, self.second = ins
        self.p1, self.p2 = outs

    def stages(self):
        return [self.plane_begin, self.plane_finish]

    def plane_begin(self):
        n = self.net
        self.copies = []
        for k in (2, 1, 3, 0):
            e = n.plane(k)
            for d in (0, 1):
                core = n.core if d == 0 else 1 - n.core
                for gu in (0, 1):
                    src = self.first.at[
                        self.layer, e, :, columns(gu * FF + n.half * FF_CORE + core * FF_DEV, FF_DEV)
                    ]
                    dst = self.p1.at[gu, n.core, n.z]
                    if k == 0 and d == 0:
                        self.copies.append(n.move(src, dst))
                    else:
                        self.copies.append(n.copy(src, dst, seq=n.seq(d), fsdp=e))
            src = self.second.at[self.layer, e, :, columns(n.half * 384, 384)]
            dst = self.p2.at[n.z]
            self.copies.append(n.move(src, dst) if k == 0 else n.copy(src, dst, fsdp=e))

    def plane_finish(self):
        wait_all(self.copies)


class ExpertFetch(ExpertPlane):
    shapes = ExpertPlane.shapes + ((2, 2, 4, 48, FF_DEV), (2, 2, 4, 48, FF_DEV)) + (
        (4, 128, 384), (4, 128, 384),
    )

    def bind(self, ins, outs, scratch):
        ExpertPlane.bind(self, ins, outs[:2], ())
        self.ax, self.ay, self.bx, self.by = outs[2:]

    def stages(self):
        def turn_over():
            self.plane_finish()
            self.near_begin()

        return [self.plane_begin, turn_over, self.near_finish]

    def near_begin(self):
        n = self.net
        self.sides = [
            n.copy(self.p1, self.ax, rep=n.partner), n.copy(self.p1, self.ay, seq=n.seq(2)),
            n.copy(self.p2, self.bx, rep=n.partner), n.copy(self.p2, self.by, seq=n.seq(2)),
        ]

    def near_finish(self):
        wait_all(self.sides)


class ExpertNear(ExpertFetch):
    inputs = ("next_p1", "next_p2")
    shapes = ExpertFetch.shapes[2:]

    def bind(self, ins, outs, scratch):
        self.p1, self.p2 = ins
        self.ax, self.ay, self.bx, self.by = outs

    def stages(self):
        return [self.near_begin, self.near_finish]


class ExpertJoin(Job):
    inputs = ("p1", "p2", "ax", "ay", "bx", "by")
    shapes = ((2, 2, 4, 4, 48, FF_DEV), (2, 4, 128, D))
    scratch = shapes

    def bind(self, ins, outs, scratch):
        self.p1, self.p2, self.ax, self.ay, self.bx, self.by = ins
        self.outs = outs
        self.w1, self.w2 = scratch

    def stages(self):
        return [self.begin, self.finish, self.written]

    def begin(self):
        n = self.net
        here, there = pl.ds(2 * n.far, 2), pl.ds(2 * (1 - n.far), 2)
        mine, rest = columns(n.half * 384, 384), columns((1 - n.half) * 384, 384)
        low, high = pl.ds(0, 2), pl.ds(2, 2)
        w1, w2 = self.w1, self.w2
        self.copies = [
            n.copy(self.ay.at[0], w1.at[n.half, 0, there], rep=n.partner),
            n.copy(self.ax.at[1], w1.at[1 - n.half, 1, here], seq=n.seq(2)),
            n.copy(self.by.at[low], w2.at[1 - n.far, low, :, mine], rep=n.partner),
            n.copy(self.bx.at[high], w2.at[n.far, high, :, rest], seq=n.seq(2)),
            n.move(self.p1, w1.at[n.half, :, here]),
            n.move(self.ax, w1.at[1 - n.half, :, here]),
            n.move(self.ay, w1.at[n.half, :, there]),
            n.move(self.p2, w2.at[n.far, :, :, mine]),
            n.move(self.bx, w2.at[n.far, :, :, rest]),
            n.move(self.by, w2.at[1 - n.far, :, :, mine]),
        ]

    def finish(self):
        wait_all(self.copies)
        self.copies = [
            self.net.move(self.w1, self.outs[0]), self.net.move(self.w2, self.outs[1])
        ]

    def written(self):
        wait_all(self.copies)


class JoinFirst(ExpertJoin):
    inputs = ()
    linked = ((2, 0), (2, 1), (2, 2), (2, 3), (2, 4), (2, 5))


class JoinNext(ExpertJoin):
    inputs = ("next_p1", "next_p2")
    linked = ((0, 0), (0, 1), (0, 2), (0, 3))


class SharedFetch(Job):
    inputs = ("shared_in", "shared_out")
    shapes = ((2, 4, 4, 48, FF_DEV), (4, 128, D))

    def bind(self, ins, outs, scratch):
        self.first, self.second = ins
        self.w_in, self.w_out = outs

    def stages(self):
        return [self.begin, self.second_hop, self.third_hop, self.finish]

    def begin(self):
        n = self.net
        self.firsts = []
        for d in (3, 2, 1, 0):
            src = self.first.at[self.layer, :, columns(n.half * FF + n.seq(d) * FF_DEV, FF_DEV)]
            dst = self.w_in.at[n.half, n.s, n.z]
            self.firsts.append(n.move(src, dst) if d == 0 else n.copy(src, dst, seq=n.seq(d)))
        src = self.second.at[self.layer, :, columns(n.half * 384, 384)]
        self.firsts.append(n.move(src, self.w_out.at[n.z, :, columns(n.half * 384, 384)]))

    def second_hop(self):
        n = self.net
        wait_all(self.firsts)
        part, low = self.w_in.at[n.half, :, n.z], self.w_out.at[n.z, :, columns(n.half * 384, 384)]
        self.sent = {}
        for k in (2, 1, 3):
            self.sent[k] = [n.copy(part, part, fsdp=n.plane(k)), n.copy(low, low, fsdp=n.plane(k))]
        self.across = [n.copy(part, part, rep=n.partner), n.copy(low, low, rep=n.partner)]

    def third_hop(self):
        n = self.net
        for k in (1, 3, 2):
            wait_all(self.sent[k])
            z = n.plane(FSDP - k)
            for part in (self.w_in.at[n.half, :, z], self.w_out.at[z, :, columns(n.half * 384, 384)]):
                self.across.append(n.copy(part, part, rep=n.partner))

    def finish(self):
        wait_all(self.across)


class AttnFetch(Job):
    inputs = ("attn_qkv", "attn_out")
    shapes = ((4, 4, 48, 3 * COLS), (4, 48, D))

    def bind(self, ins, outs, scratch):
        self.qkv, self.out = ins
        self.w_qkv, self.w_out = outs

    def stages(self):
        return [self.begin, self.second_hop, self.third_hop, self.finish]

    def begin(self):
        n = self.net
        self.firsts, self.seconds = [], []
        for d in (3, 2, 1, 0):
            src, dst = self.qkv.at[self.layer, n.seq(d)], self.w_qkv.at[n.s, n.z]
            self.firsts.append(n.move(src, dst) if d == 0 else n.copy(src, dst, seq=n.seq(d)))
        for k in (2, 1, 3, 0):
            src = self.out.at[self.layer, :, columns(n.half * 384, 384)]
            dst = self.w_out.at[n.z, :, columns(n.half * 384, 384)]
            self.seconds.append(n.move(src, dst) if k == 0 else n.copy(src, dst, fsdp=n.plane(k)))

    def second_hop(self):
        n = self.net
        wait_all(self.firsts)
        part = self.w_qkv.at[pl.ds(2 * n.half, 2), n.z]
        self.firsts = [n.copy(part, part, fsdp=n.plane(k)) for k in (2, 1, 3)]
        wait_all(self.seconds)
        part = self.w_out.at[:, :, columns(n.half * 384, 384)]
        self.across = [n.copy(part, part, rep=n.partner)]

    def third_hop(self):
        n = self.net
        for copy, k in zip(self.firsts[1:] + self.firsts[:1], (1, 3, 2)):
            copy.wait()
            part = self.w_qkv.at[pl.ds(2 * n.half, 2), n.plane(FSDP - k)]
            self.across.append(n.copy(part, part, rep=n.partner))

    def finish(self):
        wait_all(self.across)


class AttnFetchHere(AttnFetch):
    out_space = pltpu.VMEM


class SmallFetch(Job):
    out_space = pltpu.VMEM

    inputs = ("small",)
    shapes = ((4, 4, 16, 128),)

    def bind(self, ins, outs, scratch):
        (self.src,), (self.dst,) = ins, outs

    def stages(self):
        return [self.begin, self.second_hop, self.finish]

    def begin(self):
        n = self.net
        dst = self.dst.at[n.s, n.z]
        self.copies = [n.copy(self.src, dst, seq=n.seq(d)) for d in (3, 2, 1)]
        self.copies.append(n.move(self.src, dst))

    def second_hop(self):
        n = self.net
        wait_all(self.copies)
        part = self.dst.at[:, n.z]
        self.copies = [n.copy(part, part, fsdp=n.plane(k)) for k in (2, 1, 3)]

    def finish(self):
        wait_all(self.copies)


def total(*parts):
    out = parts[0].astype(f32)
    for part in parts[1:]:
        out = out + part.astype(f32)
    return out.astype(bf16)


class FirstSides(Job):
    inputs = ("d_w1",)
    out_space = pltpu.VMEM
    shapes = ((2, 4, 48, FF_DEV),)
    scratch = ((2, 2, 4, 48, FF_DEV), (2, 2, 4, 48, FF_DEV))

    def bind(self, ins, outs, scratch):
        (self.d,), (self.q,) = ins, outs
        self.own, self.got = scratch

    def stages(self):
        return [self.sides_begin, self.sides_second, self.sides_finish]

    def sides_begin(self):
        n = self.net
        if self.gu == 0:
            src = [self.d.at[1 - n.half, 0, pl.ds(2 * f, 2)] for f in (0, 1)]
            kept = [self.d.at[n.half, 0, pl.ds(2 * f, 2)] for f in (0, 1)]
            device = {"rep": n.partner}
        else:
            src = [self.d.at[h, 1, pl.ds(2 * (1 - n.far), 2)] for h in (0, 1)]
            kept = [self.d.at[h, 1, pl.ds(2 * n.far, 2)] for h in (0, 1)]
            device = {"seq": n.seq(2)}
        self.sent = [n.copy(src[i], self.got.at[i], **device) for i in (0, 1)]
        self.sent += [n.move(kept[i], self.own.at[i]) for i in (0, 1)]

    def sides_second(self):
        n = self.net
        wait_all(self.sent)
        stays = n.far if self.gu == 0 else n.half
        device = {"seq": n.seq(2)} if self.gu == 0 else {"rep": n.partner}
        goes = 1 - stays
        self.got[goes] = total(self.got[goes], self.own[goes])
        self.sent = [n.copy(self.got.at[goes], self.q, **device)]
        self.got[stays] = total(self.got[stays], self.own[stays])

    def sides_finish(self):
        n = self.net
        wait_all(self.sent)
        self.q[...] = total(self.q[...], self.got[n.far if self.gu == 0 else n.half])


class FirstPlane(Job):
    space = pltpu.VMEM
    shapes = ((EXPERTS, 48, FF),)
    half_only = False

    def bind(self, ins, outs, scratch):
        (self.q,), (self.o,) = ins, outs

    def stages(self):
        return [self.plane_begin, self.plane_second, self.plane_finish]

    def plane_begin(self):
        n = self.net
        self.sent = []
        at = n.core * FF_DEV if self.half_only else n.half * FF_CORE + n.core * FF_DEV
        dst = self.o.at[n.z, :, columns(at, FF_DEV)]
        for k in (2, 1, 3, 0):
            for d in (1, 0):
                core = n.core if d == 0 else 1 - n.core
                src = self.q.at[core, n.plane(k)]
                if k == 0 and d == 0:
                    self.sent.append(n.move(src, dst))
                else:
                    self.sent.append(n.copy(src, dst, seq=n.seq(d), fsdp=n.plane(k)))

    def plane_second(self):
        n = self.net
        wait_all(self.sent)
        part = self.o.at[:, :, columns(n.half * FF_CORE, FF_CORE)]
        self.sent = [n.copy(part, part, rep=n.partner)]

    def plane_finish(self):
        wait_all(self.sent)


class FirstReturn(FirstSides, FirstPlane):
    shapes = FirstPlane.shapes
    scratch = FirstSides.scratch + FirstSides.shapes
    space = pl.ANY
    out_space = pl.ANY

    def bind(self, ins, outs, scratch):
        FirstSides.bind(self, ins, scratch[2:], scratch[:2])
        FirstPlane.bind(self, scratch[2:], outs, ())

    def turn_over(self):
        self.sides_finish()
        self.plane_begin()

    def stages(self):
        return [
            self.sides_begin, self.sides_second, self.turn_over, self.plane_second,
            self.plane_finish,
        ]


class FirstToPlane(FirstReturn):
    shapes = ((EXPERTS, 48, FF_CORE),)
    half_only = True

    def stages(self):
        return [self.sides_begin, self.sides_second, self.turn_over, self.plane_finish]


class FirstFinal(Job):
    shapes = ((EXPERTS, 48, FF),)

    def bind(self, ins, outs, scratch):
        (self.q,), (self.o,) = ins, outs

    def stages(self):
        return [self.begin, self.finish]

    def begin(self):
        n = self.net
        part = self.o.at[:, :, columns(n.half * FF_CORE, FF_CORE)]
        self.sent = [n.copy(self.q, part, rep=n.partner), n.move(self.q, part)]

    def finish(self):
        wait_all(self.sent)


class GateReturn(FirstReturn):
    gu = 0


class UpReturn(FirstReturn):
    gu = 1


class GateToPlane(FirstToPlane):
    gu = 0


class UpToPlane(FirstToPlane):
    gu = 1


class GateFinal(FirstFinal):
    inputs = ("q_gate",)


class UpFinal(FirstFinal):
    inputs = ("q_up",)


class SecondReturn(Job):
    inputs = ("d_w2",)
    shapes = ((EXPERTS, 128, D),)
    scratch = ((2, 4, 128, 384), (2, 4, 128, 384), (4, 128, 384))
    rep_first = True

    def bind(self, ins, outs, scratch):
        (self.d,), (self.o,) = ins, outs
        self.own, self.got, self.q = scratch

    def stages(self):
        return [
            self.sides_begin, self.sides_second, self.turn_over, self.plane_second,
            self.plane_finish,
        ]

    def sides_begin(self):
        n = self.net
        halves = [columns(h * 384, 384) for h in (0, 1)]
        mine, rest = columns(n.half * 384, 384), columns((1 - n.half) * 384, 384)
        if self.rep_first:
            src = [self.d.at[f, :, :, rest] for f in (0, 1)]
            kept = [self.d.at[f, :, :, mine] for f in (0, 1)]
            device = {"rep": n.partner}
        else:
            src = [self.d.at[1 - n.far, :, :, h] for h in halves]
            kept = [self.d.at[n.far, :, :, h] for h in halves]
            device = {"seq": n.seq(2)}
        self.sent = [n.copy(src[i], self.got.at[i], **device) for i in (0, 1)]
        self.sent += [n.move(kept[i], self.own.at[i]) for i in (0, 1)]

    def sides_second(self):
        n = self.net
        wait_all(self.sent)
        self.stays = n.far if self.rep_first else n.half
        device = {"seq": n.seq(2)} if self.rep_first else {"rep": n.partner}
        goes = 1 - self.stays
        self.got[goes] = total(self.got[goes], self.own[goes])
        self.sent = [n.copy(self.got.at[goes], self.q, **device)]
        self.got[self.stays] = total(self.got[self.stays], self.own[self.stays])

    def target(self):
        return columns(self.net.half * 384, 384)

    def turn_over(self):
        n = self.net
        wait_all(self.sent)
        self.q[...] = total(self.q[...], self.got[self.stays])
        self.sent = []
        dst = self.o.at[n.z, :, self.target()]
        for k in (2, 1, 3, 0):
            src = self.q.at[n.plane(k)]
            self.sent.append(n.move(src, dst) if k == 0 else n.copy(src, dst, fsdp=n.plane(k)))

    def plane_second(self):
        n = self.net
        wait_all(self.sent)
        part = self.o.at[:, :, columns(n.half * 384, 384)]
        self.sent = [n.copy(part, part, rep=n.partner)]

    def plane_finish(self):
        wait_all(self.sent)


class SecondToPlane(SecondReturn):
    shapes = ((EXPERTS, 128, 384),)

    def stages(self):
        return [self.sides_begin, self.sides_second, self.turn_over, self.plane_finish]

    def target(self):
        return pl.ds(0, 384)


class SecondFinal(FirstFinal):
    inputs = ("q_second",)
    shapes = ((EXPERTS, 128, D),)

    def begin(self):
        n = self.net
        part = self.o.at[:, :, columns(n.half * 384, 384)]
        self.sent = [n.copy(self.q, part, rep=n.partner), n.move(self.q, part)]


class SharedAcross(Job):
    inputs = ()
    own = (-2, -1)
    out_space = pltpu.VMEM
    shapes = ((4, 4, 48, FF_DEV), (4, 128, 384))

    def bind(self, ins, outs, scratch):
        self.d1, self.d2 = ins
        self.r1, self.r2 = outs

    def stages(self):
        return [self.begin, self.finish]

    def begin(self):
        n = self.net
        part = self.d2.at[:, :, columns((1 - n.half) * 384, 384)]
        self.sent = [
            n.copy(self.d1.at[1 - n.half], self.r1, rep=n.partner),
            n.copy(part, self.r2, rep=n.partner),
        ]

    def finish(self):
        n = self.net
        wait_all(self.sent)
        self.r1[...] = total(self.r1[...], self.d1[n.half])
        self.r2[...] = total(self.r2[...], self.d2[:, :, columns(n.half * 384, 384)])


class SharedReturn(Job):
    space = pltpu.VMEM
    inputs = ("r1", "r2")
    shapes = ((48, 2 * FF), (128, D))
    scratch = ((3, 4, 48, FF_DEV), (4, 48, FF_DEV), (3, 128, 384), (128, 384))

    def bind(self, ins, outs, scratch):
        self.r1, self.r2 = ins
        self.o1, self.o2 = outs
        self.r1z, self.s1, self.r2z, self.s2 = scratch

    def stages(self):
        return [self.second_hop, self.third_hop, self.fourth_hop, self.finish]

    def second_hop(self):
        n = self.net
        self.firsts = [
            n.copy(self.r1.at[:, n.plane(k)], self.r1z.at[k - 1], fsdp=n.plane(k))
            for k in (2, 1, 3)
        ]
        self.seconds = [
            n.copy(self.r2.at[n.plane(k)], self.r2z.at[k - 1], fsdp=n.plane(k)) for k in (2, 1, 3)
        ]

    def third_hop(self):
        n = self.net
        wait_all(self.firsts + self.seconds)
        self.s1[...] = total(self.r1[:, n.z], self.r1z[0], self.r1z[1], self.r1z[2])
        self.firsts = []
        for d in (3, 2, 1, 0):
            src = self.s1.at[n.seq(d)]
            dst = self.o1.at[:, columns(n.half * FF + n.s * FF_DEV, FF_DEV)]
            self.firsts.append(n.move(src, dst) if d == 0 else n.copy(src, dst, seq=n.seq(d)))
        self.s2[...] = total(self.r2[n.z], self.r2z[0], self.r2z[1], self.r2z[2])
        dst = self.o2.at[:, columns(n.half * 384, 384)]
        self.seconds = [n.copy(self.s2, dst, rep=n.partner), n.move(self.s2, dst)]

    def fourth_hop(self):
        n = self.net
        wait_all(self.firsts)
        part = self.o1.at[:, columns(n.half * FF, FF)]
        self.firsts = [n.copy(part, part, rep=n.partner)]

    def finish(self):
        wait_all(self.firsts + self.seconds)


class AttnReturn(Job):
    space = pltpu.VMEM
    inputs = ("d_w_qkv", "d_w_out")
    shapes = ((4, 48, 3 * COLS), (48, D))
    scratch = (
        (2, 4, 48, 3 * COLS), (3, 2, 48, 3 * COLS), (4, 48, 3 * COLS), (4, 48, 384), (3, 48, 384),
        (48, 384),
    )

    def bind(self, ins, outs, scratch):
        self.d1, self.d2 = ins
        self.o1, self.o2 = outs
        self.r1, self.r1z, self.s1, self.r2, self.r2z, self.s2 = scratch

    def stages(self):
        return [self.begin, self.second_hop, self.third_hop, self.fourth_hop, self.finish]

    def begin(self):
        n = self.net
        self.firsts = [n.copy(self.d1.at[pl.ds(2 * (1 - n.half), 2)], self.r1, rep=n.partner)]
        part = self.d2.at[:, :, columns((1 - n.half) * 384, 384)]
        self.seconds = [n.copy(part, self.r2, rep=n.partner)]

    def second_hop(self):
        n = self.net
        wait_all(self.firsts)
        self.r1[...] = total(self.r1[...], self.d1[pl.ds(2 * n.half, 2)])
        self.firsts = [
            n.copy(self.r1.at[:, n.plane(k)], self.r1z.at[k - 1], fsdp=n.plane(k))
            for k in (2, 1, 3)
        ]
        wait_all(self.seconds)
        self.r2[...] = total(self.r2[...], self.d2[:, :, columns(n.half * 384, 384)])
        self.seconds = [
            n.copy(self.r2.at[n.plane(k)], self.r2z.at[k - 1], fsdp=n.plane(k)) for k in (2, 1, 3)
        ]

    def third_hop(self):
        n = self.net
        wait_all(self.firsts + self.seconds)
        pair = pl.ds(2 * n.half, 2)
        self.s1[pair] = total(self.r1[:, n.z], self.r1z[0], self.r1z[1], self.r1z[2])
        self.firsts = [n.copy(self.s1.at[pair], self.s1.at[pair], rep=n.partner)]
        self.s2[...] = total(self.r2[n.z], self.r2z[0], self.r2z[1], self.r2z[2])
        dst = self.o2.at[:, columns(n.half * 384, 384)]
        self.seconds = [n.copy(self.s2, dst, rep=n.partner), n.move(self.s2, dst)]

    def fourth_hop(self):
        n = self.net
        wait_all(self.firsts)
        self.firsts = []
        for d in (3, 2, 1, 0):
            src, dst = self.s1.at[n.seq(d)], self.o1.at[n.s]
            self.firsts.append(n.move(src, dst) if d == 0 else n.copy(src, dst, seq=n.seq(d)))

    def finish(self):
        wait_all(self.firsts + self.seconds)


class AttnReturnHere(AttnReturn):
    inputs = ()
    own = (2, 3)


class SmallReturnHere(Job):
    inputs = ("small_0", "gain_1", "small_1")
    space = pltpu.VMEM
    out_space = pltpu.VMEM
    kind = f32
    own = (1,)
    shapes = ((16, D),)
    scratch = ((16, D), (16, D), (3, 16, D), (3, 16, D))

    def bind(self, ins, outs, scratch):
        self.zero, self.gain_one, self.one, self.gain = ins
        (self.out,) = outs
        self.acc, self.rx, self.rz, self.rs = scratch

    def stages(self):
        return [self.begin, self.second_hop, self.third_hop, self.finish]

    def begin(self):
        n = self.net
        self.acc[12:16] = jnp.zeros((4, D), f32)
        for at, gain, rest in ((0, self.gain, self.zero), (6, self.gain_one, self.one)):
            self.acc[at : at + 1] = gain[0:1]
            self.acc[at + 1 : at + 2] = rest[0:1]
            self.acc[at + 2 : at + 6] = rest[8:12]
        self.copies = [n.copy(self.acc, self.rx, rep=n.partner)]

    def second_hop(self):
        n = self.net
        wait_all(self.copies)
        self.rx[...] = self.acc[...] + self.rx[...]
        self.copies = [n.copy(self.rx, self.rz.at[k - 1], fsdp=n.plane(k)) for k in (2, 1, 3)]

    def third_hop(self):
        n = self.net
        wait_all(self.copies)
        self.acc[...] = self.rx[...] + self.rz[0] + self.rz[1] + self.rz[2]
        self.copies = [n.copy(self.acc, self.rs.at[d - 1], seq=n.seq(d)) for d in (3, 2, 1)]

    def finish(self):
        wait_all(self.copies)
        self.out[...] = self.acc[...] + self.rs[0] + self.rs[1] + self.rs[2]


class Background:
    def __init__(self, net, jobs, ins, own_outs, outs, scratch):
        self.queues, self.made = [], []
        for job, layer, points in jobs:
            a, b, c = len(job.inputs), len(job.shapes), len(job.scratch)
            given = list(ins[:a]) + [own_outs[i] for i in getattr(job, "own", ())]
            given += [self.made[i][1][k] for i, k in getattr(job, "linked", ())]
            made = job(net, layer, given, outs[:b], scratch[:c])
            self.made.append((made, outs[:b]))
            stages = made.stages()
            last = points[-1]
            points = tuple(points) + (last,) * (len(stages) - len(points))
            self.queues.append(list(zip(points, stages)))
            ins, outs, scratch = ins[a:], outs[b:], scratch[c:]

    def at(self, point):
        for queue in self.queues:
            while queue and queue[0][0] <= point:
                queue.pop(0)[1]()

    def drain(self):
        for point in range(9, 70):
            self.at(point)


COPIES = 160
MOVES = 64


class Late:
    def __init__(self, array):
        self.array = array


def call(kernel, inputs, outputs, scratch, jobs, shards, cid):
    given = [shards[name] for job, *_ in jobs for name in job.inputs]
    results = [
        (jax.ShapeDtypeStruct(shape, job.kind), job.out_space)
        for job, *_ in jobs
        for shape in job.shapes
    ]
    vmem, anywhere = pl.BlockSpec(memory_space=pltpu.VMEM), pl.BlockSpec(memory_space=pl.ANY)
    job_scratch = [pltpu.VMEM(shape, job.kind) for job, *_ in jobs for shape in job.scratch]
    late_in = [i for i, x in enumerate(inputs) if isinstance(x, Late)]
    arrays = [x.array if isinstance(x, Late) else x for x in inputs]
    late_out = [i for i, x in enumerate(outputs) if len(x) == 3]
    late = [pltpu.VMEM(arrays[i].shape, arrays[i].dtype) for i in late_in]
    late += [pltpu.VMEM(outputs[i][0], outputs[i][1]) for i in late_out]

    def body(*refs):
        a = len(inputs)
        b = a + len(given)
        c = b + len(outputs)
        d = c + len(results)
        e = d + len(scratch)
        f = e + len(job_scratch)
        g = f + len(late)
        net = Net(*refs[g:])
        ins, outs = list(refs[:a]), list(refs[b:c])
        net.coming, net.going = {}, []
        for i, ref in zip(late_in, refs[f:]):
            net.coming[id(ref)] = net.move(ins[i], ref)
            ins[i] = ref
        there = {}
        for i, ref in zip(late_out, refs[f + len(late_in) : g]):
            there[id(ref)] = outs[i]
            outs[i] = ref
        net.there = there
        ground = Background(net, jobs, refs[a:b], outs + list(refs[d:e]), refs[c:d], refs[e:f])
        kernel(net, ground, *ins, *outs, *refs[d:e])
        assert not net.coming and not there
        assert net.count <= COPIES and net.local_count <= MOVES
        wait_all(net.going)

    made = pl.pallas_call(
        body,
        out_shape=[jax.ShapeDtypeStruct(x[0], x[1]) for x in outputs] + [shape for shape, _ in results],
        in_specs=[anywhere if i in late_in else vmem for i in range(len(inputs))]
        + [pl.BlockSpec(memory_space=job.space) for job, *_ in jobs for _ in job.inputs],
        out_specs=[anywhere if i in late_out else vmem for i in range(len(outputs))]
        + [pl.BlockSpec(memory_space=where) for _, where in results],
        scratch_shapes=[pltpu.VMEM(shape, kind) for shape, kind in scratch]
        + job_scratch
        + late
        + [
            pltpu.SemaphoreType.DMA((COPIES,)),
            pltpu.SemaphoreType.DMA((COPIES,)),
            pltpu.SemaphoreType.DMA((MOVES,)),
        ],
        compiler_params=pltpu.CompilerParams(
            collective_id=cid, has_side_effects=True, vmem_limit_bytes=60 << 20
        ),
        cost_estimate=pl.CostEstimate(flops=0, bytes_accessed=1 << 20, transcendentals=0),
    )(*arrays, *given)
    return made[: len(outputs)], made[len(outputs) :]


def rms_rows(x):
    return lax.rsqrt(jnp.mean(x * x, -1, keepdims=True) + EPS)


def turn(x, cosine, sine):
    half = HEAD_DIM // 2
    return x * cosine + jnp.concatenate([x[:, half:], x[:, :half]], 1) * sine


def spread(small):
    lane = lax.broadcasted_iota(jnp.int32, (128, D), 0)
    col = lax.broadcasted_iota(jnp.int32, (128, D), 1)
    out = jnp.zeros((16, D), f32)
    for i in range(16):
        place = jnp.where((col == lane + 48 * i) & (lane < 48), 1.0, 0.0).astype(bf16)
        out = out + dot(small[i // 4, i % 4], place)
    return out


def attn_forward_part(layer, net, ground, h, cosine, sine, small, w_qkv, w_out, refs):
    (
        middle, second, every, queries, keys, values, attended, totals,
        near_out, near_in, away_out, away_in,
    ) = refs
    here = layer == 0
    net.greet(net.everyone())
    x = h[...].astype(f32)
    factor = rms_rows(x)
    if here:
        net.met()
        for point in (-2, -1, 0):
            ground.at(point)
        small[...] = spread(ground.made[0][1][0])
    gain_one, gain_two = small[6 * layer : 6 * layer + 1, :], small[6 * layer + 1 : 6 * layer + 2, :]
    every[net.s] = (x * factor * gain_one).astype(bf16)
    if not here:
        net.met()
        ground.at(0)
    far = net.copy(every.at[net.s], every.at[net.s], seq=net.seq(2))
    near = net.copy(every.at[net.s], every.at[net.s], seq=net.seq(1))
    ground.at(1)

    def project(b):
        joint = dot(every[b], w_qkv[...].reshape(D, 3 * COLS))
        c, sn = cosine[b], sine[b]
        for i in range(HEADS_DEV):
            at = i * HEAD_DIM
            queries[i, b] = turn(joint[:, at : at + HEAD_DIM], c, sn).astype(bf16)
            at += COLS
            keys[i, b] = turn(joint[:, at : at + HEAD_DIM], c, sn).astype(bf16)
            at += COLS
            values[i, b] = joint[:, at : at + HEAD_DIM].astype(bf16)

    if not here:
        project(net.s)
    near.wait_recv()
    ground.at(2)
    if not here:
        project(net.seq(1))
    far.wait_recv()
    passed = net.copy(every.at[net.seq(2)], every.at[net.seq(2)], seq=net.seq(1))
    ground.at(3)
    if here:
        project(net.s)
        project(net.seq(1))
    project(net.seq(2))
    passed.wait_recv()
    project(net.seq(3))
    net.done(every, queries, keys, values)
    ground.at(4)
    tokens = h.shape[0]

    def head(i):
        for b in range(SEQ):
            size = (b + 1) * tokens
            scores = dot_nt(queries[i, b], keys[i, : b + 1].reshape(size, HEAD_DIM))
            row = lax.broadcasted_iota(jnp.int32, (tokens, size), 0) + b * tokens
            col = lax.broadcasted_iota(jnp.int32, (tokens, size), 1)
            scores = jnp.where(row >= col, scores * HEAD_DIM**-0.5, MASKED)
            top = jnp.max(scores, -1, keepdims=True)
            weights = jnp.exp(scores - top)
            total = jnp.sum(weights, -1, keepdims=True)
            weights = (weights * (1.0 / total)).astype(bf16)
            attended[i, b] = dot(weights, values[i, : b + 1].reshape(size, HEAD_DIM))
            totals[i, b] = jnp.broadcast_to(top + jnp.log(total), (tokens, 128))

    for i in range(HEADS_DEV):
        head(i)
        ground.at(5 + i)
    net.done(attended, totals)

    def part(b):
        low = jnp.concatenate([attended[i, b].astype(bf16) for i in range(HEADS_DEV)], 1)
        return dot(low, w_out[...].reshape(COLS, D))

    near_out[0] = part(net.seq(1)).astype(bf16)
    near_out[1] = part(net.seq(3)).astype(bf16)
    near_sum = net.copy(near_out, near_in, seq=net.seq(1))
    away = part(net.seq(2))
    own = part(net.s)
    near_sum.wait_recv()
    away_out[...] = (away + near_in[1].astype(f32)).astype(bf16)
    away_sum = net.copy(away_out, away_in, seq=net.seq(2))
    own = h[...].astype(f32) + own + near_in[0].astype(f32)
    ground.at(8)
    away_sum.wait_recv()
    own = own + away_in[...].astype(f32)
    middle[...] = own
    second[...] = (own * rms_rows(own) * gain_two).astype(bf16)
    for copy in (far, near, passed, near_sum, away_sum):
        copy.wait_send()


def silu_gate(g, u):
    return g / (1.0 + jnp.exp(-g)) * u


CHUNKS = ((0, 64), (64, 80))


class SlotTrip:
    def __init__(self, net, out, into):
        self.net, self.into = net, into
        self.sent, self.passed = {}, {}
        for c, (at, size) in enumerate(CHUNKS):
            for k in (2, 1, 3):
                e = net.plane(k)
                self.sent[c, k] = net.copy(
                    out.at[e, pl.ds(at, size)], into.at[net.core, net.z, pl.ds(at, size)], fsdp=e
                )
        into[net.core, net.z] = out[net.z]

    def hand_on(self, c):
        net, (at, size) = self.net, CHUNKS[c]
        self.passed[c] = []
        for k in (0, 1, 3, 2):
            if k:
                self.sent[c, k].wait_recv()
            part = self.into.at[net.core, net.plane(FSDP - k), pl.ds(at, size)]
            self.passed[c].append(net.copy(part, part, seq=net.seq(1)))

    def here(self, c):
        for copy in self.passed[c]:
            copy.wait_recv()

    def close(self):
        for copy in [*self.sent.values(), *self.passed[0], *self.passed[1]]:
            copy.wait_send()


class SlotReturn:
    def __init__(self, net, out, into, own, back, home):
        self.net, self.out, self.into, self.own = net, out, into, own
        self.back, self.home = back, home
        self.near, self.sent = {}, []

    def other(self, c, rows):
        at, size = CHUNKS[c]
        self.out[:, at : at + size] = rows.astype(bf16).reshape(EXPERTS, size, D)
        part = pl.ds(at, size)
        self.near[c] = self.net.copy(self.out.at[:, part], self.into.at[:, part], seq=self.net.seq(1))

    def mine(self, c, rows):
        net, (at, size) = self.net, CHUNKS[c]
        self.own[0 : EXPERTS * size] = rows
        self.near[c].wait_recv()
        got = self.into[:, at : at + size].astype(f32).reshape(EXPERTS * size, D)
        both = (self.own[0 : EXPERTS * size] + got).astype(bf16)
        self.back[:, at : at + size] = both.reshape(EXPERTS, size, D)
        for k in (2, 1, 3):
            e = net.plane(k)
            part = pl.ds(at, size)
            self.sent.append(net.copy(self.back.at[e, part], self.home.at[net.z, part], fsdp=e))
        self.home[net.z, at : at + size] = self.back[net.z, at : at + size]

    def wait(self):
        for copy in self.sent:
            copy.wait_recv()

    def close(self):
        for copy in [*self.sent, *self.near.values()]:
            copy.wait_send()


def ffn_forward_part(layer, net, ground, second, middle, small, onehot, chosen, jobs, refs):
    (
        result, gates, gathered, every, joint, hidden, rows, joint_e, hidden_e,
        rows_out, prod_out, prod_in, prod_own, back_out, yields, near_out, near_in, away_out,
        away_in, w_in, w_so, router,
    ) = refs
    t = second.shape[0]
    shared_job, join = jobs
    w1, w2 = join.w1, join.w2
    picked = chosen[:, :t] + chosen[:, t:]
    rows_out[...] = dot(picked, second[...]).astype(bf16).reshape(EXPERTS, CAP, D)
    every[net.s] = second[...]
    trip = SlotTrip(net, rows_out, rows)
    far = net.copy(every.at[net.s], every.at[net.s], seq=net.seq(2))
    near = net.copy(every.at[net.s], every.at[net.s], seq=net.seq(1))
    ground.at(30)
    loads = [net.move(shared_job.w_in, w_in), net.move(shared_job.w_out, w_so)]
    router[4:8, :] = jnp.zeros((4, D), f32)
    router[0:4, :] = small[6 * layer + 2 : 6 * layer + 6, :]
    logits = dot_nt(second[...], router[...].astype(bf16))
    l0 = jnp.sum(onehot[0, :, 0:8] * logits, -1, keepdims=True)
    l1 = jnp.sum(onehot[1, :, 0:8] * logits, -1, keepdims=True)
    top = jnp.maximum(l0, l1)
    e0, e1 = jnp.exp(l0 - top), jnp.exp(l1 - top)
    g0, g1 = e0 / (e0 + e1), e1 / (e0 + e1)
    lane = lax.broadcasted_iota(jnp.int32, (t, 128), 1)
    gates[...] = jnp.where(lane == 0, g0, jnp.where(lane == 1, g1, 0.0))
    wait_all(loads)

    def shared(b):
        g, u = dot(every[b], w_in[0].reshape(D, FF_DEV)), dot(every[b], w_in[1].reshape(D, FF_DEV))
        joint[0, b] = g.astype(bf16)
        joint[1, b] = u.astype(bf16)
        low = silu_gate(g, u).astype(bf16)
        hidden[b] = low
        return dot(low, w_so[...].reshape(FF_DEV, D))

    own_part = shared(net.s)
    ground.at(31)
    near.wait_recv()
    near_out[0] = shared(net.seq(1)).astype(bf16)
    far.wait_recv()
    passed_far = net.copy(every.at[net.seq(2)], every.at[net.seq(2)], seq=net.seq(1))
    away_out[...] = shared(net.seq(2)).astype(bf16)
    trip.hand_on(0)
    ground.at(32)
    passed_far.wait_recv()
    near_out[1] = shared(net.seq(3)).astype(bf16)
    near_sum = net.copy(near_out, near_in, seq=net.seq(1))
    net.done(every, joint, hidden)

    def expert(core, c):
        at, size = CHUNKS[c]
        part = slice(at, at + size)
        x = rows[core, :, part].reshape(EXPERTS * size, D)
        total = None
        for half in (0, 1):
            g = dot(x, w1[half, 0].reshape(D, FF_DEV))
            u = dot(x, w1[half, 1].reshape(D, FF_DEV))
            shape = (EXPERTS, size, FF_DEV)
            joint_e[core, half, 0, :, part] = g.astype(bf16).reshape(shape)
            joint_e[core, half, 1, :, part] = u.astype(bf16).reshape(shape)
            low = silu_gate(g, u).astype(bf16)
            hidden_e[core, half, :, part] = low.reshape(shape)
            new = dot(low, w2[half].reshape(FF_DEV, D))
            total = new if total is None else total + new
        return total

    trip.here(0)
    ground.at(33)
    back = SlotReturn(net, prod_out, prod_in, prod_own, back_out, yields)
    back.other(0, expert(1 - net.core, 0))
    trip.hand_on(1)
    near_sum.wait_recv()
    away_out[...] = (away_out[...].astype(f32) + near_in[1].astype(f32)).astype(bf16)
    away_sum = net.copy(away_out, away_in, seq=net.seq(2))
    ground.at(34)
    back.mine(0, expert(net.core, 0))
    ground.at(35)
    trip.here(1)
    back.other(1, expert(1 - net.core, 1))
    back.mine(1, expert(net.core, 1))
    net.done(rows, joint_e, hidden_e)
    ground.at(36)
    away_sum.wait_recv()
    base = middle[...] + own_part + near_in[0].astype(f32) + away_in[...].astype(f32)
    back.wait()
    got = dot_tn(chosen[...], yields[...].reshape(SLOTS, D))
    gathered[...] = got.astype(bf16)
    result[...] = base + g0 * got[:t] + g1 * got[t:]
    for copy in [far, near, passed_far, near_sum, away_sum]:
        copy.wait_send()
    trip.close()
    back.close()


def layer_forward_kernel(layer, places, net, ground, h, cosine, sine, onehot, chosen, *refs):
    if layer == 0:
        small, *refs = refs
        w_qkv, w_out = ground.made[1][1]
    else:
        small, w_qkv, w_out, *refs = refs
    attn, ffn = refs[:8] + refs[17:21], refs[8:17] + refs[21:]
    attn_forward_part(layer, net, ground, h, cosine, sine, small, w_qkv, w_out, attn)
    jobs = [ground.made[i][0] for i in places]
    ffn_forward_part(layer, net, ground, attn[1], attn[0], small, onehot, chosen, jobs, ffn)
    ground.drain()


def layer_forward(layer, h, tables, onehot, chosen, small, weights, jobs, shards, cid):
    t = h.shape[0]
    head = (HEADS_DEV, SEQ, t, HEAD_DIM)
    slots = (EXPERTS, CAP, FF_DEV)
    sums = [((2, t, D), bf16), ((2, t, D), bf16), ((t, D), bf16), ((t, D), bf16)]
    names = [job.__name__ for job, *_ in jobs]
    places = (names.index("SharedFetch"), names.index("JoinNext" if layer else "JoinFirst"))
    return call(
        functools.partial(layer_forward_kernel, layer, places),
        [h, *tables, onehot, chosen] + ([small, *weights] if layer else []),
        ([] if layer else [((16, D), f32)])
        + [
            ((t, D), f32), ((t, D), bf16), ((SEQ, t, D), bf16, 1), (head, bf16, 1), (head, bf16, 1),
            (head, bf16, 1), (head, f32, 1), ((HEADS_DEV, SEQ, t, 128), f32, 1),
        ]
        + [
            ((t, D), f32), ((t, 128), f32), ((2 * t, D), bf16), ((SEQ, t, D), bf16, 1),
            ((2, SEQ, t, FF_DEV), bf16, 1), ((SEQ, t, FF_DEV), bf16, 1),
            ((2, EXPERTS, CAP, D), bf16, 1), ((2, 2, 2, *slots), bf16, 1), ((2, 2, *slots), bf16, 1),
        ],
        sums
        + [
            ((EXPERTS, CAP, D), bf16), ((EXPERTS, CAP, D), bf16), ((EXPERTS, CAP, D), bf16),
            ((EXPERTS * CHUNKS[1][1], D), f32), ((EXPERTS, CAP, D), bf16),
            ((EXPERTS, CAP, D), bf16),
        ]
        + sums
        + [((2, 4, 4, 48, FF_DEV), bf16), ((4, 128, D), bf16), ((8, D), f32)],
        jobs, shards, cid,
    )


def norm_back(x, gain, gradient):
    factor = rms_rows(x)
    weighted = gradient * gain
    inner = jnp.mean(weighted * x, -1, keepdims=True)
    d_x = factor * weighted - x * (factor * factor * factor) * inner
    return d_x, jnp.sum(gradient * x * factor, 0, keepdims=True)


def gate_back(g, u, gradient):
    sig = 1.0 / (1.0 + jnp.exp(-g))
    d_g = gradient * u * sig * (1.0 + g * (1.0 - sig))
    return d_g.astype(bf16), (gradient * g * sig).astype(bf16)


def ffn_backward_kernel(
    net, ground, grad, gates, onehot, chosen, gathered, middle, second, gains, router, every,
    joint, hidden, rows, joint_e, hidden_e, w_in, w_so, w1, w2,
    d_middle, small, d_w1, d_w2,
    every_g, d_joint, rows_out, d_rows, d_joint_e, prod_out, prod_in, prod_own, back_out, back_in,
    near_out, near_in, away_out, away_in, d_w_in, d_w_so,
):
    t = grad.shape[0]
    net.greet(net.everyone())
    g0, g1 = gates[:, 0:1], gates[:, 1:2]
    up = grad[...].astype(f32)
    pairs = jnp.concatenate([(up * g0).astype(bf16), (up * g1).astype(bf16)], 0)
    rows_out[...] = dot(chosen[...], pairs).astype(bf16).reshape(EXPERTS, CAP, D)
    every_g[net.s] = up.astype(bf16)
    net.met()
    trip = SlotTrip(net, rows_out, d_rows)
    far = net.copy(every_g.at[net.s], every_g.at[net.s], seq=net.seq(2))
    near = net.copy(every_g.at[net.s], every_g.at[net.s], seq=net.seq(1))
    ground.at(0)
    net.need(w_so, joint, w_in)

    def shared(b):
        d_hidden = dot_nt(every_g[b], w_so[...])
        d_g, d_u = gate_back(joint[0, b].astype(f32), joint[1, b].astype(f32), d_hidden)
        d_joint[0, b] = d_g
        d_joint[1, b] = d_u
        return dot_nt(d_g, w_in[0]) + dot_nt(d_u, w_in[1])

    local = shared(net.s)
    ground.at(1)
    near.wait_recv()
    near_out[0] = shared(net.seq(1)).astype(bf16)
    far.wait_recv()
    passed_far = net.copy(every_g.at[net.seq(2)], every_g.at[net.seq(2)], seq=net.seq(1))
    away_out[...] = shared(net.seq(2)).astype(bf16)
    trip.hand_on(0)
    ground.at(2)
    passed_far.wait_recv()
    near_out[1] = shared(net.seq(3)).astype(bf16)
    near_sum = net.copy(near_out, near_in, seq=net.seq(1))
    net.need(every, hidden)
    tokens = every[...].reshape(SEQ * t, D)
    for gu in (0, 1):
        d_w = dot_tn(tokens, d_joint[gu].reshape(SEQ * t, FF_DEV))
        d_w_in[gu] = d_w.astype(bf16).reshape(4, 4, 48, FF_DEV)
    d_w = dot_tn(hidden[...].reshape(SEQ * t, FF_DEV), every_g[...].reshape(SEQ * t, D))
    d_w_so[...] = d_w.astype(bf16).reshape(4, 128, D)
    net.need(w2, w1, joint_e)

    def expert(core, c):
        at, size = CHUNKS[c]
        part = slice(at, at + size)
        x = d_rows[core, :, part].reshape(EXPERTS * size, D)
        out = None
        for half in (0, 1):
            d_hidden = dot_nt(x, w2[half].reshape(FF_DEV, D))
            flat, shape = (EXPERTS * size, FF_DEV), (EXPERTS, size, FF_DEV)
            g = joint_e[core, half, 0, :, part].astype(f32).reshape(flat)
            u = joint_e[core, half, 1, :, part].astype(f32).reshape(flat)
            d_g, d_u = gate_back(g, u, d_hidden)
            d_joint_e[half, 0, core, :, part] = d_g.reshape(shape)
            d_joint_e[half, 1, core, :, part] = d_u.reshape(shape)
            new = dot_nt(d_g, w1[half, 0].reshape(D, FF_DEV))
            new = new + dot_nt(d_u, w1[half, 1].reshape(D, FF_DEV))
            out = new if out is None else out + new
        return out

    trip.here(0)
    ground.at(3)
    back = SlotReturn(net, prod_out, prod_in, prod_own, back_out, back_in)
    back.other(0, expert(1 - net.core, 0))
    trip.hand_on(1)
    near_sum.wait_recv()
    away_out[...] = (away_out[...].astype(f32) + near_in[1].astype(f32)).astype(bf16)
    away_sum = net.copy(away_out, away_in, seq=net.seq(2))
    ground.at(4)
    back.mine(0, expert(net.core, 0))
    ground.at(5)
    trip.here(1)
    back.other(1, expert(1 - net.core, 1))
    back.mine(1, expert(net.core, 1))
    ground.at(6)
    net.need(rows, hidden_e)
    for half in (0, 1):
        d_rows_all = d_rows[...].reshape(2 * SLOTS, D)
        for gu in (0, 1):
            d_w = dot_tn(
                rows[...].reshape(2 * SLOTS, D), d_joint_e[half, gu].reshape(2 * SLOTS, FF_DEV)
            )
            d_w1[half, gu] = d_w.astype(bf16).reshape(4, 4, 48, FF_DEV)
        low = jnp.concatenate(
            [hidden_e[core, half].reshape(SLOTS, FF_DEV) for core in (0, 1)], 0
        )
        d_w2[half] = dot_tn(low, d_rows_all).astype(bf16).reshape(4, 128, D)
        ground.at(7 + half)
    net.done(d_w1, d_w2)
    net.need(gathered, onehot, second, router, middle)
    d0 = jnp.sum(up * gathered[:t].astype(f32), -1, keepdims=True)
    d1 = jnp.sum(up * gathered[t:].astype(f32), -1, keepdims=True)
    mean = g0 * d0 + g1 * d1
    d_logits = (g0 * (d0 - mean) * onehot[0] + g1 * (d1 - mean) * onehot[1]).astype(bf16)
    small[8:16, :] = dot_tn(d_logits, second[...])[:8]
    local = local + dot_nt(d_logits, router[...])
    away_sum.wait_recv()
    local = local + near_in[0].astype(f32) + away_in[...].astype(f32)
    back.wait()
    picked = chosen[:, :t] + chosen[:, t:]
    d_normed = local + dot_tn(picked, back_in[...].reshape(SLOTS, D))
    d_x, d_gain = norm_back(middle[...], gains[1:2, :], d_normed)
    d_middle[...] = up + d_x
    small[0:8, :] = jnp.broadcast_to(d_gain, (8, D))
    for copy in [far, near, passed_far, near_sum, away_sum]:
        copy.wait_send()
    trip.close()
    back.close()
    ground.drain()


def ffn_backward(grad, saved, gains, router, weights, jobs, shards, cid):
    t = grad.shape[0]
    gates, onehot, chosen, gathered, middle, second, every, joint, hidden, rows, joint_e, hidden_e = saved
    w_in, w_so, w1, w2 = weights
    slots = (EXPERTS, CAP, D)
    late = {}
    for name, x in (
        ("w_so", w_so), ("joint", joint), ("w_in", w_in), ("every", every), ("hidden", hidden),
        ("w2", w2), ("joint_e", joint_e), ("w1", w1), ("rows", rows), ("hidden_e", hidden_e),
        ("gathered", gathered), ("onehot", onehot), ("second", second), ("router", router),
        ("middle", middle),
    ):
        late[name] = Late(x)
    return call(
        ffn_backward_kernel,
        [
            grad, gates, late["onehot"], chosen, late["gathered"], late["middle"], late["second"],
            gains, late["router"], late["every"], late["joint"], late["hidden"], late["rows"],
            late["joint_e"], late["hidden_e"], late["w_in"], late["w_so"], late["w1"], late["w2"],
        ],
        [
            ((t, D), f32), ((16, D), f32), ((2, 2, 4, 4, 48, FF_DEV), bf16, 1),
            ((2, 4, 128, D), bf16, 1),
        ],
        [
            ((SEQ, t, D), bf16), ((2, SEQ, t, FF_DEV), bf16), (slots, bf16), ((2, *slots), bf16),
            ((2, 2, 2, EXPERTS, CAP, FF_DEV), bf16), (slots, bf16), (slots, bf16),
            ((EXPERTS * CHUNKS[1][1], D), f32), (slots, bf16), (slots, bf16), ((2, t, D), bf16),
            ((2, t, D), bf16), ((t, D), bf16), ((t, D), bf16), ((2, 4, 4, 48, FF_DEV), bf16),
            ((4, 128, D), bf16),
        ],
        jobs, shards, cid,
    )


def attn_backward_kernel(
    net, ground, d_middle, h, gains, every, queries, keys, values, attended, totals, w_qkv, w_out,
    cosine, sine,
    grad, d_gain, d_w_qkv, d_w_out,
    every_m, d_att, d_q, d_k, d_v, d_joint, near_out, near_in, away_out, away_in,
):
    t = h.shape[0]
    net.greet(net.everyone())
    up = d_middle[...]
    every_m[net.s] = up.astype(bf16)
    net.met()
    far = net.copy(every_m.at[net.s], every_m.at[net.s], seq=net.seq(2))
    near = net.copy(every_m.at[net.s], every_m.at[net.s], seq=net.seq(1))
    ground.at(0)

    net.need(w_out)

    def project(b):
        d = dot_nt(every_m[b], w_out[...].reshape(COLS, D)).astype(bf16)
        for i in range(HEADS_DEV):
            d_att[i, b] = d[:, i * HEAD_DIM : (i + 1) * HEAD_DIM]

    project(net.s)
    near.wait_recv()
    project(net.seq(1))
    far.wait_recv()
    passed = net.copy(every_m.at[net.seq(2)], every_m.at[net.seq(2)], seq=net.seq(1))
    project(net.seq(2))
    passed.wait_recv()
    project(net.seq(3))
    ground.at(1)
    net.need(attended)
    tokens = every_m[...].reshape(SEQ * t, D)
    low = jnp.concatenate(
        [attended[i].reshape(SEQ * t, HEAD_DIM).astype(bf16) for i in range(HEADS_DEV)], 1
    )
    d_w_out[...] = dot_tn(low, tokens).astype(bf16).reshape(SEQ, 48, D)
    scale = HEAD_DIM**-0.5
    net.need(queries, keys, values, totals)

    def head(i):
        d_k[i] = jnp.zeros_like(d_k[i])
        d_v[i] = jnp.zeros_like(d_v[i])
        for b in range(SEQ):
            size = (b + 1) * t
            q, d = queries[i, b], d_att[i, b]
            k = keys[i, : b + 1].reshape(size, HEAD_DIM)
            v = values[i, : b + 1].reshape(size, HEAD_DIM)
            delta = jnp.sum(d.astype(f32) * attended[i, b], -1, keepdims=True)
            row = lax.broadcasted_iota(jnp.int32, (t, size), 0) + b * t
            col = lax.broadcasted_iota(jnp.int32, (t, size), 1)
            scores = jnp.where(row >= col, dot_nt(q, k) * scale, MASKED)
            weights = jnp.exp(scores - totals[i, b][:, 0:1])
            d_scores = (weights * (dot_nt(d, v) - delta)).astype(bf16)
            d_q[i, b] = dot(d_scores, k) * scale
            shape = (b + 1, t, HEAD_DIM)
            d_k[i, : b + 1] += (dot_tn(d_scores, q) * scale).reshape(shape)
            d_v[i, : b + 1] += dot_tn(weights.astype(bf16), d).reshape(shape)

    for i in range(HEADS_DEV):
        head(i)
        ground.at(2 + i)

    net.need(cosine, sine, w_qkv)

    def part(b):
        c, sn = cosine[b], -sine[b]
        pieces = [turn(d_q[i, b], c, sn) for i in range(HEADS_DEV)]
        pieces += [turn(d_k[i, b], c, sn) for i in range(HEADS_DEV)]
        pieces += [d_v[i, b] for i in range(HEADS_DEV)]
        d = jnp.concatenate(pieces, 1).astype(bf16)
        d_joint[b] = d
        return dot_nt(d, w_qkv[...].reshape(D, 3 * COLS))

    near_out[0] = part(net.seq(1)).astype(bf16)
    near_out[1] = part(net.seq(3)).astype(bf16)
    near_sum = net.copy(near_out, near_in, seq=net.seq(1))
    away = part(net.seq(2))
    own = part(net.s)
    near_sum.wait_recv()
    away_out[...] = (away + near_in[1].astype(f32)).astype(bf16)
    away_sum = net.copy(away_out, away_in, seq=net.seq(2))
    own = own + near_in[0].astype(f32)
    ground.at(5)
    net.need(every)
    d_w = dot_tn(every[...].reshape(SEQ * t, D), d_joint[...].reshape(SEQ * t, 3 * COLS))
    d_w_qkv[...] = d_w.astype(bf16).reshape(4, 4, 48, 3 * COLS)
    ground.at(6)
    away_sum.wait_recv()
    net.need(h)
    d_x, gain = norm_back(h[...].astype(f32), gains[0:1, :], own + away_in[...].astype(f32))
    grad[...] = up + d_x
    row = lax.broadcasted_iota(jnp.int32, (8, D), 0)
    d_gain[...] = jnp.where(row == 0, gain, 0.0)
    ground.at(7)
    for copy in (far, near, passed, near_sum, away_sum):
        copy.wait_send()
    ground.drain()


def attn_backward(d_middle, saved, gains, weights, tables, jobs, shards, cid):
    t = d_middle.shape[0]
    h, every, queries, keys, values, attended, totals = saved
    head = (HEADS_DEV, SEQ, t, HEAD_DIM)
    return call(
        attn_backward_kernel,
        [d_middle, Late(h), gains]
        + [Late(x) for x in (every, queries, keys, values, attended, totals, *weights, *tables)],
        [((t, D), f32), ((8, D), f32), ((4, 4, 48, 3 * COLS), bf16), ((4, 48, D), bf16)],
        [
            ((SEQ, t, D), bf16), (head, bf16), (head, f32), (head, f32), (head, f32),
            ((SEQ, t, 3 * COLS), bf16), ((2, t, D), bf16), ((2, t, D), bf16), ((t, D), bf16),
            ((t, D), bf16),
        ],
        jobs, shards, cid,
    )


FORWARD_FIRST = (
    (SmallFetch, 0, (-2, -1, 0)),
    (AttnFetchHere, 0, (-2, -1, 2, 3)),
    (ExpertFetch, 0, (-2, 3, 30)),
    (SharedFetch, 0, (1, 3, 7, 30)),
    (JoinFirst, 0, (30, 33, 39)),
    (ExpertPlane, 1, (8, 40)),
    (AttnFetch, 1, (30, 33, 36, 40)),
)
FORWARD_NEXT = (
    (ExpertNear, 1, (2, 30)),
    (SharedFetch, 1, (0, 1, 4, 30)),
    (JoinNext, 1, (30, 33, 39)),
)
BACKWARD_FFN_FIRST = ((SharedAcross, 1, (3, 9)),)
BACKWARD_ATTN = (
    (GateToPlane, 1, (0, 3, 5, 9)),
    (UpToPlane, 1, (0, 3, 5, 9)),
    (SecondToPlane, 1, (0, 4, 6, 9)),
    (SharedReturn, 1, (0, 4, 5, 9)),
)
BACKWARD_FFN = (
    (SharedAcross, 0, (3, 9)),
    (AttnReturn, 1, (0, 3, 6, 8, 9)),
    (GateFinal, 1, (0, 9)),
    (UpFinal, 1, (0, 9)),
    (SecondFinal, 1, (0, 9)),
)
BACKWARD_ATTN_LAST = (
    (GateReturn, 0, (0, 3, 5, 9, 11)),
    (UpReturn, 0, (0, 3, 5, 9, 11)),
    (SharedReturn, 0, (0, 4, 5, 11)),
    (SecondReturn, 0, (0, 4, 6, 9, 11)),
    (AttnReturnHere, 0, (6, 9, 10, 11, 12)),
    (SmallReturnHere, 0, (7, 8, 9, 10)),
)


def local(
    reps, inputs, expert_choice, pair_order, norm_gains, attn_qkv, attn_out, router, shared_in,
    shared_out, expert_in, expert_out, cotangent,
):
    r, s, z = lax.axis_index("rep"), lax.axis_index("seq"), lax.axis_index("fsdp")
    tokens = inputs.shape[1]
    half = HEAD_DIM // 2
    inverse = np.exp(-np.log(np.float32(10000.0)) * np.arange(half, dtype=np.float32) * np.float32(2.0 / HEAD_DIM))
    angle = np.arange(SEQ * tokens, dtype=np.float32)[:, None] * inverse.astype(np.float32)[None, :]
    cosine, sine = np.cos(angle.astype(np.float64)), np.sin(angle.astype(np.float64))
    shape = (SEQ, tokens, HEAD_DIM)
    table_cos = jnp.asarray(np.concatenate([cosine, cosine], -1).reshape(shape), f32)
    table_sin = jnp.asarray(np.concatenate([-sine, sine], -1).reshape(shape), f32)
    small = jnp.concatenate([norm_gains, router.transpose(0, 2, 1)], 1).reshape(12, 48)
    shards = {
        "small": jnp.pad(small, ((0, 4), (0, 80))),
        "attn_qkv": attn_qkv.reshape(LAYERS, 48, 3, SEQ, COLS)
        .transpose(0, 3, 1, 2, 4)
        .reshape(LAYERS, SEQ, 48, 3 * COLS),
        "attn_out": attn_out,
        "shared_in": shared_in,
        "shared_out": shared_out,
        "expert_in": expert_in,
        "expert_out": expert_out,
    }
    h = inputs[0]
    kept_layers = []
    tables = (table_cos, table_sin)
    attn, gains, small = (), [None] * LAYERS, None
    for layer in range(LAYERS):
        first = layer == 0
        routes = routing(expert_choice[layer, 0], pair_order[layer, 0, 0])
        onehot = expert_choice[layer, 0].T[..., None] == jnp.arange(128, dtype=jnp.int32)
        onehot = onehot.astype(f32)
        outs, fetched = layer_forward(
            layer, h, tables, onehot, routes[1], small, attn, FORWARD_FIRST if first else FORWARD_NEXT,
            shards, 12 + layer,
        )
        if first:
            small, *outs = outs
            spread_small = small[:12].reshape(LAYERS, 6, D)
            gains, routers = spread_small[:, :2], spread_small[:, 2:].astype(bf16)
            attn, shared, w1, w2 = fetched[1:3], fetched[9:11], fetched[11], fetched[12]
            shards["next_p1"], shards["next_p2"] = fetched[13:15]
            next_attn = fetched[15:17]
        else:
            shared, w1, w2 = fetched[4:6], fetched[6], fetched[7]
        middle, second, every_one, queries, keys, values, attended, totals = outs[:8]
        result, gates, gathered, every_two, joint, hidden, rows, joint_e, hidden_e = outs[8:]
        w_in, w_so = shared[0].reshape(2, D, FF_DEV), shared[1].reshape(FF_DEV, D)
        router_pad = jnp.pad(routers[layer].T, ((0, 0), (0, 124)))
        attn_weights, ffn_weights = attn, (w_in, w_so, w1, w2)
        if first:
            attn = next_attn
        attn_saved = (h, every_one, queries, keys, values, attended, totals)
        ffn_saved = (
            gates, onehot, routes[1], gathered, middle, second, every_two, joint, hidden, rows,
            joint_e, hidden_e,
        )
        h = result
        kept_layers.append((attn_weights, ffn_weights, attn_saved, ffn_saved, router_pad))
    output = h.astype(bf16)[None]
    grad = cotangent[0]
    returned = {}
    grads = {}
    for layer in reversed(range(LAYERS)):
        last = layer == 0
        attn_weights, ffn_weights, attn_saved, ffn_saved, router_pad = kept_layers[layer]
        (d_middle, small, grads["d_w1"], grads["d_w2"]), done = ffn_backward(
            grad, ffn_saved, gains[layer], router_pad, ffn_weights,
            BACKWARD_FFN if last else BACKWARD_FFN_FIRST, grads, 18 + layer,
        )
        grads["r1"], grads["r2"] = done[:2]
        if last:
            returned["d_attn", 1], returned["d_expert", 1] = done[2:4], done[4:]
        grads[f"small_{layer}"] = small
        (grad, d_gain, d_w_qkv, d_w_out), done = attn_backward(
            d_middle, attn_saved, gains[layer], attn_weights, tables,
            BACKWARD_ATTN_LAST if last else BACKWARD_ATTN, grads, 16 + layer,
        )
        if last:
            returned["d_expert", 0], returned["d_shared", 0] = [*done[:2], done[4]], done[2:4]
            returned["d_attn", 0], total_small = done[5:7], done[7]
        else:
            grads["q_gate"], grads["q_up"], grads["q_second"] = done[:3]
            returned["d_shared", 1] = done[3:]
            grads["d_w_qkv"], grads["d_w_out"], grads["gain_1"] = d_w_qkv, d_w_out, d_gain
    total_small = rep_rest(total_small, reps)[:12].reshape(LAYERS, 6, D)
    total_small = lax.dynamic_slice_in_dim(total_small, (s * FSDP + z) * 48, 48, 2)

    def stack(name, k):
        return jnp.stack([rep_rest(returned[name, i][k], reps) for i in range(LAYERS)]).astype(f32)

    d_qkv = stack("d_attn", 0).reshape(LAYERS, SEQ, 48, 3, COLS).transpose(0, 2, 3, 1, 4)
    return (
        output, grad[None], total_small[:, :2], d_qkv.reshape(LAYERS, 48, 3 * D),
        stack("d_attn", 1), total_small[:, 2:].transpose(0, 2, 1), stack("d_shared", 0),
        stack("d_shared", 1), jnp.concatenate([stack("d_expert", 0), stack("d_expert", 1)], -1),
        stack("d_expert", 2),
    )


def solution(mesh):
    tokens = P(("rep", "fsdp"), "seq", None)
    routes = P(None, ("rep", "fsdp"), "seq", None)
    gains = P(None, None, ("seq", "fsdp"))
    dense = P(None, ("seq", "fsdp"), None)
    expert = P(None, None, ("seq", "fsdp"), None)
    in_specs = (
        tokens, routes, routes, gains, dense, dense, dense, dense, dense, expert, expert, tokens,
    )
    out_specs = (tokens, tokens, gains, dense, dense, dense, dense, dense, expert, expert)
    return jax.shard_map(
        functools.partial(local, mesh.shape["rep"]),
        mesh=mesh, in_specs=in_specs, out_specs=out_specs, check_vma=False,
    )
```
